32 devices in a mesh: dp: 2 (over core), expert: 4 (over z), tensor: 4 (over y, x).
Axes of the slice: x: 2, y: 2, z: 4, core: 2. Of those that a mesh axis runs over, the one named last changes fastest.
Arguments:
- tokens: bfloat16 [12288, 768], P(('dp', 'expert', 'tensor')), may hold values from -6 to 6
- cotangent: bfloat16 [12288, 768], P(('dp', 'expert', 'tensor')), may hold values from -6 to 6
- query_key_value_weight: bfloat16 [3, 768, 768], P(None, ('dp', 'expert'), 'tensor'), may hold values from -0.21875 to 0.21875
- attention_output_weight: bfloat16 [768, 768], P('tensor', ('dp', 'expert')), may hold values from -2 to 2
- rel_bias: bfloat16 [12, 32], P('tensor'), may hold values from -6 to 6
- gain_attn: bfloat16 [768], P(('dp', 'expert', 'tensor')), may hold values from 0.5 to 1.5
- gain_moe: bfloat16 [768], P(('dp', 'expert', 'tensor')), may hold values from 0.5 to 1.5
- w_router: bfloat16 [768, 16], P(('dp', 'expert', 'tensor')), may hold values from -0.109375 to 0.109375
- w_in: bfloat16 [16, 768, 3072], P('expert', 'dp', 'tensor'), may hold values from -0.21875 to 0.21875
- w_out: bfloat16 [16, 3072, 768], P('expert', 'tensor', 'dp'), may hold values from -3 to 3
- expert_index: int32 [12288], P(('dp', 'expert', 'tensor')), may hold values from 0 to 15, as said below
- slot_index: int32 [12288], P(('dp', 'expert', 'tensor')), may hold values from 0 to 35, as said below
- kept_mask: int32 [12288], P(('dp', 'expert', 'tensor')), may hold values from 0 to 1, as said below
Outputs:
- output: bfloat16 [12288, 768], P(('dp', 'expert', 'tensor'))
- grad_tokens: float32 [12288, 768], P(('dp', 'expert', 'tensor'))
- grad_w_qkv: float32 [3, 768, 768], P(None, ('dp', 'expert'), 'tensor')
- grad_w_attn_out: float32 [768, 768], P('tensor', ('dp', 'expert'))
- grad_rel_bias: float32 [12, 32], P('tensor')
- grad_gain_attn: float32 [768], P(('dp', 'expert', 'tensor'))
- grad_gain_moe: float32 [768], P(('dp', 'expert', 'tensor'))
- grad_w_router: float32 [768, 16], P(('dp', 'expert', 'tensor'))
- grad_w_in: float32 [16, 768, 3072], P('expert', 'dp', 'tensor')
- grad_w_out: float32 [16, 3072, 768], P('expert', 'tensor', 'dp')
The draws below stay inside these ranges and needn't reach their ends.
Inputs may be any that keep to these rules, and one draw needn't show every extreme that they name: `expert_index`: in every aligned block of 384 rows (the rows of one device) some expert is named by more than 36 rows. `slot_index`: the number of earlier rows of the same block of 384 rows (the rows of one device) with the same expert, or 35 where that number is 36 or more. `kept_mask`: 1 where that number of earlier rows is below 36, else 0.
All inputs are finite; a program needn't handle non-finite values.
Results may differ from the reference program's by a relative error of at most 0.024.
Values may be sent and summed in bfloat16 or wider, within the bound.
No kernel may reach another device: no remote copies, remote signals or barrier semaphores. Data moves between devices by JAX's collectives and lax.ppermute only.
A program may use at most 128 MiB of HBM per device.

```python
import jax
import jax.numpy as jnp
from jax import lax

D = 768
HEADS = 12
HEAD_DIM = 64
FF = 3072
BUCKETS = 32
LENGTH = 512
TOK_DEV = 384
EXPERTS = 16
CAP = 36
GROUP_SEQS = 3
TOKENS = 12288


def routing(key):
    blocks = TOKENS // TOK_DEV
    key_hot, key_base, key_order = jax.random.split(key, 3)
    hottest = jax.random.randint(key_hot, (), 0, EXPERTS, dtype=jnp.int32)
    base_route = jax.random.randint(key_base, (blocks, TOK_DEV), 0, EXPERTS, dtype=jnp.int32)

    def shuffled(single_key):
        return jax.random.permutation(single_key, TOK_DEV)
    orders = jax.vmap(shuffled)(jax.random.split(key_order, blocks))
    crowd = CAP + CAP // 2 + 1
    routes_all = jnp.where(orders < crowd, hottest, base_route).astype(jnp.int32)

    def ranks(block_routes):
        chosen = (block_routes[:, None] == jnp.arange(EXPERTS, dtype=jnp.int32)[None, :]).astype(jnp.int32)
        before = jnp.cumsum(chosen, axis=0) - chosen
        return jnp.sum(before * chosen, axis=1)
    placed = lax.map(ranks, routes_all)
    kept_all = (placed < CAP).astype(jnp.int32)
    slots = jnp.minimum(placed, CAP - 1).astype(jnp.int32)
    return (routes_all.reshape(-1), slots.reshape(-1), kept_all.reshape(-1))


def draw_expert_index(key, part):
    return routing(key)[0]


def draw_slot_index(key, part):
    return routing(key)[1]


def draw_kept_mask(key, part):
    return routing(key)[2]


def level_of(stream_key, dims, shards, least, top_value):
    factor_of = 1.0
    for dim, parts in shards:
        steps = jax.random.uniform(jax.random.fold_in(jax.random.fold_in(stream_key, 6), dim), (parts,), jnp.float32, least / len(shards), top_value / len(shards))
        factor_of = factor_of * jnp.repeat(jnp.exp(steps), dims[dim] // parts).reshape((-1,) + (1,) * (len(dims) - 1 - dim))
    return factor_of


def gaussian(stream_key, dims, deviation, bound, cuts=(), kind=jnp.bfloat16):
    gain = level_of(stream_key, dims, cuts, -0.22, 0.18) if cuts else 1.0
    values = jax.random.normal(stream_key, dims, jnp.float32) * deviation * gain
    return jnp.minimum(jnp.maximum(values, -bound), bound).astype(kind)


def setup_inputs(seed: int = 0) -> dict:
    seeds = jax.random.split(jax.random.key(seed), 14)
    return {
        "tokens": gaussian(seeds[0], (TOKENS, D), 1.0, 6.0, ((0, 32),)),
        "cotangent": gaussian(seeds[1], (TOKENS, D), 1.0, 6.0, ((0, 32),)),
        "query_key_value_weight": gaussian(seeds[2], (3, D, D), D ** -0.5, 0.21875, ((1, 8), (2, 4))),
        "attention_output_weight": gaussian(seeds[3], (D, D), (D // 96) ** -0.5, 2.0, ((0, 4), (1, 8))),
        "rel_bias": gaussian(seeds[4], (HEADS, BUCKETS), 1.0, 6.0, ((0, 4),)),
        "gain_attn": jnp.clip(1.0 + 0.1 * jax.random.normal(seeds[5], (D,), jnp.float32), 0.5, 1.5).astype(jnp.bfloat16),
        "gain_moe": jnp.clip(1.0 + 0.1 * jax.random.normal(seeds[6], (D,), jnp.float32), 0.5, 1.5).astype(jnp.bfloat16),
        "w_router": gaussian(seeds[7], (D, EXPERTS), (4 * D) ** -0.5, 0.109375, ((0, 32),)),
        "w_in": gaussian(seeds[8], (EXPERTS, D, FF), D ** -0.5, 0.21875, ((0, 4), (1, 2), (2, 4))),
        "w_out": gaussian(seeds[9], (EXPERTS, FF, D), (EXPERTS * 0.03125), 3.0, ((0, 4), (1, 4), (2, 2))),
        "expert_index": draw_expert_index(jax.random.fold_in(seeds[13], 71), 0),
        "slot_index": draw_slot_index(jax.random.fold_in(seeds[13], 71), 0),
        "kept_mask": draw_kept_mask(jax.random.fold_in(seeds[13], 71), 0),
    }


EXACT_PRECISION = lax.Precision.HIGHEST
EPSILON = 1e-06
BORDERS = (12, 16, 23, 32, 46, 64, 91)

@jax.custom_vjp
def reduced_precision_cast(v):
    return lax.optimization_barrier(v.astype(jnp.bfloat16)).astype(jnp.float32)

@jax.custom_vjp
def reduced_precision_back(v):
    return v

def low_keep(v):
    return (reduced_precision_cast(v), None)

def low_pass(kept, grad):
    return (grad,)

def back_keep(v):
    return (v, None)

def back_low(kept, grad):
    return (reduced_precision_cast(grad),)
reduced_precision_cast.defvjp(low_keep, low_pass)
reduced_precision_back.defvjp(back_keep, back_low)

def bucket_ids(length):
    places = jnp.arange(length, dtype=jnp.int32)
    offset = places[None, :] - places[:, None]
    distance = jnp.abs(offset)
    bucket = jnp.minimum(distance, 8)
    for border in BORDERS:
        bucket = bucket + (distance >= border).astype(jnp.int32)
    return bucket + jnp.where(offset > 0, 16, 0).astype(jnp.int32)

def rms_scaled(values, scaling):
    return values * lax.rsqrt(lax.optimization_barrier(jnp.mean(values * values, axis=-1, keepdims=True)) + EPSILON) * scaling

def block_forward(tokens, query_key_value_weight, attention_output_weight, rel_bias, gain_attn, gain_moe, w_router, w_in, w_out, expert_index, slot_index, kept_mask):
    normed = reduced_precision_cast(rms_scaled(tokens, gain_attn))
    onehot_table = (bucket_ids(LENGTH)[:, :, None] == jnp.arange(BUCKETS, dtype=jnp.int32)[None, None, :]).astype(jnp.float32)
    bias_full = jnp.einsum('qkb,hb->hqk', onehot_table, rel_bias, precision=EXACT_PRECISION)
    score_scale = HEAD_DIM ** (-0.5)

    def attend(grouped_token_rows):
        output_projected = reduced_precision_cast(reduced_precision_back(jnp.einsum('bgt,itz->ibgz', grouped_token_rows, query_key_value_weight, precision=EXACT_PRECISION)))
        heads_view = output_projected.reshape(3, GROUP_SEQS, LENGTH, HEADS, HEAD_DIM)
        scores = jnp.einsum('sqhe,skhe->shqk', heads_view[0], heads_view[1], precision=EXACT_PRECISION) * score_scale + bias_full[None]
        attention = jax.nn.softmax(reduced_precision_back(scores), axis=-1)
        attention_mixed_rows = jnp.einsum('shqk,skhe->sqhe', reduced_precision_cast(attention), heads_view[2], precision=EXACT_PRECISION)
        attention_mixed_rows = reduced_precision_cast(reduced_precision_back(attention_mixed_rows)).reshape(GROUP_SEQS, LENGTH, D)
        return reduced_precision_back(jnp.einsum('jhk,kw->jhw', attention_mixed_rows, attention_output_weight, precision=EXACT_PRECISION))
    blocks = normed.reshape(-1, GROUP_SEQS, LENGTH, D)
    attn_rows = lax.map(jax.checkpoint(attend), blocks).reshape(TOKENS, D)
    hidden_one = tokens + attn_rows
    moe_in = reduced_precision_cast(rms_scaled(hidden_one, gain_moe))
    logits = reduced_precision_back(jnp.dot(moe_in, w_router, precision=EXACT_PRECISION))
    router_probs = jax.nn.softmax(logits, axis=-1)
    chosen = (expert_index[:, None] == jnp.arange(EXPERTS, dtype=jnp.int32)[None, :]).astype(jnp.float32)
    gate_value = lax.optimization_barrier(jnp.sum(router_probs * chosen, axis=1)) * kept_mask.astype(jnp.float32)
    rows_each = TOKENS // TOK_DEV * CAP
    block_of = jnp.arange(TOKENS, dtype=jnp.int32) // TOK_DEV
    target = expert_index * rows_each + block_of * CAP + slot_index
    target = jnp.where(kept_mask > 0, target, EXPERTS * rows_each).astype(jnp.int32)
    dispatched = jnp.zeros((EXPERTS * rows_each, D), jnp.float32).at[target].set(moe_in, mode='drop')

    def expert(packed):
        rows_in, first_matrix, second_matrix = packed
        inner_rows = reduced_precision_back(jnp.dot(rows_in, first_matrix, precision=EXACT_PRECISION))
        hidden_units = reduced_precision_cast(jax.nn.gelu(inner_rows))
        return reduced_precision_back(jnp.dot(hidden_units, second_matrix, precision=EXACT_PRECISION))
    results = lax.map(jax.checkpoint(expert), (dispatched.reshape(EXPERTS, rows_each, D), w_in, w_out))
    source = jnp.minimum(target, EXPERTS * rows_each - 1).astype(jnp.int32)
    expert_rows = results.reshape(EXPERTS * rows_each, D)[source]
    return hidden_one + gate_value[:, None] * expert_rows

def reference(tokens, cotangent, query_key_value_weight, attention_output_weight, rel_bias, gain_attn, gain_moe, w_router, w_in, w_out, expert_index, slot_index, kept_mask):
    floats = (tokens.astype(jnp.float32), query_key_value_weight.astype(jnp.float32), attention_output_weight.astype(jnp.float32), rel_bias.astype(jnp.float32), gain_attn.astype(jnp.float32), gain_moe.astype(jnp.float32), w_router.astype(jnp.float32), w_in.astype(jnp.float32), w_out.astype(jnp.float32))

    def forward(tok_rows, qkv_rows, out_rows, bias_rows, gain_one, gain_two, router_rows, first_rows, second_rows):
        return block_forward(tok_rows, qkv_rows, out_rows, bias_rows, gain_one, gain_two, router_rows, first_rows, second_rows, expert_index, slot_index, kept_mask)
    result, pullback = jax.vjp(forward, *floats)
    grads = pullback(cotangent.astype(jnp.float32))
    return (result.astype(jnp.bfloat16), grads[0], grads[1], grads[2], grads[3], grads[4], grads[5], grads[6], grads[7], grads[8])
```

```python
import functools

import jax
import jax.numpy as jnp
from jax import lax
from jax.experimental import pallas as pl
from jax.experimental.pallas import tpu as pltpu
from jax.sharding import PartitionSpec as P

HEAD_DIM = 64
BUCKETS = 32
LENGTH = 512
TILE = 128
EPSILON = 1e-06
BORDERS = (12, 16, 23, 32, 46, 64, 91)
F32 = jnp.float32
BF16 = jnp.bfloat16
GELU_A = 0.7978845608028654
GELU_B = 0.044715
ROWS_NN = (((1,), (0,)), ((), ()))
ROWS_NT = (((1,), (1,)), ((), ()))
ROWS_TN = (((0,), (0,)), ((), ()))
VMEM_BYTES = 56 * 1024 * 1024
GROUPS = 1


def dot(a, b, dims=ROWS_NN):
    return lax.dot_general(a, b, dims, preferred_element_type=F32)


def params(**more):
    return pltpu.CompilerParams(vmem_limit_bytes=VMEM_BYTES, **more)


def cost(flops, moved, special=0):
    return pl.CostEstimate(flops=int(flops), bytes_accessed=int(moved), transcendentals=int(special))


def whole(shape):
    return pl.BlockSpec(shape, lambda *_: (0,) * len(shape))


def tile_bucket(step):
    rows = lax.broadcasted_iota(jnp.int32, (TILE, TILE), 0)
    cols = lax.broadcasted_iota(jnp.int32, (TILE, TILE), 1)
    offset = cols - rows + step * TILE
    distance = jnp.abs(offset)
    bucket = jnp.minimum(distance, 8)
    for border in BORDERS:
        bucket = bucket + jnp.where(distance >= border, 1, 0)
    return bucket + jnp.where(offset > 0, 16, 0)


def tile_range(step):
    return {-1: range(1, 16), 0: range(0, 32), 1: range(17, 32)}[step]


def fill_bias(bias_ref, table, heads):
    blocks = LENGTH // TILE
    buckets = {step: tile_bucket(step) for step in (-1, 0, 1)}
    for head in range(heads):
        near = {}
        for step in (-1, 0, 1):
            value = jnp.zeros((TILE, TILE), F32)
            for k in tile_range(step):
                value = jnp.where(buckets[step] == k, bias_ref[head, k], value)
            near[step] = value
        low = jnp.full((TILE, TILE), bias_ref[head, 15], F32)
        high = jnp.full((TILE, TILE), bias_ref[head, 31], F32)
        for i in range(blocks):
            for j in range(blocks):
                step = j - i
                value = near[step] if abs(step) <= 1 else (low if step < 0 else high)
                table[head, i * TILE : (i + 1) * TILE, j * TILE : (j + 1) * TILE] = value


def unit_rows(values):
    scale = lax.rsqrt(jnp.mean(values * values, axis=-1, keepdims=True) + EPSILON)
    return values * scale, scale


def attend_kernel(heads, bias_ref, tok_ref, gain_ref, w_ref, part_ref, qkv_ref, mixed_ref, log_ref, table, wo):
    inner = heads * HEAD_DIM

    @pl.when(pl.program_id(0) == 0)
    def _():
        fill_bias(bias_ref, table, heads)
        wo[...] = w_ref[:, 3 * inner :]

    unit, _ = unit_rows(tok_ref[...].astype(F32))
    normed = (unit * gain_ref[...]).astype(BF16)
    qkv_ref[...] = dot(normed, w_ref[:, : 3 * inner]).astype(BF16)
    lanes = lax.broadcasted_iota(jnp.int32, (LENGTH, TILE), 1)
    logs = jnp.zeros((LENGTH, TILE), F32)
    for head in range(heads):
        at = head * HEAD_DIM
        query = qkv_ref[:, at : at + HEAD_DIM] * HEAD_DIM ** (-0.5)
        key = qkv_ref[:, inner + at : inner + at + HEAD_DIM]
        value = qkv_ref[:, 2 * inner + at : 2 * inner + at + HEAD_DIM]
        scores = dot(query.astype(BF16), key, ROWS_NT) + table[head]
        top = jnp.max(scores, axis=-1, keepdims=True)
        exponent = jnp.exp(scores - top)
        total = jnp.sum(exponent, axis=-1, keepdims=True)
        attention = (exponent * (1.0 / total)).astype(BF16)
        mixed_ref[:, at : at + HEAD_DIM] = dot(attention, value).astype(BF16)
        logs = jnp.where(lanes == head, top + jnp.log(total), logs)
    log_ref[...] = logs
    part_ref[...] = dot(mixed_ref[...], wo[...], ROWS_NT).astype(BF16)


def attend(bias, tokens, gain, weights):
    rows, width = tokens.shape
    heads = bias.shape[0]
    inner = heads * HEAD_DIM
    seqs = rows // LENGTH
    by_seq = lambda cols: pl.BlockSpec((LENGTH, cols), lambda s: (s, 0))
    return pl.pallas_call(
        functools.partial(attend_kernel, heads),
        grid=(seqs,),
        in_specs=[
            pl.BlockSpec(memory_space=pltpu.SMEM),
            by_seq(width),
            whole((1, width)),
            whole((width, 4 * inner)),
        ],
        out_specs=[by_seq(width), by_seq(3 * inner), by_seq(inner), by_seq(TILE)],
        out_shape=[
            jax.ShapeDtypeStruct((rows, width), BF16),
            jax.ShapeDtypeStruct((rows, 3 * inner), BF16),
            jax.ShapeDtypeStruct((rows, inner), BF16),
            jax.ShapeDtypeStruct((rows, TILE), F32),
        ],
        scratch_shapes=[pltpu.VMEM((heads, LENGTH, LENGTH), F32), pltpu.VMEM((width, inner), BF16)],
        compiler_params=params(),
        cost_estimate=cost(8 * rows * width * inner + 4 * rows * LENGTH * inner, rows * width * 8, rows * LENGTH * heads),
        name="attend",
    )(bias, tokens, gain, weights)


def attend_back_kernel(
    heads, bias_ref, tok_ref, gain_ref, w_ref, qkv_ref, mixed_ref, log_ref, grad_ref,
    normed_ref, weight_ref, buckets_ref, gain_out, table, wo, gmix, gproj, near, far, rows_s,
):
    inner = heads * HEAD_DIM
    blocks = LENGTH // TILE
    step_id = pl.program_id(0)

    @pl.when(step_id == 0)
    def _():
        fill_bias(bias_ref, table, heads)
        wo[...] = w_ref[:, 3 * inner :]
        near[...] = jnp.zeros_like(near)
        far[...] = jnp.zeros_like(far)
        weight_ref[...] = jnp.zeros_like(weight_ref)
        gain_out[...] = jnp.zeros_like(gain_out)

    gmix[...] = dot(grad_ref[...], wo[...]).astype(BF16)
    for head in range(heads):
        at = head * HEAD_DIM
        query = (qkv_ref[:, at : at + HEAD_DIM] * HEAD_DIM ** (-0.5)).astype(BF16)
        key = qkv_ref[:, inner + at : inner + at + HEAD_DIM]
        value = qkv_ref[:, 2 * inner + at : 2 * inner + at + HEAD_DIM]
        grad_rows = gmix[:, at : at + HEAD_DIM]
        scores = dot(query, key, ROWS_NT) + table[head]
        attention = jnp.exp(scores - log_ref[:, head : head + 1])
        grad_weights = dot(grad_rows, value, ROWS_NT)
        inner_sum = jnp.sum(attention * grad_weights, axis=-1, keepdims=True)
        grad_scores = attention * (grad_weights - inner_sum)
        low = jnp.zeros((TILE, TILE), F32)
        high = jnp.zeros((TILE, TILE), F32)
        mid = [jnp.zeros((TILE, TILE), F32) for _ in range(3)]
        for i in range(blocks):
            for j in range(blocks):
                piece = grad_scores[i * TILE : (i + 1) * TILE, j * TILE : (j + 1) * TILE]
                if abs(j - i) <= 1:
                    mid[j - i + 1] = mid[j - i + 1] + piece
                elif j < i:
                    low = low + piece
                else:
                    high = high + piece
        for k in range(3):
            near[head * 3 + k] += mid[k]
        far[head * 2] += low
        far[head * 2 + 1] += high
        rounded = grad_scores.astype(BF16)
        gproj[:, at : at + HEAD_DIM] = (dot(rounded, key) * HEAD_DIM ** (-0.5)).astype(BF16)
        gproj[:, inner + at : inner + at + HEAD_DIM] = dot(rounded, query, ROWS_TN).astype(BF16)
        gproj[:, 2 * inner + at : 2 * inner + at + HEAD_DIM] = dot(
            attention.astype(BF16), grad_rows, ROWS_TN
        ).astype(BF16)
    unit, _ = unit_rows(tok_ref[...].astype(F32))
    normed = (unit * gain_ref[...]).astype(BF16)
    grad_normed = dot(gproj[...], w_ref[:, : 3 * inner], ROWS_NT)
    normed_ref[...] = grad_normed.astype(BF16)
    gain_out[...] += jnp.sum(grad_normed * unit, axis=0, keepdims=True)
    weight_ref[:, : 3 * inner] += dot(normed, gproj[...], ROWS_TN)
    weight_ref[:, 3 * inner :] += dot(grad_ref[...], mixed_ref[...], ROWS_TN)

    @pl.when(step_id == pl.num_programs(0) - 1)
    def _():
        ids = [tile_bucket(step) for step in (-1, 0, 1)]
        for head in range(heads):
            for k in range(BUCKETS):
                total = jnp.zeros((TILE, TILE), F32)
                for step in (-1, 0, 1):
                    if k in tile_range(step):
                        total = total + jnp.where(ids[step + 1] == k, near[head * 3 + step + 1], 0.0)
                if k == 15:
                    total = total + far[head * 2]
                if k == 31:
                    total = total + far[head * 2 + 1]
                at = head * BUCKETS + k
                rows_s[at : at + 1, :] = jnp.sum(total, axis=0, keepdims=True)
        buckets_ref[...] = jnp.sum(rows_s[...], axis=1, keepdims=True)


def attend_back(bias, tokens, gain, weights, projected, mixed, logs, grad):
    rows, width = tokens.shape
    heads = bias.shape[0]
    inner = heads * HEAD_DIM
    seqs = rows // LENGTH
    by_seq = lambda cols: pl.BlockSpec((LENGTH, cols), lambda s: (s, 0))
    return pl.pallas_call(
        functools.partial(attend_back_kernel, heads),
        grid=(seqs,),
        in_specs=[
            pl.BlockSpec(memory_space=pltpu.SMEM),
            by_seq(width),
            whole((1, width)),
            whole((width, 4 * inner)),
            by_seq(3 * inner),
            by_seq(inner),
            by_seq(TILE),
            by_seq(width),
        ],
        out_specs=[
            by_seq(width),
            whole((width, 4 * inner)),
            whole((heads * BUCKETS, 1)),
            whole((1, width)),
        ],
        out_shape=[
            jax.ShapeDtypeStruct((rows, width), BF16),
            jax.ShapeDtypeStruct((width, 4 * inner), F32),
            jax.ShapeDtypeStruct((heads * BUCKETS, 1), F32),
            jax.ShapeDtypeStruct((1, width), F32),
        ],
        scratch_shapes=[
            pltpu.VMEM((heads, LENGTH, LENGTH), F32),
            pltpu.VMEM((width, inner), BF16),
            pltpu.VMEM((LENGTH, inner), BF16),
            pltpu.VMEM((LENGTH, 3 * inner), BF16),
            pltpu.VMEM((heads * 3, TILE, TILE), F32),
            pltpu.VMEM((heads * 2, TILE, TILE), F32),
            pltpu.VMEM((heads * BUCKETS, TILE), F32),
        ],
        compiler_params=params(),
        cost_estimate=cost(18 * rows * width * inner + 10 * rows * LENGTH * inner, rows * width * 12, rows * LENGTH * heads),
        name="attend_back",
    )(bias, tokens, gain, weights, projected, mixed, logs, grad)


def place_kernel(target_ref, rows_ref, out_ref):
    count = out_ref.shape[0]
    rows = lax.broadcasted_iota(jnp.int32, (count, rows_ref.shape[0]), 0)
    chosen = jnp.where(rows == target_ref[...], 1.0, 0.0).astype(BF16)
    out_ref[...] = dot(chosen, rows_ref[...]).astype(BF16)


def place(target_row, rows, count):
    return pl.pallas_call(
        place_kernel,
        out_shape=jax.ShapeDtypeStruct((count, rows.shape[1]), BF16),
        compiler_params=params(),
        cost_estimate=cost(2 * count * rows.size, 4 * rows.size),
        name="place",
    )(target_row, rows)


def softmax_rows(logits):
    exponent = jnp.exp(logits - jnp.max(logits, axis=-1, keepdims=True))
    return exponent * (1.0 / jnp.sum(exponent, axis=-1, keepdims=True))


def route_kernel(tok_ref, attn_ref, gain_ref, router_ref, target_ref, index_ref, kept_ref, hidden_ref, sent_ref, gate_ref):
    hidden = tok_ref[...].astype(F32) + attn_ref[...].astype(F32)
    hidden_ref[...] = hidden
    unit, _ = unit_rows(hidden)
    moe_in = (unit * gain_ref[...]).astype(BF16)
    count = sent_ref.shape[0]
    rows = lax.broadcasted_iota(jnp.int32, (count, hidden.shape[0]), 0)
    chosen = jnp.where(rows == target_ref[...], 1.0, 0.0).astype(BF16)
    sent_ref[...] = dot(chosen, moe_in).astype(BF16)
    probs = softmax_rows(dot(moe_in, router_ref[...]))
    lanes = lax.broadcasted_iota(jnp.int32, probs.shape, 1)
    picked = jnp.sum(jnp.where(lanes == index_ref[...], probs, 0.0), axis=-1, keepdims=True)
    gate_ref[...] = picked * kept_ref[...].astype(F32)


def route(tokens, attn, gain, router, target_row, index_col, kept_col, count):
    rows, width = tokens.shape
    return pl.pallas_call(
        route_kernel,
        out_shape=[
            jax.ShapeDtypeStruct((rows, width), F32),
            jax.ShapeDtypeStruct((count, width), BF16),
            jax.ShapeDtypeStruct((rows, 1), F32),
        ],
        compiler_params=params(),
        cost_estimate=cost(2 * count * rows * width, 12 * rows * width),
        name="route",
    )(tokens, attn, gain, router, target_row, index_col, kept_col)


def rest_choice(blocks, locals_, rest, expert):
    rows = lax.broadcasted_iota(jnp.int32, (blocks * rest, blocks * locals_ * rest), 0)
    cols = lax.broadcasted_iota(jnp.int32, (blocks * rest, blocks * locals_ * rest), 1)
    block = lax.div(rows, rest)
    wanted = block * (locals_ * rest) + expert * rest + (rows - block * rest)
    return jnp.where(cols == wanted, 1.0, 0.0).astype(BF16)


def pick_rows(out_ref, main_refs, rest_refs, choice, main_rows):
    at = 0
    for ref in main_refs:
        count = ref.shape[0] * ref.shape[1]
        out_ref[at : at + count, :] = ref[...].reshape(count, ref.shape[2])
        at += count
    pieces = [ref[...].reshape(ref.shape[0] * ref.shape[1], ref.shape[2]) for ref in rest_refs]
    together = pieces[0] if len(pieces) == 1 else jnp.concatenate(pieces, axis=0)
    out_ref[main_rows:, :] = dot(choice, together).astype(BF16)


def put_rows(out_refs, value_ref, choice, main_rows, main, locals_, rest, expert):
    at = 0
    spread = dot(choice, value_ref[main_rows:, :], ROWS_TN).astype(BF16)
    rest_at = 0
    for ref in out_refs:
        blocks, _, width = ref.shape
        if main:
            count = blocks * main
            start = pl.multiple_of(expert * main, main)
            ref[:, pl.ds(start, main), :] = value_ref[at : at + count, :].reshape(blocks, main, width)
            at += count
        part = spread[rest_at : rest_at + blocks * locals_ * rest].reshape(blocks, locals_ * rest, width)
        rest_at += blocks * locals_ * rest

        @pl.when(expert == 0)
        def _():
            ref[:, locals_ * main :, :] = part

        @pl.when(expert > 0)
        def _():
            ref[:, locals_ * main :, :] = ref[:, locals_ * main :, :] + part


def join_halves(place_ref, own_in, peer_in, own_out, peer_out, win, wout):
    half = own_in.shape[1]
    mine = pl.multiple_of(place_ref[0] * half, half)
    other = pl.multiple_of((1 - place_ref[0]) * half, half)
    if win is not None:
        win[pl.ds(mine, half), :] = own_in[0]
        win[pl.ds(other, half), :] = peer_in[0]
    half_out = own_out.shape[2]
    mine = pl.multiple_of(place_ref[0] * half_out, half_out)
    other = pl.multiple_of((1 - place_ref[0]) * half_out, half_out)
    wout[:, pl.ds(mine, half_out)] = own_out[0]
    wout[:, pl.ds(other, half_out)] = peer_out[0]


def expert_kernel(groups, main, locals_, rest, place_ref, *refs):
    take = lambda n: [refs_iter.pop(0) for _ in range(n)]
    refs_iter = list(refs)
    mains = groups if main else 0
    x_main, x_rest = take(mains), take(groups)
    g_main, g_rest = take(mains), take(groups)
    own_in, peer_in, own_out, peer_out, router = take(5)
    back_refs = take(groups)
    x_ref, ge_ref, hid_ref, gi_ref, gl_ref = take(5)
    win, wout, grows, inner, gunits, gate_s, dots, back = take(8)
    expert = pl.program_id(0)
    blocks = sum(ref.shape[0] for ref in x_rest)
    main_rows = blocks * main
    rows, width = x_ref.shape[1:]
    choice = rest_choice(blocks, locals_, rest, expert)
    pick_rows(x_ref.at[0], x_main, x_rest, choice, main_rows)
    pick_rows(grows, g_main, g_rest, choice, main_rows)
    join_halves(place_ref, own_in, peer_in, own_out, peer_out, win, wout)
    inner[...] = dot(x_ref[0], win[...])
    gunits[...] = dot(grows[...], wout[...], ROWS_NT)
    probs = softmax_rows(dot(x_ref[0], router[...]))
    lanes = lax.broadcasted_iota(jnp.int32, probs.shape, 1)
    mine = lanes == place_ref[1] * locals_ + expert
    picked = jnp.sum(jnp.where(mine, probs, 0.0), axis=-1, keepdims=True)
    gate_s[...] = picked
    chunk = 64

    def body(step, _):
        at = pl.ds(pl.multiple_of(step * chunk, chunk), chunk)
        value = inner[at, :]
        square = value * value
        wave = jnp.tanh(GELU_A * value * (1.0 + GELU_B * square))
        half = 0.5 * (1.0 + wave)
        hidden = (value * half).astype(BF16)
        slope = half + (0.5 * GELU_A) * value * (1.0 - wave * wave) * (1.0 + 3.0 * GELU_B * square)
        units = gunits[at, :]
        gate = gate_s[at, :]
        hid_ref[0, at, :] = hidden
        gi_ref[0, at, :] = (gate * units * slope).astype(BF16)
        ge_ref[0, at, :] = (gate * grows[at, :].astype(F32)).astype(BF16)
        dots[at, :] = jnp.sum(hidden.astype(F32) * units, axis=-1, keepdims=True)
        return 0

    lax.fori_loop(0, rows // chunk, body, 0)
    grad_logits = (dots[...] * probs * (jnp.where(mine, 1.0, 0.0) - picked)).astype(BF16)
    gl_ref[0] = grad_logits
    back[...] = (dot(gi_ref[0], win[...], ROWS_NT) + dot(grad_logits, router[...], ROWS_NT)).astype(BF16)
    put_rows(back_refs, back, choice, main_rows, main, locals_, rest, expert)


def group_specs(arrays, main, locals_, rest):
    mains, rests = [], []
    for array in arrays:
        blocks, _, width = array.shape
        if main:
            mains.append(pl.BlockSpec((blocks, main, width), lambda e, *_: (0, e, 0)))
        at = locals_ * main // (locals_ * rest)
        rests.append(pl.BlockSpec((blocks, locals_ * rest, width), lambda e, *_, at=at: (0, at, 0)))
    return mains, rests


def expert_forward_back(places, xs, gs, own_in, peer_in, own_out, peer_out, router, main, rest):
    locals_, half, wide = own_in.shape
    width, experts = router.shape
    groups = len(xs)
    blocks = sum(x.shape[0] for x in xs)
    rows = blocks * (main + rest)
    mains, rests = group_specs(xs, main, locals_, rest)
    per = lambda *shape: pl.BlockSpec((1,) + shape, lambda e, *_: (e, 0, 0))
    repeated = list(xs) if main else []
    saved = jax.ShapeDtypeStruct((locals_, rows, width), BF16)
    saved_wide = jax.ShapeDtypeStruct((locals_, rows, wide), BF16)
    result = pl.pallas_call(
        functools.partial(expert_kernel, groups, main, locals_, rest),
        grid_spec=pltpu.PrefetchScalarGridSpec(
            num_scalar_prefetch=1,
            grid=(locals_,),
            in_specs=mains + rests + mains + rests
            + [per(half, wide)] * 2 + [per(wide, half)] * 2 + [whole((width, experts))],
            out_specs=[whole(x.shape) for x in xs]
            + [per(rows, width), per(rows, width), per(rows, wide), per(rows, wide), per(rows, experts)],
            scratch_shapes=[
                pltpu.VMEM((width, wide), BF16),
                pltpu.VMEM((wide, width), BF16),
                pltpu.VMEM((rows, width), BF16),
                pltpu.VMEM((rows, wide), F32),
                pltpu.VMEM((rows, wide), F32),
                pltpu.VMEM((rows, 1), F32),
                pltpu.VMEM((rows, 1), F32),
                pltpu.VMEM((rows, width), BF16),
            ],
        ),
        out_shape=[jax.ShapeDtypeStruct(x.shape, BF16) for x in xs]
        + [saved, saved, saved_wide, saved_wide, jax.ShapeDtypeStruct((locals_, rows, experts), BF16)],
        compiler_params=params(),
        cost_estimate=cost(6 * locals_ * rows * width * wide, locals_ * rows * width * 14, locals_ * rows * wide),
        name="experts",
    )(places, *repeated, *xs, *(list(gs) if main else []), *gs, own_in, peer_in, own_out, peer_out, router)
    return result[:groups], result[groups:]


def expert_weights_kernel(groups, main, locals_, rest, place_ref, x_ref, ge_ref, hid_ref, gi_ref, gl_ref, own_out, peer_out, *refs):
    forward_refs = refs[:groups]
    in_own, in_send, out_own, out_send, router_ref, wout, value = refs[groups:]
    expert = pl.program_id(0)
    blocks = sum(ref.shape[0] for ref in forward_refs)
    choice = rest_choice(blocks, locals_, rest, expert)
    join_halves(place_ref, own_out, peer_out, own_out, peer_out, None, wout)
    value[...] = dot(hid_ref[0], wout[...]).astype(BF16)
    put_rows(forward_refs, value, choice, blocks * main, main, locals_, rest, expert)
    half = in_own.shape[1]
    mine = pl.ds(pl.multiple_of(place_ref[0] * half, half), half)
    other = pl.ds(pl.multiple_of((1 - place_ref[0]) * half, half), half)
    in_own[0] = dot(x_ref[0, :, mine], gi_ref[0], ROWS_TN)
    in_send[0] = dot(x_ref[0, :, other], gi_ref[0], ROWS_TN).astype(BF16)
    out_own[0] = dot(hid_ref[0], ge_ref[0, :, mine], ROWS_TN)
    out_send[0] = dot(hid_ref[0], ge_ref[0, :, other], ROWS_TN).astype(BF16)

    @pl.when(expert == 0)
    def _():
        router_ref[...] = jnp.zeros_like(router_ref)

    router_ref[...] += dot(x_ref[0], gl_ref[0], ROWS_TN)


def expert_weights(places, saved, own_out, peer_out, shapes, main, rest):
    x, ge, hidden, gi, gl = saved
    locals_, rows, width = x.shape
    wide = hidden.shape[2]
    experts = gl.shape[2]
    half = own_out.shape[2]
    groups = len(shapes)
    per = lambda *shape: pl.BlockSpec((1,) + shape, lambda e, *_: (e, 0, 0))
    result = pl.pallas_call(
        functools.partial(expert_weights_kernel, groups, main, locals_, rest),
        grid_spec=pltpu.PrefetchScalarGridSpec(
            num_scalar_prefetch=1,
            grid=(locals_,),
            in_specs=[per(rows, width), per(rows, width), per(rows, wide), per(rows, wide), per(rows, experts)]
            + [per(wide, half)] * 2,
            out_specs=[whole(s) for s in shapes]
            + [per(half, wide), per(half, wide), per(wide, half), per(wide, half), whole((width, experts))],
            scratch_shapes=[pltpu.VMEM((wide, width), BF16), pltpu.VMEM((rows, width), BF16)],
        ),
        out_shape=[jax.ShapeDtypeStruct(s, BF16) for s in shapes]
        + [
            jax.ShapeDtypeStruct((locals_, half, wide), F32),
            jax.ShapeDtypeStruct((locals_, half, wide), BF16),
            jax.ShapeDtypeStruct((locals_, wide, half), F32),
            jax.ShapeDtypeStruct((locals_, wide, half), BF16),
            jax.ShapeDtypeStruct((width, experts), F32),
        ],
        compiler_params=params(),
        cost_estimate=cost(6 * locals_ * rows * width * wide, locals_ * rows * width * 14),
        name="expert_weights",
    )(places, x, ge, hidden, gi, gl, own_out, peer_out)
    return result[:groups], result[groups:]


def hidden_back_kernel(target_ref, back_ref, hidden_ref, cot_ref, gain_ref, grad_ref, attn_ref, gain_out):
    count = back_ref.shape[0]
    cols = lax.broadcasted_iota(jnp.int32, (target_ref.shape[0], count), 1)
    chosen = jnp.where(cols == target_ref[...], 1.0, 0.0).astype(BF16)
    grad_in = dot(chosen, back_ref[...])
    unit, scale = unit_rows(hidden_ref[...])
    gain_out[...] = jnp.sum(grad_in * unit, axis=0, keepdims=True)
    scaled = grad_in * gain_ref[...]
    inside = jnp.mean(unit * scaled, axis=-1, keepdims=True)
    grad = cot_ref[...].astype(F32) + scale * (scaled - unit * inside)
    grad_ref[...] = grad
    attn_ref[...] = grad.astype(BF16)


def hidden_back(target_col, back, hidden, cotangent, gain):
    rows, width = hidden.shape
    return pl.pallas_call(
        hidden_back_kernel,
        out_shape=[
            jax.ShapeDtypeStruct((rows, width), F32),
            jax.ShapeDtypeStruct((rows, width), BF16),
            jax.ShapeDtypeStruct((1, width), F32),
        ],
        compiler_params=params(),
        cost_estimate=cost(2 * back.shape[0] * rows * width, 16 * rows * width),
        name="hidden_back",
    )(target_col, back, hidden, cotangent, gain)


def output_kernel(target_ref, rows_ref, hidden_ref, gate_ref, out_ref):
    count = rows_ref.shape[0]
    cols = lax.broadcasted_iota(jnp.int32, (target_ref.shape[0], count), 1)
    chosen = jnp.where(cols == target_ref[...], 1.0, 0.0).astype(BF16)
    out_ref[...] = (hidden_ref[...] + gate_ref[...] * dot(chosen, rows_ref[...])).astype(BF16)


def output_rows(target_col, expert_rows, hidden, gate):
    return pl.pallas_call(
        output_kernel,
        out_shape=jax.ShapeDtypeStruct(hidden.shape, BF16),
        compiler_params=params(),
        cost_estimate=cost(2 * expert_rows.shape[0] * hidden.size, 10 * hidden.size),
        name="output_rows",
    )(target_col, expert_rows, hidden, gate)


def tokens_back_kernel(tok_ref, normed_ref, gain_ref, hidden_ref, out_ref):
    unit, scale = unit_rows(tok_ref[...].astype(F32))
    scaled = normed_ref[...].astype(F32) * gain_ref[...]
    inside = jnp.mean(unit * scaled, axis=-1, keepdims=True)
    out_ref[...] = hidden_ref[...] + scale * (scaled - unit * inside)


def tokens_back(tokens, grad_normed, gain, grad_hidden):
    return pl.pallas_call(
        tokens_back_kernel,
        out_shape=jax.ShapeDtypeStruct(tokens.shape, F32),
        compiler_params=params(),
        cost_estimate=cost(10 * tokens.size, 12 * tokens.size),
        name="tokens_back",
    )(tokens, grad_normed, gain, grad_hidden)


def shifted(value, axis, count, step):
    return lax.ppermute(value, axis, [(s, (s + step) % count) for s in range(count)])


def gather_ring(value, axis, count):
    me = lax.axis_index(axis)
    parts = [value] + [shifted(value, axis, count, -k) for k in range(1, count)]
    return jnp.roll(jnp.stack(parts), me, axis=0)


def send_chunks(chunks, axis, count):
    return [chunks[0]] + [shifted(chunks[k], axis, count, k) for k in range(1, count)]


def return_chunks(chunks, axis, count):
    return [chunks[0]] + [shifted(chunks[k], axis, count, -k) for k in range(1, count)]


def grouped(count):
    bounds = [count * i // GROUPS for i in range(GROUPS + 1)]
    return [range(a, b) for a, b in zip(bounds[:-1], bounds[1:]) if b > a]


def on_device(
    sizes,
    tokens,
    cotangent,
    query_key_value_weight,
    attention_output_weight,
    rel_bias,
    gain_attn,
    gain_moe,
    w_router,
    w_in,
    w_out,
    expert_index,
    slot_index,
    kept_mask,
):
    dp_count, z_count, t_count = sizes
    tok_rows, width = tokens.shape
    experts_all = w_router.shape[1]
    capacity = max(2, 3 * tok_rows // (2 * experts_all))
    locals_ = w_in.shape[0]
    main = capacity // 16 * 16
    rest = capacity - main
    block = locals_ * capacity
    heads = rel_bias.shape[0]
    inner = heads * HEAD_DIM
    part = query_key_value_weight.shape[1]
    fine = w_router.shape[0]
    my_dp = lax.axis_index("dp")
    my_z = lax.axis_index("expert")
    bias = rel_bias.astype(F32)

    group_tokens = lax.all_gather(tokens, "tensor", axis=0, tiled=True)

    small = jnp.concatenate([gain_attn[:, None], gain_moe[:, None], w_router], axis=1)
    small = gather_ring(small, "tensor", t_count).reshape(-1)
    extra = -(-small.shape[0] // (16 * width)) * 16
    packed = jnp.concatenate(
        [
            query_key_value_weight.transpose(1, 0, 2).reshape(part, 3 * inner),
            attention_output_weight.T,
        ],
        axis=1,
    )
    packed = jnp.concatenate(
        [packed, jnp.pad(small, (0, extra * width - small.shape[0])).reshape(extra, width)], axis=0
    )
    packed = gather_ring(packed, "expert", z_count)
    packed = gather_ring(packed, "dp", dp_count).reshape(dp_count * z_count, part + extra, width)
    weights = packed[:, :part].reshape(width, 4 * inner)
    smalls = packed[:, part:].reshape(dp_count * z_count, -1)[:, : small.shape[0]].reshape(width, 2 + experts_all)
    gain_one = smalls[:, 0].astype(F32)[None]
    gain_two = smalls[:, 1].astype(F32)[None]
    router = smalls[:, 2:]

    peer_in = shifted(w_in, "dp", dp_count, 1)
    peer_out = shifted(w_out, "dp", dp_count, 1)

    z_of = expert_index // locals_
    local = expert_index - z_of * locals_
    inside = jnp.where(
        slot_index < main, local * main + slot_index, locals_ * main + local * rest + slot_index - main
    )
    target = lax.rem(z_of - my_z + z_count, z_count) * block + inside
    target = jnp.where(kept_mask > 0, target, -1)
    target_row, target_col = target[None, :], target[:, None]
    count = z_count * block
    split = grouped(z_count)

    def to_experts(rows):
        chunks = send_chunks(list(rows.reshape(z_count, block, width)), "expert", z_count)
        gathered = []
        for members in split:
            joined = jnp.concatenate([chunks[k] for k in members], axis=0)
            full = lax.all_gather(joined, "tensor", axis=0, tiled=True)
            gathered.append(full.reshape(t_count * len(members), block, width))
        return gathered

    def from_experts(parts):
        chunks = [None] * z_count
        for members, value in zip(split, parts):
            value = value.reshape(t_count * len(members) * block, width)
            summed = lax.psum_scatter(value, "tensor", scatter_dimension=0, tiled=True)
            for place_, k in enumerate(members):
                chunks[k] = summed[place_ * block : (place_ + 1) * block]
        return jnp.concatenate(return_chunks(chunks, "expert", z_count), axis=0)

    grad_arrived = to_experts(place(target_row, cotangent, count))

    partial_, projected, mixed, logs = attend(bias, group_tokens, gain_one, weights)
    attn = lax.psum_scatter(partial_, "tensor", scatter_dimension=0, tiled=True)
    hidden_one, sent, gate = route(
        tokens, attn, gain_two, router, target_row, expert_index[:, None], kept_mask[:, None], count
    )
    arrived = to_experts(sent)
    places = jnp.stack([my_dp, my_z]).astype(jnp.int32)
    back_parts, saved = expert_forward_back(
        places, arrived, grad_arrived, w_in, peer_in, w_out, peer_out, router, main, rest
    )
    grad_back = from_experts(back_parts)
    forward_parts, (in_own, in_send, out_own, out_send, router_part) = expert_weights(
        places, saved, w_out, peer_out, [x.shape for x in arrived], main, rest
    )
    grad_w_in = in_own + shifted(in_send, "dp", dp_count, 1).astype(F32)
    grad_w_out = out_own + shifted(out_send, "dp", dp_count, 1).astype(F32)
    grad_hidden, grad_attn, gain_two_part = hidden_back(target_col, grad_back, hidden_one, cotangent, gain_two)
    group_grad = lax.all_gather(grad_attn, "tensor", axis=0, tiled=True)
    grad_normed_part, weight_part, bucket_part, gain_one_part = attend_back(
        bias, group_tokens, gain_one, weights, projected, mixed, logs, group_grad
    )
    grad_normed = lax.psum_scatter(grad_normed_part, "tensor", scatter_dimension=0, tiled=True)
    output = output_rows(target_col, from_experts(forward_parts), hidden_one, gate)
    grad_tokens = tokens_back(tokens, grad_normed, gain_one, grad_hidden)

    owners = dp_count * z_count
    smalls = jnp.concatenate(
        [
            gain_one_part.reshape(owners, part),
            gain_two_part.reshape(owners, part),
            router_part.reshape(owners, part * experts_all),
            jnp.broadcast_to(bucket_part.reshape(1, heads * BUCKETS), (owners, heads * BUCKETS)),
        ],
        axis=1,
    )
    extra = -(-smalls.shape[1] // (16 * width)) * 16
    smalls = jnp.pad(smalls, ((0, 0), (0, extra * width - smalls.shape[1]))).reshape(owners, extra, width)
    payload = jnp.concatenate([weight_part.reshape(owners, part, width), smalls], axis=1)
    payload = payload.reshape(dp_count, z_count, part + extra, width)
    own = lax.dynamic_index_in_dim(payload, my_dp, 0, keepdims=False)
    other = lax.dynamic_index_in_dim(payload, 1 - my_dp, 0, keepdims=False)
    summed = own + shifted(other.astype(BF16), "dp", dp_count, 1).astype(F32)
    turned = jnp.roll(summed, -my_z, axis=0)
    pieces = send_chunks(
        [turned[0]] + [turned[k].astype(BF16) for k in range(1, z_count)], "expert", z_count
    )
    total = pieces[0]
    for piece in pieces[1:]:
        total = total + piece.astype(F32)
    weight_total = total[:part].reshape(part, 4, inner)
    grad_w_qkv = weight_total[:, :3].transpose(1, 0, 2)
    grad_w_attn_out = weight_total[:, 3].T
    flat = total[part:].reshape(-1)
    ends = [part, 2 * part, 2 * part + part * experts_all]
    grad_rel_bias = flat[ends[2] : ends[2] + heads * BUCKETS].reshape(heads, BUCKETS)
    rows_left = jnp.concatenate(
        [
            flat[: ends[0]].reshape(t_count, fine),
            flat[ends[0] : ends[1]].reshape(t_count, fine),
            flat[ends[1] : ends[2]].reshape(t_count, fine * experts_all),
        ],
        axis=1,
    )
    turned = jnp.roll(rows_left, -lax.axis_index("tensor"), axis=0)
    left = turned[0]
    for piece in send_chunks([turned[k] for k in range(t_count)], "tensor", t_count)[1:]:
        left = left + piece
    grad_gain_attn = left[:fine]
    grad_gain_moe = left[fine : 2 * fine]
    grad_w_router = left[2 * fine :].reshape(fine, experts_all)
    return (
        output,
        grad_tokens,
        grad_w_qkv,
        grad_w_attn_out,
        grad_rel_bias,
        grad_gain_attn,
        grad_gain_moe,
        grad_w_router,
        grad_w_in,
        grad_w_out,
    )


def solution(mesh):
    placed = (
        P(("dp", "expert", "tensor"), None),
        P(("dp", "expert", "tensor"), None),
        P(None, ("dp", "expert"), "tensor"),
        P("tensor", ("dp", "expert")),
        P("tensor", None),
        P(("dp", "expert", "tensor")),
        P(("dp", "expert", "tensor")),
        P(("dp", "expert", "tensor"), None),
        P("expert", "dp", "tensor"),
        P("expert", "tensor", "dp"),
        P(("dp", "expert", "tensor")),
        P(("dp", "expert", "tensor")),
        P(("dp", "expert", "tensor")),
    )
    sizes = tuple(mesh.shape[name] for name in ("dp", "expert", "tensor"))
    return jax.shard_map(
        functools.partial(on_device, sizes),
        mesh=mesh,
        in_specs=placed,
        out_specs=(
            P(("dp", "expert", "tensor"), None),
            P(("dp", "expert", "tensor"), None),
            P(None, ("dp", "expert"), "tensor"),
            P("tensor", ("dp", "expert")),
            P("tensor", None),
            P(("dp", "expert", "tensor")),
            P(("dp", "expert", "tensor")),
            P(("dp", "expert", "tensor"), None),
            P("expert", "dp", "tensor"),
            P("expert", "tensor", "dp"),
        ),
        check_vma=False,
    )
```

```python
import functools

import jax
import jax.numpy as jnp
from jax import lax
from jax.experimental import pallas as pl
from jax.experimental.pallas import tpu as pltpu
from jax.sharding import PartitionSpec as P

HEAD_DIM = 64
BUCKETS = 32
LENGTH = 512
TILE = 128
EPSILON = 1e-06
BORDERS = (12, 16, 23, 32, 46, 64, 91)
F32 = jnp.float32
BF16 = jnp.bfloat16
GELU_A = 0.7978845608028654
GELU_B = 0.044715
ROWS_NN = (((1,), (0,)), ((), ()))
ROWS_NT = (((1,), (1,)), ((), ()))
ROWS_TN = (((0,), (0,)), ((), ()))
VMEM_BYTES = 56 * 1024 * 1024


def dot(a, b, dims=ROWS_NN):
    return lax.dot_general(a, b, dims, preferred_element_type=F32)


def params(**more):
    return pltpu.CompilerParams(vmem_limit_bytes=VMEM_BYTES, **more)


def cost(flops, moved, special=0):
    return pl.CostEstimate(flops=int(flops), bytes_accessed=int(moved), transcendentals=int(special))


def whole(shape):
    return pl.BlockSpec(shape, lambda *_: (0,) * len(shape))


def tile_bucket(step):
    rows = lax.broadcasted_iota(jnp.int32, (TILE, TILE), 0)
    cols = lax.broadcasted_iota(jnp.int32, (TILE, TILE), 1)
    offset = cols - rows + step * TILE
    distance = jnp.abs(offset)
    bucket = jnp.minimum(distance, 8)
    for border in BORDERS:
        bucket = bucket + jnp.where(distance >= border, 1, 0)
    return bucket + jnp.where(offset > 0, 16, 0)


def tile_range(step):
    return {-1: range(1, 16), 0: range(0, 32), 1: range(17, 32)}[step]


def fill_bias(bias_ref, table, heads):
    blocks = LENGTH // TILE
    buckets = {step: tile_bucket(step) for step in (-1, 0, 1)}
    for head in range(heads):
        near = {}
        for step in (-1, 0, 1):
            value = jnp.zeros((TILE, TILE), F32)
            for k in tile_range(step):
                value = jnp.where(buckets[step] == k, bias_ref[head, k], value)
            near[step] = value
        low = jnp.full((TILE, TILE), bias_ref[head, 15], F32)
        high = jnp.full((TILE, TILE), bias_ref[head, 31], F32)
        for i in range(blocks):
            for j in range(blocks):
                step = j - i
                value = near[step] if abs(step) <= 1 else (low if step < 0 else high)
                table[head, i * TILE : (i + 1) * TILE, j * TILE : (j + 1) * TILE] = value


def unit_rows(values):
    scale = lax.rsqrt(jnp.mean(values * values, axis=-1, keepdims=True) + EPSILON)
    return values * scale, scale


def group_rows(place_ref, out, pieces):
    rows = pieces[0].shape[0]
    for j, piece in enumerate(pieces):
        at = pl.multiple_of((place_ref[2] ^ j) * rows, rows)
        out[pl.ds(at, rows), :] = piece[...]


def part_rows(place_ref, pieces, source):
    rows = pieces[0].shape[0]
    for j, piece in enumerate(pieces):
        at = pl.multiple_of((place_ref[2] ^ j) * rows, rows)
        piece[...] = source[pl.ds(at, rows), :]


def attend_kernel(heads, tensors, place_ref, bias_ref, *refs):
    pieces = refs[:tensors]
    gain_ref, w_ref = refs[tensors : tensors + 2]
    parts = refs[tensors + 2 : 2 * tensors + 2]
    tok_ref, qkv_ref, mixed_ref, log_ref, table, wo, group, result = refs[2 * tensors + 2 :]
    inner = heads * HEAD_DIM
    step_id = pl.program_id(0)

    @pl.when(step_id == 0)
    def _():
        fill_bias(bias_ref, table, heads)
        wo[...] = w_ref[:, 3 * inner :]
        group_rows(place_ref, group, pieces)

    here = pl.ds(pl.multiple_of(step_id * LENGTH, LENGTH), LENGTH)
    tok_ref[...] = group[here, :]
    unit, _ = unit_rows(tok_ref[...].astype(F32))
    normed = (unit * gain_ref[...]).astype(BF16)
    qkv_ref[...] = dot(normed, w_ref[:, : 3 * inner]).astype(BF16)
    lanes = lax.broadcasted_iota(jnp.int32, (LENGTH, TILE), 1)
    logs = jnp.zeros((LENGTH, TILE), F32)
    for head in range(heads):
        at = head * HEAD_DIM
        query = qkv_ref[:, at : at + HEAD_DIM] * HEAD_DIM ** (-0.5)
        key = qkv_ref[:, inner + at : inner + at + HEAD_DIM]
        value = qkv_ref[:, 2 * inner + at : 2 * inner + at + HEAD_DIM]
        scores = dot(query.astype(BF16), key, ROWS_NT) + table[head]
        top = jnp.max(scores, axis=-1, keepdims=True)
        exponent = jnp.exp(scores - top)
        total = jnp.sum(exponent, axis=-1, keepdims=True)
        attention = (exponent * (1.0 / total)).astype(BF16)
        mixed_ref[:, at : at + HEAD_DIM] = dot(attention, value).astype(BF16)
        logs = jnp.where(lanes == head, top + jnp.log(total), logs)
    log_ref[...] = logs
    result[here, :] = dot(mixed_ref[...], wo[...], ROWS_NT).astype(BF16)

    @pl.when(step_id == pl.num_programs(0) - 1)
    def _():
        part_rows(place_ref, parts, result)


def attend(places, bias, pieces, gain, weights):
    tensors = len(pieces)
    piece_rows, width = pieces[0].shape
    rows = tensors * piece_rows
    heads = bias.shape[0]
    inner = heads * HEAD_DIM
    seqs = rows // LENGTH
    by_seq = lambda cols: pl.BlockSpec((LENGTH, cols), lambda s, *_: (s, 0))
    result = pl.pallas_call(
        functools.partial(attend_kernel, heads, tensors),
        grid_spec=pltpu.PrefetchScalarGridSpec(
            num_scalar_prefetch=1,
            grid=(seqs,),
            in_specs=[pl.BlockSpec(memory_space=pltpu.SMEM)]
            + [whole((piece_rows, width))] * tensors
            + [whole((1, width)), whole((width, 4 * inner))],
            out_specs=[whole((piece_rows, width))] * tensors
            + [by_seq(width), by_seq(3 * inner), by_seq(inner), by_seq(TILE)],
            scratch_shapes=[
                pltpu.VMEM((heads, LENGTH, LENGTH), F32),
                pltpu.VMEM((width, inner), BF16),
                pltpu.VMEM((rows, width), BF16),
                pltpu.VMEM((rows, width), BF16),
            ],
        ),
        out_shape=[jax.ShapeDtypeStruct((piece_rows, width), BF16)] * tensors
        + [
            jax.ShapeDtypeStruct((rows, width), BF16),
            jax.ShapeDtypeStruct((rows, 3 * inner), BF16),
            jax.ShapeDtypeStruct((rows, inner), BF16),
            jax.ShapeDtypeStruct((rows, TILE), F32),
        ],
        compiler_params=params(),
        cost_estimate=cost(8 * rows * width * inner + 4 * rows * LENGTH * inner, rows * width * 8, rows * LENGTH * heads),
        name="attend",
    )(places, bias, *pieces, gain, weights)
    return result[:tensors], result[tensors:]


def attend_back_kernel(
    heads, tensors, place_ref, bias_ref, tok_ref, gain_ref, w_ref, qkv_ref, mixed_ref, log_ref, *refs
):
    pieces, parts = refs[:tensors], refs[tensors : 2 * tensors]
    weight_ref, buckets_ref, gain_out, table, wo, gmix, gproj, near, far, rows_s, group, result = refs[2 * tensors :]
    inner = heads * HEAD_DIM
    blocks = LENGTH // TILE
    step_id = pl.program_id(0)

    @pl.when(step_id == 0)
    def _():
        fill_bias(bias_ref, table, heads)
        wo[...] = w_ref[:, 3 * inner :]
        near[...] = jnp.zeros_like(near)
        far[...] = jnp.zeros_like(far)
        weight_ref[...] = jnp.zeros_like(weight_ref)
        gain_out[...] = jnp.zeros_like(gain_out)
        group_rows(place_ref, group, pieces)

    here = pl.ds(pl.multiple_of(step_id * LENGTH, LENGTH), LENGTH)
    gmix[...] = dot(group[here, :], wo[...]).astype(BF16)
    for head in range(heads):
        at = head * HEAD_DIM
        query = (qkv_ref[:, at : at + HEAD_DIM] * HEAD_DIM ** (-0.5)).astype(BF16)
        key = qkv_ref[:, inner + at : inner + at + HEAD_DIM]
        value = qkv_ref[:, 2 * inner + at : 2 * inner + at + HEAD_DIM]
        grad_rows = gmix[:, at : at + HEAD_DIM]
        scores = dot(query, key, ROWS_NT) + table[head]
        attention = jnp.exp(scores - log_ref[:, head : head + 1])
        grad_weights = dot(grad_rows, value, ROWS_NT)
        inner_sum = jnp.sum(attention * grad_weights, axis=-1, keepdims=True)
        grad_scores = attention * (grad_weights - inner_sum)
        low = jnp.zeros((TILE, TILE), F32)
        high = jnp.zeros((TILE, TILE), F32)
        mid = [jnp.zeros((TILE, TILE), F32) for _ in range(3)]
        for i in range(blocks):
            for j in range(blocks):
                piece = grad_scores[i * TILE : (i + 1) * TILE, j * TILE : (j + 1) * TILE]
                if abs(j - i) <= 1:
                    mid[j - i + 1] = mid[j - i + 1] + piece
                elif j < i:
                    low = low + piece
                else:
                    high = high + piece
        for k in range(3):
            near[head * 3 + k] += mid[k]
        far[head * 2] += low
        far[head * 2 + 1] += high
        rounded = grad_scores.astype(BF16)
        gproj[:, at : at + HEAD_DIM] = (dot(rounded, key) * HEAD_DIM ** (-0.5)).astype(BF16)
        gproj[:, inner + at : inner + at + HEAD_DIM] = dot(rounded, query, ROWS_TN).astype(BF16)
        gproj[:, 2 * inner + at : 2 * inner + at + HEAD_DIM] = dot(
            attention.astype(BF16), grad_rows, ROWS_TN
        ).astype(BF16)
    unit, _ = unit_rows(tok_ref[...].astype(F32))
    normed = (unit * gain_ref[...]).astype(BF16)
    grad_normed = dot(gproj[...], w_ref[:, : 3 * inner], ROWS_NT)
    result[here, :] = grad_normed.astype(BF16)
    gain_out[...] += jnp.sum(grad_normed * unit, axis=0, keepdims=True)
    weight_ref[:, : 3 * inner] += dot(normed, gproj[...], ROWS_TN)
    weight_ref[:, 3 * inner :] += dot(group[here, :], mixed_ref[...], ROWS_TN)

    @pl.when(step_id == pl.num_programs(0) - 1)
    def _():
        part_rows(place_ref, parts, result)
        ids = [tile_bucket(step) for step in (-1, 0, 1)]
        for head in range(heads):
            for k in range(BUCKETS):
                total = jnp.zeros((TILE, TILE), F32)
                for step in (-1, 0, 1):
                    if k in tile_range(step):
                        total = total + jnp.where(ids[step + 1] == k, near[head * 3 + step + 1], 0.0)
                if k == 15:
                    total = total + far[head * 2]
                if k == 31:
                    total = total + far[head * 2 + 1]
                at = head * BUCKETS + k
                rows_s[at : at + 1, :] = jnp.sum(total, axis=0, keepdims=True)
        buckets_ref[...] = jnp.sum(rows_s[...], axis=1, keepdims=True)


def attend_back(places, bias, tokens, gain, weights, projected, mixed, logs, pieces):
    rows, width = tokens.shape
    tensors = len(pieces)
    piece = whole(pieces[0].shape)
    heads = bias.shape[0]
    inner = heads * HEAD_DIM
    seqs = rows // LENGTH
    by_seq = lambda cols: pl.BlockSpec((LENGTH, cols), lambda s, *_: (s, 0))
    result = pl.pallas_call(
        functools.partial(attend_back_kernel, heads, tensors),
        grid_spec=pltpu.PrefetchScalarGridSpec(
            num_scalar_prefetch=1,
            grid=(seqs,),
            in_specs=[
                pl.BlockSpec(memory_space=pltpu.SMEM),
                by_seq(width),
                whole((1, width)),
                whole((width, 4 * inner)),
                by_seq(3 * inner),
                by_seq(inner),
                by_seq(TILE),
            ]
            + [piece] * tensors,
            out_specs=[piece] * tensors
            + [whole((width, 4 * inner)), whole((heads * BUCKETS, 1)), whole((1, width))],
            scratch_shapes=[
                pltpu.VMEM((heads, LENGTH, LENGTH), F32),
                pltpu.VMEM((width, inner), BF16),
                pltpu.VMEM((LENGTH, inner), BF16),
                pltpu.VMEM((LENGTH, 3 * inner), BF16),
                pltpu.VMEM((heads * 3, TILE, TILE), F32),
                pltpu.VMEM((heads * 2, TILE, TILE), F32),
                pltpu.VMEM((heads * BUCKETS, TILE), F32),
                pltpu.VMEM((rows, width), BF16),
                pltpu.VMEM((rows, width), BF16),
            ],
        ),
        out_shape=[jax.ShapeDtypeStruct(pieces[0].shape, BF16)] * tensors
        + [
            jax.ShapeDtypeStruct((width, 4 * inner), F32),
            jax.ShapeDtypeStruct((heads * BUCKETS, 1), F32),
            jax.ShapeDtypeStruct((1, width), F32),
        ],
        compiler_params=params(),
        cost_estimate=cost(18 * rows * width * inner + 10 * rows * LENGTH * inner, rows * width * 12, rows * LENGTH * heads),
        name="attend_back",
    )(places, bias, tokens, gain, weights, projected, mixed, logs, *pieces)
    return result[:tensors], result[tensors:]


def place_kernel(target_ref, rows_ref, out_ref):
    count = out_ref.shape[0]
    rows = lax.broadcasted_iota(jnp.int32, (count, rows_ref.shape[0]), 0)
    chosen = jnp.where(rows == target_ref[...], 1.0, 0.0).astype(BF16)
    out_ref[...] = dot(chosen, rows_ref[...]).astype(BF16)


def place(target_row, rows, count):
    return pl.pallas_call(
        place_kernel,
        out_shape=jax.ShapeDtypeStruct((count, rows.shape[1]), BF16),
        compiler_params=params(),
        cost_estimate=cost(2 * count * rows.size, 4 * rows.size),
        name="place",
    )(target_row, rows)


def softmax_rows(logits):
    exponent = jnp.exp(logits - jnp.max(logits, axis=-1, keepdims=True))
    return exponent * (1.0 / jnp.sum(exponent, axis=-1, keepdims=True))


def sum_pieces(refs):
    total = refs[0][...].astype(F32)
    for ref in refs[1:]:
        total = total + ref[...].astype(F32)
    return total


def route_kernel(tensors, tok_ref, *refs):
    attn_refs = refs[:tensors]
    gain_ref, router_ref, target_ref, index_ref, kept_ref, hidden_ref, sent_ref, gate_ref = refs[tensors:]
    hidden = tok_ref[...].astype(F32) + sum_pieces(attn_refs)
    hidden_ref[...] = hidden
    unit, _ = unit_rows(hidden)
    moe_in = (unit * gain_ref[...]).astype(BF16)
    count = sent_ref.shape[0]
    rows = lax.broadcasted_iota(jnp.int32, (count, hidden.shape[0]), 0)
    chosen = jnp.where(rows == target_ref[...], 1.0, 0.0).astype(BF16)
    sent_ref[...] = dot(chosen, moe_in).astype(BF16)
    probs = softmax_rows(dot(moe_in, router_ref[...]))
    lanes = lax.broadcasted_iota(jnp.int32, probs.shape, 1)
    picked = jnp.sum(jnp.where(lanes == index_ref[...], probs, 0.0), axis=-1, keepdims=True)
    gate_ref[...] = picked * kept_ref[...].astype(F32)


def route(tokens, attn, gain, router, target_row, index_col, kept_col, count):
    rows, width = tokens.shape
    return pl.pallas_call(
        functools.partial(route_kernel, len(attn)),
        out_shape=[
            jax.ShapeDtypeStruct((rows, width), F32),
            jax.ShapeDtypeStruct((count, width), BF16),
            jax.ShapeDtypeStruct((rows, 1), F32),
        ],
        compiler_params=params(),
        cost_estimate=cost(2 * count * rows * width, 12 * rows * width),
        name="route",
    )(tokens, *attn, gain, router, target_row, index_col, kept_col)


def rest_choice(blocks, locals_, rest, expert):
    rows = lax.broadcasted_iota(jnp.int32, (blocks * rest, blocks * locals_ * rest), 0)
    cols = lax.broadcasted_iota(jnp.int32, (blocks * rest, blocks * locals_ * rest), 1)
    block = lax.div(rows, rest)
    wanted = block * (locals_ * rest) + expert * rest + (rows - block * rest)
    return jnp.where(cols == wanted, 1.0, 0.0).astype(BF16)


def pick_rows(out_ref, views, choice, main_rows, main, expert):
    at = 0
    pieces = []
    for view in views:
        blocks, size, width = view.shape
        if main:
            start = pl.multiple_of(expert * main, main)
            out_ref[at : at + blocks * main, :] = view[:, pl.ds(start, main), :].reshape(blocks * main, width)
            at += blocks * main
        rest = size - size * main_rows // out_ref.shape[0]
        pieces.append(view[:, size - rest :, :].reshape(blocks * rest, width))
    out_ref[main_rows:, :] = dot(choice, jnp.concatenate(pieces, axis=0)).astype(BF16)


def put_rows(views, value_ref, choice, main_rows, main, locals_, rest, expert):
    at = 0
    spread = dot(choice, value_ref[main_rows:, :], ROWS_TN).astype(BF16)
    rest_at = 0
    for view in views:
        blocks, _, width = view.shape
        if main:
            count = blocks * main
            start = pl.multiple_of(expert * main, main)
            view[:, pl.ds(start, main), :] = value_ref[at : at + count, :].reshape(blocks, main, width)
            at += count
        part = spread[rest_at : rest_at + blocks * locals_ * rest].reshape(blocks, locals_ * rest, width)
        rest_at += blocks * locals_ * rest

        @pl.when(expert == 0)
        def _():
            view[:, locals_ * main :, :] = part

        @pl.when(expert > 0)
        def _():
            view[:, locals_ * main :, :] = view[:, locals_ * main :, :] + part


def group_views(place_ref, ref, tensors, chunks):
    size = ref.shape[1] // chunks
    return [ref.at[place_ref[2] ^ j, k * size : (k + 1) * size] for k in range(chunks) for j in range(tensors)]


def join_halves(place_ref, own_in, peer_in, own_out, peer_out, win, wout):
    half = own_in.shape[1]
    mine = pl.multiple_of(place_ref[0] * half, half)
    other = pl.multiple_of((1 - place_ref[0]) * half, half)
    if win is not None:
        win[pl.ds(mine, half), :] = own_in[0]
        win[pl.ds(other, half), :] = peer_in[0]
    half_out = own_out.shape[2]
    mine = pl.multiple_of(place_ref[0] * half_out, half_out)
    other = pl.multiple_of((1 - place_ref[0]) * half_out, half_out)
    wout[:, pl.ds(mine, half_out)] = own_out[0]
    wout[:, pl.ds(other, half_out)] = peer_out[0]


def expert_kernel(chunks, tensors, main, locals_, rest, place_ref, *refs):
    refs = list(refs)
    take = lambda n: [refs.pop(0) for _ in range(n)]
    xs = take(chunks * tensors)
    (g_ref,) = take(1)
    own_in, peer_in, own_out, peer_out, router = take(5)
    back_refs = take(chunks * tensors)
    x_ref, ge_ref, hid_ref, gi_ref, gl_ref = take(5)
    win, wout, grows, inner, gunits, gate_s, dots, back = take(8)
    expert = pl.program_id(0)
    blocks = sum(ref.shape[0] for ref in xs)
    main_rows = blocks * main
    rows, width = x_ref.shape[1:]
    choice = rest_choice(blocks, locals_, rest, expert)
    pick_rows(x_ref.at[0], xs, choice, main_rows, main, expert)
    pick_rows(grows, group_views(place_ref, g_ref, tensors, chunks), choice, main_rows, main, expert)
    join_halves(place_ref, own_in, peer_in, own_out, peer_out, win, wout)
    inner[...] = dot(x_ref[0], win[...])
    gunits[...] = dot(grows[...], wout[...], ROWS_NT)
    probs = softmax_rows(dot(x_ref[0], router[...]))
    lanes = lax.broadcasted_iota(jnp.int32, probs.shape, 1)
    mine = lanes == place_ref[1] * locals_ + expert
    picked = jnp.sum(jnp.where(mine, probs, 0.0), axis=-1, keepdims=True)
    gate_s[...] = picked
    chunk = 16

    def body(step, _):
        at = pl.ds(pl.multiple_of(step * chunk, chunk), chunk)
        value = inner[at, :]
        square = value * value
        wave = jnp.tanh(GELU_A * value * (1.0 + GELU_B * square))
        half = 0.5 * (1.0 + wave)
        hidden = (value * half).astype(BF16)
        slope = half + (0.5 * GELU_A) * value * (1.0 - wave * wave) * (1.0 + 3.0 * GELU_B * square)
        units = gunits[at, :]
        gate = gate_s[at, :]
        hid_ref[0, at, :] = hidden
        gi_ref[0, at, :] = (gate * units * slope).astype(BF16)
        ge_ref[0, at, :] = (gate * grows[at, :].astype(F32)).astype(BF16)
        dots[at, :] = jnp.sum(hidden.astype(F32) * units, axis=-1, keepdims=True)
        return 0

    lax.fori_loop(0, rows // chunk, body, 0)
    grad_logits = (dots[...] * probs * (jnp.where(mine, 1.0, 0.0) - picked)).astype(BF16)
    gl_ref[0] = grad_logits
    back[...] = (dot(gi_ref[0], win[...], ROWS_NT) + dot(grad_logits, router[...], ROWS_NT)).astype(BF16)
    put_rows(back_refs, back, choice, main_rows, main, locals_, rest, expert)


def expert_forward_back(places, xs, gs, own_in, peer_in, own_out, peer_out, router, main, rest, chunks):
    locals_, half, wide = own_in.shape
    width, experts = router.shape
    blocks = sum(x.shape[0] for x in xs)
    rows = blocks * (main + rest)
    per = lambda *shape: pl.BlockSpec((1,) + shape, lambda e, *_: (e, 0, 0))
    saved = jax.ShapeDtypeStruct((locals_, rows, width), BF16)
    saved_wide = jax.ShapeDtypeStruct((locals_, rows, wide), BF16)
    result = pl.pallas_call(
        functools.partial(expert_kernel, chunks, len(xs) // chunks, main, locals_, rest),
        grid_spec=pltpu.PrefetchScalarGridSpec(
            num_scalar_prefetch=1,
            grid=(locals_,),
            in_specs=[whole(x.shape) for x in xs]
            + [whole(gs.shape)]
            + [per(half, wide)] * 2 + [per(wide, half)] * 2 + [whole((width, experts))],
            out_specs=[whole(x.shape) for x in xs]
            + [per(rows, width), per(rows, width), per(rows, wide), per(rows, wide), per(rows, experts)],
            scratch_shapes=[
                pltpu.VMEM((width, wide), BF16),
                pltpu.VMEM((wide, width), BF16),
                pltpu.VMEM((rows, width), BF16),
                pltpu.VMEM((rows, wide), F32),
                pltpu.VMEM((rows, wide), F32),
                pltpu.VMEM((rows, 1), F32),
                pltpu.VMEM((rows, 1), F32),
                pltpu.VMEM((rows, width), BF16),
            ],
        ),
        out_shape=[jax.ShapeDtypeStruct(x.shape, BF16) for x in xs]
        + [saved, saved, saved_wide, saved_wide, jax.ShapeDtypeStruct((locals_, rows, experts), BF16)],
        compiler_params=params(),
        cost_estimate=cost(6 * locals_ * rows * width * wide, locals_ * rows * width * 14, locals_ * rows * wide),
        name="experts",
    )(places, *xs, gs, own_in, peer_in, own_out, peer_out, router)
    return result[: len(xs)], result[len(xs) :]


def expert_weights_kernel(
    chunks, main, locals_, rest, place_ref, x_ref, ge_ref, hid_ref, gi_ref, gl_ref, own_out, peer_out, *refs
):
    forward_ref, in_own, in_send, out_own, out_send, router_ref, wout, value = refs
    expert = pl.program_id(0)
    tensors = forward_ref.shape[0]
    blocks = tensors * forward_ref.shape[1]
    forward_refs = group_views(place_ref, forward_ref, tensors, chunks)
    choice = rest_choice(blocks, locals_, rest, expert)
    join_halves(place_ref, own_out, peer_out, own_out, peer_out, None, wout)
    value[...] = dot(hid_ref[0], wout[...]).astype(BF16)
    put_rows(forward_refs, value, choice, blocks * main, main, locals_, rest, expert)
    half = in_own.shape[1]
    mine = pl.ds(pl.multiple_of(place_ref[0] * half, half), half)
    other = pl.ds(pl.multiple_of((1 - place_ref[0]) * half, half), half)
    in_own[0] = dot(x_ref[0, :, mine], gi_ref[0], ROWS_TN)
    in_send[0] = dot(x_ref[0, :, other], gi_ref[0], ROWS_TN).astype(BF16)
    out_own[0] = dot(hid_ref[0], ge_ref[0, :, mine], ROWS_TN)
    out_send[0] = dot(hid_ref[0], ge_ref[0, :, other], ROWS_TN).astype(BF16)

    @pl.when(expert == 0)
    def _():
        router_ref[...] = jnp.zeros_like(router_ref)

    router_ref[...] += dot(x_ref[0], gl_ref[0], ROWS_TN)


def expert_weights(places, saved, own_out, peer_out, shape, main, rest, chunks):
    x, ge, hidden, gi, gl = saved
    locals_, rows, width = x.shape
    wide = hidden.shape[2]
    experts = gl.shape[2]
    half = own_out.shape[2]
    per = lambda *shape: pl.BlockSpec((1,) + shape, lambda e, *_: (e, 0, 0))
    result = pl.pallas_call(
        functools.partial(expert_weights_kernel, chunks, main, locals_, rest),
        grid_spec=pltpu.PrefetchScalarGridSpec(
            num_scalar_prefetch=1,
            grid=(locals_,),
            in_specs=[per(rows, width), per(rows, width), per(rows, wide), per(rows, wide), per(rows, experts)]
            + [per(wide, half)] * 2,
            out_specs=[whole(shape)]
            + [per(half, wide), per(half, wide), per(wide, half), per(wide, half), whole((width, experts))],
            scratch_shapes=[pltpu.VMEM((wide, width), BF16), pltpu.VMEM((rows, width), BF16)],
        ),
        out_shape=[jax.ShapeDtypeStruct(shape, BF16)]
        + [
            jax.ShapeDtypeStruct((locals_, half, wide), F32),
            jax.ShapeDtypeStruct((locals_, half, wide), BF16),
            jax.ShapeDtypeStruct((locals_, wide, half), F32),
            jax.ShapeDtypeStruct((locals_, wide, half), BF16),
            jax.ShapeDtypeStruct((width, experts), F32),
        ],
        compiler_params=params(),
        cost_estimate=cost(6 * locals_ * rows * width * wide, locals_ * rows * width * 14),
        name="expert_weights",
    )(places, x, ge, hidden, gi, gl, own_out, peer_out)
    return result[0], result[1:]


def take_rows(target_ref, refs):
    total, at = None, 0
    for ref in refs:
        count = ref.shape[0]
        cols = lax.broadcasted_iota(jnp.int32, (target_ref.shape[0], count), 1) + at
        chosen = jnp.where(cols == target_ref[...], 1.0, 0.0).astype(BF16)
        part = dot(chosen, ref[...])
        total = part if total is None else total + part
        at += count
    return total


def hidden_back_kernel(target_ref, *refs):
    hidden_ref, cot_ref, gain_ref, grad_ref, attn_ref, gain_out = refs[-6:]
    grad_in = take_rows(target_ref, refs[:-6])
    unit, scale = unit_rows(hidden_ref[...])
    gain_out[...] = jnp.sum(grad_in * unit, axis=0, keepdims=True)
    scaled = grad_in * gain_ref[...]
    inside = jnp.mean(unit * scaled, axis=-1, keepdims=True)
    grad = cot_ref[...].astype(F32) + scale * (scaled - unit * inside)
    grad_ref[...] = grad
    attn_ref[...] = grad.astype(BF16)


def hidden_back(target_col, back, hidden, cotangent, gain):
    rows, width = hidden.shape
    return pl.pallas_call(
        hidden_back_kernel,
        out_shape=[
            jax.ShapeDtypeStruct((rows, width), F32),
            jax.ShapeDtypeStruct((rows, width), BF16),
            jax.ShapeDtypeStruct((1, width), F32),
        ],
        compiler_params=params(),
        cost_estimate=cost(3 * rows * rows * width, 16 * rows * width),
        name="hidden_back",
    )(target_col, *back, hidden, cotangent, gain)


def output_kernel(target_ref, *refs):
    hidden_ref, gate_ref, out_ref = refs[-3:]
    out_ref[...] = (hidden_ref[...] + gate_ref[...] * take_rows(target_ref, refs[:-3])).astype(BF16)


def output_rows(target_col, expert_rows, hidden, gate):
    return pl.pallas_call(
        output_kernel,
        out_shape=jax.ShapeDtypeStruct(hidden.shape, BF16),
        compiler_params=params(),
        cost_estimate=cost(3 * hidden.shape[0] * hidden.size, 10 * hidden.size),
        name="output_rows",
    )(target_col, *expert_rows, hidden, gate)


def tokens_back_kernel(tok_ref, *refs):
    gain_ref, hidden_ref, out_ref = refs[-3:]
    unit, scale = unit_rows(tok_ref[...].astype(F32))
    scaled = sum_pieces(refs[:-3]) * gain_ref[...]
    inside = jnp.mean(unit * scaled, axis=-1, keepdims=True)
    out_ref[...] = hidden_ref[...] + scale * (scaled - unit * inside)


def tokens_back(tokens, grad_normed, gain, grad_hidden):
    return pl.pallas_call(
        tokens_back_kernel,
        out_shape=jax.ShapeDtypeStruct(tokens.shape, F32),
        compiler_params=params(),
        cost_estimate=cost(10 * tokens.size, 12 * tokens.size),
        name="tokens_back",
    )(tokens, *grad_normed, gain, grad_hidden)


def shifted(value, axis, count, step):
    return lax.ppermute(value, axis, [(s, (s + step) % count) for s in range(count)])


def gather_ring(value, axis, count):
    me = lax.axis_index(axis)
    parts = [value] + [shifted(value, axis, count, -k) for k in range(1, count)]
    return jnp.roll(jnp.stack(parts), me, axis=0)


def swapped(value, axis, count, bits):
    return lax.ppermute(value, axis, [(s, s ^ bits) for s in range(count)])


def gather_pieces(value, axis, count):
    return [value] + [swapped(value, axis, count, k) for k in range(1, count)]


def swap_pieces(pieces, axis, count):
    return [pieces[0]] + [swapped(pieces[k], axis, count, k) for k in range(1, count)]


def on_device(
    sizes,
    tokens,
    cotangent,
    query_key_value_weight,
    attention_output_weight,
    rel_bias,
    gain_attn,
    gain_moe,
    w_router,
    w_in,
    w_out,
    expert_index,
    slot_index,
    kept_mask,
):
    dp_count, z_count, t_count = sizes
    tok_rows, width = tokens.shape
    experts_all = w_router.shape[1]
    capacity = max(2, 3 * tok_rows // (2 * experts_all))
    locals_ = w_in.shape[0]
    main = capacity // 16 * 16
    rest = capacity - main
    block = locals_ * capacity
    heads = rel_bias.shape[0]
    inner = heads * HEAD_DIM
    part = query_key_value_weight.shape[1]
    fine = w_router.shape[0]
    my_dp = lax.axis_index("dp")
    my_z = lax.axis_index("expert")
    bias = rel_bias.astype(F32)

    my_t = lax.axis_index("tensor")
    places = jnp.stack([my_dp, my_z, my_t]).astype(jnp.int32)
    token_pieces = gather_pieces(tokens, "tensor", t_count)

    small = jnp.concatenate([gain_attn[:, None], gain_moe[:, None], w_router], axis=1)
    smalls = gather_ring(small, "tensor", t_count)
    smalls = gather_ring(smalls, "expert", z_count)
    smalls = gather_ring(smalls, "dp", dp_count).reshape(width, 2 + experts_all)
    packed = jnp.concatenate(
        [
            query_key_value_weight.transpose(1, 0, 2).reshape(part, 3 * inner),
            attention_output_weight.T,
        ],
        axis=1,
    )
    packed = gather_ring(packed, "expert", z_count)
    weights = gather_ring(packed, "dp", dp_count).reshape(width, 4 * inner)
    gain_one = smalls[:, 0].astype(F32)[None]
    gain_two = smalls[:, 1].astype(F32)[None]
    router = smalls[:, 2:]

    peer_in = shifted(w_in, "dp", dp_count, 1)
    peer_out = shifted(w_out, "dp", dp_count, 1)

    z_of = expert_index // locals_
    local = expert_index - z_of * locals_
    inside = jnp.where(
        slot_index < main, local * main + slot_index, locals_ * main + local * rest + slot_index - main
    )
    target = (z_of ^ my_z) * block + inside
    target = jnp.where(kept_mask > 0, target, -1)
    target_row, target_col = target[None, :], target[:, None]
    count = z_count * block
    chunks = min(z_count, 4)
    many = z_count // chunks

    def over_expert(rows):
        pieces = swap_pieces(list(rows.reshape(z_count, block, width)), "expert", z_count)
        if many == 1:
            return pieces
        return [jnp.concatenate(pieces[k * many : (k + 1) * many], axis=0) for k in range(chunks)]

    def back_over_expert(groups):
        if many > 1:
            groups = [g[i * block : (i + 1) * block] for g in groups for i in range(many)]
        pieces = swap_pieces(groups, "expert", z_count)
        if many == 1:
            return pieces
        return [jnp.concatenate(pieces[k * many : (k + 1) * many], axis=0) for k in range(chunks)]

    grad_rows = jnp.concatenate(over_expert(place(target_row, cotangent, count)), axis=0)
    grad_arrived = lax.all_gather(grad_rows, "tensor", axis=0).reshape(t_count, z_count, block, width)

    parts, (group_tokens, projected, mixed, logs) = attend(places, bias, token_pieces, gain_one, weights)
    attn = swap_pieces(parts, "tensor", t_count)
    hidden_one, sent, gate = route(
        tokens, attn, gain_two, router, target_row, expert_index[:, None], kept_mask[:, None], count
    )
    arrived = [
        piece.reshape(many, block, width)
        for group in over_expert(sent)
        for piece in gather_pieces(group, "tensor", t_count)
    ]
    back_parts, saved = expert_forward_back(
        places, arrived, grad_arrived, w_in, peer_in, w_out, peer_out, router, main, rest, chunks
    )
    back_swapped = [
        swap_pieces(
            [piece.reshape(many * block, width) for piece in back_parts[k * t_count : (k + 1) * t_count]],
            "tensor",
            t_count,
        )
        for k in range(chunks)
    ]
    forward_part, (in_own, in_send, out_own, out_send, router_part) = expert_weights(
        places, saved, w_out, peer_out, grad_arrived.shape, main, rest, chunks
    )
    back_swapped, forward_part, in_send, out_send = lax.optimization_barrier(
        (back_swapped, forward_part, in_send, out_send)
    )

    def summed(pieces):
        total = pieces[0].astype(F32)
        for piece in pieces[1:]:
            total = total + piece.astype(F32)
        return total.astype(BF16)

    grad_back = back_over_expert([summed(pieces) for pieces in back_swapped])
    grad_w_in = in_own + shifted(in_send, "dp", dp_count, 1).astype(F32)
    grad_w_out = out_own + shifted(out_send, "dp", dp_count, 1).astype(F32)
    grad_hidden, grad_attn, gain_two_part = hidden_back(target_col, grad_back, hidden_one, cotangent, gain_two)
    normed_parts, (weight_part, bucket_part, gain_one_part) = attend_back(
        places, bias, group_tokens, gain_one, weights, projected, mixed, logs,
        gather_pieces(grad_attn, "tensor", t_count),
    )
    grad_normed = swap_pieces(normed_parts, "tensor", t_count)
    forward_sum = lax.psum_scatter(
        forward_part.reshape(t_count * z_count * block, width), "tensor", scatter_dimension=0, tiled=True
    )
    forward_rows = back_over_expert(list(forward_sum.reshape(chunks, many * block, width)))
    output = output_rows(target_col, forward_rows, hidden_one, gate)
    grad_tokens = tokens_back(tokens, grad_normed, gain_one, grad_hidden)

    owners = dp_count * z_count
    smalls = jnp.concatenate(
        [
            gain_one_part.reshape(owners, part),
            gain_two_part.reshape(owners, part),
            router_part.reshape(owners, part * experts_all),
            jnp.broadcast_to(bucket_part.reshape(1, heads * BUCKETS), (owners, heads * BUCKETS)),
        ],
        axis=1,
    )
    extra = -(-smalls.shape[1] // (16 * width)) * 16
    smalls = jnp.pad(smalls, ((0, 0), (0, extra * width - smalls.shape[1]))).reshape(owners, extra, width)
    payload = jnp.concatenate([weight_part.reshape(owners, part, width), smalls], axis=1)
    payload = payload.reshape(dp_count, z_count, part + extra, width)
    own = lax.dynamic_index_in_dim(payload, my_dp, 0, keepdims=False)
    other = lax.dynamic_index_in_dim(payload, 1 - my_dp, 0, keepdims=False)
    summed_half = own + shifted(other.astype(BF16), "dp", dp_count, 1).astype(F32)
    turned = [lax.dynamic_index_in_dim(summed_half, my_z ^ k, 0, keepdims=False) for k in range(z_count)]
    pieces = swap_pieces([turned[0]] + [t.astype(BF16) for t in turned[1:]], "expert", z_count)
    total = pieces[0]
    for piece in pieces[1:]:
        total = total + piece.astype(F32)
    weight_total = total[:part].reshape(part, 4, inner)
    grad_w_qkv = weight_total[:, :3].transpose(1, 0, 2)
    grad_w_attn_out = weight_total[:, 3].T
    flat = total[part:].reshape(-1)
    ends = [part, 2 * part, 2 * part + part * experts_all]
    grad_rel_bias = flat[ends[2] : ends[2] + heads * BUCKETS].reshape(heads, BUCKETS)
    rows_left = jnp.concatenate(
        [
            flat[: ends[0]].reshape(t_count, fine),
            flat[ends[0] : ends[1]].reshape(t_count, fine),
            flat[ends[1] : ends[2]].reshape(t_count, fine * experts_all),
        ],
        axis=1,
    )
    turned = [lax.dynamic_index_in_dim(rows_left, my_t ^ k, 0, keepdims=False) for k in range(t_count)]
    left = turned[0]
    for piece in swap_pieces(turned, "tensor", t_count)[1:]:
        left = left + piece
    grad_gain_attn = left[:fine]
    grad_gain_moe = left[fine : 2 * fine]
    grad_w_router = left[2 * fine :].reshape(fine, experts_all)
    return (
        output,
        grad_tokens,
        grad_w_qkv,
        grad_w_attn_out,
        grad_rel_bias,
        grad_gain_attn,
        grad_gain_moe,
        grad_w_router,
        grad_w_in,
        grad_w_out,
    )


def solution(mesh):
    placed = (
        P(("dp", "expert", "tensor"), None),
        P(("dp", "expert", "tensor"), None),
        P(None, ("dp", "expert"), "tensor"),
        P("tensor", ("dp", "expert")),
        P("tensor", None),
        P(("dp", "expert", "tensor")),
        P(("dp", "expert", "tensor")),
        P(("dp", "expert", "tensor"), None),
        P("expert", "dp", "tensor"),
        P("expert", "tensor", "dp"),
        P(("dp", "expert", "tensor")),
        P(("dp", "expert", "tensor")),
        P(("dp", "expert", "tensor")),
    )
    sizes = tuple(mesh.shape[name] for name in ("dp", "expert", "tensor"))
    return jax.shard_map(
        functools.partial(on_device, sizes),
        mesh=mesh,
        in_specs=placed,
        out_specs=(
            P(("dp", "expert", "tensor"), None),
            P(("dp", "expert", "tensor"), None),
            P(None, ("dp", "expert"), "tensor"),
            P("tensor", ("dp", "expert")),
            P("tensor", None),
            P(("dp", "expert", "tensor")),
            P(("dp", "expert", "tensor")),
            P(("dp", "expert", "tensor"), None),
            P("expert", "dp", "tensor"),
            P("expert", "tensor", "dp"),
        ),
        check_vma=False,
    )
```

```python
import functools

import jax
import jax.numpy as jnp
from jax import lax
from jax.experimental import pallas as pl
from jax.experimental.pallas import tpu as pltpu
from jax.sharding import PartitionSpec as P

HEAD_DIM = 64
BUCKETS = 32
LENGTH = 512
TILE = 128
EPSILON = 1e-06
BORDERS = (12, 16, 23, 32, 46, 64, 91)
F32 = jnp.float32
BF16 = jnp.bfloat16
GELU_A = 0.7978845608028654
GELU_B = 0.044715
ROWS_NN = (((1,), (0,)), ((), ()))
ROWS_NT = (((1,), (1,)), ((), ()))
ROWS_TN = (((0,), (0,)), ((), ()))
VMEM_BYTES = 56 * 1024 * 1024


def dot(a, b, dims=ROWS_NN):
    return lax.dot_general(a, b, dims, preferred_element_type=F32)


def params(**more):
    return pltpu.CompilerParams(vmem_limit_bytes=VMEM_BYTES, **more)


def cost(flops, moved, special=0):
    return pl.CostEstimate(flops=int(flops), bytes_accessed=int(moved), transcendentals=int(special))


def whole(shape):
    return pl.BlockSpec(shape, lambda *_: (0,) * len(shape))


def tile_bucket(step):
    rows = lax.broadcasted_iota(jnp.int32, (TILE, TILE), 0)
    cols = lax.broadcasted_iota(jnp.int32, (TILE, TILE), 1)
    offset = cols - rows + step * TILE
    distance = jnp.abs(offset)
    bucket = jnp.minimum(distance, 8)
    for border in BORDERS:
        bucket = bucket + jnp.where(distance >= border, 1, 0)
    return bucket + jnp.where(offset > 0, 16, 0)


def tile_range(step):
    return {-1: range(1, 16), 0: range(0, 32), 1: range(17, 32)}[step]


def fill_bias(bias_ref, table, heads):
    blocks = LENGTH // TILE
    buckets = {step: tile_bucket(step) for step in (-1, 0, 1)}
    for head in range(heads):
        near = {}
        for step in (-1, 0, 1):
            value = jnp.zeros((TILE, TILE), F32)
            for k in tile_range(step):
                value = jnp.where(buckets[step] == k, bias_ref[head, k], value)
            near[step] = value
        low = jnp.full((TILE, TILE), bias_ref[head, 15], F32)
        high = jnp.full((TILE, TILE), bias_ref[head, 31], F32)
        for i in range(blocks):
            for j in range(blocks):
                step = j - i
                value = near[step] if abs(step) <= 1 else (low if step < 0 else high)
                table[head, i * TILE : (i + 1) * TILE, j * TILE : (j + 1) * TILE] = value


def unit_rows(values):
    scale = lax.rsqrt(jnp.mean(values * values, axis=-1, keepdims=True) + EPSILON)
    return values * scale, scale


def group_rows(place_ref, out, pieces):
    rows = pieces[0].shape[0]
    for j, piece in enumerate(pieces):
        at = pl.multiple_of((place_ref[2] ^ j) * rows, rows)
        out[pl.ds(at, rows), :] = piece[...]


def part_rows(place_ref, pieces, source):
    rows = pieces[0].shape[0]
    for j, piece in enumerate(pieces):
        at = pl.multiple_of((place_ref[2] ^ j) * rows, rows)
        piece[...] = source[pl.ds(at, rows), :]


def attend_kernel(heads, tensors, owners, part, place_ref, bias_ref, *refs):
    refs = list(refs)
    take = lambda n: [refs.pop(0) for _ in range(n)]
    pieces, owned, (gain_ref,), parts = take(tensors), take(owners), take(1), take(tensors)
    tok_ref, qkv_ref, mixed_ref, log_ref, w_ref, table, wo, group, result = refs
    inner = heads * HEAD_DIM
    step_id = pl.program_id(0)

    @pl.when(step_id == 0)
    def _():
        fill_bias(bias_ref, table, heads)
        group_rows(place_ref, group, pieces)
        for k, piece in enumerate(owned):
            at = pl.multiple_of((place_ref[3] ^ k) * part, part) if owners > 1 else 0
            w_ref[pl.ds(at, part), :] = piece[:part, :]
        wo[...] = w_ref[:, 3 * inner :]

    here = pl.ds(pl.multiple_of(step_id * LENGTH, LENGTH), LENGTH)
    tok_ref[...] = group[here, :]
    unit, _ = unit_rows(tok_ref[...].astype(F32))
    normed = (unit * gain_ref[...]).astype(BF16)
    qkv_ref[...] = dot(normed, w_ref[:, : 3 * inner]).astype(BF16)
    lanes = lax.broadcasted_iota(jnp.int32, (LENGTH, TILE), 1)
    logs = jnp.zeros((LENGTH, TILE), F32)
    for head in range(heads):
        at = head * HEAD_DIM
        query = qkv_ref[:, at : at + HEAD_DIM] * HEAD_DIM ** (-0.5)
        key = qkv_ref[:, inner + at : inner + at + HEAD_DIM]
        value = qkv_ref[:, 2 * inner + at : 2 * inner + at + HEAD_DIM]
        scores = dot(query.astype(BF16), key, ROWS_NT) + table[head]
        top = jnp.max(scores, axis=-1, keepdims=True)
        exponent = jnp.exp(scores - top)
        total = jnp.sum(exponent, axis=-1, keepdims=True)
        attention = (exponent * (1.0 / total)).astype(BF16)
        mixed_ref[:, at : at + HEAD_DIM] = dot(attention, value).astype(BF16)
        logs = jnp.where(lanes == head, top + jnp.log(total), logs)
    log_ref[...] = logs
    result[here, :] = dot(mixed_ref[...], wo[...], ROWS_NT).astype(BF16)

    @pl.when(step_id == pl.num_programs(0) - 1)
    def _():
        part_rows(place_ref, parts, result)


def attend(places, bias, pieces, owned, part, gain):
    tensors = len(pieces)
    piece_rows, width = pieces[0].shape
    rows = tensors * piece_rows
    heads = bias.shape[0]
    inner = heads * HEAD_DIM
    seqs = rows // LENGTH
    by_seq = lambda cols: pl.BlockSpec((LENGTH, cols), lambda s, *_: (s, 0))
    result = pl.pallas_call(
        functools.partial(attend_kernel, heads, tensors, len(owned), part),
        grid_spec=pltpu.PrefetchScalarGridSpec(
            num_scalar_prefetch=1,
            grid=(seqs,),
            in_specs=[pl.BlockSpec(memory_space=pltpu.SMEM)]
            + [whole((piece_rows, width))] * tensors
            + [whole(o.shape) for o in owned]
            + [whole((1, width))],
            out_specs=[whole((piece_rows, width))] * tensors
            + [by_seq(width), by_seq(3 * inner), by_seq(inner), by_seq(TILE), whole((width, 4 * inner))],
            scratch_shapes=[
                pltpu.VMEM((heads, LENGTH, LENGTH), F32),
                pltpu.VMEM((width, inner), BF16),
                pltpu.VMEM((rows, width), BF16),
                pltpu.VMEM((rows, width), BF16),
            ],
        ),
        out_shape=[jax.ShapeDtypeStruct((piece_rows, width), BF16)] * tensors
        + [
            jax.ShapeDtypeStruct((rows, width), BF16),
            jax.ShapeDtypeStruct((rows, 3 * inner), BF16),
            jax.ShapeDtypeStruct((rows, inner), BF16),
            jax.ShapeDtypeStruct((rows, TILE), F32),
            jax.ShapeDtypeStruct((width, 4 * inner), BF16),
        ],
        compiler_params=params(),
        cost_estimate=cost(8 * rows * width * inner + 4 * rows * LENGTH * inner, rows * width * 8, rows * LENGTH * heads),
        name="attend",
    )(places, bias, *pieces, *owned, gain)
    return result[:tensors], result[tensors:]


def attend_back_kernel(
    heads, tensors, place_ref, bias_ref, tok_ref, gain_ref, w_ref, qkv_ref, mixed_ref, log_ref, *refs
):
    pieces, parts = refs[:tensors], refs[tensors : 2 * tensors]
    weight_ref, buckets_ref, gain_out, table, wo, gmix, gproj, near, far, rows_s, group, result = refs[2 * tensors :]
    inner = heads * HEAD_DIM
    blocks = LENGTH // TILE
    step_id = pl.program_id(0)

    @pl.when(step_id == 0)
    def _():
        fill_bias(bias_ref, table, heads)
        wo[...] = w_ref[:, 3 * inner :]
        near[...] = jnp.zeros_like(near)
        far[...] = jnp.zeros_like(far)
        weight_ref[...] = jnp.zeros_like(weight_ref)
        gain_out[...] = jnp.zeros_like(gain_out)
        group_rows(place_ref, group, pieces)

    here = pl.ds(pl.multiple_of(step_id * LENGTH, LENGTH), LENGTH)
    gmix[...] = dot(group[here, :], wo[...]).astype(BF16)
    for head in range(heads):
        at = head * HEAD_DIM
        query = (qkv_ref[:, at : at + HEAD_DIM] * HEAD_DIM ** (-0.5)).astype(BF16)
        key = qkv_ref[:, inner + at : inner + at + HEAD_DIM]
        value = qkv_ref[:, 2 * inner + at : 2 * inner + at + HEAD_DIM]
        grad_rows = gmix[:, at : at + HEAD_DIM]
        scores = dot(query, key, ROWS_NT) + table[head]
        attention = jnp.exp(scores - log_ref[:, head : head + 1])
        grad_weights = dot(grad_rows, value, ROWS_NT)
        inner_sum = jnp.sum(attention * grad_weights, axis=-1, keepdims=True)
        grad_scores = attention * (grad_weights - inner_sum)
        low = jnp.zeros((TILE, TILE), F32)
        high = jnp.zeros((TILE, TILE), F32)
        mid = [jnp.zeros((TILE, TILE), F32) for _ in range(3)]
        for i in range(blocks):
            for j in range(blocks):
                piece = grad_scores[i * TILE : (i + 1) * TILE, j * TILE : (j + 1) * TILE]
                if abs(j - i) <= 1:
                    mid[j - i + 1] = mid[j - i + 1] + piece
                elif j < i:
                    low = low + piece
                else:
                    high = high + piece
        for k in range(3):
            near[head * 3 + k] += mid[k]
        far[head * 2] += low
        far[head * 2 + 1] += high
        rounded = grad_scores.astype(BF16)
        gproj[:, at : at + HEAD_DIM] = (dot(rounded, key) * HEAD_DIM ** (-0.5)).astype(BF16)
        gproj[:, inner + at : inner + at + HEAD_DIM] = dot(rounded, query, ROWS_TN).astype(BF16)
        gproj[:, 2 * inner + at : 2 * inner + at + HEAD_DIM] = dot(
            attention.astype(BF16), grad_rows, ROWS_TN
        ).astype(BF16)
    unit, _ = unit_rows(tok_ref[...].astype(F32))
    normed = (unit * gain_ref[...]).astype(BF16)
    grad_normed = dot(gproj[...], w_ref[:, : 3 * inner], ROWS_NT)
    result[here, :] = grad_normed.astype(BF16)
    gain_out[...] += jnp.sum(grad_normed * unit, axis=0, keepdims=True)
    weight_ref[:, : 3 * inner] += dot(normed, gproj[...], ROWS_TN)
    weight_ref[:, 3 * inner :] += dot(group[here, :], mixed_ref[...], ROWS_TN)

    @pl.when(step_id == pl.num_programs(0) - 1)
    def _():
        part_rows(place_ref, parts, result)
        ids = [tile_bucket(step) for step in (-1, 0, 1)]
        for head in range(heads):
            for k in range(BUCKETS):
                total = jnp.zeros((TILE, TILE), F32)
                for step in (-1, 0, 1):
                    if k in tile_range(step):
                        total = total + jnp.where(ids[step + 1] == k, near[head * 3 + step + 1], 0.0)
                if k == 15:
                    total = total + far[head * 2]
                if k == 31:
                    total = total + far[head * 2 + 1]
                at = head * BUCKETS + k
                rows_s[at : at + 1, :] = jnp.sum(total, axis=0, keepdims=True)
        buckets_ref[...] = jnp.sum(rows_s[...], axis=1, keepdims=True)


def attend_back(places, bias, tokens, gain, weights, projected, mixed, logs, pieces):
    rows, width = tokens.shape
    tensors = len(pieces)
    piece = whole(pieces[0].shape)
    heads = bias.shape[0]
    inner = heads * HEAD_DIM
    seqs = rows // LENGTH
    by_seq = lambda cols: pl.BlockSpec((LENGTH, cols), lambda s, *_: (s, 0))
    result = pl.pallas_call(
        functools.partial(attend_back_kernel, heads, tensors),
        grid_spec=pltpu.PrefetchScalarGridSpec(
            num_scalar_prefetch=1,
            grid=(seqs,),
            in_specs=[
                pl.BlockSpec(memory_space=pltpu.SMEM),
                by_seq(width),
                whole((1, width)),
                whole((width, 4 * inner)),
                by_seq(3 * inner),
                by_seq(inner),
                by_seq(TILE),
            ]
            + [piece] * tensors,
            out_specs=[piece] * tensors
            + [whole((width, 4 * inner)), whole((heads * BUCKETS, 1)), whole((1, width))],
            scratch_shapes=[
                pltpu.VMEM((heads, LENGTH, LENGTH), F32),
                pltpu.VMEM((width, inner), BF16),
                pltpu.VMEM((LENGTH, inner), BF16),
                pltpu.VMEM((LENGTH, 3 * inner), BF16),
                pltpu.VMEM((heads * 3, TILE, TILE), F32),
                pltpu.VMEM((heads * 2, TILE, TILE), F32),
                pltpu.VMEM((heads * BUCKETS, TILE), F32),
                pltpu.VMEM((rows, width), BF16),
                pltpu.VMEM((rows, width), BF16),
            ],
        ),
        out_shape=[jax.ShapeDtypeStruct(pieces[0].shape, BF16)] * tensors
        + [
            jax.ShapeDtypeStruct((width, 4 * inner), F32),
            jax.ShapeDtypeStruct((heads * BUCKETS, 1), F32),
            jax.ShapeDtypeStruct((1, width), F32),
        ],
        compiler_params=params(),
        cost_estimate=cost(18 * rows * width * inner + 10 * rows * LENGTH * inner, rows * width * 12, rows * LENGTH * heads),
        name="attend_back",
    )(places, bias, tokens, gain, weights, projected, mixed, logs, *pieces)
    return result[:tensors], result[tensors:]


def place_kernel(target_ref, rows_ref, out_ref):
    count = out_ref.shape[0]
    rows = lax.broadcasted_iota(jnp.int32, (count, rows_ref.shape[0]), 0)
    chosen = jnp.where(rows == target_ref[...], 1.0, 0.0).astype(BF16)
    out_ref[...] = dot(chosen, rows_ref[...]).astype(BF16)


def place(target_row, rows, count):
    return pl.pallas_call(
        place_kernel,
        out_shape=jax.ShapeDtypeStruct((count, rows.shape[1]), BF16),
        compiler_params=params(),
        cost_estimate=cost(2 * count * rows.size, 4 * rows.size),
        name="place",
    )(target_row, rows)


def softmax_rows(logits):
    exponent = jnp.exp(logits - jnp.max(logits, axis=-1, keepdims=True))
    return exponent * (1.0 / jnp.sum(exponent, axis=-1, keepdims=True))


def sum_pieces(refs):
    total = refs[0][...].astype(F32)
    for ref in refs[1:]:
        total = total + ref[...].astype(F32)
    return total


def route_kernel(tensors, tok_ref, *refs):
    attn_refs = refs[:tensors]
    gain_ref, router_ref, target_ref, index_ref, kept_ref, hidden_ref, sent_ref, gate_ref = refs[tensors:]
    hidden = tok_ref[...].astype(F32) + sum_pieces(attn_refs)
    hidden_ref[...] = hidden
    unit, _ = unit_rows(hidden)
    moe_in = (unit * gain_ref[...]).astype(BF16)
    count = sent_ref.shape[0]
    rows = lax.broadcasted_iota(jnp.int32, (count, hidden.shape[0]), 0)
    chosen = jnp.where(rows == target_ref[...], 1.0, 0.0).astype(BF16)
    sent_ref[...] = dot(chosen, moe_in).astype(BF16)
    probs = softmax_rows(dot(moe_in, router_ref[...]))
    lanes = lax.broadcasted_iota(jnp.int32, probs.shape, 1)
    picked = jnp.sum(jnp.where(lanes == index_ref[...], probs, 0.0), axis=-1, keepdims=True)
    gate_ref[...] = picked * kept_ref[...].astype(F32)


def route(tokens, attn, gain, router, target_row, index_col, kept_col, count):
    rows, width = tokens.shape
    return pl.pallas_call(
        functools.partial(route_kernel, len(attn)),
        out_shape=[
            jax.ShapeDtypeStruct((rows, width), F32),
            jax.ShapeDtypeStruct((count, width), BF16),
            jax.ShapeDtypeStruct((rows, 1), F32),
        ],
        compiler_params=params(),
        cost_estimate=cost(2 * count * rows * width, 12 * rows * width),
        name="route",
    )(tokens, *attn, gain, router, target_row, index_col, kept_col)


def rest_choice(blocks, locals_, rest, expert):
    rows = lax.broadcasted_iota(jnp.int32, (blocks * rest, blocks * locals_ * rest), 0)
    cols = lax.broadcasted_iota(jnp.int32, (blocks * rest, blocks * locals_ * rest), 1)
    block = lax.div(rows, rest)
    wanted = block * (locals_ * rest) + expert * rest + (rows - block * rest)
    return jnp.where(cols == wanted, 1.0, 0.0).astype(BF16)


def pick_rows(out_ref, views, choice, main_rows, main, expert):
    at = 0
    pieces = []
    for view in views:
        blocks, size, width = view.shape
        if main:
            start = pl.multiple_of(expert * main, main)
            out_ref[at : at + blocks * main, :] = view[:, pl.ds(start, main), :].reshape(blocks * main, width)
            at += blocks * main
        rest = size - size * main_rows // out_ref.shape[0]
        pieces.append(view[:, size - rest :, :].reshape(blocks * rest, width))
    out_ref[main_rows:, :] = dot(choice, jnp.concatenate(pieces, axis=0)).astype(BF16)


def put_rows(views, value_ref, choice, main_rows, main, locals_, rest, expert):
    at = 0
    spread = dot(choice, value_ref[main_rows:, :], ROWS_TN).astype(BF16)
    rest_at = 0
    for view in views:
        blocks, _, width = view.shape
        if main:
            count = blocks * main
            start = pl.multiple_of(expert * main, main)
            view[:, pl.ds(start, main), :] = value_ref[at : at + count, :].reshape(blocks, main, width)
            at += count
        part = spread[rest_at : rest_at + blocks * locals_ * rest].reshape(blocks, locals_ * rest, width)
        rest_at += blocks * locals_ * rest

        @pl.when(expert == 0)
        def _():
            view[:, locals_ * main :, :] = part

        @pl.when(expert > 0)
        def _():
            view[:, locals_ * main :, :] = view[:, locals_ * main :, :] + part


def group_views(place_ref, ref, tensors, chunks):
    size = ref.shape[1] // chunks
    return [ref.at[place_ref[2] ^ j, k * size : (k + 1) * size] for k in range(chunks) for j in range(tensors)]


def join_halves(place_ref, own_in, peer_in, own_out, peer_out, win, wout):
    half = own_in.shape[1]
    mine = pl.multiple_of(place_ref[0] * half, half)
    other = pl.multiple_of((1 - place_ref[0]) * half, half)
    if win is not None:
        win[pl.ds(mine, half), :] = own_in[0]
        win[pl.ds(other, half), :] = peer_in[0]
    half_out = own_out.shape[2]
    mine = pl.multiple_of(place_ref[0] * half_out, half_out)
    other = pl.multiple_of((1 - place_ref[0]) * half_out, half_out)
    wout[:, pl.ds(mine, half_out)] = own_out[0]
    wout[:, pl.ds(other, half_out)] = peer_out[0]


def expert_kernel(chunks, tensors, main, locals_, rest, place_ref, *refs):
    refs = list(refs)
    take = lambda n: [refs.pop(0) for _ in range(n)]
    xs = take(chunks * tensors)
    (g_ref,) = take(1)
    own_in, peer_in, own_out, peer_out, router = take(5)
    back_refs = take(chunks * tensors)
    x_ref, ge_ref, hid_ref, gi_ref, gl_ref = take(5)
    win, wout, grows, inner, gunits, gate_s, dots, back = take(8)
    expert = pl.program_id(0)
    blocks = sum(ref.shape[0] for ref in xs)
    main_rows = blocks * main
    rows, width = x_ref.shape[1:]
    wide = win.shape[1]
    choice = rest_choice(blocks, locals_, rest, expert)
    pick_rows(x_ref.at[0], xs, choice, main_rows, main, expert)
    pick_rows(grows, group_views(place_ref, g_ref, tensors, chunks), choice, main_rows, main, expert)
    join_halves(place_ref, own_in, peer_in, own_out, peer_out, win, wout)
    inner[...] = dot(x_ref[0], win[...])
    gunits[...] = dot(grows[...], wout[...], ROWS_NT)
    probs = softmax_rows(dot(x_ref[0], router[...]))
    lanes = lax.broadcasted_iota(jnp.int32, probs.shape, 1)
    mine = lanes == place_ref[1] * locals_ + expert
    picked = jnp.sum(jnp.where(mine, probs, 0.0), axis=-1, keepdims=True)
    gate_s[...] = jnp.broadcast_to(picked, gate_s.shape)
    chunk = 16
    half_wide = wide // 2 if wide % (2 * TILE) == 0 else wide

    def body(step, _):
        at = pl.ds(pl.multiple_of(step * chunk, chunk), chunk)
        gate_tile = gate_s[at, :]
        gate = jnp.concatenate([gate_tile] * (half_wide // TILE), axis=1)
        total = None
        for start in range(0, wide, half_wide):
            lanes_at = slice(start, start + half_wide)
            value = inner[at, lanes_at]
            square = value * value
            wave = jnp.tanh(value * (GELU_A + (GELU_A * GELU_B) * square))
            half = 0.5 + 0.5 * wave
            hidden = (value * half).astype(BF16)
            bend = value * (0.5 * GELU_A + (1.5 * GELU_A * GELU_B) * square)
            slope = half + bend * (1.0 - wave * wave)
            units = gunits[at, lanes_at]
            hid_ref[0, at, lanes_at] = hidden
            gi_ref[0, at, lanes_at] = (gate * (units * slope)).astype(BF16)
            product = hidden.astype(F32) * units
            for tile in range(0, half_wide, TILE):
                part = product[:, tile : tile + TILE]
                total = part if total is None else total + part
        dots[at, :] = total
        gate = jnp.concatenate([gate_tile] * (width // TILE), axis=1)
        ge_ref[0, at, :] = (gate * grows[at, :].astype(F32)).astype(BF16)
        return 0

    lax.fori_loop(0, rows // chunk, body, 0, unroll=4)
    grad_logits = (jnp.sum(dots[...], axis=-1, keepdims=True) * probs * (jnp.where(mine, 1.0, 0.0) - picked)).astype(BF16)
    gl_ref[0] = grad_logits
    back[...] = (dot(gi_ref[0], win[...], ROWS_NT) + dot(grad_logits, router[...], ROWS_NT)).astype(BF16)
    put_rows(back_refs, back, choice, main_rows, main, locals_, rest, expert)


def expert_forward_back(places, xs, gs, own_in, peer_in, own_out, peer_out, router, main, rest, chunks):
    locals_, half, wide = own_in.shape
    width, experts = router.shape
    blocks = sum(x.shape[0] for x in xs)
    rows = blocks * (main + rest)
    per = lambda *shape: pl.BlockSpec((1,) + shape, lambda e, *_: (e, 0, 0))
    saved = jax.ShapeDtypeStruct((locals_, rows, width), BF16)
    saved_wide = jax.ShapeDtypeStruct((locals_, rows, wide), BF16)
    result = pl.pallas_call(
        functools.partial(expert_kernel, chunks, len(xs) // chunks, main, locals_, rest),
        grid_spec=pltpu.PrefetchScalarGridSpec(
            num_scalar_prefetch=1,
            grid=(locals_,),
            in_specs=[whole(x.shape) for x in xs]
            + [whole(gs.shape)]
            + [per(half, wide)] * 2 + [per(wide, half)] * 2 + [whole((width, experts))],
            out_specs=[whole(x.shape) for x in xs]
            + [per(rows, width), per(rows, width), per(rows, wide), per(rows, wide), per(rows, experts)],
            scratch_shapes=[
                pltpu.VMEM((width, wide), BF16),
                pltpu.VMEM((wide, width), BF16),
                pltpu.VMEM((rows, width), BF16),
                pltpu.VMEM((rows, wide), F32),
                pltpu.VMEM((rows, wide), F32),
                pltpu.VMEM((rows, TILE), F32),
                pltpu.VMEM((rows, TILE), F32),
                pltpu.VMEM((rows, width), BF16),
            ],
        ),
        out_shape=[jax.ShapeDtypeStruct(x.shape, BF16) for x in xs]
        + [saved, saved, saved_wide, saved_wide, jax.ShapeDtypeStruct((locals_, rows, experts), BF16)],
        compiler_params=params(),
        cost_estimate=cost(6 * locals_ * rows * width * wide, locals_ * rows * width * 14, locals_ * rows * wide),
        name="experts",
    )(places, *xs, gs, own_in, peer_in, own_out, peer_out, router)
    return result[: len(xs)], result[len(xs) :]


def expert_rows_kernel(chunks, main, locals_, rest, place_ref, hid_ref, own_out, peer_out, forward_ref, wout, value):
    expert = pl.program_id(0)
    tensors = forward_ref.shape[0]
    blocks = tensors * forward_ref.shape[1]
    choice = rest_choice(blocks, locals_, rest, expert)
    join_halves(place_ref, own_out, peer_out, own_out, peer_out, None, wout)
    value[...] = dot(hid_ref[0], wout[...]).astype(BF16)
    views = group_views(place_ref, forward_ref, tensors, chunks)
    put_rows(views, value, choice, blocks * main, main, locals_, rest, expert)


def expert_rows(places, hidden, own_out, peer_out, shape, main, rest, chunks):
    locals_, rows, wide = hidden.shape
    half = own_out.shape[2]
    width = shape[-1]
    per = lambda *shape: pl.BlockSpec((1,) + shape, lambda e, *_: (e, 0, 0))
    return pl.pallas_call(
        functools.partial(expert_rows_kernel, chunks, main, locals_, rest),
        grid_spec=pltpu.PrefetchScalarGridSpec(
            num_scalar_prefetch=1,
            grid=(locals_,),
            in_specs=[per(rows, wide)] + [per(wide, half)] * 2,
            out_specs=whole(shape),
            scratch_shapes=[pltpu.VMEM((wide, width), BF16), pltpu.VMEM((rows, width), BF16)],
        ),
        out_shape=jax.ShapeDtypeStruct(shape, BF16),
        compiler_params=params(),
        cost_estimate=cost(2 * locals_ * rows * width * wide, locals_ * rows * width * 6),
        name="expert_rows",
    )(places, hidden, own_out, peer_out)


def expert_weights_kernel(place_ref, x_ref, ge_ref, hid_ref, gi_ref, gl_ref, *refs):
    in_own, in_send, out_own, out_send, router_ref = refs
    half = in_own.shape[1]
    mine = pl.ds(pl.multiple_of(place_ref[0] * half, half), half)
    other = pl.ds(pl.multiple_of((1 - place_ref[0]) * half, half), half)
    in_own[0] = dot(x_ref[0, :, mine], gi_ref[0], ROWS_TN)
    in_send[0] = dot(x_ref[0, :, other], gi_ref[0], ROWS_TN).astype(BF16)
    out_own[0] = dot(hid_ref[0], ge_ref[0, :, mine], ROWS_TN)
    out_send[0] = dot(hid_ref[0], ge_ref[0, :, other], ROWS_TN).astype(BF16)

    @pl.when(pl.program_id(0) == 0)
    def _():
        router_ref[...] = jnp.zeros_like(router_ref)

    router_ref[...] += dot(x_ref[0], gl_ref[0], ROWS_TN)


def expert_weights(places, saved, half):
    x, ge, hidden, gi, gl = saved
    locals_, rows, width = x.shape
    wide = hidden.shape[2]
    experts = gl.shape[2]
    per = lambda *shape: pl.BlockSpec((1,) + shape, lambda e, *_: (e, 0, 0))
    return pl.pallas_call(
        expert_weights_kernel,
        grid_spec=pltpu.PrefetchScalarGridSpec(
            num_scalar_prefetch=1,
            grid=(locals_,),
            in_specs=[per(rows, width), per(rows, width), per(rows, wide), per(rows, wide), per(rows, experts)],
            out_specs=[per(half, wide), per(half, wide), per(wide, half), per(wide, half), whole((width, experts))],
        ),
        out_shape=[
            jax.ShapeDtypeStruct((locals_, half, wide), F32),
            jax.ShapeDtypeStruct((locals_, half, wide), BF16),
            jax.ShapeDtypeStruct((locals_, wide, half), F32),
            jax.ShapeDtypeStruct((locals_, wide, half), BF16),
            jax.ShapeDtypeStruct((width, experts), F32),
        ],
        compiler_params=params(),
        cost_estimate=cost(4 * locals_ * rows * width * wide, locals_ * rows * width * 14),
        name="expert_weights",
    )(places, x, ge, hidden, gi, gl)


def take_rows(target_ref, refs):
    total, at = None, 0
    for ref in refs:
        count = ref.shape[0]
        cols = lax.broadcasted_iota(jnp.int32, (target_ref.shape[0], count), 1) + at
        chosen = jnp.where(cols == target_ref[...], 1.0, 0.0).astype(BF16)
        part = dot(chosen, ref[...])
        total = part if total is None else total + part
        at += count
    return total


def hidden_back_kernel(target_ref, *refs):
    hidden_ref, cot_ref, gain_ref, grad_ref, attn_ref, gain_out = refs[-6:]
    grad_in = take_rows(target_ref, refs[:-6])
    unit, scale = unit_rows(hidden_ref[...])
    gain_out[...] = jnp.sum(grad_in * unit, axis=0, keepdims=True)
    scaled = grad_in * gain_ref[...]
    inside = jnp.mean(unit * scaled, axis=-1, keepdims=True)
    grad = cot_ref[...].astype(F32) + scale * (scaled - unit * inside)
    grad_ref[...] = grad
    attn_ref[...] = grad.astype(BF16)


def hidden_back(target_col, back, hidden, cotangent, gain):
    rows, width = hidden.shape
    return pl.pallas_call(
        hidden_back_kernel,
        out_shape=[
            jax.ShapeDtypeStruct((rows, width), F32),
            jax.ShapeDtypeStruct((rows, width), BF16),
            jax.ShapeDtypeStruct((1, width), F32),
        ],
        compiler_params=params(),
        cost_estimate=cost(3 * rows * rows * width, 16 * rows * width),
        name="hidden_back",
    )(target_col, *back, hidden, cotangent, gain)


def output_kernel(target_ref, *refs):
    hidden_ref, gate_ref, out_ref = refs[-3:]
    out_ref[...] = (hidden_ref[...] + gate_ref[...] * take_rows(target_ref, refs[:-3])).astype(BF16)


def output_rows(target_col, expert_rows, hidden, gate):
    return pl.pallas_call(
        output_kernel,
        out_shape=jax.ShapeDtypeStruct(hidden.shape, BF16),
        compiler_params=params(),
        cost_estimate=cost(3 * hidden.shape[0] * hidden.size, 10 * hidden.size),
        name="output_rows",
    )(target_col, *expert_rows, hidden, gate)


def tokens_back_kernel(tok_ref, *refs):
    gain_ref, hidden_ref, out_ref = refs[-3:]
    unit, scale = unit_rows(tok_ref[...].astype(F32))
    scaled = sum_pieces(refs[:-3]) * gain_ref[...]
    inside = jnp.mean(unit * scaled, axis=-1, keepdims=True)
    out_ref[...] = hidden_ref[...] + scale * (scaled - unit * inside)


def tokens_back(tokens, grad_normed, gain, grad_hidden):
    return pl.pallas_call(
        tokens_back_kernel,
        out_shape=jax.ShapeDtypeStruct(tokens.shape, F32),
        compiler_params=params(),
        cost_estimate=cost(10 * tokens.size, 12 * tokens.size),
        name="tokens_back",
    )(tokens, *grad_normed, gain, grad_hidden)


def shifted(value, axis, count, step):
    return lax.ppermute(value, axis, [(s, (s + step) % count) for s in range(count)])


def gather_ring(value, axis, count):
    me = lax.axis_index(axis)
    parts = [value] + [shifted(value, axis, count, -k) for k in range(1, count)]
    return jnp.roll(jnp.stack(parts), me, axis=0)


def swapped(value, axis, count, bits):
    return lax.ppermute(value, axis, [(s, s ^ bits) for s in range(count)])


def gather_pieces(value, axis, count):
    return [value] + [swapped(value, axis, count, k) for k in range(1, count)]


def swap_pieces(pieces, axis, count):
    return [pieces[0]] + [swapped(pieces[k], axis, count, k) for k in range(1, count)]


def on_device(
    sizes,
    tokens,
    cotangent,
    query_key_value_weight,
    attention_output_weight,
    rel_bias,
    gain_attn,
    gain_moe,
    w_router,
    w_in,
    w_out,
    expert_index,
    slot_index,
    kept_mask,
):
    dp_count, z_count, t_count = sizes
    tok_rows, width = tokens.shape
    experts_all = w_router.shape[1]
    capacity = max(2, 3 * tok_rows // (2 * experts_all))
    locals_ = w_in.shape[0]
    main = capacity // 16 * 16
    rest = capacity - main
    block = locals_ * capacity
    heads = rel_bias.shape[0]
    inner = heads * HEAD_DIM
    part = query_key_value_weight.shape[1]
    fine = w_router.shape[0]
    my_dp = lax.axis_index("dp")
    my_z = lax.axis_index("expert")
    bias = rel_bias.astype(F32)

    my_t = lax.axis_index("tensor")
    owners = dp_count * z_count
    my_owner = my_dp * z_count + my_z
    places = jnp.stack([my_dp, my_z, my_t, my_owner]).astype(jnp.int32)
    token_pieces = gather_pieces(tokens, "tensor", t_count)

    small = jnp.concatenate([gain_attn[:, None], gain_moe[:, None], w_router], axis=1).reshape(-1)
    extra = -(-small.shape[0] // (16 * width)) * 16
    packed = jnp.concatenate(
        [
            query_key_value_weight.transpose(1, 0, 2).reshape(part, 3 * inner),
            attention_output_weight.T,
        ],
        axis=1,
    )
    packed = jnp.concatenate(
        [packed, jnp.pad(small, (0, extra * width - small.shape[0])).reshape(extra, width)], axis=0
    )
    owned = gather_pieces(packed, "expert", z_count)
    ring_done = owned
    owned = owned + [swapped(piece, "dp", dp_count, 1) for piece in owned]
    smalls = jnp.stack([piece[part:].reshape(-1)[: small.shape[0]] for piece in owned])
    smalls = jnp.stack(gather_pieces(smalls, "tensor", t_count)).reshape(t_count * owners, -1)
    owner_ids = jnp.arange(owners, dtype=jnp.int32)[:, None] ^ my_owner
    t_ids = jnp.arange(t_count, dtype=jnp.int32)[None, :] ^ my_t
    smalls = smalls[(t_ids * owners + owner_ids).reshape(-1)].reshape(width, 2 + experts_all)
    if part % 16:
        order = jnp.arange(owners, dtype=jnp.int32) ^ my_owner
        owned = [jnp.stack([piece[:part] for piece in owned])[order].reshape(width, 4 * inner)]
    rows_owned = part if len(owned) > 1 else width
    gain_one = smalls[:, 0].astype(F32)[None]
    gain_two = smalls[:, 1].astype(F32)[None]
    router = smalls[:, 2:]

    z_of = expert_index // locals_
    local = expert_index - z_of * locals_
    inside = jnp.where(
        slot_index < main, local * main + slot_index, locals_ * main + local * rest + slot_index - main
    )
    target = (z_of ^ my_z) * block + inside
    target = jnp.where(kept_mask > 0, target, -1)
    target_row, target_col = target[None, :], target[:, None]
    count = z_count * block
    chunks = min(z_count, 4)
    many = z_count // chunks

    def over_expert(rows):
        pieces = swap_pieces(list(rows.reshape(z_count, block, width)), "expert", z_count)
        if many == 1:
            return pieces
        return [jnp.concatenate(pieces[k * many : (k + 1) * many], axis=0) for k in range(chunks)]

    def back_over_expert(groups):
        if many > 1:
            groups = [g[i * block : (i + 1) * block] for g in groups for i in range(many)]
        pieces = swap_pieces(groups, "expert", z_count)
        if many == 1:
            return pieces
        return [jnp.concatenate(pieces[k * many : (k + 1) * many], axis=0) for k in range(chunks)]

    late_cotangent, _ = lax.optimization_barrier((cotangent, ring_done))
    grad_rows = jnp.concatenate(over_expert(place(target_row, late_cotangent, count)), axis=0)
    late_in, late_out, token_pieces = lax.optimization_barrier((w_in, w_out, token_pieces))
    peer_in = shifted(late_in, "dp", dp_count, 1)
    peer_out = shifted(late_out, "dp", dp_count, 1)

    parts, (group_tokens, projected, mixed, logs, weights) = attend(
        places, bias, token_pieces, owned, rows_owned, gain_one
    )
    parts, peer_in, peer_out, grad_rows = lax.optimization_barrier((parts, peer_in, peer_out, grad_rows))
    grad_arrived = lax.all_gather(grad_rows, "tensor", axis=0).reshape(t_count, z_count, block, width)
    attn = swap_pieces(parts, "tensor", t_count)
    hidden_one, sent, gate = route(
        tokens, attn, gain_two, router, target_row, expert_index[:, None], kept_mask[:, None], count
    )
    arrived = [
        piece.reshape(many, block, width)
        for group in over_expert(sent)
        for piece in gather_pieces(group, "tensor", t_count)
    ]
    back_parts, saved = expert_forward_back(
        places, arrived, grad_arrived, w_in, peer_in, w_out, peer_out, router, main, rest, chunks
    )

    def summed(pieces):
        total = pieces[0].astype(F32)
        for piece in pieces[1:]:
            total = total + piece.astype(F32)
        return total.astype(BF16)

    size = many * block

    def swap_group(group):
        joined = [
            jnp.concatenate([back_parts[k * t_count + j].reshape(size, width) for k in group], axis=0)
            for j in range(t_count)
        ]
        return swap_pieces(joined, "tensor", t_count)

    half = chunks // 2
    far = swap_group(range(half, chunks))
    forward_part = expert_rows(places, saved[2], w_out, peer_out, grad_arrived.shape, main, rest, chunks)
    far, forward_part, saved = lax.optimization_barrier((far, forward_part, saved))
    near = swap_group(range(half))
    in_own, in_send, out_own, out_send, router_part = expert_weights(places, saved, w_in.shape[1])
    near, forward_part, in_send, out_send = lax.optimization_barrier((near, forward_part, in_send, out_send))
    groups = [value[k * size : (k + 1) * size] for value in (summed(near), summed(far)) for k in range(half)]
    grad_back = back_over_expert(groups)
    forward_sum = lax.psum_scatter(
        forward_part.reshape(t_count * z_count * block, width), "tensor", scatter_dimension=0, tiled=True
    )
    grad_hidden, grad_attn, gain_two_part = hidden_back(target_col, grad_back, hidden_one, cotangent, gain_two)
    grad_w_in = in_own + shifted(in_send, "dp", dp_count, 1).astype(F32)
    grad_w_out = out_own + shifted(out_send, "dp", dp_count, 1).astype(F32)
    grad_pieces, grad_w_in, grad_w_out, forward_sum = lax.optimization_barrier(
        (gather_pieces(grad_attn, "tensor", t_count), grad_w_in, grad_w_out, forward_sum)
    )
    normed_parts, (weight_part, bucket_part, gain_one_part) = attend_back(
        places, bias, group_tokens, gain_one, weights, projected, mixed, logs, grad_pieces
    )
    grad_normed = swap_pieces(normed_parts, "tensor", t_count)
    forward_rows = back_over_expert(list(forward_sum.reshape(chunks, many * block, width)))
    output = output_rows(target_col, forward_rows, hidden_one, gate)
    grad_tokens = tokens_back(tokens, grad_normed, gain_one, grad_hidden)

    smalls = jnp.concatenate(
        [
            gain_one_part.reshape(owners, part),
            gain_two_part.reshape(owners, part),
            router_part.reshape(owners, part * experts_all),
            jnp.broadcast_to(bucket_part.reshape(1, heads * BUCKETS), (owners, heads * BUCKETS)),
        ],
        axis=1,
    )
    extra = -(-smalls.shape[1] // (16 * width)) * 16
    smalls = jnp.pad(smalls, ((0, 0), (0, extra * width - smalls.shape[1]))).reshape(owners, extra, width)
    payload = jnp.concatenate([weight_part.reshape(owners, part, width), smalls], axis=1)
    payload = payload.reshape(dp_count, z_count, part + extra, width)
    own = lax.dynamic_index_in_dim(payload, my_dp, 0, keepdims=False)
    other = lax.dynamic_index_in_dim(payload, 1 - my_dp, 0, keepdims=False)
    summed_half = own + shifted(other.astype(BF16), "dp", dp_count, 1).astype(F32)
    turned = [lax.dynamic_index_in_dim(summed_half, my_z ^ k, 0, keepdims=False) for k in range(z_count)]
    pieces = swap_pieces([turned[0]] + [t.astype(BF16) for t in turned[1:]], "expert", z_count)
    total = pieces[0]
    for piece in pieces[1:]:
        total = total + piece.astype(F32)
    weight_total = total[:part].reshape(part, 4, inner)
    grad_w_qkv = weight_total[:, :3].transpose(1, 0, 2)
    grad_w_attn_out = weight_total[:, 3].T
    flat = total[part:].reshape(-1)
    ends = [part, 2 * part, 2 * part + part * experts_all]
    grad_rel_bias = flat[ends[2] : ends[2] + heads * BUCKETS].reshape(heads, BUCKETS)
    rows_left = jnp.concatenate(
        [
            flat[: ends[0]].reshape(t_count, fine),
            flat[ends[0] : ends[1]].reshape(t_count, fine),
            flat[ends[1] : ends[2]].reshape(t_count, fine * experts_all),
        ],
        axis=1,
    )
    turned = [lax.dynamic_index_in_dim(rows_left, my_t ^ k, 0, keepdims=False) for k in range(t_count)]
    left = turned[0]
    for piece in swap_pieces(turned, "tensor", t_count)[1:]:
        left = left + piece
    grad_gain_attn = left[:fine]
    grad_gain_moe = left[fine : 2 * fine]
    grad_w_router = left[2 * fine :].reshape(fine, experts_all)
    return (
        output,
        grad_tokens,
        grad_w_qkv,
        grad_w_attn_out,
        grad_rel_bias,
        grad_gain_attn,
        grad_gain_moe,
        grad_w_router,
        grad_w_in,
        grad_w_out,
    )


def solution(mesh):
    placed = (
        P(("dp", "expert", "tensor"), None),
        P(("dp", "expert", "tensor"), None),
        P(None, ("dp", "expert"), "tensor"),
        P("tensor", ("dp", "expert")),
        P("tensor", None),
        P(("dp", "expert", "tensor")),
        P(("dp", "expert", "tensor")),
        P(("dp", "expert", "tensor"), None),
        P("expert", "dp", "tensor"),
        P("expert", "tensor", "dp"),
        P(("dp", "expert", "tensor")),
        P(("dp", "expert", "tensor")),
        P(("dp", "expert", "tensor")),
    )
    sizes = tuple(mesh.shape[name] for name in ("dp", "expert", "tensor"))
    return jax.shard_map(
        functools.partial(on_device, sizes),
        mesh=mesh,
        in_specs=placed,
        out_specs=(
            P(("dp", "expert", "tensor"), None),
            P(("dp", "expert", "tensor"), None),
            P(None, ("dp", "expert"), "tensor"),
            P("tensor", ("dp", "expert")),
            P("tensor", None),
            P(("dp", "expert", "tensor")),
            P(("dp", "expert", "tensor")),
            P(("dp", "expert", "tensor"), None),
            P("expert", "dp", "tensor"),
            P("expert", "tensor", "dp"),
        ),
        check_vma=False,
    )
```

```python
import functools

import jax
import jax.numpy as jnp
from jax import lax
from jax.experimental import pallas as pl
from jax.experimental.pallas import tpu as pltpu
from jax.sharding import PartitionSpec as P

HEAD_DIM = 64
BUCKETS = 32
LENGTH = 512
TILE = 128
EPSILON = 1e-06
BORDERS = (12, 16, 23, 32, 46, 64, 91)
F32 = jnp.float32
BF16 = jnp.bfloat16
GELU_A = 0.7978845608028654
GELU_B = 0.044715
ROWS_NN = (((1,), (0,)), ((), ()))
ROWS_NT = (((1,), (1,)), ((), ()))
ROWS_TN = (((0,), (0,)), ((), ()))
VMEM_BYTES = 56 * 1024 * 1024


def dot(a, b, dims=ROWS_NN):
    return lax.dot_general(a, b, dims, preferred_element_type=F32)


def params(**more):
    return pltpu.CompilerParams(vmem_limit_bytes=VMEM_BYTES, **more)


def cost(flops, moved, special=0):
    return pl.CostEstimate(flops=int(flops), bytes_accessed=int(moved), transcendentals=int(special))


def whole(shape):
    return pl.BlockSpec(shape, lambda *_: (0,) * len(shape))


def tile_bucket(step):
    rows = lax.broadcasted_iota(jnp.int32, (TILE, TILE), 0)
    cols = lax.broadcasted_iota(jnp.int32, (TILE, TILE), 1)
    offset = cols - rows + step * TILE
    distance = jnp.abs(offset)
    bucket = jnp.minimum(distance, 8)
    for border in BORDERS:
        bucket = bucket + jnp.where(distance >= border, 1, 0)
    return bucket + jnp.where(offset > 0, 16, 0)


def tile_range(step):
    return {-1: range(1, 16), 0: range(0, 32), 1: range(17, 32)}[step]


def fill_bias(bias_ref, table, heads):
    blocks = LENGTH // TILE
    buckets = {step: tile_bucket(step) for step in (-1, 0, 1)}
    for head in range(heads):
        near = {}
        for step in (-1, 0, 1):
            value = jnp.zeros((TILE, TILE), F32)
            for k in tile_range(step):
                value = jnp.where(buckets[step] == k, bias_ref[head, k], value)
            near[step] = value
        low = jnp.full((TILE, TILE), bias_ref[head, 15], F32)
        high = jnp.full((TILE, TILE), bias_ref[head, 31], F32)
        for i in range(blocks):
            for j in range(blocks):
                step = j - i
                value = near[step] if abs(step) <= 1 else (low if step < 0 else high)
                table[head, i * TILE : (i + 1) * TILE, j * TILE : (j + 1) * TILE] = value


def unit_rows(values):
    scale = lax.rsqrt(jnp.mean(values * values, axis=-1, keepdims=True) + EPSILON)
    return values * scale, scale


HOPS = ((1, 2), (2, 1))


def group_rows(place_ref, out, pieces):
    rows = pieces[0].shape[0]
    for j, piece in enumerate(pieces):
        at = pl.multiple_of((place_ref[2] ^ j) * rows, rows)
        out[pl.ds(at, rows), :] = piece[...]


def group_halves(place_ref, out, pieces):
    rows = pieces[0].shape[0]
    half = rows // 2
    at = pl.multiple_of(place_ref[2] * rows, rows)
    out[pl.ds(at, rows), :] = pieces[0][...]
    for h, (a, b) in enumerate(HOPS):
        first, second = pieces[1 + 2 * h : 3 + 2 * h]
        for j, value in ((a, first[...]), (b, second[:half, :]), (a | b, second[half:, :])):
            at = pl.multiple_of((place_ref[2] ^ j) * rows + h * half, half)
            out[pl.ds(at, half), :] = value


def part_halves(place_ref, pieces, source):
    half = pieces[0].shape[0] // 2
    for h, (a, b) in enumerate(HOPS):
        for piece, order in zip(pieces[2 * h : 2 * h + 2], ((0, b), (a, a | b))):
            for n, j in enumerate(order):
                at = pl.multiple_of((place_ref[2] ^ j) * 2 * half + h * half, half)
                piece[n * half : (n + 1) * half, :] = source[pl.ds(at, half), :]


def part_rows(place_ref, pieces, source):
    rows = pieces[0].shape[0]
    for j, piece in enumerate(pieces):
        at = pl.multiple_of((place_ref[2] ^ j) * rows, rows)
        piece[...] = source[pl.ds(at, rows), :]


def attend_kernel(heads, tensors, owners, part, place_ref, bias_ref, *refs):
    refs = list(refs)
    take = lambda n: [refs.pop(0) for _ in range(n)]
    pieces, owned, (gain_ref,), parts = take(tensors), take(owners), take(1), take(tensors)
    tok_ref, qkv_ref, mixed_ref, log_ref, w_ref, table, wo, group, result = refs
    inner = heads * HEAD_DIM
    step_id = pl.program_id(0)

    @pl.when(step_id == 0)
    def _():
        fill_bias(bias_ref, table, heads)
        group_rows(place_ref, group, pieces)
        for k, piece in enumerate(owned):
            at = pl.multiple_of((place_ref[3] ^ k) * part, part) if owners > 1 else 0
            w_ref[pl.ds(at, part), :] = piece[:part, :]
        wo[...] = w_ref[:, 3 * inner :]

    here = pl.ds(pl.multiple_of(step_id * LENGTH, LENGTH), LENGTH)
    tok_ref[...] = group[here, :]
    unit, _ = unit_rows(tok_ref[...].astype(F32))
    normed = (unit * gain_ref[...]).astype(BF16)
    qkv_ref[...] = dot(normed, w_ref[:, : 3 * inner]).astype(BF16)
    lanes = lax.broadcasted_iota(jnp.int32, (LENGTH, TILE), 1)
    logs = jnp.zeros((LENGTH, TILE), F32)
    for head in range(heads):
        at = head * HEAD_DIM
        query = qkv_ref[:, at : at + HEAD_DIM] * HEAD_DIM ** (-0.5)
        key = qkv_ref[:, inner + at : inner + at + HEAD_DIM]
        value = qkv_ref[:, 2 * inner + at : 2 * inner + at + HEAD_DIM]
        scores = dot(query.astype(BF16), key, ROWS_NT) + table[head]
        top = jnp.max(scores, axis=-1, keepdims=True)
        exponent = jnp.exp(scores - top)
        total = jnp.sum(exponent, axis=-1, keepdims=True)
        attention = (exponent * (1.0 / total)).astype(BF16)
        mixed_ref[:, at : at + HEAD_DIM] = dot(attention, value).astype(BF16)
        logs = jnp.where(lanes == head, top + jnp.log(total), logs)
    log_ref[...] = logs
    result[here, :] = dot(mixed_ref[...], wo[...], ROWS_NT).astype(BF16)

    @pl.when(step_id == pl.num_programs(0) - 1)
    def _():
        part_halves(place_ref, parts, result)


def attend(places, bias, pieces, owned, part, gain):
    tensors = len(pieces)
    piece_rows, width = pieces[0].shape
    rows = tensors * piece_rows
    heads = bias.shape[0]
    inner = heads * HEAD_DIM
    seqs = rows // LENGTH
    by_seq = lambda cols: pl.BlockSpec((LENGTH, cols), lambda s, *_: (s, 0))
    result = pl.pallas_call(
        functools.partial(attend_kernel, heads, tensors, len(owned), part),
        grid_spec=pltpu.PrefetchScalarGridSpec(
            num_scalar_prefetch=1,
            grid=(seqs,),
            in_specs=[pl.BlockSpec(memory_space=pltpu.SMEM)]
            + [whole((piece_rows, width))] * tensors
            + [whole(o.shape) for o in owned]
            + [whole((1, width))],
            out_specs=[whole((piece_rows, width))] * tensors
            + [by_seq(width), by_seq(3 * inner), by_seq(inner), by_seq(TILE), whole((width, 4 * inner))],
            scratch_shapes=[
                pltpu.VMEM((heads, LENGTH, LENGTH), F32),
                pltpu.VMEM((width, inner), BF16),
                pltpu.VMEM((rows, width), BF16),
                pltpu.VMEM((rows, width), BF16),
            ],
        ),
        out_shape=[jax.ShapeDtypeStruct((piece_rows, width), BF16)] * tensors
        + [
            jax.ShapeDtypeStruct((rows, width), BF16),
            jax.ShapeDtypeStruct((rows, 3 * inner), BF16),
            jax.ShapeDtypeStruct((rows, inner), BF16),
            jax.ShapeDtypeStruct((rows, TILE), F32),
            jax.ShapeDtypeStruct((width, 4 * inner), BF16),
        ],
        compiler_params=params(),
        cost_estimate=cost(8 * rows * width * inner + 4 * rows * LENGTH * inner, rows * width * 8, rows * LENGTH * heads),
        name="attend",
    )(places, bias, *pieces, *owned, gain)
    return result[:tensors], result[tensors:]


def attend_back_kernel(
    heads, tensors, place_ref, bias_ref, tok_ref, gain_ref, w_ref, qkv_ref, mixed_ref, log_ref, *refs
):
    refs = list(refs)
    pieces = [refs.pop(0) for _ in range(5)]
    parts = [refs.pop(0) for _ in range(tensors)]
    weight_ref, buckets_ref, gain_out, table, wo, gmix, gproj, near, far, rows_s, group, result = refs
    inner = heads * HEAD_DIM
    blocks = LENGTH // TILE
    step_id = pl.program_id(0)

    @pl.when(step_id == 0)
    def _():
        fill_bias(bias_ref, table, heads)
        wo[...] = w_ref[:, 3 * inner :]
        near[...] = jnp.zeros_like(near)
        far[...] = jnp.zeros_like(far)
        weight_ref[...] = jnp.zeros_like(weight_ref)
        gain_out[...] = jnp.zeros_like(gain_out)
        group_halves(place_ref, group, pieces)

    here = pl.ds(pl.multiple_of(step_id * LENGTH, LENGTH), LENGTH)
    gmix[...] = dot(group[here, :], wo[...]).astype(BF16)
    for head in range(heads):
        at = head * HEAD_DIM
        query = (qkv_ref[:, at : at + HEAD_DIM] * HEAD_DIM ** (-0.5)).astype(BF16)
        key = qkv_ref[:, inner + at : inner + at + HEAD_DIM]
        value = qkv_ref[:, 2 * inner + at : 2 * inner + at + HEAD_DIM]
        grad_rows = gmix[:, at : at + HEAD_DIM]
        scores = dot(query, key, ROWS_NT) + table[head]
        attention = jnp.exp(scores - log_ref[:, head : head + 1])
        grad_weights = dot(grad_rows, value, ROWS_NT)
        inner_sum = jnp.sum(attention * grad_weights, axis=-1, keepdims=True)
        grad_scores = attention * (grad_weights - inner_sum)
        low = jnp.zeros((TILE, TILE), F32)
        high = jnp.zeros((TILE, TILE), F32)
        mid = [jnp.zeros((TILE, TILE), F32) for _ in range(3)]
        for i in range(blocks):
            for j in range(blocks):
                piece = grad_scores[i * TILE : (i + 1) * TILE, j * TILE : (j + 1) * TILE]
                if abs(j - i) <= 1:
                    mid[j - i + 1] = mid[j - i + 1] + piece
                elif j < i:
                    low = low + piece
                else:
                    high = high + piece
        for k in range(3):
            near[head * 3 + k] += mid[k]
        far[head * 2] += low
        far[head * 2 + 1] += high
        rounded = grad_scores.astype(BF16)
        gproj[:, at : at + HEAD_DIM] = (dot(rounded, key) * HEAD_DIM ** (-0.5)).astype(BF16)
        gproj[:, inner + at : inner + at + HEAD_DIM] = dot(rounded, query, ROWS_TN).astype(BF16)
        gproj[:, 2 * inner + at : 2 * inner + at + HEAD_DIM] = dot(
            attention.astype(BF16), grad_rows, ROWS_TN
        ).astype(BF16)
    unit, _ = unit_rows(tok_ref[...].astype(F32))
    normed = (unit * gain_ref[...]).astype(BF16)
    grad_normed = dot(gproj[...], w_ref[:, : 3 * inner], ROWS_NT)
    result[here, :] = grad_normed.astype(BF16)
    gain_out[...] += jnp.sum(grad_normed * unit, axis=0, keepdims=True)
    weight_ref[:, : 3 * inner] += dot(normed, gproj[...], ROWS_TN)
    weight_ref[:, 3 * inner :] += dot(group[here, :], mixed_ref[...], ROWS_TN)

    @pl.when(step_id == pl.num_programs(0) - 1)
    def _():
        part_rows(place_ref, parts, result)
        ids = [tile_bucket(step) for step in (-1, 0, 1)]
        for head in range(heads):
            for k in range(BUCKETS):
                total = jnp.zeros((TILE, TILE), F32)
                for step in (-1, 0, 1):
                    if k in tile_range(step):
                        total = total + jnp.where(ids[step + 1] == k, near[head * 3 + step + 1], 0.0)
                if k == 15:
                    total = total + far[head * 2]
                if k == 31:
                    total = total + far[head * 2 + 1]
                at = head * BUCKETS + k
                rows_s[at : at + 1, :] = jnp.sum(total, axis=0, keepdims=True)
        buckets_ref[...] = jnp.sum(rows_s[...], axis=1, keepdims=True)


def attend_back(places, bias, tokens, gain, weights, projected, mixed, logs, pieces):
    rows, width = tokens.shape
    tensors = rows // pieces[0].shape[0]
    piece = whole(pieces[0].shape)
    heads = bias.shape[0]
    inner = heads * HEAD_DIM
    seqs = rows // LENGTH
    by_seq = lambda cols: pl.BlockSpec((LENGTH, cols), lambda s, *_: (s, 0))
    result = pl.pallas_call(
        functools.partial(attend_back_kernel, heads, tensors),
        grid_spec=pltpu.PrefetchScalarGridSpec(
            num_scalar_prefetch=1,
            grid=(seqs,),
            in_specs=[
                pl.BlockSpec(memory_space=pltpu.SMEM),
                by_seq(width),
                whole((1, width)),
                whole((width, 4 * inner)),
                by_seq(3 * inner),
                by_seq(inner),
                by_seq(TILE),
            ]
            + [whole(p.shape) for p in pieces],
            out_specs=[piece] * tensors
            + [whole((width, 4 * inner)), whole((heads * BUCKETS, 1)), whole((1, width))],
            scratch_shapes=[
                pltpu.VMEM((heads, LENGTH, LENGTH), F32),
                pltpu.VMEM((width, inner), BF16),
                pltpu.VMEM((LENGTH, inner), BF16),
                pltpu.VMEM((LENGTH, 3 * inner), BF16),
                pltpu.VMEM((heads * 3, TILE, TILE), F32),
                pltpu.VMEM((heads * 2, TILE, TILE), F32),
                pltpu.VMEM((heads * BUCKETS, TILE), F32),
                pltpu.VMEM((rows, width), BF16),
                pltpu.VMEM((rows, width), BF16),
            ],
        ),
        out_shape=[jax.ShapeDtypeStruct(pieces[0].shape, BF16)] * tensors
        + [
            jax.ShapeDtypeStruct((width, 4 * inner), F32),
            jax.ShapeDtypeStruct((heads * BUCKETS, 1), F32),
            jax.ShapeDtypeStruct((1, width), F32),
        ],
        compiler_params=params(),
        cost_estimate=cost(18 * rows * width * inner + 10 * rows * LENGTH * inner, rows * width * 12, rows * LENGTH * heads),
        name="attend_back",
    )(places, bias, tokens, gain, weights, projected, mixed, logs, *pieces)
    return result[:tensors], result[tensors:]


def place_kernel(target_ref, rows_ref, out_ref):
    count = out_ref.shape[0]
    rows = lax.broadcasted_iota(jnp.int32, (count, rows_ref.shape[0]), 0)
    chosen = jnp.where(rows == target_ref[...], 1.0, 0.0).astype(BF16)
    out_ref[...] = dot(chosen, rows_ref[...]).astype(BF16)


def place(target_row, rows, count):
    return pl.pallas_call(
        place_kernel,
        out_shape=jax.ShapeDtypeStruct((count, rows.shape[1]), BF16),
        compiler_params=params(),
        cost_estimate=cost(2 * count * rows.size, 4 * rows.size),
        name="place",
    )(target_row, rows)


def softmax_rows(logits):
    exponent = jnp.exp(logits - jnp.max(logits, axis=-1, keepdims=True))
    return exponent * (1.0 / jnp.sum(exponent, axis=-1, keepdims=True))


def sum_pieces(refs):
    total = refs[0][...].astype(F32)
    for ref in refs[1:]:
        total = total + ref[...].astype(F32)
    return total


def route_kernel(tok_ref, *refs):
    gain_ref, router_ref, target_ref, index_ref, kept_ref, hidden_ref, sent_ref, gate_ref = refs[6:]
    half = tok_ref.shape[0] // 2
    for h in range(2):
        keep, got, last = refs[3 * h : 3 * h + 3]
        here = slice(h * half, (h + 1) * half)
        added = keep[:half, :].astype(F32) + got[:half, :].astype(F32) + last[...].astype(F32)
        hidden_ref[here, :] = tok_ref[here, :].astype(F32) + added
    hidden = hidden_ref[...]
    unit, _ = unit_rows(hidden)
    moe_in = (unit * gain_ref[...]).astype(BF16)
    count = sent_ref.shape[0]
    rows = lax.broadcasted_iota(jnp.int32, (count, hidden.shape[0]), 0)
    chosen = jnp.where(rows == target_ref[...], 1.0, 0.0).astype(BF16)
    sent_ref[...] = dot(chosen, moe_in).astype(BF16)
    probs = softmax_rows(dot(moe_in, router_ref[...]))
    lanes = lax.broadcasted_iota(jnp.int32, probs.shape, 1)
    picked = jnp.sum(jnp.where(lanes == index_ref[...], probs, 0.0), axis=-1, keepdims=True)
    gate_ref[...] = picked * kept_ref[...].astype(F32)


def route(tokens, attn, gain, router, target_row, index_col, kept_col, count):
    rows, width = tokens.shape
    return pl.pallas_call(
        route_kernel,
        out_shape=[
            jax.ShapeDtypeStruct((rows, width), F32),
            jax.ShapeDtypeStruct((count, width), BF16),
            jax.ShapeDtypeStruct((rows, 1), F32),
        ],
        compiler_params=params(),
        cost_estimate=cost(2 * count * rows * width, 12 * rows * width),
        name="route",
    )(tokens, *attn, gain, router, target_row, index_col, kept_col)


def rest_choice(blocks, locals_, rest, expert):
    rows = lax.broadcasted_iota(jnp.int32, (blocks * rest, blocks * locals_ * rest), 0)
    cols = lax.broadcasted_iota(jnp.int32, (blocks * rest, blocks * locals_ * rest), 1)
    block = lax.div(rows, rest)
    wanted = block * (locals_ * rest) + expert * rest + (rows - block * rest)
    return jnp.where(cols == wanted, 1.0, 0.0).astype(BF16)


def pick_rows(out_ref, views, choice, main_rows, main, expert):
    at = 0
    pieces = []
    for view in views:
        blocks, size, width = view.shape
        if main:
            start = pl.multiple_of(expert * main, main)
            out_ref[at : at + blocks * main, :] = view[:, pl.ds(start, main), :].reshape(blocks * main, width)
            at += blocks * main
        rest = size - size * main_rows // out_ref.shape[0]
        pieces.append(view[:, size - rest :, :].reshape(blocks * rest, width))
    out_ref[main_rows:, :] = dot(choice, jnp.concatenate(pieces, axis=0)).astype(BF16)


def put_rows(views, value_ref, choice, main_rows, main, locals_, rest, expert):
    at = 0
    spread = dot(choice, value_ref[main_rows:, :], ROWS_TN).astype(BF16)
    rest_at = 0
    for view in views:
        blocks, _, width = view.shape
        if main:
            count = blocks * main
            start = pl.multiple_of(expert * main, main)
            view[:, pl.ds(start, main), :] = value_ref[at : at + count, :].reshape(blocks, main, width)
            at += count
        part = spread[rest_at : rest_at + blocks * locals_ * rest].reshape(blocks, locals_ * rest, width)
        rest_at += blocks * locals_ * rest

        @pl.when(expert == 0)
        def _():
            view[:, locals_ * main :, :] = part

        @pl.when(expert > 0)
        def _():
            view[:, locals_ * main :, :] = view[:, locals_ * main :, :] + part


def group_views(place_ref, ref, tensors, chunks):
    size = ref.shape[1] // chunks
    views = []
    for k in range(chunks):
        a, b = HOPS[k % 2]
        views += [ref.at[place_ref[2] ^ j, k * size : (k + 1) * size] for j in (0, a, b, a | b)]
    return views


def join_halves(place_ref, own_in, peer_in, own_out, peer_out, win, wout):
    half = own_in.shape[1]
    mine = pl.multiple_of(place_ref[0] * half, half)
    other = pl.multiple_of((1 - place_ref[0]) * half, half)
    if win is not None:
        win[pl.ds(mine, half), :] = own_in[0]
        win[pl.ds(other, half), :] = peer_in[0]
    half_out = own_out.shape[2]
    mine = pl.multiple_of(place_ref[0] * half_out, half_out)
    other = pl.multiple_of((1 - place_ref[0]) * half_out, half_out)
    wout[:, pl.ds(mine, half_out)] = own_out[0]
    wout[:, pl.ds(other, half_out)] = peer_out[0]


def expert_kernel(chunks, tensors, main, locals_, rest, place_ref, *refs):
    refs = list(refs)
    take = lambda n: [refs.pop(0) for _ in range(n)]
    xs = take(3 * chunks)
    (g_ref,) = take(1)
    own_in, peer_in, own_out, peer_out, router = take(5)
    backs = take(2 * chunks)
    x_ref, ge_ref, hid_ref, gi_ref, gl_ref = take(5)
    win, wout, grows, inner, gunits, gate_s, dots, back = take(8)
    expert = pl.program_id(0)
    blocks = sum(ref.shape[0] for ref in xs)
    main_rows = blocks * main
    rows, width = x_ref.shape[1:]
    wide = win.shape[1]
    choice = rest_choice(blocks, locals_, rest, expert)
    many = xs[0].shape[0]
    back_refs = []
    for k in range(chunks):
        keep, send = backs[2 * k : 2 * k + 2]
        back_refs += [ref.at[n * many : (n + 1) * many] for n in range(2) for ref in (keep, send)]
    pick_rows(x_ref.at[0], xs, choice, main_rows, main, expert)
    pick_rows(grows, group_views(place_ref, g_ref, tensors, chunks), choice, main_rows, main, expert)
    join_halves(place_ref, own_in, peer_in, own_out, peer_out, win, wout)
    inner[...] = dot(x_ref[0], win[...])
    gunits[...] = dot(grows[...], wout[...], ROWS_NT)
    probs = softmax_rows(dot(x_ref[0], router[...]))
    lanes = lax.broadcasted_iota(jnp.int32, probs.shape, 1)
    mine = lanes == place_ref[1] * locals_ + expert
    picked = jnp.sum(jnp.where(mine, probs, 0.0), axis=-1, keepdims=True)
    gate_s[...] = jnp.broadcast_to(picked, gate_s.shape)
    chunk = 16
    half_wide = wide // 2 if wide % (2 * TILE) == 0 else wide

    def body(step, _):
        at = pl.ds(pl.multiple_of(step * chunk, chunk), chunk)
        gate_tile = gate_s[at, :]
        gate = jnp.concatenate([gate_tile] * (half_wide // TILE), axis=1)
        total = None
        for start in range(0, wide, half_wide):
            lanes_at = slice(start, start + half_wide)
            value = inner[at, lanes_at]
            square = value * value
            wave = jnp.tanh(value * (GELU_A + (GELU_A * GELU_B) * square))
            half = 0.5 + 0.5 * wave
            hidden = (value * half).astype(BF16)
            bend = value * (0.5 * GELU_A + (1.5 * GELU_A * GELU_B) * square)
            slope = half + bend * (1.0 - wave * wave)
            units = gunits[at, lanes_at]
            hid_ref[0, at, lanes_at] = hidden
            gi_ref[0, at, lanes_at] = (gate * (units * slope)).astype(BF16)
            product = hidden.astype(F32) * units
            for tile in range(0, half_wide, TILE):
                part = product[:, tile : tile + TILE]
                total = part if total is None else total + part
        dots[at, :] = total
        gate = jnp.concatenate([gate_tile] * (width // TILE), axis=1)
        ge_ref[0, at, :] = (gate * grows[at, :].astype(F32)).astype(BF16)
        return 0

    lax.fori_loop(0, rows // chunk, body, 0, unroll=4)
    grad_logits = (jnp.sum(dots[...], axis=-1, keepdims=True) * probs * (jnp.where(mine, 1.0, 0.0) - picked)).astype(BF16)
    gl_ref[0] = grad_logits
    back[...] = (dot(gi_ref[0], win[...], ROWS_NT) + dot(grad_logits, router[...], ROWS_NT)).astype(BF16)
    put_rows(back_refs, back, choice, main_rows, main, locals_, rest, expert)


def expert_forward_back(places, xs, gs, own_in, peer_in, own_out, peer_out, router, main, rest, chunks):
    locals_, half, wide = own_in.shape
    width, experts = router.shape
    many, block = xs[0].shape[:2]
    tensors = gs.shape[0]
    blocks = tensors * chunks * many
    back = (2 * many, block, width)
    rows = blocks * (main + rest)
    per = lambda *shape: pl.BlockSpec((1,) + shape, lambda e, *_: (e, 0, 0))
    saved = jax.ShapeDtypeStruct((locals_, rows, width), BF16)
    saved_wide = jax.ShapeDtypeStruct((locals_, rows, wide), BF16)
    result = pl.pallas_call(
        functools.partial(expert_kernel, chunks, tensors, main, locals_, rest),
        grid_spec=pltpu.PrefetchScalarGridSpec(
            num_scalar_prefetch=1,
            grid=(locals_,),
            in_specs=[whole(x.shape) for x in xs]
            + [whole(gs.shape)]
            + [per(half, wide)] * 2 + [per(wide, half)] * 2 + [whole((width, experts))],
            out_specs=[whole(back)] * (2 * chunks)
            + [per(rows, width), per(rows, width), per(rows, wide), per(rows, wide), per(rows, experts)],
            scratch_shapes=[
                pltpu.VMEM((width, wide), BF16),
                pltpu.VMEM((wide, width), BF16),
                pltpu.VMEM((rows, width), BF16),
                pltpu.VMEM((rows, wide), F32),
                pltpu.VMEM((rows, wide), F32),
                pltpu.VMEM((rows, TILE), F32),
                pltpu.VMEM((rows, TILE), F32),
                pltpu.VMEM((rows, width), BF16),
            ],
        ),
        out_shape=[jax.ShapeDtypeStruct(back, BF16)] * (2 * chunks)
        + [saved, saved, saved_wide, saved_wide, jax.ShapeDtypeStruct((locals_, rows, experts), BF16)],
        compiler_params=params(),
        cost_estimate=cost(6 * locals_ * rows * width * wide, locals_ * rows * width * 14, locals_ * rows * wide),
        name="experts",
    )(places, *xs, gs, own_in, peer_in, own_out, peer_out, router)
    return result[: 2 * chunks], result[2 * chunks :]


def expert_rows_kernel(chunks, main, locals_, rest, place_ref, hid_ref, own_out, peer_out, forward_ref, wout, value):
    expert = pl.program_id(0)
    tensors = forward_ref.shape[0]
    blocks = tensors * forward_ref.shape[1]
    choice = rest_choice(blocks, locals_, rest, expert)
    join_halves(place_ref, own_out, peer_out, own_out, peer_out, None, wout)
    value[...] = dot(hid_ref[0], wout[...]).astype(BF16)
    views = group_views(place_ref, forward_ref, tensors, chunks)
    put_rows(views, value, choice, blocks * main, main, locals_, rest, expert)


def expert_rows(places, hidden, own_out, peer_out, shape, main, rest, chunks):
    locals_, rows, wide = hidden.shape
    half = own_out.shape[2]
    width = shape[-1]
    per = lambda *shape: pl.BlockSpec((1,) + shape, lambda e, *_: (e, 0, 0))
    return pl.pallas_call(
        functools.partial(expert_rows_kernel, chunks, main, locals_, rest),
        grid_spec=pltpu.PrefetchScalarGridSpec(
            num_scalar_prefetch=1,
            grid=(locals_,),
            in_specs=[per(rows, wide)] + [per(wide, half)] * 2,
            out_specs=whole(shape),
            scratch_shapes=[pltpu.VMEM((wide, width), BF16), pltpu.VMEM((rows, width), BF16)],
        ),
        out_shape=jax.ShapeDtypeStruct(shape, BF16),
        compiler_params=params(),
        cost_estimate=cost(2 * locals_ * rows * width * wide, locals_ * rows * width * 6),
        name="expert_rows",
    )(places, hidden, own_out, peer_out)


def expert_weights_kernel(place_ref, x_ref, ge_ref, hid_ref, gi_ref, gl_ref, *refs):
    in_own, in_send, out_own, out_send, router_ref = refs
    half = in_own.shape[1]
    mine = pl.ds(pl.multiple_of(place_ref[0] * half, half), half)
    other = pl.ds(pl.multiple_of((1 - place_ref[0]) * half, half), half)
    in_own[0] = dot(x_ref[0, :, mine], gi_ref[0], ROWS_TN)
    in_send[0] = dot(x_ref[0, :, other], gi_ref[0], ROWS_TN).astype(BF16)
    out_own[0] = dot(hid_ref[0], ge_ref[0, :, mine], ROWS_TN)
    out_send[0] = dot(hid_ref[0], ge_ref[0, :, other], ROWS_TN).astype(BF16)

    @pl.when(pl.program_id(0) == 0)
    def _():
        router_ref[...] = jnp.zeros_like(router_ref)

    router_ref[...] += dot(x_ref[0], gl_ref[0], ROWS_TN)


def expert_weights(places, saved, half):
    x, ge, hidden, gi, gl = saved
    locals_, rows, width = x.shape
    wide = hidden.shape[2]
    experts = gl.shape[2]
    per = lambda *shape: pl.BlockSpec((1,) + shape, lambda e, *_: (e, 0, 0))
    return pl.pallas_call(
        expert_weights_kernel,
        grid_spec=pltpu.PrefetchScalarGridSpec(
            num_scalar_prefetch=1,
            grid=(locals_,),
            in_specs=[per(rows, width), per(rows, width), per(rows, wide), per(rows, wide), per(rows, experts)],
            out_specs=[per(half, wide), per(half, wide), per(wide, half), per(wide, half), whole((width, experts))],
        ),
        out_shape=[
            jax.ShapeDtypeStruct((locals_, half, wide), F32),
            jax.ShapeDtypeStruct((locals_, half, wide), BF16),
            jax.ShapeDtypeStruct((locals_, wide, half), F32),
            jax.ShapeDtypeStruct((locals_, wide, half), BF16),
            jax.ShapeDtypeStruct((width, experts), F32),
        ],
        compiler_params=params(),
        cost_estimate=cost(4 * locals_ * rows * width * wide, locals_ * rows * width * 14),
        name="expert_weights",
    )(places, x, ge, hidden, gi, gl)


def take_rows(target_ref, refs):
    total, at = None, 0
    for ref in refs:
        count = ref.shape[0]
        cols = lax.broadcasted_iota(jnp.int32, (target_ref.shape[0], count), 1) + at
        chosen = jnp.where(cols == target_ref[...], 1.0, 0.0).astype(BF16)
        part = dot(chosen, ref[...])
        total = part if total is None else total + part
        at += count
    return total


def hidden_back_kernel(target_ref, *refs):
    hidden_ref, cot_ref, gain_ref, grad_ref, attn_ref, gain_out = refs[-6:]
    grad_in = take_rows(target_ref, refs[:-6])
    unit, scale = unit_rows(hidden_ref[...])
    gain_out[...] = jnp.sum(grad_in * unit, axis=0, keepdims=True)
    scaled = grad_in * gain_ref[...]
    inside = jnp.mean(unit * scaled, axis=-1, keepdims=True)
    grad = cot_ref[...].astype(F32) + scale * (scaled - unit * inside)
    grad_ref[...] = grad
    attn_ref[...] = grad.astype(BF16)


def hidden_back(target_col, back, hidden, cotangent, gain):
    rows, width = hidden.shape
    return pl.pallas_call(
        hidden_back_kernel,
        out_shape=[
            jax.ShapeDtypeStruct((rows, width), F32),
            jax.ShapeDtypeStruct((rows, width), BF16),
            jax.ShapeDtypeStruct((1, width), F32),
        ],
        compiler_params=params(),
        cost_estimate=cost(3 * rows * rows * width, 16 * rows * width),
        name="hidden_back",
    )(target_col, *back, hidden, cotangent, gain)


def output_kernel(target_ref, *refs):
    hidden_ref, gate_ref, out_ref = refs[-3:]
    out_ref[...] = (hidden_ref[...] + gate_ref[...] * take_rows(target_ref, refs[:-3])).astype(BF16)


def output_rows(target_col, expert_rows, hidden, gate):
    return pl.pallas_call(
        output_kernel,
        out_shape=jax.ShapeDtypeStruct(hidden.shape, BF16),
        compiler_params=params(),
        cost_estimate=cost(3 * hidden.shape[0] * hidden.size, 10 * hidden.size),
        name="output_rows",
    )(target_col, *expert_rows, hidden, gate)


def tokens_back_kernel(tok_ref, *refs):
    gain_ref, hidden_ref, out_ref = refs[-3:]
    unit, scale = unit_rows(tok_ref[...].astype(F32))
    scaled = sum_pieces(refs[:-3]) * gain_ref[...]
    inside = jnp.mean(unit * scaled, axis=-1, keepdims=True)
    out_ref[...] = hidden_ref[...] + scale * (scaled - unit * inside)


def tokens_back(tokens, grad_normed, gain, grad_hidden):
    return pl.pallas_call(
        tokens_back_kernel,
        out_shape=jax.ShapeDtypeStruct(tokens.shape, F32),
        compiler_params=params(),
        cost_estimate=cost(10 * tokens.size, 12 * tokens.size),
        name="tokens_back",
    )(tokens, *grad_normed, gain, grad_hidden)


def shifted(value, axis, count, step):
    return lax.ppermute(value, axis, [(s, (s + step) % count) for s in range(count)])


def gather_ring(value, axis, count):
    me = lax.axis_index(axis)
    parts = [value] + [shifted(value, axis, count, -k) for k in range(1, count)]
    return jnp.roll(jnp.stack(parts), me, axis=0)


def swapped(value, axis, count, bits):
    return lax.ppermute(value, axis, [(s, s ^ bits) for s in range(count)])


def gather_pieces(value, axis, count):
    return [value] + [swapped(value, axis, count, k) for k in range(1, count)]


def gather_hops(value, hops):
    a, b = hops
    first = swapped(value, "tensor", 4, a)
    second = swapped(jnp.concatenate([value, first], axis=0), "tensor", 4, b)
    return first, second


def added(a, b):
    return (a.astype(F32) + b.astype(F32)).astype(BF16)


def swap_pieces(pieces, axis, count):
    return [pieces[0]] + [swapped(pieces[k], axis, count, k) for k in range(1, count)]


def on_device(
    sizes,
    tokens,
    cotangent,
    query_key_value_weight,
    attention_output_weight,
    rel_bias,
    gain_attn,
    gain_moe,
    w_router,
    w_in,
    w_out,
    expert_index,
    slot_index,
    kept_mask,
):
    dp_count, z_count, t_count = sizes
    tok_rows, width = tokens.shape
    experts_all = w_router.shape[1]
    capacity = max(2, 3 * tok_rows // (2 * experts_all))
    locals_ = w_in.shape[0]
    main = capacity // 16 * 16
    rest = capacity - main
    block = locals_ * capacity
    heads = rel_bias.shape[0]
    inner = heads * HEAD_DIM
    part = query_key_value_weight.shape[1]
    fine = w_router.shape[0]
    my_dp = lax.axis_index("dp")
    my_z = lax.axis_index("expert")
    bias = rel_bias.astype(F32)

    my_t = lax.axis_index("tensor")
    owners = dp_count * z_count
    my_owner = my_dp * z_count + my_z
    places = jnp.stack([my_dp, my_z, my_t, my_owner]).astype(jnp.int32)
    token_pieces = gather_pieces(tokens, "tensor", t_count)

    small = jnp.concatenate([gain_attn[:, None], gain_moe[:, None], w_router], axis=1).reshape(-1)
    extra = -(-small.shape[0] // (16 * width)) * 16
    packed = jnp.concatenate(
        [
            query_key_value_weight.transpose(1, 0, 2).reshape(part, 3 * inner),
            attention_output_weight.T,
        ],
        axis=1,
    )
    packed = jnp.concatenate(
        [packed, jnp.pad(small, (0, extra * width - small.shape[0])).reshape(extra, width)], axis=0
    )
    owned = gather_pieces(packed, "expert", z_count)
    ring_done = owned
    owned = owned + [swapped(piece, "dp", dp_count, 1) for piece in owned]
    smalls = jnp.stack([piece[part:].reshape(-1)[: small.shape[0]] for piece in owned])
    smalls = jnp.stack(gather_pieces(smalls, "tensor", t_count)).reshape(t_count * owners, -1)
    owner_ids = jnp.arange(owners, dtype=jnp.int32)[:, None] ^ my_owner
    t_ids = jnp.arange(t_count, dtype=jnp.int32)[None, :] ^ my_t
    smalls = smalls[(t_ids * owners + owner_ids).reshape(-1)].reshape(width, 2 + experts_all)
    if part % 16:
        order = jnp.arange(owners, dtype=jnp.int32) ^ my_owner
        owned = [jnp.stack([piece[:part] for piece in owned])[order].reshape(width, 4 * inner)]
    rows_owned = part if len(owned) > 1 else width
    gain_one = smalls[:, 0].astype(F32)[None]
    gain_two = smalls[:, 1].astype(F32)[None]
    router = smalls[:, 2:]

    z_of = expert_index // locals_
    local = expert_index - z_of * locals_
    inside = jnp.where(
        slot_index < main, local * main + slot_index, locals_ * main + local * rest + slot_index - main
    )
    target = (z_of ^ my_z) * block + inside
    target = jnp.where(kept_mask > 0, target, -1)
    target_row, target_col = target[None, :], target[:, None]
    count = z_count * block
    chunks = min(z_count, 4)
    many = z_count // chunks

    def over_expert(rows):
        pieces = swap_pieces(list(rows.reshape(z_count, block, width)), "expert", z_count)
        if many == 1:
            return pieces
        return [jnp.concatenate(pieces[k * many : (k + 1) * many], axis=0) for k in range(chunks)]

    def back_over_expert(groups):
        if many > 1:
            groups = [g[i * block : (i + 1) * block] for g in groups for i in range(many)]
        pieces = swap_pieces(groups, "expert", z_count)
        if many == 1:
            return pieces
        return [jnp.concatenate(pieces[k * many : (k + 1) * many], axis=0) for k in range(chunks)]

    late_cotangent, _ = lax.optimization_barrier((cotangent, ring_done))
    grad_rows = jnp.concatenate(over_expert(place(target_row, late_cotangent, count)), axis=0)
    late_in, late_out, gain_one = lax.optimization_barrier((w_in, w_out, gain_one))
    peer_in = shifted(late_in, "dp", dp_count, 1)
    peer_out = shifted(late_out, "dp", dp_count, 1)

    parts, (group_tokens, projected, mixed, logs, weights) = attend(
        places, bias, token_pieces, owned, rows_owned, gain_one
    )
    parts, peer_in, peer_out, grad_rows = lax.optimization_barrier((parts, peer_in, peer_out, grad_rows))
    grad_arrived = lax.all_gather(grad_rows, "tensor", axis=0).reshape(t_count, z_count, block, width)
    half_rows = tok_rows // 2
    attn = []
    for h, (a, b) in enumerate(HOPS):
        keep, send = parts[2 * h : 2 * h + 2]
        got = swapped(send, "tensor", t_count, a)
        last = swapped(added(keep[half_rows:], got[half_rows:]), "tensor", t_count, b)
        attn += [keep, got, last]
    hidden_one, sent, gate = route(
        tokens, attn, gain_two, router, target_row, expert_index[:, None], kept_mask[:, None], count
    )
    arrived = []
    for k, group in enumerate(over_expert(sent)):
        pieces = (group,) + gather_hops(group, HOPS[k % 2])
        arrived += [piece.reshape(-1, block, width) for piece in pieces]
    back_parts, saved = expert_forward_back(
        places, arrived, grad_arrived, w_in, peer_in, w_out, peer_out, router, main, rest, chunks
    )

    size = many * block
    back_parts = [piece.reshape(2 * size, width) for piece in back_parts]
    keeps, sends = back_parts[::2], back_parts[1::2]
    got = [swapped(sends[k], "tensor", t_count, HOPS[k % 2][0]) for k in reversed(range(chunks))][::-1]
    forward_part = expert_rows(places, saved[2], w_out, peer_out, grad_arrived.shape, main, rest, chunks)
    got, forward_part = lax.optimization_barrier((got, forward_part))
    groups = []
    for k in range(chunks):
        last = swapped(added(keeps[k][size:], got[k][size:]), "tensor", t_count, HOPS[k % 2][1])
        total = keeps[k][:size].astype(F32) + got[k][:size].astype(F32) + last.astype(F32)
        groups.append(total.astype(BF16))
    grad_back = back_over_expert(groups)
    forward_part, groups = lax.optimization_barrier((forward_part, groups))
    forward_sum = lax.psum_scatter(
        forward_part.reshape(t_count * z_count * block, width), "tensor", scatter_dimension=0, tiled=True
    )
    grad_hidden, grad_attn, gain_two_part = hidden_back(target_col, grad_back, hidden_one, cotangent, gain_two)
    grad_attn, saved = lax.optimization_barrier((grad_attn, saved))
    grad_pieces = [grad_attn]
    for h, hops in enumerate(HOPS):
        grad_pieces += list(gather_hops(grad_attn[h * half_rows : (h + 1) * half_rows], hops))
    in_own, in_send, out_own, out_send, router_part = expert_weights(places, saved, w_in.shape[1])
    grad_pieces, in_send, out_send, forward_sum = lax.optimization_barrier(
        (grad_pieces, in_send, out_send, forward_sum)
    )
    in_got = shifted(in_send, "dp", dp_count, 1)
    out_got = shifted(out_send, "dp", dp_count, 1)
    normed_parts, (weight_part, bucket_part, gain_one_part) = attend_back(
        places, bias, group_tokens, gain_one, weights, projected, mixed, logs, grad_pieces
    )
    normed_parts, weight_part, in_got, out_got = lax.optimization_barrier(
        (normed_parts, weight_part, in_got, out_got)
    )
    grad_normed = swap_pieces(normed_parts, "tensor", t_count)
    grad_w_in = in_own + in_got.astype(F32)
    grad_w_out = out_own + out_got.astype(F32)
    forward_rows = back_over_expert(list(forward_sum.reshape(chunks, many * block, width)))
    output = output_rows(target_col, forward_rows, hidden_one, gate)
    grad_tokens = tokens_back(tokens, grad_normed, gain_one, grad_hidden)

    smalls = jnp.concatenate(
        [
            gain_one_part.reshape(owners, part),
            gain_two_part.reshape(owners, part),
            router_part.reshape(owners, part * experts_all),
            jnp.broadcast_to(bucket_part.reshape(1, heads * BUCKETS), (owners, heads * BUCKETS)),
        ],
        axis=1,
    )
    extra = -(-smalls.shape[1] // (16 * width)) * 16
    smalls = jnp.pad(smalls, ((0, 0), (0, extra * width - smalls.shape[1]))).reshape(owners, extra, width)
    payload = jnp.concatenate([weight_part.reshape(owners, part, width), smalls], axis=1)
    payload = payload.reshape(dp_count, z_count, part + extra, width)
    own = lax.dynamic_index_in_dim(payload, my_dp, 0, keepdims=False)
    other = lax.dynamic_index_in_dim(payload, 1 - my_dp, 0, keepdims=False)
    summed_half = own + shifted(other.astype(BF16), "dp", dp_count, 1).astype(F32)
    turned = [lax.dynamic_index_in_dim(summed_half, my_z ^ k, 0, keepdims=False) for k in range(z_count)]
    pieces = swap_pieces([turned[0]] + [t.astype(BF16) for t in turned[1:]], "expert", z_count)
    total = pieces[0]
    for piece in pieces[1:]:
        total = total + piece.astype(F32)
    weight_total = total[:part].reshape(part, 4, inner)
    grad_w_qkv = weight_total[:, :3].transpose(1, 0, 2)
    grad_w_attn_out = weight_total[:, 3].T
    flat = total[part:].reshape(-1)
    ends = [part, 2 * part, 2 * part + part * experts_all]
    grad_rel_bias = flat[ends[2] : ends[2] + heads * BUCKETS].reshape(heads, BUCKETS)
    rows_left = jnp.concatenate(
        [
            flat[: ends[0]].reshape(t_count, fine),
            flat[ends[0] : ends[1]].reshape(t_count, fine),
            flat[ends[1] : ends[2]].reshape(t_count, fine * experts_all),
        ],
        axis=1,
    )
    turned = [lax.dynamic_index_in_dim(rows_left, my_t ^ k, 0, keepdims=False) for k in range(t_count)]
    left = turned[0]
    for piece in swap_pieces(turned, "tensor", t_count)[1:]:
        left = left + piece
    grad_gain_attn = left[:fine]
    grad_gain_moe = left[fine : 2 * fine]
    grad_w_router = left[2 * fine :].reshape(fine, experts_all)
    return (
        output,
        grad_tokens,
        grad_w_qkv,
        grad_w_attn_out,
        grad_rel_bias,
        grad_gain_attn,
        grad_gain_moe,
        grad_w_router,
        grad_w_in,
        grad_w_out,
    )


def solution(mesh):
    placed = (
        P(("dp", "expert", "tensor"), None),
        P(("dp", "expert", "tensor"), None),
        P(None, ("dp", "expert"), "tensor"),
        P("tensor", ("dp", "expert")),
        P("tensor", None),
        P(("dp", "expert", "tensor")),
        P(("dp", "expert", "tensor")),
        P(("dp", "expert", "tensor"), None),
        P("expert", "dp", "tensor"),
        P("expert", "tensor", "dp"),
        P(("dp", "expert", "tensor")),
        P(("dp", "expert", "tensor")),
        P(("dp", "expert", "tensor")),
    )
    sizes = tuple(mesh.shape[name] for name in ("dp", "expert", "tensor"))
    return jax.shard_map(
        functools.partial(on_device, sizes),
        mesh=mesh,
        in_specs=placed,
        out_specs=(
            P(("dp", "expert", "tensor"), None),
            P(("dp", "expert", "tensor"), None),
            P(None, ("dp", "expert"), "tensor"),
            P("tensor", ("dp", "expert")),
            P("tensor", None),
            P(("dp", "expert", "tensor")),
            P(("dp", "expert", "tensor")),
            P(("dp", "expert", "tensor"), None),
            P("expert", "dp", "tensor"),
            P("expert", "tensor", "dp"),
        ),
        check_vma=False,
    )
```

```python
import functools

import jax
import jax.numpy as jnp
from jax import lax
from jax.experimental import pallas as pl
from jax.experimental.pallas import tpu as pltpu
from jax.sharding import PartitionSpec as P

HEAD_DIM = 64
BUCKETS = 32
LENGTH = 512
TILE = 128
EPSILON = 1e-06
BORDERS = (12, 16, 23, 32, 46, 64, 91)
F32 = jnp.float32
BF16 = jnp.bfloat16
GELU_A = 0.7978845608028654
GELU_B = 0.044715
ROWS_NN = (((1,), (0,)), ((), ()))
ROWS_NT = (((1,), (1,)), ((), ()))
ROWS_TN = (((0,), (0,)), ((), ()))
VMEM_BYTES = 56 * 1024 * 1024


def dot(a, b, dims=ROWS_NN):
    return lax.dot_general(a, b, dims, preferred_element_type=F32)


def params(**more):
    return pltpu.CompilerParams(vmem_limit_bytes=VMEM_BYTES, **more)


def cost(flops, moved, special=0):
    return pl.CostEstimate(flops=int(flops), bytes_accessed=int(moved), transcendentals=int(special))


def whole(shape):
    return pl.BlockSpec(shape, lambda *_: (0,) * len(shape))


def tile_bucket(step):
    rows = lax.broadcasted_iota(jnp.int32, (TILE, TILE), 0)
    cols = lax.broadcasted_iota(jnp.int32, (TILE, TILE), 1)
    offset = cols - rows + step * TILE
    distance = jnp.abs(offset)
    bucket = jnp.minimum(distance, 8)
    for border in BORDERS:
        bucket = bucket + jnp.where(distance >= border, 1, 0)
    return bucket + jnp.where(offset > 0, 16, 0)


def tile_range(step):
    return {-1: range(1, 16), 0: range(0, 32), 1: range(17, 32)}[step]


def fill_bias(bias_ref, table, heads):
    blocks = LENGTH // TILE
    buckets = {step: tile_bucket(step) for step in (-1, 0, 1)}
    for head in range(heads):
        near = {}
        for step in (-1, 0, 1):
            value = jnp.zeros((TILE, TILE), F32)
            for k in tile_range(step):
                value = jnp.where(buckets[step] == k, bias_ref[head, k], value)
            near[step] = value
        low = jnp.full((TILE, TILE), bias_ref[head, 15], F32)
        high = jnp.full((TILE, TILE), bias_ref[head, 31], F32)
        for i in range(blocks):
            for j in range(blocks):
                step = j - i
                value = near[step] if abs(step) <= 1 else (low if step < 0 else high)
                table[head, i * TILE : (i + 1) * TILE, j * TILE : (j + 1) * TILE] = value


def unit_rows(values):
    scale = lax.rsqrt(jnp.mean(values * values, axis=-1, keepdims=True) + EPSILON)
    return values * scale, scale


HOPS = ((1, 2), (2, 1))


def group_rows(place_ref, out, pieces):
    rows = pieces[0].shape[0]
    for j, piece in enumerate(pieces):
        at = pl.multiple_of((place_ref[2] ^ j) * rows, rows)
        out[pl.ds(at, rows), :] = piece[...]


def group_halves(place_ref, out, pieces):
    rows = pieces[0].shape[0]
    half = rows // 2
    at = pl.multiple_of(place_ref[2] * rows, rows)
    out[pl.ds(at, rows), :] = pieces[0][...]
    for h, (a, b) in enumerate(HOPS):
        first, second = pieces[1 + 2 * h : 3 + 2 * h]
        for j, value in ((a, first[...]), (b, second[:half, :]), (a | b, second[half:, :])):
            at = pl.multiple_of((place_ref[2] ^ j) * rows + h * half, half)
            out[pl.ds(at, half), :] = value


def part_halves(place_ref, pieces, source):
    half = pieces[0].shape[0] // 2
    for h, (a, b) in enumerate(HOPS):
        for piece, order in zip(pieces[2 * h : 2 * h + 2], ((0, b), (a, a | b))):
            for n, j in enumerate(order):
                at = pl.multiple_of((place_ref[2] ^ j) * 2 * half + h * half, half)
                piece[n * half : (n + 1) * half, :] = source[pl.ds(at, half), :]


def part_rows(place_ref, pieces, source):
    rows = pieces[0].shape[0]
    for j, piece in enumerate(pieces):
        at = pl.multiple_of((place_ref[2] ^ j) * rows, rows)
        piece[...] = source[pl.ds(at, rows), :]


def attend_kernel(heads, tensors, owners, part, place_ref, bias_ref, *refs):
    refs = list(refs)
    take = lambda n: [refs.pop(0) for _ in range(n)]
    pieces, owned, (gain_ref,), parts = take(tensors), take(owners), take(1), take(tensors)
    tok_ref, qkv_ref, mixed_ref, log_ref, w_ref, table, wo, group, result = refs
    inner = heads * HEAD_DIM
    step_id = pl.program_id(0)

    @pl.when(step_id == 0)
    def _():
        fill_bias(bias_ref, table, heads)
        group_rows(place_ref, group, pieces)
        for k, piece in enumerate(owned):
            at = pl.multiple_of((place_ref[3] ^ k) * part, part) if owners > 1 else 0
            w_ref[pl.ds(at, part), :] = piece[:part, :]
        wo[...] = w_ref[:, 3 * inner :]

    here = pl.ds(pl.multiple_of(step_id * LENGTH, LENGTH), LENGTH)
    tok_ref[...] = group[here, :]
    unit, _ = unit_rows(tok_ref[...].astype(F32))
    normed = (unit * gain_ref[...]).astype(BF16)
    qkv_ref[...] = dot(normed, w_ref[:, : 3 * inner]).astype(BF16)
    lanes = lax.broadcasted_iota(jnp.int32, (LENGTH, TILE), 1)
    logs = jnp.zeros((LENGTH, TILE), F32)
    for head in range(heads):
        at = head * HEAD_DIM
        query = qkv_ref[:, at : at + HEAD_DIM] * HEAD_DIM ** (-0.5)
        key = qkv_ref[:, inner + at : inner + at + HEAD_DIM]
        value = qkv_ref[:, 2 * inner + at : 2 * inner + at + HEAD_DIM]
        scores = dot(query.astype(BF16), key, ROWS_NT) + table[head]
        top = jnp.max(scores, axis=-1, keepdims=True)
        exponent = jnp.exp(scores - top)
        total = jnp.sum(exponent, axis=-1, keepdims=True)
        attention = (exponent * (1.0 / total)).astype(BF16)
        mixed_ref[:, at : at + HEAD_DIM] = dot(attention, value).astype(BF16)
        logs = jnp.where(lanes == head, top + jnp.log(total), logs)
    log_ref[...] = logs
    result[here, :] = dot(mixed_ref[...], wo[...], ROWS_NT).astype(BF16)

    @pl.when(step_id == pl.num_programs(0) - 1)
    def _():
        part_halves(place_ref, parts, result)


def attend(places, bias, pieces, owned, part, gain):
    tensors = len(pieces)
    piece_rows, width = pieces[0].shape
    rows = tensors * piece_rows
    heads = bias.shape[0]
    inner = heads * HEAD_DIM
    seqs = rows // LENGTH
    by_seq = lambda cols: pl.BlockSpec((LENGTH, cols), lambda s, *_: (s, 0))
    result = pl.pallas_call(
        functools.partial(attend_kernel, heads, tensors, len(owned), part),
        grid_spec=pltpu.PrefetchScalarGridSpec(
            num_scalar_prefetch=1,
            grid=(seqs,),
            in_specs=[pl.BlockSpec(memory_space=pltpu.SMEM)]
            + [whole((piece_rows, width))] * tensors
            + [whole(o.shape) for o in owned]
            + [whole((1, width))],
            out_specs=[whole((piece_rows, width))] * tensors
            + [by_seq(width), by_seq(3 * inner), by_seq(inner), by_seq(TILE), whole((width, 4 * inner))],
            scratch_shapes=[
                pltpu.VMEM((heads, LENGTH, LENGTH), F32),
                pltpu.VMEM((width, inner), BF16),
                pltpu.VMEM((rows, width), BF16),
                pltpu.VMEM((rows, width), BF16),
            ],
        ),
        out_shape=[jax.ShapeDtypeStruct((piece_rows, width), BF16)] * tensors
        + [
            jax.ShapeDtypeStruct((rows, width), BF16),
            jax.ShapeDtypeStruct((rows, 3 * inner), BF16),
            jax.ShapeDtypeStruct((rows, inner), BF16),
            jax.ShapeDtypeStruct((rows, TILE), F32),
            jax.ShapeDtypeStruct((width, 4 * inner), BF16),
        ],
        compiler_params=params(),
        cost_estimate=cost(8 * rows * width * inner + 4 * rows * LENGTH * inner, rows * width * 8, rows * LENGTH * heads),
        name="attend",
    )(places, bias, *pieces, *owned, gain)
    return result[:tensors], result[tensors:]


def attend_back_kernel(
    heads, tensors, place_ref, bias_ref, tok_ref, gain_ref, w_ref, qkv_ref, mixed_ref, log_ref, *refs
):
    refs = list(refs)
    pieces = [refs.pop(0) for _ in range(5)]
    parts = [refs.pop(0) for _ in range(tensors)]
    weight_ref, buckets_ref, gain_out, table, wo, gmix, gproj, near, far, rows_s, group, result = refs
    inner = heads * HEAD_DIM
    blocks = LENGTH // TILE
    step_id = pl.program_id(0)

    @pl.when(step_id == 0)
    def _():
        fill_bias(bias_ref, table, heads)
        wo[...] = w_ref[:, 3 * inner :]
        near[...] = jnp.zeros_like(near)
        far[...] = jnp.zeros_like(far)
        weight_ref[...] = jnp.zeros_like(weight_ref)
        gain_out[...] = jnp.zeros_like(gain_out)
        group_halves(place_ref, group, pieces)

    here = pl.ds(pl.multiple_of(step_id * LENGTH, LENGTH), LENGTH)
    gmix[...] = dot(group[here, :], wo[...]).astype(BF16)
    for head in range(heads):
        at = head * HEAD_DIM
        query = (qkv_ref[:, at : at + HEAD_DIM] * HEAD_DIM ** (-0.5)).astype(BF16)
        key = qkv_ref[:, inner + at : inner + at + HEAD_DIM]
        value = qkv_ref[:, 2 * inner + at : 2 * inner + at + HEAD_DIM]
        grad_rows = gmix[:, at : at + HEAD_DIM]
        scores = dot(query, key, ROWS_NT) + table[head]
        attention = jnp.exp(scores - log_ref[:, head : head + 1])
        grad_weights = dot(grad_rows, value, ROWS_NT)
        inner_sum = jnp.sum(attention * grad_weights, axis=-1, keepdims=True)
        grad_scores = attention * (grad_weights - inner_sum)
        low = jnp.zeros((TILE, TILE), F32)
        high = jnp.zeros((TILE, TILE), F32)
        mid = [jnp.zeros((TILE, TILE), F32) for _ in range(3)]
        for i in range(blocks):
            for j in range(blocks):
                piece = grad_scores[i * TILE : (i + 1) * TILE, j * TILE : (j + 1) * TILE]
                if abs(j - i) <= 1:
                    mid[j - i + 1] = mid[j - i + 1] + piece
                elif j < i:
                    low = low + piece
                else:
                    high = high + piece
        for k in range(3):
            near[head * 3 + k] += mid[k]
        far[head * 2] += low
        far[head * 2 + 1] += high
        rounded = grad_scores.astype(BF16)
        gproj[:, at : at + HEAD_DIM] = (dot(rounded, key) * HEAD_DIM ** (-0.5)).astype(BF16)
        gproj[:, inner + at : inner + at + HEAD_DIM] = dot(rounded, query, ROWS_TN).astype(BF16)
        gproj[:, 2 * inner + at : 2 * inner + at + HEAD_DIM] = dot(
            attention.astype(BF16), grad_rows, ROWS_TN
        ).astype(BF16)
    unit, _ = unit_rows(tok_ref[...].astype(F32))
    normed = (unit * gain_ref[...]).astype(BF16)
    grad_normed = dot(gproj[...], w_ref[:, : 3 * inner], ROWS_NT)
    result[here, :] = grad_normed.astype(BF16)
    gain_out[...] += jnp.sum(grad_normed * unit, axis=0, keepdims=True)
    weight_ref[:, : 3 * inner] += dot(normed, gproj[...], ROWS_TN)
    weight_ref[:, 3 * inner :] += dot(group[here, :], mixed_ref[...], ROWS_TN)

    @pl.when(step_id == pl.num_programs(0) - 1)
    def _():
        part_rows(place_ref, parts, result)
        ids = [tile_bucket(step) for step in (-1, 0, 1)]
        for head in range(heads):
            for k in range(BUCKETS):
                total = jnp.zeros((TILE, TILE), F32)
                for step in (-1, 0, 1):
                    if k in tile_range(step):
                        total = total + jnp.where(ids[step + 1] == k, near[head * 3 + step + 1], 0.0)
                if k == 15:
                    total = total + far[head * 2]
                if k == 31:
                    total = total + far[head * 2 + 1]
                at = head * BUCKETS + k
                rows_s[at : at + 1, :] = jnp.sum(total, axis=0, keepdims=True)
        buckets_ref[...] = jnp.sum(rows_s[...], axis=1, keepdims=True)


def attend_back(places, bias, tokens, gain, weights, projected, mixed, logs, pieces):
    rows, width = tokens.shape
    tensors = rows // pieces[0].shape[0]
    piece = whole(pieces[0].shape)
    heads = bias.shape[0]
    inner = heads * HEAD_DIM
    seqs = rows // LENGTH
    by_seq = lambda cols: pl.BlockSpec((LENGTH, cols), lambda s, *_: (s, 0))
    result = pl.pallas_call(
        functools.partial(attend_back_kernel, heads, tensors),
        grid_spec=pltpu.PrefetchScalarGridSpec(
            num_scalar_prefetch=1,
            grid=(seqs,),
            in_specs=[
                pl.BlockSpec(memory_space=pltpu.SMEM),
                by_seq(width),
                whole((1, width)),
                whole((width, 4 * inner)),
                by_seq(3 * inner),
                by_seq(inner),
                by_seq(TILE),
            ]
            + [whole(p.shape) for p in pieces],
            out_specs=[piece] * tensors
            + [whole((width, 4 * inner)), whole((heads * BUCKETS, 1)), whole((1, width))],
            scratch_shapes=[
                pltpu.VMEM((heads, LENGTH, LENGTH), F32),
                pltpu.VMEM((width, inner), BF16),
                pltpu.VMEM((LENGTH, inner), BF16),
                pltpu.VMEM((LENGTH, 3 * inner), BF16),
                pltpu.VMEM((heads * 3, TILE, TILE), F32),
                pltpu.VMEM((heads * 2, TILE, TILE), F32),
                pltpu.VMEM((heads * BUCKETS, TILE), F32),
                pltpu.VMEM((rows, width), BF16),
                pltpu.VMEM((rows, width), BF16),
            ],
        ),
        out_shape=[jax.ShapeDtypeStruct(pieces[0].shape, BF16)] * tensors
        + [
            jax.ShapeDtypeStruct((width, 4 * inner), F32),
            jax.ShapeDtypeStruct((heads * BUCKETS, 1), F32),
            jax.ShapeDtypeStruct((1, width), F32),
        ],
        compiler_params=params(),
        cost_estimate=cost(18 * rows * width * inner + 10 * rows * LENGTH * inner, rows * width * 12, rows * LENGTH * heads),
        name="attend_back",
    )(places, bias, tokens, gain, weights, projected, mixed, logs, *pieces)
    return result[:tensors], result[tensors:]


def first_rows_kernel(count, *refs):
    out_ref = refs[-1]
    for k, ref in enumerate(refs[:-1]):
        out_ref[k] = ref[:count, :]


def first_rows(pieces, start, extra, count):
    width = pieces[0].shape[1]
    return pl.pallas_call(
        functools.partial(first_rows_kernel, count),
        grid=(1,),
        in_specs=[pl.BlockSpec((extra, width), lambda i: (start // extra, 0))] * len(pieces),
        out_specs=whole((len(pieces), count, width)),
        out_shape=jax.ShapeDtypeStruct((len(pieces), count, width), BF16),
        compiler_params=params(),
        cost_estimate=cost(0, 4 * len(pieces) * extra * width),
        name="first_rows",
    )(*pieces)


def place_kernel(target_ref, rows_ref, out_ref):
    count = out_ref.shape[0]
    rows = lax.broadcasted_iota(jnp.int32, (count, rows_ref.shape[0]), 0)
    chosen = jnp.where(rows == target_ref[...], 1.0, 0.0).astype(BF16)
    out_ref[...] = dot(chosen, rows_ref[...]).astype(BF16)


def place(target_row, rows, count):
    return pl.pallas_call(
        place_kernel,
        out_shape=jax.ShapeDtypeStruct((count, rows.shape[1]), BF16),
        compiler_params=params(),
        cost_estimate=cost(2 * count * rows.size, 4 * rows.size),
        name="place",
    )(target_row, rows)


def softmax_rows(logits):
    exponent = jnp.exp(logits - jnp.max(logits, axis=-1, keepdims=True))
    return exponent * (1.0 / jnp.sum(exponent, axis=-1, keepdims=True))


def sum_pieces(refs):
    total = refs[0][...].astype(F32)
    for ref in refs[1:]:
        total = total + ref[...].astype(F32)
    return total


def route_kernel(tok_ref, *refs):
    gain_ref, router_ref, target_ref, index_ref, kept_ref, hidden_ref, sent_ref, gate_ref = refs[6:]
    half = tok_ref.shape[0] // 2
    for h in range(2):
        keep, got, last = refs[3 * h : 3 * h + 3]
        here = slice(h * half, (h + 1) * half)
        added = keep[:half, :].astype(F32) + got[:half, :].astype(F32) + last[...].astype(F32)
        hidden_ref[here, :] = tok_ref[here, :].astype(F32) + added
    hidden = hidden_ref[...]
    unit, _ = unit_rows(hidden)
    moe_in = (unit * gain_ref[...]).astype(BF16)
    count = sent_ref.shape[0]
    rows = lax.broadcasted_iota(jnp.int32, (count, hidden.shape[0]), 0)
    chosen = jnp.where(rows == target_ref[...], 1.0, 0.0).astype(BF16)
    sent_ref[...] = dot(chosen, moe_in).astype(BF16)
    probs = softmax_rows(dot(moe_in, router_ref[...]))
    lanes = lax.broadcasted_iota(jnp.int32, probs.shape, 1)
    picked = jnp.sum(jnp.where(lanes == index_ref[...], probs, 0.0), axis=-1, keepdims=True)
    gate_ref[...] = picked * kept_ref[...].astype(F32)


def route(tokens, attn, gain, router, target_row, index_col, kept_col, count):
    rows, width = tokens.shape
    return pl.pallas_call(
        route_kernel,
        out_shape=[
            jax.ShapeDtypeStruct((rows, width), F32),
            jax.ShapeDtypeStruct((count, width), BF16),
            jax.ShapeDtypeStruct((rows, 1), F32),
        ],
        compiler_params=params(),
        cost_estimate=cost(2 * count * rows * width, 12 * rows * width),
        name="route",
    )(tokens, *attn, gain, router, target_row, index_col, kept_col)


def rest_choice(blocks, locals_, rest, expert):
    rows = lax.broadcasted_iota(jnp.int32, (blocks * rest, blocks * locals_ * rest), 0)
    cols = lax.broadcasted_iota(jnp.int32, (blocks * rest, blocks * locals_ * rest), 1)
    block = lax.div(rows, rest)
    wanted = block * (locals_ * rest) + expert * rest + (rows - block * rest)
    return jnp.where(cols == wanted, 1.0, 0.0).astype(BF16)


def pick_rows(out_ref, views, choice, main_rows, main, expert):
    at = 0
    pieces = []
    for view in views:
        blocks, size, width = view.shape
        if main:
            start = pl.multiple_of(expert * main, main)
            out_ref[at : at + blocks * main, :] = view[:, pl.ds(start, main), :].reshape(blocks * main, width)
            at += blocks * main
        rest = size - size * main_rows // out_ref.shape[0]
        pieces.append(view[:, size - rest :, :].reshape(blocks * rest, width))
    out_ref[main_rows:, :] = dot(choice, jnp.concatenate(pieces, axis=0)).astype(BF16)


def put_rows(views, value_ref, choice, main_rows, main, locals_, rest, expert):
    at = 0
    spread = dot(choice, value_ref[main_rows:, :], ROWS_TN).astype(BF16)
    rest_at = 0
    for view in views:
        blocks, _, width = view.shape
        if main:
            count = blocks * main
            start = pl.multiple_of(expert * main, main)
            view[:, pl.ds(start, main), :] = value_ref[at : at + count, :].reshape(blocks, main, width)
            at += count
        part = spread[rest_at : rest_at + blocks * locals_ * rest].reshape(blocks, locals_ * rest, width)
        rest_at += blocks * locals_ * rest

        @pl.when(expert == 0)
        def _():
            view[:, locals_ * main :, :] = part

        @pl.when(expert > 0)
        def _():
            view[:, locals_ * main :, :] = view[:, locals_ * main :, :] + part


def group_views(place_ref, ref, tensors, chunks):
    size = ref.shape[1] // chunks
    views = []
    for k in range(chunks):
        a, b = HOPS[k % 2]
        views += [ref.at[place_ref[2] ^ j, k * size : (k + 1) * size] for j in (0, a, b, a | b)]
    return views


def join_halves(place_ref, own_in, peer_in, own_out, peer_out, win, wout):
    half = own_in.shape[1]
    mine = pl.multiple_of(place_ref[0] * half, half)
    other = pl.multiple_of((1 - place_ref[0]) * half, half)
    if win is not None:
        win[pl.ds(mine, half), :] = own_in[0]
        win[pl.ds(other, half), :] = peer_in[0]
    half_out = own_out.shape[2]
    mine = pl.multiple_of(place_ref[0] * half_out, half_out)
    other = pl.multiple_of((1 - place_ref[0]) * half_out, half_out)
    wout[:, pl.ds(mine, half_out)] = own_out[0]
    wout[:, pl.ds(other, half_out)] = peer_out[0]


def expert_kernel(chunks, tensors, main, locals_, rest, place_ref, *refs):
    refs = list(refs)
    take = lambda n: [refs.pop(0) for _ in range(n)]
    xs = take(3 * chunks)
    (g_ref,) = take(1)
    own_in, peer_in, own_out, peer_out, router = take(5)
    backs = take(2 * chunks)
    x_ref, ge_ref, hid_ref, gi_ref, gl_ref = take(5)
    win, wout, grows, inner, gunits, gate_s, dots, back = take(8)
    expert = pl.program_id(0)
    blocks = sum(ref.shape[0] for ref in xs)
    main_rows = blocks * main
    rows, width = x_ref.shape[1:]
    wide = win.shape[1]
    choice = rest_choice(blocks, locals_, rest, expert)
    many = xs[0].shape[0]
    back_refs = []
    for k in range(chunks):
        keep, send = backs[2 * k : 2 * k + 2]
        back_refs += [ref.at[n * many : (n + 1) * many] for n in range(2) for ref in (keep, send)]
    pick_rows(x_ref.at[0], xs, choice, main_rows, main, expert)
    pick_rows(grows, group_views(place_ref, g_ref, tensors, chunks), choice, main_rows, main, expert)
    join_halves(place_ref, own_in, peer_in, own_out, peer_out, win, wout)
    inner[...] = dot(x_ref[0], win[...])
    gunits[...] = dot(grows[...], wout[...], ROWS_NT)
    probs = softmax_rows(dot(x_ref[0], router[...]))
    lanes = lax.broadcasted_iota(jnp.int32, probs.shape, 1)
    mine = lanes == place_ref[1] * locals_ + expert
    picked = jnp.sum(jnp.where(mine, probs, 0.0), axis=-1, keepdims=True)
    gate_s[...] = jnp.broadcast_to(picked, gate_s.shape)
    chunk = 16
    half_wide = wide // 2 if wide % (2 * TILE) == 0 else wide

    def body(step, _):
        at = pl.ds(pl.multiple_of(step * chunk, chunk), chunk)
        gate_tile = gate_s[at, :]
        gate = jnp.concatenate([gate_tile] * (half_wide // TILE), axis=1)
        total = None
        for start in range(0, wide, half_wide):
            lanes_at = slice(start, start + half_wide)
            value = inner[at, lanes_at]
            square = value * value
            wave = jnp.tanh(value * (GELU_A + (GELU_A * GELU_B) * square))
            half = 0.5 + 0.5 * wave
            hidden = (value * half).astype(BF16)
            bend = value * (0.5 * GELU_A + (1.5 * GELU_A * GELU_B) * square)
            slope = half + bend * (1.0 - wave * wave)
            units = gunits[at, lanes_at]
            hid_ref[0, at, lanes_at] = hidden
            gi_ref[0, at, lanes_at] = (gate * (units * slope)).astype(BF16)
            product = hidden.astype(F32) * units
            for tile in range(0, half_wide, TILE):
                part = product[:, tile : tile + TILE]
                total = part if total is None else total + part
        dots[at, :] = total
        gate = jnp.concatenate([gate_tile] * (width // TILE), axis=1)
        ge_ref[0, at, :] = (gate * grows[at, :].astype(F32)).astype(BF16)
        return 0

    lax.fori_loop(0, rows // chunk, body, 0, unroll=4)
    grad_logits = (jnp.sum(dots[...], axis=-1, keepdims=True) * probs * (jnp.where(mine, 1.0, 0.0) - picked)).astype(BF16)
    gl_ref[0] = grad_logits
    back[...] = (dot(gi_ref[0], win[...], ROWS_NT) + dot(grad_logits, router[...], ROWS_NT)).astype(BF16)
    put_rows(back_refs, back, choice, main_rows, main, locals_, rest, expert)


def expert_forward_back(places, xs, gs, own_in, peer_in, own_out, peer_out, router, main, rest, chunks):
    locals_, half, wide = own_in.shape
    width, experts = router.shape
    many, block = xs[0].shape[:2]
    tensors = gs.shape[0]
    blocks = tensors * chunks * many
    back = (2 * many, block, width)
    rows = blocks * (main + rest)
    per = lambda *shape: pl.BlockSpec((1,) + shape, lambda e, *_: (e, 0, 0))
    saved = jax.ShapeDtypeStruct((locals_, rows, width), BF16)
    saved_wide = jax.ShapeDtypeStruct((locals_, rows, wide), BF16)
    result = pl.pallas_call(
        functools.partial(expert_kernel, chunks, tensors, main, locals_, rest),
        grid_spec=pltpu.PrefetchScalarGridSpec(
            num_scalar_prefetch=1,
            grid=(locals_,),
            in_specs=[whole(x.shape) for x in xs]
            + [whole(gs.shape)]
            + [per(half, wide)] * 2 + [per(wide, half)] * 2 + [whole((width, experts))],
            out_specs=[whole(back)] * (2 * chunks)
            + [per(rows, width), per(rows, width), per(rows, wide), per(rows, wide), per(rows, experts)],
            scratch_shapes=[
                pltpu.VMEM((width, wide), BF16),
                pltpu.VMEM((wide, width), BF16),
                pltpu.VMEM((rows, width), BF16),
                pltpu.VMEM((rows, wide), F32),
                pltpu.VMEM((rows, wide), F32),
                pltpu.VMEM((rows, TILE), F32),
                pltpu.VMEM((rows, TILE), F32),
                pltpu.VMEM((rows, width), BF16),
            ],
        ),
        out_shape=[jax.ShapeDtypeStruct(back, BF16)] * (2 * chunks)
        + [saved, saved, saved_wide, saved_wide, jax.ShapeDtypeStruct((locals_, rows, experts), BF16)],
        compiler_params=params(),
        cost_estimate=cost(6 * locals_ * rows * width * wide, locals_ * rows * width * 14, locals_ * rows * wide),
        name="experts",
    )(places, *xs, gs, own_in, peer_in, own_out, peer_out, router)
    return result[: 2 * chunks], result[2 * chunks :]


def expert_rows_kernel(chunks, main, locals_, rest, place_ref, hid_ref, own_out, peer_out, forward_ref, wout, value):
    expert = pl.program_id(0)
    tensors = forward_ref.shape[0]
    blocks = tensors * forward_ref.shape[1]
    choice = rest_choice(blocks, locals_, rest, expert)
    join_halves(place_ref, own_out, peer_out, own_out, peer_out, None, wout)
    value[...] = dot(hid_ref[0], wout[...]).astype(BF16)
    views = group_views(place_ref, forward_ref, tensors, chunks)
    put_rows(views, value, choice, blocks * main, main, locals_, rest, expert)


def expert_rows(places, hidden, own_out, peer_out, shape, main, rest, chunks):
    locals_, rows, wide = hidden.shape
    half = own_out.shape[2]
    width = shape[-1]
    per = lambda *shape: pl.BlockSpec((1,) + shape, lambda e, *_: (e, 0, 0))
    return pl.pallas_call(
        functools.partial(expert_rows_kernel, chunks, main, locals_, rest),
        grid_spec=pltpu.PrefetchScalarGridSpec(
            num_scalar_prefetch=1,
            grid=(locals_,),
            in_specs=[per(rows, wide)] + [per(wide, half)] * 2,
            out_specs=whole(shape),
            scratch_shapes=[pltpu.VMEM((wide, width), BF16), pltpu.VMEM((rows, width), BF16)],
        ),
        out_shape=jax.ShapeDtypeStruct(shape, BF16),
        compiler_params=params(),
        cost_estimate=cost(2 * locals_ * rows * width * wide, locals_ * rows * width * 6),
        name="expert_rows",
    )(places, hidden, own_out, peer_out)


def expert_weights_kernel(place_ref, x_ref, ge_ref, hid_ref, gi_ref, gl_ref, *refs):
    in_own, in_send, out_own, out_send, router_ref = refs
    half = in_own.shape[1]
    mine = pl.ds(pl.multiple_of(place_ref[0] * half, half), half)
    other = pl.ds(pl.multiple_of((1 - place_ref[0]) * half, half), half)
    in_own[0] = dot(x_ref[0, :, mine], gi_ref[0], ROWS_TN)
    in_send[0] = dot(x_ref[0, :, other], gi_ref[0], ROWS_TN).astype(BF16)
    out_own[0] = dot(hid_ref[0], ge_ref[0, :, mine], ROWS_TN)
    out_send[0] = dot(hid_ref[0], ge_ref[0, :, other], ROWS_TN).astype(BF16)

    @pl.when(pl.program_id(0) == 0)
    def _():
        router_ref[...] = jnp.zeros_like(router_ref)

    router_ref[...] += dot(x_ref[0], gl_ref[0], ROWS_TN)


def expert_weights(places, saved, half):
    x, ge, hidden, gi, gl = saved
    locals_, rows, width = x.shape
    wide = hidden.shape[2]
    experts = gl.shape[2]
    per = lambda *shape: pl.BlockSpec((1,) + shape, lambda e, *_: (e, 0, 0))
    return pl.pallas_call(
        expert_weights_kernel,
        grid_spec=pltpu.PrefetchScalarGridSpec(
            num_scalar_prefetch=1,
            grid=(locals_,),
            in_specs=[per(rows, width), per(rows, width), per(rows, wide), per(rows, wide), per(rows, experts)],
            out_specs=[per(half, wide), per(half, wide), per(wide, half), per(wide, half), whole((width, experts))],
        ),
        out_shape=[
            jax.ShapeDtypeStruct((locals_, half, wide), F32),
            jax.ShapeDtypeStruct((locals_, half, wide), BF16),
            jax.ShapeDtypeStruct((locals_, wide, half), F32),
            jax.ShapeDtypeStruct((locals_, wide, half), BF16),
            jax.ShapeDtypeStruct((width, experts), F32),
        ],
        compiler_params=params(),
        cost_estimate=cost(4 * locals_ * rows * width * wide, locals_ * rows * width * 14),
        name="expert_weights",
    )(places, x, ge, hidden, gi, gl)


def take_rows(target_ref, refs):
    total, at = None, 0
    for ref in refs:
        count = ref.shape[0]
        cols = lax.broadcasted_iota(jnp.int32, (target_ref.shape[0], count), 1) + at
        chosen = jnp.where(cols == target_ref[...], 1.0, 0.0).astype(BF16)
        part = dot(chosen, ref[...])
        total = part if total is None else total + part
        at += count
    return total


def hidden_back_kernel(target_ref, *refs):
    hidden_ref, cot_ref, gain_ref, grad_ref, attn_ref, gain_out = refs[-6:]
    grad_in = take_rows(target_ref, refs[:-6])
    unit, scale = unit_rows(hidden_ref[...])
    gain_out[...] = jnp.sum(grad_in * unit, axis=0, keepdims=True)
    scaled = grad_in * gain_ref[...]
    inside = jnp.mean(unit * scaled, axis=-1, keepdims=True)
    grad = cot_ref[...].astype(F32) + scale * (scaled - unit * inside)
    grad_ref[...] = grad
    attn_ref[...] = grad.astype(BF16)


def hidden_back(target_col, back, hidden, cotangent, gain):
    rows, width = hidden.shape
    return pl.pallas_call(
        hidden_back_kernel,
        out_shape=[
            jax.ShapeDtypeStruct((rows, width), F32),
            jax.ShapeDtypeStruct((rows, width), BF16),
            jax.ShapeDtypeStruct((1, width), F32),
        ],
        compiler_params=params(),
        cost_estimate=cost(3 * rows * rows * width, 16 * rows * width),
        name="hidden_back",
    )(target_col, *back, hidden, cotangent, gain)


def output_kernel(target_ref, *refs):
    hidden_ref, gate_ref, out_ref = refs[-3:]
    out_ref[...] = (hidden_ref[...] + gate_ref[...] * take_rows(target_ref, refs[:-3])).astype(BF16)


def output_rows(target_col, expert_rows, hidden, gate):
    return pl.pallas_call(
        output_kernel,
        out_shape=jax.ShapeDtypeStruct(hidden.shape, BF16),
        compiler_params=params(),
        cost_estimate=cost(3 * hidden.shape[0] * hidden.size, 10 * hidden.size),
        name="output_rows",
    )(target_col, *expert_rows, hidden, gate)


def tokens_back_kernel(tok_ref, *refs):
    gain_ref, hidden_ref, out_ref = refs[-3:]
    unit, scale = unit_rows(tok_ref[...].astype(F32))
    scaled = sum_pieces(refs[:-3]) * gain_ref[...]
    inside = jnp.mean(unit * scaled, axis=-1, keepdims=True)
    out_ref[...] = hidden_ref[...] + scale * (scaled - unit * inside)


def tokens_back(tokens, grad_normed, gain, grad_hidden):
    return pl.pallas_call(
        tokens_back_kernel,
        out_shape=jax.ShapeDtypeStruct(tokens.shape, F32),
        compiler_params=params(),
        cost_estimate=cost(10 * tokens.size, 12 * tokens.size),
        name="tokens_back",
    )(tokens, *grad_normed, gain, grad_hidden)


def shifted(value, axis, count, step):
    return lax.ppermute(value, axis, [(s, (s + step) % count) for s in range(count)])


def gather_ring(value, axis, count):
    me = lax.axis_index(axis)
    parts = [value] + [shifted(value, axis, count, -k) for k in range(1, count)]
    return jnp.roll(jnp.stack(parts), me, axis=0)


def swapped(value, axis, count, bits):
    return lax.ppermute(value, axis, [(s, s ^ bits) for s in range(count)])


def gather_pieces(value, axis, count):
    return [value] + [swapped(value, axis, count, k) for k in range(1, count)]


def gather_hops(value, hops):
    a, b = hops
    first = swapped(value, "tensor", 4, a)
    second = swapped(jnp.concatenate([value, first], axis=0), "tensor", 4, b)
    return first, second


def added(a, b):
    return (a.astype(F32) + b.astype(F32)).astype(BF16)


def swap_pieces(pieces, axis, count):
    return [pieces[0]] + [swapped(pieces[k], axis, count, k) for k in range(1, count)]


def on_device(
    sizes,
    tokens,
    cotangent,
    query_key_value_weight,
    attention_output_weight,
    rel_bias,
    gain_attn,
    gain_moe,
    w_router,
    w_in,
    w_out,
    expert_index,
    slot_index,
    kept_mask,
):
    dp_count, z_count, t_count = sizes
    tok_rows, width = tokens.shape
    experts_all = w_router.shape[1]
    capacity = max(2, 3 * tok_rows // (2 * experts_all))
    locals_ = w_in.shape[0]
    main = capacity // 16 * 16
    rest = capacity - main
    block = locals_ * capacity
    heads = rel_bias.shape[0]
    inner = heads * HEAD_DIM
    part = query_key_value_weight.shape[1]
    fine = w_router.shape[0]
    my_dp = lax.axis_index("dp")
    my_z = lax.axis_index("expert")
    bias = rel_bias.astype(F32)

    my_t = lax.axis_index("tensor")
    owners = dp_count * z_count
    my_owner = my_dp * z_count + my_z
    places = jnp.stack([my_dp, my_z, my_t, my_owner]).astype(jnp.int32)
    token_pieces = gather_pieces(tokens, "tensor", t_count)

    small = jnp.concatenate([gain_attn[:, None], gain_moe[:, None], w_router], axis=1).reshape(-1)
    small = jnp.concatenate(gather_pieces(small, "tensor", t_count))
    extra = -(-small.shape[0] // (16 * width)) * 16
    packed = jnp.concatenate(
        [
            query_key_value_weight.transpose(1, 0, 2).reshape(part, 3 * inner),
            attention_output_weight.T,
        ],
        axis=1,
    )
    packed = jnp.concatenate(
        [packed, jnp.pad(small, (0, extra * width - small.shape[0])).reshape(extra, width)], axis=0
    )
    owned = gather_pieces(packed, "expert", z_count)
    token_pieces, owned = lax.optimization_barrier((token_pieces, owned))
    owned = owned + [swapped(piece, "dp", dp_count, 1) for piece in owned]
    if part % 16 or part % extra:
        smalls = jnp.stack([piece[part:] for piece in owned])
    else:
        smalls = first_rows(owned, part, extra, -(-small.shape[0] // width))
    smalls = smalls.reshape(owners, -1)[:, : small.shape[0]].reshape(owners * t_count, -1)
    owner_ids = jnp.arange(owners, dtype=jnp.int32)[:, None] ^ my_owner
    t_ids = jnp.arange(t_count, dtype=jnp.int32)[None, :] ^ my_t
    smalls = smalls[(owner_ids * t_count + t_ids).reshape(-1)].reshape(width, 2 + experts_all)
    if part % 16:
        order = jnp.arange(owners, dtype=jnp.int32) ^ my_owner
        owned = [jnp.stack([piece[:part] for piece in owned])[order].reshape(width, 4 * inner)]
    rows_owned = part if len(owned) > 1 else width
    gain_one = smalls[:, 0].astype(F32)[None]
    gain_two = smalls[:, 1].astype(F32)[None]
    router = smalls[:, 2:]

    z_of = expert_index // locals_
    local = expert_index - z_of * locals_
    inside = jnp.where(
        slot_index < main, local * main + slot_index, locals_ * main + local * rest + slot_index - main
    )
    target = (z_of ^ my_z) * block + inside
    target = jnp.where(kept_mask > 0, target, -1)
    target_row, target_col = target[None, :], target[:, None]
    count = z_count * block
    chunks = min(z_count, 4)
    many = z_count // chunks

    def over_expert(rows):
        pieces = swap_pieces(list(rows.reshape(z_count, block, width)), "expert", z_count)
        if many == 1:
            return pieces
        return [jnp.concatenate(pieces[k * many : (k + 1) * many], axis=0) for k in range(chunks)]

    def back_over_expert(groups):
        if many > 1:
            groups = [g[i * block : (i + 1) * block] for g in groups for i in range(many)]
        pieces = swap_pieces(groups, "expert", z_count)
        if many == 1:
            return pieces
        return [jnp.concatenate(pieces[k * many : (k + 1) * many], axis=0) for k in range(chunks)]

    late_cotangent, late_in, late_out, token_pieces, owned, gain_one = lax.optimization_barrier(
        (cotangent, w_in, w_out, token_pieces, owned, gain_one)
    )
    grad_rows = jnp.concatenate(over_expert(place(target_row, late_cotangent, count)), axis=0)
    peer_in = shifted(late_in, "dp", dp_count, 1)
    peer_out = shifted(late_out, "dp", dp_count, 1)

    parts, (group_tokens, projected, mixed, logs, weights) = attend(
        places, bias, token_pieces, owned, rows_owned, gain_one
    )
    parts, peer_in, peer_out, grad_rows = lax.optimization_barrier((parts, peer_in, peer_out, grad_rows))
    grad_arrived = lax.all_gather(grad_rows, "tensor", axis=0).reshape(t_count, z_count, block, width)
    half_rows = tok_rows // 2
    attn = []
    for h, (a, b) in enumerate(HOPS):
        keep, send = parts[2 * h : 2 * h + 2]
        got = swapped(send, "tensor", t_count, a)
        last = swapped(added(keep[half_rows:], got[half_rows:]), "tensor", t_count, b)
        attn += [keep, got, last]
    hidden_one, sent, gate = route(
        tokens, attn, gain_two, router, target_row, expert_index[:, None], kept_mask[:, None], count
    )
    arrived = []
    for k, group in enumerate(over_expert(sent)):
        pieces = (group,) + gather_hops(group, HOPS[k % 2])
        arrived += [piece.reshape(-1, block, width) for piece in pieces]
    back_parts, saved = expert_forward_back(
        places, arrived, grad_arrived, w_in, peer_in, w_out, peer_out, router, main, rest, chunks
    )

    size = many * block
    back_parts = [piece.reshape(2 * size, width) for piece in back_parts]
    keeps, sends = back_parts[::2], back_parts[1::2]
    got = [swapped(sends[k], "tensor", t_count, HOPS[k % 2][0]) for k in reversed(range(chunks))][::-1]
    forward_part = expert_rows(places, saved[2], w_out, peer_out, grad_arrived.shape, main, rest, chunks)
    got, forward_part = lax.optimization_barrier((got, forward_part))
    groups = []
    for k in range(chunks):
        last = swapped(added(keeps[k][size:], got[k][size:]), "tensor", t_count, HOPS[k % 2][1])
        total = keeps[k][:size].astype(F32) + got[k][:size].astype(F32) + last.astype(F32)
        groups.append(total.astype(BF16))
    grad_back = back_over_expert(groups)
    forward_part, groups = lax.optimization_barrier((forward_part, groups))
    forward_sum = lax.psum_scatter(
        forward_part.reshape(t_count * z_count * block, width), "tensor", scatter_dimension=0, tiled=True
    )
    grad_hidden, grad_attn, gain_two_part = hidden_back(target_col, grad_back, hidden_one, cotangent, gain_two)
    grad_attn, saved = lax.optimization_barrier((grad_attn, saved))
    grad_pieces = [grad_attn]
    for h, hops in enumerate(HOPS):
        grad_pieces += list(gather_hops(grad_attn[h * half_rows : (h + 1) * half_rows], hops))
    in_own, in_send, out_own, out_send, router_part = expert_weights(places, saved, w_in.shape[1])
    grad_pieces, in_send, out_send, forward_sum = lax.optimization_barrier(
        (grad_pieces, in_send, out_send, forward_sum)
    )
    in_got = shifted(in_send, "dp", dp_count, 1)
    out_got = shifted(out_send, "dp", dp_count, 1)
    normed_parts, (weight_part, bucket_part, gain_one_part) = attend_back(
        places, bias, group_tokens, gain_one, weights, projected, mixed, logs, grad_pieces
    )
    forward_rows = back_over_expert(list(forward_sum.reshape(chunks, many * block, width)))
    normed_parts, weight_part, in_got, out_got, forward_rows = lax.optimization_barrier(
        (normed_parts, weight_part, in_got, out_got, forward_rows)
    )
    grad_normed = swap_pieces(normed_parts, "tensor", t_count)
    grad_w_in = in_own + in_got.astype(F32)
    grad_w_out = out_own + out_got.astype(F32)
    output = output_rows(target_col, forward_rows, hidden_one, gate)
    grad_tokens = tokens_back(tokens, grad_normed, gain_one, grad_hidden)

    smalls = jnp.concatenate(
        [
            gain_one_part.reshape(owners, part),
            gain_two_part.reshape(owners, part),
            router_part.reshape(owners, part * experts_all),
            jnp.broadcast_to(bucket_part.reshape(1, heads * BUCKETS), (owners, heads * BUCKETS)),
        ],
        axis=1,
    )
    extra = -(-smalls.shape[1] // (16 * width)) * 16
    smalls = jnp.pad(smalls, ((0, 0), (0, extra * width - smalls.shape[1]))).reshape(owners, extra, width)
    payload = jnp.concatenate([weight_part.reshape(owners, part, width), smalls], axis=1)
    payload = payload.reshape(dp_count, z_count, part + extra, width)
    own = lax.dynamic_index_in_dim(payload, my_dp, 0, keepdims=False)
    other = lax.dynamic_index_in_dim(payload, 1 - my_dp, 0, keepdims=False)
    summed_half = own + shifted(other.astype(BF16), "dp", dp_count, 1).astype(F32)
    turned = [lax.dynamic_index_in_dim(summed_half, my_z ^ k, 0, keepdims=False) for k in range(z_count)]
    pieces = swap_pieces([turned[0]] + [t.astype(BF16) for t in turned[1:]], "expert", z_count)
    total = pieces[0]
    for piece in pieces[1:]:
        total = total + piece.astype(F32)
    weight_total = total[:part].reshape(part, 4, inner)
    grad_w_qkv = weight_total[:, :3].transpose(1, 0, 2)
    grad_w_attn_out = weight_total[:, 3].T
    flat = total[part:].reshape(-1)
    ends = [part, 2 * part, 2 * part + part * experts_all]
    grad_rel_bias = flat[ends[2] : ends[2] + heads * BUCKETS].reshape(heads, BUCKETS)
    rows_left = jnp.concatenate(
        [
            flat[: ends[0]].reshape(t_count, fine),
            flat[ends[0] : ends[1]].reshape(t_count, fine),
            flat[ends[1] : ends[2]].reshape(t_count, fine * experts_all),
        ],
        axis=1,
    )
    turned = [lax.dynamic_index_in_dim(rows_left, my_t ^ k, 0, keepdims=False) for k in range(t_count)]
    left = turned[0]
    for piece in swap_pieces(turned, "tensor", t_count)[1:]:
        left = left + piece
    grad_gain_attn = left[:fine]
    grad_gain_moe = left[fine : 2 * fine]
    grad_w_router = left[2 * fine :].reshape(fine, experts_all)
    return (
        output,
        grad_tokens,
        grad_w_qkv,
        grad_w_attn_out,
        grad_rel_bias,
        grad_gain_attn,
        grad_gain_moe,
        grad_w_router,
        grad_w_in,
        grad_w_out,
    )


def solution(mesh):
    placed = (
        P(("dp", "expert", "tensor"), None),
        P(("dp", "expert", "tensor"), None),
        P(None, ("dp", "expert"), "tensor"),
        P("tensor", ("dp", "expert")),
        P("tensor", None),
        P(("dp", "expert", "tensor")),
        P(("dp", "expert", "tensor")),
        P(("dp", "expert", "tensor"), None),
        P("expert", "dp", "tensor"),
        P("expert", "tensor", "dp"),
        P(("dp", "expert", "tensor")),
        P(("dp", "expert", "tensor")),
        P(("dp", "expert", "tensor")),
    )
    sizes = tuple(mesh.shape[name] for name in ("dp", "expert", "tensor"))
    return jax.shard_map(
        functools.partial(on_device, sizes),
        mesh=mesh,
        in_specs=placed,
        out_specs=(
            P(("dp", "expert", "tensor"), None),
            P(("dp", "expert", "tensor"), None),
            P(None, ("dp", "expert"), "tensor"),
            P("tensor", ("dp", "expert")),
            P("tensor", None),
            P(("dp", "expert", "tensor")),
            P(("dp", "expert", "tensor")),
            P(("dp", "expert", "tensor"), None),
            P("expert", "dp", "tensor"),
            P("expert", "tensor", "dp"),
        ),
        check_vma=False,
    )
```

```python
import functools

import jax
import jax.numpy as jnp
from jax import lax
from jax.experimental import pallas as pl
from jax.experimental.pallas import tpu as pltpu
from jax.sharding import PartitionSpec as P

HEAD_DIM = 64
BUCKETS = 32
LENGTH = 512
TILE = 128
EPSILON = 1e-06
BORDERS = (12, 16, 23, 32, 46, 64, 91)
F32 = jnp.float32
BF16 = jnp.bfloat16
GELU_A = 0.7978845608028654
GELU_B = 0.044715
ROWS_NN = (((1,), (0,)), ((), ()))
ROWS_NT = (((1,), (1,)), ((), ()))
ROWS_TN = (((0,), (0,)), ((), ()))
VMEM_BYTES = 56 * 1024 * 1024


def dot(a, b, dims=ROWS_NN):
    return lax.dot_general(a, b, dims, preferred_element_type=F32)


def params(**more):
    return pltpu.CompilerParams(vmem_limit_bytes=VMEM_BYTES, **more)


def cost(flops, moved, special=0):
    return pl.CostEstimate(flops=int(flops), bytes_accessed=int(moved), transcendentals=int(special))


def whole(shape):
    return pl.BlockSpec(shape, lambda *_: (0,) * len(shape))


def tile_bucket(step):
    rows = lax.broadcasted_iota(jnp.int32, (TILE, TILE), 0)
    cols = lax.broadcasted_iota(jnp.int32, (TILE, TILE), 1)
    offset = cols - rows + step * TILE
    distance = jnp.abs(offset)
    bucket = jnp.minimum(distance, 8)
    for border in BORDERS:
        bucket = bucket + jnp.where(distance >= border, 1, 0)
    return bucket + jnp.where(offset > 0, 16, 0)


def tile_range(step):
    return {-1: range(1, 16), 0: range(0, 32), 1: range(17, 32)}[step]


def fill_bias(bias_ref, table, heads):
    blocks = LENGTH // TILE
    buckets = {step: tile_bucket(step) for step in (-1, 0, 1)}
    for head in range(heads):
        near = {}
        for step in (-1, 0, 1):
            value = jnp.zeros((TILE, TILE), F32)
            for k in tile_range(step):
                value = jnp.where(buckets[step] == k, bias_ref[head, k], value)
            near[step] = value
        low = jnp.full((TILE, TILE), bias_ref[head, 15], F32)
        high = jnp.full((TILE, TILE), bias_ref[head, 31], F32)
        for i in range(blocks):
            for j in range(blocks):
                step = j - i
                value = near[step] if abs(step) <= 1 else (low if step < 0 else high)
                table[head, i * TILE : (i + 1) * TILE, j * TILE : (j + 1) * TILE] = value


def unit_rows(values):
    scale = lax.rsqrt(jnp.mean(values * values, axis=-1, keepdims=True) + EPSILON)
    return values * scale, scale


HOPS = ((1, 2), (2, 1))


def group_halves(place_ref, out, pieces):
    rows = pieces[0].shape[0]
    half = rows // 2
    at = pl.multiple_of(place_ref[2] * rows, rows)
    out[pl.ds(at, rows), :] = pieces[0][...]
    for h, (a, b) in enumerate(HOPS):
        first, second = pieces[1 + 2 * h : 3 + 2 * h]
        for j, value in ((a, first[...]), (b, second[:half, :]), (a | b, second[half:, :])):
            at = pl.multiple_of((place_ref[2] ^ j) * rows + h * half, half)
            out[pl.ds(at, half), :] = value


def part_halves(place_ref, pieces, source):
    half = pieces[0].shape[0] // 2
    for h, (a, b) in enumerate(HOPS):
        for piece, order in zip(pieces[2 * h : 2 * h + 2], ((0, b), (a, a | b))):
            for n, j in enumerate(order):
                at = pl.multiple_of((place_ref[2] ^ j) * 2 * half + h * half, half)
                piece[n * half : (n + 1) * half, :] = source[pl.ds(at, half), :]


def part_rows(place_ref, pieces, source):
    rows = pieces[0].shape[0]
    for j, piece in enumerate(pieces):
        at = pl.multiple_of((place_ref[2] ^ j) * rows, rows)
        piece[...] = source[pl.ds(at, rows), :]


def attend_kernel(heads, tensors, owners, part, place_ref, bias_ref, *refs):
    refs = list(refs)
    take = lambda n: [refs.pop(0) for _ in range(n)]
    pieces, owned, (gain_ref,), parts = take(5), take(owners), take(1), take(tensors)
    tok_ref, qkv_ref, mixed_ref, log_ref, w_ref, table, wo, group, result = refs
    inner = heads * HEAD_DIM
    step_id = pl.program_id(0)

    @pl.when(step_id == 0)
    def _():
        fill_bias(bias_ref, table, heads)
        group_halves(place_ref, group, pieces)
        blocks = [piece.at[n] for piece in owned for n in range(piece.shape[0])]
        for k, piece in enumerate(blocks):
            at = pl.multiple_of((place_ref[3] ^ k) * part, part) if owners > 1 else 0
            w_ref[pl.ds(at, part), :] = piece[:part, :]
        wo[...] = w_ref[:, 3 * inner :]

    here = pl.ds(pl.multiple_of(step_id * LENGTH, LENGTH), LENGTH)
    tok_ref[...] = group[here, :]
    unit, _ = unit_rows(tok_ref[...].astype(F32))
    normed = (unit * gain_ref[...]).astype(BF16)
    qkv_ref[...] = dot(normed, w_ref[:, : 3 * inner]).astype(BF16)
    lanes = lax.broadcasted_iota(jnp.int32, (LENGTH, TILE), 1)
    logs = jnp.zeros((LENGTH, TILE), F32)
    for head in range(heads):
        at = head * HEAD_DIM
        query = qkv_ref[:, at : at + HEAD_DIM] * HEAD_DIM ** (-0.5)
        key = qkv_ref[:, inner + at : inner + at + HEAD_DIM]
        value = qkv_ref[:, 2 * inner + at : 2 * inner + at + HEAD_DIM]
        scores = dot(query.astype(BF16), key, ROWS_NT) + table[head]
        top = jnp.max(scores, axis=-1, keepdims=True)
        exponent = jnp.exp(scores - top)
        total = jnp.sum(exponent, axis=-1, keepdims=True)
        attention = (exponent * (1.0 / total)).astype(BF16)
        mixed_ref[:, at : at + HEAD_DIM] = dot(attention, value).astype(BF16)
        logs = jnp.where(lanes == head, top + jnp.log(total), logs)
    log_ref[...] = logs
    result[here, :] = dot(mixed_ref[...], wo[...], ROWS_NT).astype(BF16)

    @pl.when(step_id == pl.num_programs(0) - 1)
    def _():
        part_halves(place_ref, parts, result)


def attend(places, bias, pieces, owned, part, gain):
    tensors = 4
    piece_rows, width = pieces[0].shape
    rows = tensors * piece_rows
    heads = bias.shape[0]
    inner = heads * HEAD_DIM
    seqs = rows // LENGTH
    by_seq = lambda cols: pl.BlockSpec((LENGTH, cols), lambda s, *_: (s, 0))
    result = pl.pallas_call(
        functools.partial(attend_kernel, heads, tensors, len(owned), part),
        grid_spec=pltpu.PrefetchScalarGridSpec(
            num_scalar_prefetch=1,
            grid=(seqs,),
            in_specs=[pl.BlockSpec(memory_space=pltpu.SMEM)]
            + [whole(p.shape) for p in pieces]
            + [whole(o.shape) for o in owned]
            + [whole((1, width))],
            out_specs=[whole((piece_rows, width))] * tensors
            + [by_seq(width), by_seq(3 * inner), by_seq(inner), by_seq(TILE), whole((width, 4 * inner))],
            scratch_shapes=[
                pltpu.VMEM((heads, LENGTH, LENGTH), F32),
                pltpu.VMEM((width, inner), BF16),
                pltpu.VMEM((rows, width), BF16),
                pltpu.VMEM((rows, width), BF16),
            ],
        ),
        out_shape=[jax.ShapeDtypeStruct((piece_rows, width), BF16)] * tensors
        + [
            jax.ShapeDtypeStruct((rows, width), BF16),
            jax.ShapeDtypeStruct((rows, 3 * inner), BF16),
            jax.ShapeDtypeStruct((rows, inner), BF16),
            jax.ShapeDtypeStruct((rows, TILE), F32),
            jax.ShapeDtypeStruct((width, 4 * inner), BF16),
        ],
        compiler_params=params(),
        cost_estimate=cost(8 * rows * width * inner + 4 * rows * LENGTH * inner, rows * width * 8, rows * LENGTH * heads),
        name="attend",
    )(places, bias, *pieces, *owned, gain)
    return result[:tensors], result[tensors:]


def attend_back_kernel(
    heads, tensors, part, place_ref, bias_ref, tok_ref, gain_ref, w_ref, qkv_ref, mixed_ref, log_ref, *refs
):
    refs = list(refs)
    pieces = [refs.pop(0) for _ in range(5)]
    gain_two_ref, router_ref = refs.pop(0), refs.pop(0)
    parts = [refs.pop(0) for _ in range(tensors)]
    own_ref, other_ref, weight_ref, gain_out, table, wo, gmix, gproj, near, far, rows_s, group, result = refs
    inner = heads * HEAD_DIM
    blocks = LENGTH // TILE
    step_id = pl.program_id(0)

    @pl.when(step_id == 0)
    def _():
        fill_bias(bias_ref, table, heads)
        wo[...] = w_ref[:, 3 * inner :]
        near[...] = jnp.zeros_like(near)
        far[...] = jnp.zeros_like(far)
        weight_ref[...] = jnp.zeros_like(weight_ref)
        gain_out[...] = jnp.zeros_like(gain_out)
        group_halves(place_ref, group, pieces)

    here = pl.ds(pl.multiple_of(step_id * LENGTH, LENGTH), LENGTH)
    gmix[...] = dot(group[here, :], wo[...]).astype(BF16)
    for head in range(heads):
        at = head * HEAD_DIM
        query = (qkv_ref[:, at : at + HEAD_DIM] * HEAD_DIM ** (-0.5)).astype(BF16)
        key = qkv_ref[:, inner + at : inner + at + HEAD_DIM]
        value = qkv_ref[:, 2 * inner + at : 2 * inner + at + HEAD_DIM]
        grad_rows = gmix[:, at : at + HEAD_DIM]
        scores = dot(query, key, ROWS_NT) + table[head]
        attention = jnp.exp(scores - log_ref[:, head : head + 1])
        grad_weights = dot(grad_rows, value, ROWS_NT)
        inner_sum = jnp.sum(attention * grad_weights, axis=-1, keepdims=True)
        grad_scores = attention * (grad_weights - inner_sum)
        low = jnp.zeros((TILE, TILE), F32)
        high = jnp.zeros((TILE, TILE), F32)
        mid = [jnp.zeros((TILE, TILE), F32) for _ in range(3)]
        for i in range(blocks):
            for j in range(blocks):
                piece = grad_scores[i * TILE : (i + 1) * TILE, j * TILE : (j + 1) * TILE]
                if abs(j - i) <= 1:
                    mid[j - i + 1] = mid[j - i + 1] + piece
                elif j < i:
                    low = low + piece
                else:
                    high = high + piece
        for k in range(3):
            near[head * 3 + k] += mid[k]
        far[head * 2] += low
        far[head * 2 + 1] += high
        rounded = grad_scores.astype(BF16)
        gproj[:, at : at + HEAD_DIM] = (dot(rounded, key) * HEAD_DIM ** (-0.5)).astype(BF16)
        gproj[:, inner + at : inner + at + HEAD_DIM] = dot(rounded, query, ROWS_TN).astype(BF16)
        gproj[:, 2 * inner + at : 2 * inner + at + HEAD_DIM] = dot(
            attention.astype(BF16), grad_rows, ROWS_TN
        ).astype(BF16)
    unit, _ = unit_rows(tok_ref[...].astype(F32))
    normed = (unit * gain_ref[...]).astype(BF16)
    grad_normed = dot(gproj[...], w_ref[:, : 3 * inner], ROWS_NT)
    result[here, :] = grad_normed.astype(BF16)
    gain_out[...] += jnp.sum(grad_normed * unit, axis=0, keepdims=True)
    weight_ref[:, : 3 * inner] += dot(normed, gproj[...], ROWS_TN)
    weight_ref[:, 3 * inner :] += dot(group[here, :], mixed_ref[...], ROWS_TN)

    @pl.when(step_id == pl.num_programs(0) - 1)
    def _():
        part_rows(place_ref, parts, result)
        ids = [tile_bucket(step) for step in (-1, 0, 1)]
        for head in range(heads):
            for k in range(BUCKETS):
                total = jnp.zeros((TILE, TILE), F32)
                for step in (-1, 0, 1):
                    if k in tile_range(step):
                        total = total + jnp.where(ids[step + 1] == k, near[head * 3 + step + 1], 0.0)
                if k == 15:
                    total = total + far[head * 2]
                if k == 31:
                    total = total + far[head * 2 + 1]
                at = head * BUCKETS + k
                rows_s[at : at + 1, :] = jnp.sum(total, axis=0, keepdims=True)
        sums = jnp.sum(rows_s[...], axis=1, keepdims=True)
        experts = router_ref.shape[0]
        if part % 16:
            own_ref[...] = jnp.broadcast_to(sums, own_ref.shape)
            return
        count = sums.shape[0]
        diagonal = lax.broadcasted_iota(jnp.int32, (count, TILE), 0) == lax.broadcasted_iota(
            jnp.int32, (count, TILE), 1
        )
        sums = jnp.sum(jnp.where(diagonal, sums, 0.0), axis=0, keepdims=True)
        width = gain_out.shape[1]
        sums = jnp.concatenate([sums, jnp.zeros((1, width - TILE), F32)], axis=1)
        head_rows = jnp.concatenate(
            [gain_out[...], gain_two_ref[...], sums, jnp.zeros((13, width), F32)], axis=0
        ).astype(BF16)
        tail = jnp.concatenate(
            [router_ref[...].astype(BF16)]
            + ([jnp.zeros((-experts % 16, width), BF16)] if experts % 16 else []),
            axis=0,
        )
        z_count = own_ref.shape[0]
        for n, ref in enumerate((own_ref, other_ref)):
            for k in range(z_count):
                at = pl.multiple_of((place_ref[3] ^ (n * z_count + k)) * part, part)
                ref[k, :part, :] = weight_ref[pl.ds(at, part), :].astype(BF16)
                ref[k, part : part + 16, :] = head_rows
                ref[k, part + 16 :, :] = tail


def attend_back(places, bias, tokens, gain, weights, projected, mixed, logs, pieces, gain_two, router, part, z_count):
    rows, width = tokens.shape
    tensors = rows // pieces[0].shape[0]
    piece = whole(pieces[0].shape)
    heads = bias.shape[0]
    inner = heads * HEAD_DIM
    seqs = rows // LENGTH
    by_seq = lambda cols: pl.BlockSpec((LENGTH, cols), lambda s, *_: (s, 0))
    experts = router.shape[0]
    sent = (z_count, part + 16 + experts + -experts % 16, width)
    if part % 16:
        sent = (heads * BUCKETS, 1)
    result = pl.pallas_call(
        functools.partial(attend_back_kernel, heads, tensors, part),
        grid_spec=pltpu.PrefetchScalarGridSpec(
            num_scalar_prefetch=1,
            grid=(seqs,),
            in_specs=[
                pl.BlockSpec(memory_space=pltpu.SMEM),
                by_seq(width),
                whole((1, width)),
                whole((width, 4 * inner)),
                by_seq(3 * inner),
                by_seq(inner),
                by_seq(TILE),
            ]
            + [whole(p.shape) for p in pieces]
            + [whole((1, width)), whole((experts, width))],
            out_specs=[piece] * tensors
            + [whole(sent), whole(sent), whole((width, 4 * inner)), whole((1, width))],
            scratch_shapes=[
                pltpu.VMEM((heads, LENGTH, LENGTH), F32),
                pltpu.VMEM((width, inner), BF16),
                pltpu.VMEM((LENGTH, inner), BF16),
                pltpu.VMEM((LENGTH, 3 * inner), BF16),
                pltpu.VMEM((heads * 3, TILE, TILE), F32),
                pltpu.VMEM((heads * 2, TILE, TILE), F32),
                pltpu.VMEM((heads * BUCKETS, TILE), F32),
                pltpu.VMEM((rows, width), BF16),
                pltpu.VMEM((rows, width), BF16),
            ],
        ),
        out_shape=[jax.ShapeDtypeStruct(pieces[0].shape, BF16)] * tensors
        + [
            jax.ShapeDtypeStruct(sent, F32 if part % 16 else BF16),
            jax.ShapeDtypeStruct(sent, F32 if part % 16 else BF16),
            jax.ShapeDtypeStruct((width, 4 * inner), F32),
            jax.ShapeDtypeStruct((1, width), F32),
        ],
        compiler_params=params(),
        cost_estimate=cost(18 * rows * width * inner + 10 * rows * LENGTH * inner, rows * width * 12, rows * LENGTH * heads),
        name="attend_back",
    )(places, bias, tokens, gain, weights, projected, mixed, logs, *pieces, gain_two, router)
    return result[:tensors], result[tensors:]


def first_rows_kernel(count, *refs):
    out_ref = refs[-1]
    at = 0
    for ref in refs[:-1]:
        for n in range(ref.shape[0]):
            out_ref[at] = ref[n, :count, :]
            at += 1


def first_rows(pieces, start, extra, count):
    width = pieces[0].shape[-1]
    total = sum(piece.shape[0] for piece in pieces)
    return pl.pallas_call(
        functools.partial(first_rows_kernel, count),
        grid=(1,),
        in_specs=[
            pl.BlockSpec((piece.shape[0], extra, width), lambda i: (0, start // extra, 0)) for piece in pieces
        ],
        out_specs=whole((total, count, width)),
        out_shape=jax.ShapeDtypeStruct((total, count, width), BF16),
        compiler_params=params(),
        cost_estimate=cost(0, 4 * total * extra * width),
        name="first_rows",
    )(*pieces)


def place_rows(target_ref, rows, out_refs):
    at = 0
    for ref in out_refs:
        count = ref.shape[0]
        index = lax.broadcasted_iota(jnp.int32, (count, rows.shape[0]), 0) + at
        chosen = jnp.where(index == target_ref[...], 1.0, 0.0).astype(BF16)
        ref[...] = dot(chosen, rows).astype(BF16)
        at += count


def place_kernel(target_ref, rows_ref, *out_refs):
    place_rows(target_ref, rows_ref[...], out_refs)


def place(target_row, rows, counts):
    return pl.pallas_call(
        place_kernel,
        out_shape=[jax.ShapeDtypeStruct((count, rows.shape[1]), BF16) for count in counts],
        compiler_params=params(),
        cost_estimate=cost(2 * sum(counts) * rows.size, 4 * rows.size),
        name="place",
    )(target_row, rows)


def softmax_rows(logits):
    exponent = jnp.exp(logits - jnp.max(logits, axis=-1, keepdims=True))
    return exponent * (1.0 / jnp.sum(exponent, axis=-1, keepdims=True))


def sum_pieces(refs):
    total = refs[0][...].astype(F32)
    for ref in refs[1:]:
        total = total + ref[...].astype(F32)
    return total


def route_kernel(tok_ref, *refs):
    gain_ref, router_ref, target_ref, index_ref, kept_ref, hidden_ref, gate_ref = refs[6:13]
    half = tok_ref.shape[0] // 2
    for h in range(2):
        keep, got, last = refs[3 * h : 3 * h + 3]
        here = slice(h * half, (h + 1) * half)
        added = keep[:half, :].astype(F32) + got[:half, :].astype(F32) + last[...].astype(F32)
        hidden_ref[here, :] = tok_ref[here, :].astype(F32) + added
    hidden = hidden_ref[...]
    unit, _ = unit_rows(hidden)
    moe_in = (unit * gain_ref[...]).astype(BF16)
    place_rows(target_ref, moe_in, refs[13:])
    probs = softmax_rows(dot(moe_in, router_ref[...]))
    lanes = lax.broadcasted_iota(jnp.int32, probs.shape, 1)
    picked = jnp.sum(jnp.where(lanes == index_ref[...], probs, 0.0), axis=-1, keepdims=True)
    gate_ref[...] = picked * kept_ref[...].astype(F32)


def route(tokens, attn, gain, router, target_row, index_col, kept_col, counts):
    rows, width = tokens.shape
    result = pl.pallas_call(
        route_kernel,
        out_shape=[
            jax.ShapeDtypeStruct((rows, width), F32),
            jax.ShapeDtypeStruct((rows, 1), F32),
        ]
        + [jax.ShapeDtypeStruct((count, width), BF16) for count in counts],
        compiler_params=params(),
        cost_estimate=cost(2 * sum(counts) * rows * width, 12 * rows * width),
        name="route",
    )(tokens, *attn, gain, router, target_row, index_col, kept_col)
    return result[0], result[1], result[2:]


def rest_choice(blocks, locals_, rest, expert):
    rows = lax.broadcasted_iota(jnp.int32, (blocks * rest, blocks * locals_ * rest), 0)
    cols = lax.broadcasted_iota(jnp.int32, (blocks * rest, blocks * locals_ * rest), 1)
    block = lax.div(rows, rest)
    wanted = block * (locals_ * rest) + expert * rest + (rows - block * rest)
    return jnp.where(cols == wanted, 1.0, 0.0).astype(BF16)


def pick_rows(out_ref, views, choice, main_rows, main, expert):
    at = 0
    pieces = []
    for view in views:
        blocks, size, width = view.shape
        if main:
            start = pl.multiple_of(expert * main, main)
            out_ref[at : at + blocks * main, :] = view[:, pl.ds(start, main), :].reshape(blocks * main, width)
            at += blocks * main
        rest = size - size * main_rows // out_ref.shape[0]
        pieces.append(view[:, size - rest :, :].reshape(blocks * rest, width))
    out_ref[main_rows:, :] = dot(choice, jnp.concatenate(pieces, axis=0)).astype(BF16)


def put_rows(views, value_ref, choice, main_rows, main, locals_, rest, expert):
    at = 0
    spread = dot(choice, value_ref[main_rows:, :], ROWS_TN).astype(BF16)
    rest_at = 0
    for view in views:
        blocks, _, width = view.shape
        if main:
            count = blocks * main
            start = pl.multiple_of(expert * main, main)
            view[:, pl.ds(start, main), :] = value_ref[at : at + count, :].reshape(blocks, main, width)
            at += count
        part = spread[rest_at : rest_at + blocks * locals_ * rest].reshape(blocks, locals_ * rest, width)
        rest_at += blocks * locals_ * rest

        @pl.when(expert == 0)
        def _():
            view[:, locals_ * main :, :] = part

        @pl.when(expert > 0)
        def _():
            view[:, locals_ * main :, :] = view[:, locals_ * main :, :] + part


def group_views(place_ref, ref, tensors, chunks):
    size = ref.shape[1] // chunks
    views = []
    for k in range(chunks):
        a, b = HOPS[k % 2]
        views += [ref.at[place_ref[2] ^ j, k * size : (k + 1) * size] for j in (0, a, b, a | b)]
    return views


def join_halves(place_ref, own_in, peer_in, own_out, peer_out, win, wout):
    half = own_in.shape[1]
    mine = pl.multiple_of(place_ref[0] * half, half)
    other = pl.multiple_of((1 - place_ref[0]) * half, half)
    if win is not None:
        win[pl.ds(mine, half), :] = own_in[0]
        win[pl.ds(other, half), :] = peer_in[0]
    half_out = own_out.shape[2]
    mine = pl.multiple_of(place_ref[0] * half_out, half_out)
    other = pl.multiple_of((1 - place_ref[0]) * half_out, half_out)
    wout[:, pl.ds(mine, half_out)] = own_out[0]
    wout[:, pl.ds(other, half_out)] = peer_out[0]


def expert_kernel(chunks, tensors, main, locals_, rest, place_ref, *refs):
    refs = list(refs)
    take = lambda n: [refs.pop(0) for _ in range(n)]
    xs = take(3 * chunks)
    (g_ref,) = take(1)
    own_in, peer_in, own_out, peer_out, router = take(5)
    backs = take(2 * chunks)
    x_ref, ge_ref, hid_ref, gi_ref, gl_ref = take(5)
    win, wout, grows, inner, gunits, gate_s, dots, back = take(8)
    expert = pl.program_id(0)
    blocks = sum(ref.shape[0] for ref in xs)
    main_rows = blocks * main
    rows, width = x_ref.shape[1:]
    wide = win.shape[1]
    choice = rest_choice(blocks, locals_, rest, expert)
    many = xs[0].shape[0]
    back_refs = []
    for k in range(chunks):
        keep, send = backs[2 * k : 2 * k + 2]
        back_refs += [ref.at[n * many : (n + 1) * many] for n in range(2) for ref in (keep, send)]
    pick_rows(x_ref.at[0], xs, choice, main_rows, main, expert)
    pick_rows(grows, group_views(place_ref, g_ref, tensors, chunks), choice, main_rows, main, expert)
    join_halves(place_ref, own_in, peer_in, own_out, peer_out, win, wout)
    inner[...] = dot(x_ref[0], win[...])
    gunits[...] = dot(grows[...], wout[...], ROWS_NT)
    probs = softmax_rows(dot(x_ref[0], router[...]))
    lanes = lax.broadcasted_iota(jnp.int32, probs.shape, 1)
    mine = lanes == place_ref[1] * locals_ + expert
    picked = jnp.sum(jnp.where(mine, probs, 0.0), axis=-1, keepdims=True)
    gate_s[...] = jnp.broadcast_to(picked, gate_s.shape)
    chunk = 16
    half_wide = wide // 2 if wide % (2 * TILE) == 0 else wide

    def body(step, _):
        at = pl.ds(pl.multiple_of(step * chunk, chunk), chunk)
        gate_tile = gate_s[at, :]
        gate = jnp.concatenate([gate_tile] * (half_wide // TILE), axis=1)
        total = None
        for start in range(0, wide, half_wide):
            lanes_at = slice(start, start + half_wide)
            value = inner[at, lanes_at]
            square = value * value
            wave = jnp.tanh(value * (GELU_A + (GELU_A * GELU_B) * square))
            half = 0.5 + 0.5 * wave
            hidden = (value * half).astype(BF16)
            bend = value * (0.5 * GELU_A + (1.5 * GELU_A * GELU_B) * square)
            slope = half + bend * (1.0 - wave * wave)
            units = gunits[at, lanes_at]
            hid_ref[0, at, lanes_at] = hidden
            gi_ref[0, at, lanes_at] = (gate * (units * slope)).astype(BF16)
            product = hidden.astype(F32) * units
            for tile in range(0, half_wide, TILE):
                part = product[:, tile : tile + TILE]
                total = part if total is None else total + part
        dots[at, :] = total
        gate = jnp.concatenate([gate_tile] * (width // TILE), axis=1)
        ge_ref[0, at, :] = (gate * grows[at, :].astype(F32)).astype(BF16)
        return 0

    lax.fori_loop(0, rows // chunk, body, 0, unroll=4)
    grad_logits = (jnp.sum(dots[...], axis=-1, keepdims=True) * probs * (jnp.where(mine, 1.0, 0.0) - picked)).astype(BF16)
    gl_ref[0] = grad_logits
    back[...] = (dot(gi_ref[0], win[...], ROWS_NT) + dot(grad_logits, router[...], ROWS_NT)).astype(BF16)
    put_rows(back_refs, back, choice, main_rows, main, locals_, rest, expert)


def expert_forward_back(places, xs, gs, own_in, peer_in, own_out, peer_out, router, main, rest, chunks):
    locals_, half, wide = own_in.shape
    width, experts = router.shape
    many, block = xs[0].shape[:2]
    tensors = gs.shape[0]
    blocks = tensors * chunks * many
    back = (2 * many, block, width)
    rows = blocks * (main + rest)
    per = lambda *shape: pl.BlockSpec((1,) + shape, lambda e, *_: (e, 0, 0))
    saved = jax.ShapeDtypeStruct((locals_, rows, width), BF16)
    saved_wide = jax.ShapeDtypeStruct((locals_, rows, wide), BF16)
    result = pl.pallas_call(
        functools.partial(expert_kernel, chunks, tensors, main, locals_, rest),
        grid_spec=pltpu.PrefetchScalarGridSpec(
            num_scalar_prefetch=1,
            grid=(locals_,),
            in_specs=[whole(x.shape) for x in xs]
            + [whole(gs.shape)]
            + [per(half, wide)] * 2 + [per(wide, half)] * 2 + [whole((width, experts))],
            out_specs=[whole(back)] * (2 * chunks)
            + [per(rows, width), per(rows, width), per(rows, wide), per(rows, wide), per(rows, experts)],
            scratch_shapes=[
                pltpu.VMEM((width, wide), BF16),
                pltpu.VMEM((wide, width), BF16),
                pltpu.VMEM((rows, width), BF16),
                pltpu.VMEM((rows, wide), F32),
                pltpu.VMEM((rows, wide), F32),
                pltpu.VMEM((rows, TILE), F32),
                pltpu.VMEM((rows, TILE), F32),
                pltpu.VMEM((rows, width), BF16),
            ],
        ),
        out_shape=[jax.ShapeDtypeStruct(back, BF16)] * (2 * chunks)
        + [saved, saved, saved_wide, saved_wide, jax.ShapeDtypeStruct((locals_, rows, experts), BF16)],
        compiler_params=params(),
        cost_estimate=cost(6 * locals_ * rows * width * wide, locals_ * rows * width * 14, locals_ * rows * wide),
        name="experts",
    )(places, *xs, gs, own_in, peer_in, own_out, peer_out, router)
    return result[: 2 * chunks], result[2 * chunks :]


def expert_rows_kernel(chunks, main, locals_, rest, place_ref, hid_ref, own_out, peer_out, forward_ref, wout, value):
    expert = pl.program_id(0)
    tensors = forward_ref.shape[0]
    blocks = tensors * forward_ref.shape[1]
    choice = rest_choice(blocks, locals_, rest, expert)
    join_halves(place_ref, own_out, peer_out, own_out, peer_out, None, wout)
    value[...] = dot(hid_ref[0], wout[...]).astype(BF16)
    views = group_views(place_ref, forward_ref, tensors, chunks)
    put_rows(views, value, choice, blocks * main, main, locals_, rest, expert)


def expert_rows(places, hidden, own_out, peer_out, shape, main, rest, chunks):
    locals_, rows, wide = hidden.shape
    half = own_out.shape[2]
    width = shape[-1]
    per = lambda *shape: pl.BlockSpec((1,) + shape, lambda e, *_: (e, 0, 0))
    return pl.pallas_call(
        functools.partial(expert_rows_kernel, chunks, main, locals_, rest),
        grid_spec=pltpu.PrefetchScalarGridSpec(
            num_scalar_prefetch=1,
            grid=(locals_,),
            in_specs=[per(rows, wide)] + [per(wide, half)] * 2,
            out_specs=whole(shape),
            scratch_shapes=[pltpu.VMEM((wide, width), BF16), pltpu.VMEM((rows, width), BF16)],
        ),
        out_shape=jax.ShapeDtypeStruct(shape, BF16),
        compiler_params=params(),
        cost_estimate=cost(2 * locals_ * rows * width * wide, locals_ * rows * width * 6),
        name="expert_rows",
    )(places, hidden, own_out, peer_out)


def expert_weights_kernel(place_ref, x_ref, ge_ref, hid_ref, gi_ref, gl_ref, *refs):
    in_own, in_send, out_own, out_send, router_ref = refs
    half = in_own.shape[1]
    mine = pl.ds(pl.multiple_of(place_ref[0] * half, half), half)
    other = pl.ds(pl.multiple_of((1 - place_ref[0]) * half, half), half)
    in_own[0] = dot(x_ref[0, :, mine], gi_ref[0], ROWS_TN)
    in_send[0] = dot(x_ref[0, :, other], gi_ref[0], ROWS_TN).astype(BF16)
    out_own[0] = dot(hid_ref[0], ge_ref[0, :, mine], ROWS_TN)
    out_send[0] = dot(hid_ref[0], ge_ref[0, :, other], ROWS_TN).astype(BF16)

    @pl.when(pl.program_id(0) == 0)
    def _():
        router_ref[...] = jnp.zeros_like(router_ref)

    router_ref[...] += dot(gl_ref[0], x_ref[0], ROWS_TN)


def expert_weights(places, saved, half):
    x, ge, hidden, gi, gl = saved
    locals_, rows, width = x.shape
    wide = hidden.shape[2]
    experts = gl.shape[2]
    per = lambda *shape: pl.BlockSpec((1,) + shape, lambda e, *_: (e, 0, 0))
    return pl.pallas_call(
        expert_weights_kernel,
        grid_spec=pltpu.PrefetchScalarGridSpec(
            num_scalar_prefetch=1,
            grid=(locals_,),
            in_specs=[per(rows, width), per(rows, width), per(rows, wide), per(rows, wide), per(rows, experts)],
            out_specs=[per(half, wide), per(half, wide), per(wide, half), per(wide, half), whole((experts, width))],
        ),
        out_shape=[
            jax.ShapeDtypeStruct((locals_, half, wide), F32),
            jax.ShapeDtypeStruct((locals_, half, wide), BF16),
            jax.ShapeDtypeStruct((locals_, wide, half), F32),
            jax.ShapeDtypeStruct((locals_, wide, half), BF16),
            jax.ShapeDtypeStruct((experts, width), F32),
        ],
        compiler_params=params(),
        cost_estimate=cost(4 * locals_ * rows * width * wide, locals_ * rows * width * 14),
        name="expert_weights",
    )(places, x, ge, hidden, gi, gl)


def take_rows(target_ref, refs):
    total, at = None, 0
    for ref in refs:
        count = ref.shape[0]
        cols = lax.broadcasted_iota(jnp.int32, (target_ref.shape[0], count), 1) + at
        chosen = jnp.where(cols == target_ref[...], 1.0, 0.0).astype(BF16)
        part = dot(chosen, ref[...])
        total = part if total is None else total + part
        at += count
    return total


def hidden_back_kernel(target_ref, *refs):
    hidden_ref, cot_ref, gain_ref, grad_ref, attn_ref, gain_out = refs[-6:]
    grad_in = take_rows(target_ref, refs[:-6])
    unit, scale = unit_rows(hidden_ref[...])
    gain_out[...] = jnp.sum(grad_in * unit, axis=0, keepdims=True)
    scaled = grad_in * gain_ref[...]
    inside = jnp.mean(unit * scaled, axis=-1, keepdims=True)
    grad = cot_ref[...].astype(F32) + scale * (scaled - unit * inside)
    grad_ref[...] = grad
    attn_ref[...] = grad.astype(BF16)


def hidden_back(target_col, back, hidden, cotangent, gain):
    rows, width = hidden.shape
    return pl.pallas_call(
        hidden_back_kernel,
        out_shape=[
            jax.ShapeDtypeStruct((rows, width), F32),
            jax.ShapeDtypeStruct((rows, width), BF16),
            jax.ShapeDtypeStruct((1, width), F32),
        ],
        compiler_params=params(),
        cost_estimate=cost(3 * rows * rows * width, 16 * rows * width),
        name="hidden_back",
    )(target_col, *back, hidden, cotangent, gain)


def output_kernel(target_ref, *refs):
    hidden_ref, gate_ref, out_ref = refs[-3:]
    out_ref[...] = (hidden_ref[...] + gate_ref[...] * take_rows(target_ref, refs[:-3])).astype(BF16)


def output_rows(target_col, expert_rows, hidden, gate):
    return pl.pallas_call(
        output_kernel,
        out_shape=jax.ShapeDtypeStruct(hidden.shape, BF16),
        compiler_params=params(),
        cost_estimate=cost(3 * hidden.shape[0] * hidden.size, 10 * hidden.size),
        name="output_rows",
    )(target_col, *expert_rows, hidden, gate)


def tokens_back_kernel(tok_ref, *refs):
    gain_ref, hidden_ref, out_ref = refs[-3:]
    unit, scale = unit_rows(tok_ref[...].astype(F32))
    scaled = sum_pieces(refs[:-3]) * gain_ref[...]
    inside = jnp.mean(unit * scaled, axis=-1, keepdims=True)
    out_ref[...] = hidden_ref[...] + scale * (scaled - unit * inside)


def tokens_back(tokens, grad_normed, gain, grad_hidden):
    return pl.pallas_call(
        tokens_back_kernel,
        out_shape=jax.ShapeDtypeStruct(tokens.shape, F32),
        compiler_params=params(),
        cost_estimate=cost(10 * tokens.size, 12 * tokens.size),
        name="tokens_back",
    )(tokens, *grad_normed, gain, grad_hidden)


def shifted(value, axis, count, step):
    return lax.ppermute(value, axis, [(s, (s + step) % count) for s in range(count)])


def gather_ring(value, axis, count):
    me = lax.axis_index(axis)
    parts = [value] + [shifted(value, axis, count, -k) for k in range(1, count)]
    return jnp.roll(jnp.stack(parts), me, axis=0)


def swapped(value, axis, count, bits):
    return lax.ppermute(value, axis, [(s, s ^ bits) for s in range(count)])


def gather_pieces(value, axis, count):
    return [value] + [swapped(value, axis, count, k) for k in range(1, count)]


def gather_hops(value, hops):
    a, b = hops
    first = swapped(value, "tensor", 4, a)
    second = swapped(jnp.concatenate([value, first], axis=0), "tensor", 4, b)
    return first, second


def added(a, b):
    return (a.astype(F32) + b.astype(F32)).astype(BF16)


def swap_pieces(pieces, axis, count):
    return [pieces[0]] + [swapped(pieces[k], axis, count, k) for k in range(1, count)]


def on_device(
    sizes,
    tokens,
    cotangent,
    query_key_value_weight,
    attention_output_weight,
    rel_bias,
    gain_attn,
    gain_moe,
    w_router,
    w_in,
    w_out,
    expert_index,
    slot_index,
    kept_mask,
):
    dp_count, z_count, t_count = sizes
    tok_rows, width = tokens.shape
    experts_all = w_router.shape[1]
    capacity = max(2, 3 * tok_rows // (2 * experts_all))
    locals_ = w_in.shape[0]
    main = capacity // 16 * 16
    rest = capacity - main
    block = locals_ * capacity
    heads = rel_bias.shape[0]
    inner = heads * HEAD_DIM
    part = query_key_value_weight.shape[1]
    fine = w_router.shape[0]
    my_dp = lax.axis_index("dp")
    my_z = lax.axis_index("expert")
    bias = rel_bias.astype(F32)

    my_t = lax.axis_index("tensor")
    owners = dp_count * z_count
    my_owner = my_dp * z_count + my_z
    places = jnp.stack([my_dp, my_z, my_t, my_owner]).astype(jnp.int32)
    half_rows = tok_rows // 2
    token_pieces = [tokens]
    for h, hops in enumerate(HOPS):
        token_pieces += list(gather_hops(tokens[h * half_rows : (h + 1) * half_rows], hops))

    small = jnp.concatenate([gain_attn[:, None], gain_moe[:, None], w_router], axis=1).reshape(-1)
    extra = -(-small.shape[0] // (16 * width)) * 16
    packed = jnp.concatenate(
        [
            query_key_value_weight.transpose(1, 0, 2).reshape(part, 3 * inner),
            attention_output_weight.T,
        ],
        axis=1,
    )
    packed = jnp.concatenate(
        [packed, jnp.pad(small, (0, extra * width - small.shape[0])).reshape(extra, width)], axis=0
    )
    owned = gather_pieces(packed[None], "expert", z_count)
    owned = owned + [swapped(jnp.concatenate(owned, axis=0), "dp", dp_count, 1)]
    if part % 16 or part % extra:
        smalls = jnp.concatenate(owned, axis=0)[:, part:]
    else:
        smalls = first_rows(owned, part, extra, -(-small.shape[0] // width))
    smalls = smalls.reshape(owners, -1)[:, : small.shape[0]]
    small_pieces = gather_pieces(smalls, "tensor", t_count)

    z_of = expert_index // locals_
    local = expert_index - z_of * locals_
    inside = jnp.where(
        slot_index < main, local * main + slot_index, locals_ * main + local * rest + slot_index - main
    )
    target = (z_of ^ my_z) * block + inside
    target = jnp.where(kept_mask > 0, target, -1)
    target_row, target_col = target[None, :], target[:, None]
    chunks = min(z_count, 4)
    many = z_count // chunks
    counts = [many * block] * chunks
    grad_sent = place(target_row, cotangent, counts)
    token_pieces, owned, small_pieces, grad_sent = lax.optimization_barrier(
        (token_pieces, owned, small_pieces, grad_sent)
    )
    smalls = jnp.stack(small_pieces).reshape(t_count * owners, -1)
    owner_ids = jnp.arange(owners, dtype=jnp.int32)[:, None] ^ my_owner
    t_ids = jnp.arange(t_count, dtype=jnp.int32)[None, :] ^ my_t
    smalls = smalls[(t_ids * owners + owner_ids).reshape(-1)].reshape(width, 2 + experts_all)
    if part % 16:
        order = jnp.arange(owners, dtype=jnp.int32) ^ my_owner
        owned = [jnp.concatenate(owned, axis=0)[:, :part][order].reshape(1, width, 4 * inner)]
    rows_owned = part if len(owned) > 1 else width
    gain_one = smalls[:, 0].astype(F32)[None]
    gain_two = smalls[:, 1].astype(F32)[None]
    router = smalls[:, 2:]

    def over_expert(groups):
        if many > 1:
            groups = [g[i * block : (i + 1) * block] for g in groups for i in range(many)]
        pieces = swap_pieces(groups, "expert", z_count)
        if many == 1:
            return pieces
        return [jnp.concatenate(pieces[k * many : (k + 1) * many], axis=0) for k in range(chunks)]

    grad_rows = jnp.concatenate(over_expert(grad_sent), axis=0)
    parts, (group_tokens, projected, mixed, logs, weights) = attend(
        places, bias, token_pieces, owned, rows_owned, gain_one
    )
    parts, late_in, late_out, grad_rows = lax.optimization_barrier((parts, w_in, w_out, grad_rows))
    peer_in = shifted(late_in, "dp", dp_count, 1)
    peer_out = shifted(late_out, "dp", dp_count, 1)
    grad_arrived = lax.all_gather(grad_rows, "tensor", axis=0).reshape(t_count, z_count, block, width)
    attn = []
    for h, (a, b) in enumerate(HOPS):
        keep, send = parts[2 * h : 2 * h + 2]
        got = swapped(send, "tensor", t_count, a)
        last = swapped(added(keep[half_rows:], got[half_rows:]), "tensor", t_count, b)
        attn += [keep, got, last]
    attn, peer_in, peer_out = lax.optimization_barrier((attn, peer_in, peer_out))
    hidden_one, gate, sent = route(
        tokens, attn, gain_two, router, target_row, expert_index[:, None], kept_mask[:, None], counts
    )
    arrived = []
    for k, group in enumerate(over_expert(sent)):
        pieces = (group,) + gather_hops(group, HOPS[k % 2])
        arrived += [piece.reshape(-1, block, width) for piece in pieces]
    back_parts, saved = expert_forward_back(
        places, arrived, grad_arrived, w_in, peer_in, w_out, peer_out, router, main, rest, chunks
    )

    size = many * block
    back_parts = [piece.reshape(2 * size, width) for piece in back_parts]
    keeps, sends = back_parts[::2], back_parts[1::2]
    got = [swapped(sends[k], "tensor", t_count, HOPS[k % 2][0]) for k in reversed(range(chunks))][::-1]
    forward_part = expert_rows(places, saved[2], w_out, peer_out, grad_arrived.shape, main, rest, chunks)
    got, forward_part = lax.optimization_barrier((got, forward_part))
    groups = []
    for k in range(chunks):
        last = swapped(added(keeps[k][size:], got[k][size:]), "tensor", t_count, HOPS[k % 2][1])
        total = keeps[k][:size].astype(F32) + got[k][:size].astype(F32) + last.astype(F32)
        groups.append(total.astype(BF16))
    forward_part, groups, saved = lax.optimization_barrier((forward_part, groups, saved))
    forward_sum = lax.psum_scatter(
        forward_part.reshape(t_count * z_count * block, width), "tensor", scatter_dimension=0, tiled=True
    )
    in_own, in_send, out_own, out_send, router_part = expert_weights(places, saved, w_in.shape[1])
    grad_back, in_send, out_send = lax.optimization_barrier((over_expert(groups), in_send, out_send))
    in_got = shifted(in_send, "dp", dp_count, 1)
    out_got = shifted(out_send, "dp", dp_count, 1)
    grad_hidden, grad_attn, gain_two_part = hidden_back(target_col, grad_back, hidden_one, cotangent, gain_two)
    grad_pieces = [grad_attn]
    for h, hops in enumerate(HOPS):
        grad_pieces += list(gather_hops(grad_attn[h * half_rows : (h + 1) * half_rows], hops))
    grad_w_in = in_own + in_got.astype(F32)
    grad_w_out = out_own + out_got.astype(F32)
    grad_pieces, grad_w_in, grad_w_out, forward_sum = lax.optimization_barrier(
        (grad_pieces, grad_w_in, grad_w_out, forward_sum)
    )
    normed_parts, (own_part, other_part, weight_part, gain_one_part) = attend_back(
        places, bias, group_tokens, gain_one, weights, projected, mixed, logs, grad_pieces,
        gain_two_part, router_part, part, z_count,
    )
    forward_rows = over_expert(list(forward_sum.reshape(chunks, many * block, width)))
    normed_parts, own_part, other_part, forward_rows = lax.optimization_barrier(
        (normed_parts, own_part, other_part, forward_rows)
    )
    grad_normed = swap_pieces(normed_parts, "tensor", t_count)
    output = output_rows(target_col, forward_rows, hidden_one, gate)
    grad_tokens = tokens_back(tokens, grad_normed, gain_one, grad_hidden)

    if part % 16:
        head_rows = jnp.concatenate(
            [
                gain_one_part,
                gain_two_part,
                jnp.pad(own_part.reshape(1, -1), ((0, 0), (0, width - own_part.shape[0]))),
                jnp.zeros((13, width), F32),
                router_part,
                jnp.zeros((-experts_all % 16, width), F32),
            ]
        )
        order = jnp.arange(owners, dtype=jnp.int32) ^ my_owner
        payload = jnp.concatenate(
            [
                weight_part.reshape(owners, part, width)[order],
                jnp.broadcast_to(head_rows[None], (owners,) + head_rows.shape),
            ],
            axis=1,
        ).astype(BF16)
        own_part, other_part = payload[:z_count], payload[z_count:]
    other_got = shifted(other_part, "dp", dp_count, 1)
    pieces = swap_pieces([added(own_part[k], other_got[k]) for k in range(z_count)], "expert", z_count)
    total = pieces[0].astype(F32)
    for piece in pieces[1:]:
        total = total + piece.astype(F32)
    weight_total = total[:part].reshape(part, 4, inner)
    grad_w_qkv = weight_total[:, :3].transpose(1, 0, 2)
    grad_w_attn_out = weight_total[:, 3].T
    grad_rel_bias = total[part + 2, : heads * BUCKETS].reshape(heads, BUCKETS)
    mine = lax.dynamic_slice_in_dim(total[part:], my_owner * part, part, axis=1)
    mine = jnp.concatenate([mine[:2], mine[16 : 16 + experts_all]], axis=0)
    turned = [
        lax.dynamic_slice_in_dim(mine, (my_t ^ k) * fine, fine, axis=1).reshape(-1) for k in range(t_count)
    ]
    left = turned[0]
    for piece in swap_pieces(turned, "tensor", t_count)[1:]:
        left = left + piece
    grad_gain_attn = left[:fine]
    grad_gain_moe = left[fine : 2 * fine]
    grad_w_router = left[2 * fine :].reshape(experts_all, fine).T
    return (
        output,
        grad_tokens,
        grad_w_qkv,
        grad_w_attn_out,
        grad_rel_bias,
        grad_gain_attn,
        grad_gain_moe,
        grad_w_router,
        grad_w_in,
        grad_w_out,
    )


def solution(mesh):
    placed = (
        P(("dp", "expert", "tensor"), None),
        P(("dp", "expert", "tensor"), None),
        P(None, ("dp", "expert"), "tensor"),
        P("tensor", ("dp", "expert")),
        P("tensor", None),
        P(("dp", "expert", "tensor")),
        P(("dp", "expert", "tensor")),
        P(("dp", "expert", "tensor"), None),
        P("expert", "dp", "tensor"),
        P("expert", "tensor", "dp"),
        P(("dp", "expert", "tensor")),
        P(("dp", "expert", "tensor")),
        P(("dp", "expert", "tensor")),
    )
    sizes = tuple(mesh.shape[name] for name in ("dp", "expert", "tensor"))
    return jax.shard_map(
        functools.partial(on_device, sizes),
        mesh=mesh,
        in_specs=placed,
        out_specs=(
            P(("dp", "expert", "tensor"), None),
            P(("dp", "expert", "tensor"), None),
            P(None, ("dp", "expert"), "tensor"),
            P("tensor", ("dp", "expert")),
            P("tensor", None),
            P(("dp", "expert", "tensor")),
            P(("dp", "expert", "tensor")),
            P(("dp", "expert", "tensor"), None),
            P("expert", "dp", "tensor"),
            P("expert", "tensor", "dp"),
        ),
        check_vma=False,
    )
```

```python
import functools

import jax
import jax.numpy as jnp
from jax import lax
from jax.experimental import pallas as pl
from jax.experimental.pallas import tpu as pltpu
from jax.sharding import PartitionSpec as P

HEAD_DIM = 64
BUCKETS = 32
LENGTH = 512
TILE = 128
EPSILON = 1e-06
BORDERS = (12, 16, 23, 32, 46, 64, 91)
F32 = jnp.float32
BF16 = jnp.bfloat16
GELU_A = 0.7978845608028654
GELU_B = 0.044715
ROWS_NN = (((1,), (0,)), ((), ()))
ROWS_NT = (((1,), (1,)), ((), ()))
ROWS_TN = (((0,), (0,)), ((), ()))
VMEM_BYTES = 56 * 1024 * 1024


def dot(a, b, dims=ROWS_NN):
    return lax.dot_general(a, b, dims, preferred_element_type=F32)


def params(**more):
    return pltpu.CompilerParams(vmem_limit_bytes=VMEM_BYTES, **more)


def cost(flops, moved, special=0):
    return pl.CostEstimate(flops=int(flops), bytes_accessed=int(moved), transcendentals=int(special))


def whole(shape):
    return pl.BlockSpec(shape, lambda *_: (0,) * len(shape))


def tile_bucket(step):
    rows = lax.broadcasted_iota(jnp.int32, (TILE, TILE), 0)
    cols = lax.broadcasted_iota(jnp.int32, (TILE, TILE), 1)
    offset = cols - rows + step * TILE
    distance = jnp.abs(offset)
    bucket = jnp.minimum(distance, 8)
    for border in BORDERS:
        bucket = bucket + jnp.where(distance >= border, 1, 0)
    return bucket + jnp.where(offset > 0, 16, 0)


def tile_range(step):
    return {-1: range(1, 16), 0: range(0, 32), 1: range(17, 32)}[step]


def fill_bias(bias_ref, table, heads):
    blocks = LENGTH // TILE
    buckets = {step: tile_bucket(step) for step in (-1, 0, 1)}
    for head in range(heads):
        near = {}
        for step in (-1, 0, 1):
            value = jnp.zeros((TILE, TILE), F32)
            for k in tile_range(step):
                value = jnp.where(buckets[step] == k, bias_ref[head, k], value)
            near[step] = value
        low = jnp.full((TILE, TILE), bias_ref[head, 15], F32)
        high = jnp.full((TILE, TILE), bias_ref[head, 31], F32)
        for i in range(blocks):
            for j in range(blocks):
                step = j - i
                value = near[step] if abs(step) <= 1 else (low if step < 0 else high)
                table[head, i * TILE : (i + 1) * TILE, j * TILE : (j + 1) * TILE] = value


def unit_rows(values):
    scale = lax.rsqrt(jnp.mean(values * values, axis=-1, keepdims=True) + EPSILON)
    return values * scale, scale


HOPS = ((1, 2), (2, 1))


def group_halves(place_ref, out, pieces):
    rows = pieces[0].shape[0]
    half = rows // 2
    at = pl.multiple_of(place_ref[2] * rows, rows)
    out[pl.ds(at, rows), :] = pieces[0][...]
    for h, (a, b) in enumerate(HOPS):
        first, second = pieces[1 + 2 * h : 3 + 2 * h]
        for j, value in ((a, first[...]), (b, second[:half, :]), (a | b, second[half:, :])):
            at = pl.multiple_of((place_ref[2] ^ j) * rows + h * half, half)
            out[pl.ds(at, half), :] = value


def part_halves(place_ref, pieces, source):
    half = pieces[0].shape[0] // 2
    for h, (a, b) in enumerate(HOPS):
        for piece, order in zip(pieces[2 * h : 2 * h + 2], ((0, b), (a, a | b))):
            for n, j in enumerate(order):
                at = pl.multiple_of((place_ref[2] ^ j) * 2 * half + h * half, half)
                piece[n * half : (n + 1) * half, :] = source[pl.ds(at, half), :]


def part_rows(place_ref, pieces, source):
    rows = pieces[0].shape[0]
    for j, piece in enumerate(pieces):
        at = pl.multiple_of((place_ref[2] ^ j) * rows, rows)
        piece[...] = source[pl.ds(at, rows), :]


def attend_kernel(heads, tensors, owners, part, place_ref, bias_ref, *refs):
    refs = list(refs)
    take = lambda n: [refs.pop(0) for _ in range(n)]
    pieces, owned, (gain_ref,), parts = take(5), take(owners), take(1), take(tensors)
    tok_ref, qkv_ref, mixed_ref, log_ref, w_ref, table, wo, group, result = refs
    inner = heads * HEAD_DIM
    step_id = pl.program_id(0)

    @pl.when(step_id == 0)
    def _():
        fill_bias(bias_ref, table, heads)
        group_halves(place_ref, group, pieces)
        blocks = [piece.at[n] for piece in owned for n in range(piece.shape[0])]
        for k, piece in enumerate(blocks):
            at = pl.multiple_of((place_ref[3] ^ k) * part, part) if owners > 1 else 0
            w_ref[pl.ds(at, part), :] = piece[:part, :]
        wo[...] = w_ref[:, 3 * inner :]

    here = pl.ds(pl.multiple_of(step_id * LENGTH, LENGTH), LENGTH)
    tok_ref[...] = group[here, :]
    unit, _ = unit_rows(tok_ref[...].astype(F32))
    normed = (unit * gain_ref[...]).astype(BF16)
    qkv_ref[...] = dot(normed, w_ref[:, : 3 * inner]).astype(BF16)
    lanes = lax.broadcasted_iota(jnp.int32, (LENGTH, TILE), 1)
    logs = jnp.zeros((LENGTH, TILE), F32)
    for head in range(heads):
        at = head * HEAD_DIM
        query = qkv_ref[:, at : at + HEAD_DIM] * HEAD_DIM ** (-0.5)
        key = qkv_ref[:, inner + at : inner + at + HEAD_DIM]
        value = qkv_ref[:, 2 * inner + at : 2 * inner + at + HEAD_DIM]
        scores = dot(query.astype(BF16), key, ROWS_NT) + table[head]
        top = jnp.max(scores, axis=-1, keepdims=True)
        exponent = jnp.exp(scores - top)
        total = jnp.sum(exponent, axis=-1, keepdims=True)
        attention = (exponent * (1.0 / total)).astype(BF16)
        mixed_ref[:, at : at + HEAD_DIM] = dot(attention, value).astype(BF16)
        logs = jnp.where(lanes == head, top + jnp.log(total), logs)
    log_ref[...] = logs
    result[here, :] = dot(mixed_ref[...], wo[...], ROWS_NT).astype(BF16)

    @pl.when(step_id == pl.num_programs(0) - 1)
    def _():
        part_halves(place_ref, parts, result)


def attend(places, bias, pieces, owned, part, gain):
    tensors = 4
    piece_rows, width = pieces[0].shape
    rows = tensors * piece_rows
    heads = bias.shape[0]
    inner = heads * HEAD_DIM
    seqs = rows // LENGTH
    by_seq = lambda cols: pl.BlockSpec((LENGTH, cols), lambda s, *_: (s, 0))
    result = pl.pallas_call(
        functools.partial(attend_kernel, heads, tensors, len(owned), part),
        grid_spec=pltpu.PrefetchScalarGridSpec(
            num_scalar_prefetch=1,
            grid=(seqs,),
            in_specs=[pl.BlockSpec(memory_space=pltpu.SMEM)]
            + [whole(p.shape) for p in pieces]
            + [whole(o.shape) for o in owned]
            + [whole((1, width))],
            out_specs=[whole((piece_rows, width))] * tensors
            + [by_seq(width), by_seq(3 * inner), by_seq(inner), by_seq(TILE), whole((width, 4 * inner))],
            scratch_shapes=[
                pltpu.VMEM((heads, LENGTH, LENGTH), F32),
                pltpu.VMEM((width, inner), BF16),
                pltpu.VMEM((rows, width), BF16),
                pltpu.VMEM((rows, width), BF16),
            ],
        ),
        out_shape=[jax.ShapeDtypeStruct((piece_rows, width), BF16)] * tensors
        + [
            jax.ShapeDtypeStruct((rows, width), BF16),
            jax.ShapeDtypeStruct((rows, 3 * inner), BF16),
            jax.ShapeDtypeStruct((rows, inner), BF16),
            jax.ShapeDtypeStruct((rows, TILE), F32),
            jax.ShapeDtypeStruct((width, 4 * inner), BF16),
        ],
        compiler_params=params(),
        cost_estimate=cost(8 * rows * width * inner + 4 * rows * LENGTH * inner, rows * width * 8, rows * LENGTH * heads),
        name="attend",
    )(places, bias, *pieces, *owned, gain)
    return result[:tensors], result[tensors:]


def attend_back_kernel(heads, place_ref, bias_ref, tok_ref, gain_ref, w_ref, qkv_ref, log_ref, *refs):
    refs = list(refs)
    pieces = [refs.pop(0) for _ in range(5)]
    parts = [refs.pop(0) for _ in range(4)]
    gproj, group_ref, near, far, gain_out, table, wo, gmix, group, result = refs
    inner = heads * HEAD_DIM
    blocks = LENGTH // TILE
    step_id = pl.program_id(0)

    @pl.when(step_id == 0)
    def _():
        fill_bias(bias_ref, table, heads)
        wo[...] = w_ref[:, 3 * inner :]
        near[...] = jnp.zeros_like(near)
        far[...] = jnp.zeros_like(far)
        gain_out[...] = jnp.zeros_like(gain_out)
        group_halves(place_ref, group, pieces)

    here = pl.ds(pl.multiple_of(step_id * LENGTH, LENGTH), LENGTH)
    group_ref[...] = group[here, :]
    gmix[...] = dot(group_ref[...], wo[...]).astype(BF16)
    for head in range(heads):
        at = head * HEAD_DIM
        query = (qkv_ref[:, at : at + HEAD_DIM] * HEAD_DIM ** (-0.5)).astype(BF16)
        key = qkv_ref[:, inner + at : inner + at + HEAD_DIM]
        value = qkv_ref[:, 2 * inner + at : 2 * inner + at + HEAD_DIM]
        grad_rows = gmix[:, at : at + HEAD_DIM]
        scores = dot(query, key, ROWS_NT) + table[head]
        attention = jnp.exp(scores - log_ref[:, head : head + 1])
        grad_weights = dot(grad_rows, value, ROWS_NT)
        inner_sum = jnp.sum(attention * grad_weights, axis=-1, keepdims=True)
        grad_scores = attention * (grad_weights - inner_sum)
        low = jnp.zeros((TILE, TILE), F32)
        high = jnp.zeros((TILE, TILE), F32)
        mid = [jnp.zeros((TILE, TILE), F32) for _ in range(3)]
        for i in range(blocks):
            for j in range(blocks):
                piece = grad_scores[i * TILE : (i + 1) * TILE, j * TILE : (j + 1) * TILE]
                if abs(j - i) <= 1:
                    mid[j - i + 1] = mid[j - i + 1] + piece
                elif j < i:
                    low = low + piece
                else:
                    high = high + piece
        for k in range(3):
            near[head * 3 + k] += mid[k]
        far[head * 2] += low
        far[head * 2 + 1] += high
        rounded = grad_scores.astype(BF16)
        gproj[:, at : at + HEAD_DIM] = (dot(rounded, key) * HEAD_DIM ** (-0.5)).astype(BF16)
        gproj[:, inner + at : inner + at + HEAD_DIM] = dot(rounded, query, ROWS_TN).astype(BF16)
        gproj[:, 2 * inner + at : 2 * inner + at + HEAD_DIM] = dot(
            attention.astype(BF16), grad_rows, ROWS_TN
        ).astype(BF16)
    unit, _ = unit_rows(tok_ref[...].astype(F32))
    grad_normed = dot(gproj[...], w_ref[:, : 3 * inner], ROWS_NT)
    result[here, :] = grad_normed.astype(BF16)
    gain_out[...] += jnp.sum(grad_normed * unit, axis=0, keepdims=True)

    @pl.when(step_id == pl.num_programs(0) - 1)
    def _():
        part_halves(place_ref, parts, result)


def attend_back(places, bias, tokens, gain, weights, projected, logs, pieces):
    rows, width = tokens.shape
    piece = whole(pieces[0].shape)
    heads = bias.shape[0]
    inner = heads * HEAD_DIM
    seqs = rows // LENGTH
    by_seq = lambda cols: pl.BlockSpec((LENGTH, cols), lambda s, *_: (s, 0))
    near, far = (heads * 3, TILE, TILE), (heads * 2, TILE, TILE)
    result = pl.pallas_call(
        functools.partial(attend_back_kernel, heads),
        grid_spec=pltpu.PrefetchScalarGridSpec(
            num_scalar_prefetch=1,
            grid=(seqs,),
            in_specs=[
                pl.BlockSpec(memory_space=pltpu.SMEM),
                by_seq(width),
                whole((1, width)),
                whole((width, 4 * inner)),
                by_seq(3 * inner),
                by_seq(TILE),
            ]
            + [whole(p.shape) for p in pieces],
            out_specs=[piece] * 4
            + [by_seq(3 * inner), by_seq(width), whole(near), whole(far), whole((1, width))],
            scratch_shapes=[
                pltpu.VMEM((heads, LENGTH, LENGTH), F32),
                pltpu.VMEM((width, inner), BF16),
                pltpu.VMEM((LENGTH, inner), BF16),
                pltpu.VMEM((rows, width), BF16),
                pltpu.VMEM((rows, width), BF16),
            ],
        ),
        out_shape=[jax.ShapeDtypeStruct(pieces[0].shape, BF16)] * 4
        + [
            jax.ShapeDtypeStruct((rows, 3 * inner), BF16),
            jax.ShapeDtypeStruct((rows, width), BF16),
            jax.ShapeDtypeStruct(near, F32),
            jax.ShapeDtypeStruct(far, F32),
            jax.ShapeDtypeStruct((1, width), F32),
        ],
        compiler_params=params(),
        cost_estimate=cost(8 * rows * width * inner + 10 * rows * LENGTH * inner, rows * width * 12, rows * LENGTH * heads),
        name="attend_back",
    )(places, bias, tokens, gain, weights, projected, logs, *pieces)
    return result[:4], result[4:]


def attend_weights_kernel(
    heads, part, place_ref, tok_ref, gain_ref, gproj, group_ref, mixed_ref, near, far,
    gain_out, gain_two_ref, router_ref, own_ref, other_ref, weight_ref, rows_s,
):
    inner = heads * HEAD_DIM

    @pl.when(pl.program_id(0) == 0)
    def _():
        weight_ref[...] = jnp.zeros_like(weight_ref)

    unit, _ = unit_rows(tok_ref[...].astype(F32))
    normed = (unit * gain_ref[...]).astype(BF16)
    weight_ref[:, : 3 * inner] += dot(normed, gproj[...], ROWS_TN)
    weight_ref[:, 3 * inner :] += dot(group_ref[...], mixed_ref[...], ROWS_TN)

    @pl.when(pl.program_id(0) == pl.num_programs(0) - 1)
    def _():
        ids = [tile_bucket(step) for step in (-1, 0, 1)]
        for head in range(heads):
            for k in range(BUCKETS):
                total = jnp.zeros((TILE, TILE), F32)
                for step in (-1, 0, 1):
                    if k in tile_range(step):
                        total = total + jnp.where(ids[step + 1] == k, near[head * 3 + step + 1], 0.0)
                if k == 15:
                    total = total + far[head * 2]
                if k == 31:
                    total = total + far[head * 2 + 1]
                at = head * BUCKETS + k
                rows_s[at : at + 1, :] = jnp.sum(total, axis=0, keepdims=True)
        sums = jnp.sum(rows_s[...], axis=1, keepdims=True)
        experts = router_ref.shape[0]
        if part % 16:
            own_ref[...] = jnp.broadcast_to(sums, own_ref.shape)
            return
        count = sums.shape[0]
        diagonal = lax.broadcasted_iota(jnp.int32, (count, TILE), 0) == lax.broadcasted_iota(
            jnp.int32, (count, TILE), 1
        )
        sums = jnp.sum(jnp.where(diagonal, sums, 0.0), axis=0, keepdims=True)
        width = gain_out.shape[1]
        sums = jnp.concatenate([sums, jnp.zeros((1, width - TILE), F32)], axis=1)
        head_rows = jnp.concatenate(
            [gain_out[...], gain_two_ref[...], sums, jnp.zeros((13, width), F32)], axis=0
        ).astype(BF16)
        tail = jnp.concatenate(
            [router_ref[...].astype(BF16)]
            + ([jnp.zeros((-experts % 16, width), BF16)] if experts % 16 else []),
            axis=0,
        )
        z_count = own_ref.shape[0]
        for n, ref in enumerate((own_ref, other_ref)):
            for k in range(z_count):
                at = pl.multiple_of((place_ref[3] ^ (n * z_count + k)) * part, part)
                ref[k, :part, :] = weight_ref[pl.ds(at, part), :].astype(BF16)
                ref[k, part : part + 16, :] = head_rows
                ref[k, part + 16 :, :] = tail


def attend_weights(places, tokens, gain, grads, mixed, gain_two, router, heads, part, z_count):
    gproj, group, near, far, gain_one = grads
    rows, width = tokens.shape
    inner = heads * HEAD_DIM
    seqs = rows // LENGTH
    by_seq = lambda cols: pl.BlockSpec((LENGTH, cols), lambda s, *_: (s, 0))
    experts = router.shape[0]
    sent = (z_count, part + 16 + experts + -experts % 16, width)
    if part % 16:
        sent = (heads * BUCKETS, 1)
    kind = F32 if part % 16 else BF16
    return pl.pallas_call(
        functools.partial(attend_weights_kernel, heads, part),
        grid_spec=pltpu.PrefetchScalarGridSpec(
            num_scalar_prefetch=1,
            grid=(seqs,),
            in_specs=[
                by_seq(width),
                whole((1, width)),
                by_seq(3 * inner),
                by_seq(width),
                by_seq(inner),
                whole(near.shape),
                whole(far.shape),
                whole((1, width)),
                whole((1, width)),
                whole((experts, width)),
            ],
            out_specs=[whole(sent), whole(sent), whole((width, 4 * inner))],
            scratch_shapes=[pltpu.VMEM((heads * BUCKETS, TILE), F32)],
        ),
        out_shape=[
            jax.ShapeDtypeStruct(sent, kind),
            jax.ShapeDtypeStruct(sent, kind),
            jax.ShapeDtypeStruct((width, 4 * inner), F32),
        ],
        compiler_params=params(),
        cost_estimate=cost(8 * rows * width * inner, rows * width * 12),
        name="attend_weights",
    )(places, tokens, gain, gproj, group, mixed, near, far, gain_one, gain_two, router)


def first_rows_kernel(count, *refs):
    out_ref = refs[-1]
    at = 0
    for ref in refs[:-1]:
        for n in range(ref.shape[0]):
            out_ref[at] = ref[n, :count, :]
            at += 1


def first_rows(pieces, start, extra, count):
    width = pieces[0].shape[-1]
    total = sum(piece.shape[0] for piece in pieces)
    return pl.pallas_call(
        functools.partial(first_rows_kernel, count),
        grid=(1,),
        in_specs=[
            pl.BlockSpec((piece.shape[0], extra, width), lambda i: (0, start // extra, 0)) for piece in pieces
        ],
        out_specs=whole((total, count, width)),
        out_shape=jax.ShapeDtypeStruct((total, count, width), BF16),
        compiler_params=params(),
        cost_estimate=cost(0, 4 * total * extra * width),
        name="first_rows",
    )(*pieces)


def place_rows(target_ref, rows, out_refs):
    at = 0
    for ref in out_refs:
        count = ref.shape[0]
        index = lax.broadcasted_iota(jnp.int32, (count, rows.shape[0]), 0) + at
        chosen = jnp.where(index == target_ref[...], 1.0, 0.0).astype(BF16)
        ref[...] = dot(chosen, rows).astype(BF16)
        at += count


def place_kernel(target_ref, rows_ref, *out_refs):
    place_rows(target_ref, rows_ref[...], out_refs)


def place(target_row, rows, counts):
    return pl.pallas_call(
        place_kernel,
        out_shape=[jax.ShapeDtypeStruct((count, rows.shape[1]), BF16) for count in counts],
        compiler_params=params(),
        cost_estimate=cost(2 * sum(counts) * rows.size, 4 * rows.size),
        name="place",
    )(target_row, rows)


def softmax_rows(logits):
    exponent = jnp.exp(logits - jnp.max(logits, axis=-1, keepdims=True))
    return exponent * (1.0 / jnp.sum(exponent, axis=-1, keepdims=True))


def sum_pieces(refs):
    total = refs[0][...].astype(F32)
    for ref in refs[1:]:
        total = total + ref[...].astype(F32)
    return total


def route_kernel(tok_ref, *refs):
    gain_ref, router_ref, target_ref, index_ref, kept_ref, hidden_ref, gate_ref = refs[6:13]
    half = tok_ref.shape[0] // 2
    for h in range(2):
        keep, got, last = refs[3 * h : 3 * h + 3]
        here = slice(h * half, (h + 1) * half)
        added = keep[:half, :].astype(F32) + got[:half, :].astype(F32) + last[...].astype(F32)
        hidden_ref[here, :] = tok_ref[here, :].astype(F32) + added
    hidden = hidden_ref[...]
    unit, _ = unit_rows(hidden)
    moe_in = (unit * gain_ref[...]).astype(BF16)
    place_rows(target_ref, moe_in, refs[13:])
    probs = softmax_rows(dot(moe_in, router_ref[...]))
    lanes = lax.broadcasted_iota(jnp.int32, probs.shape, 1)
    picked = jnp.sum(jnp.where(lanes == index_ref[...], probs, 0.0), axis=-1, keepdims=True)
    gate_ref[...] = picked * kept_ref[...].astype(F32)


def route(tokens, attn, gain, router, target_row, index_col, kept_col, counts):
    rows, width = tokens.shape
    result = pl.pallas_call(
        route_kernel,
        out_shape=[
            jax.ShapeDtypeStruct((rows, width), F32),
            jax.ShapeDtypeStruct((rows, 1), F32),
        ]
        + [jax.ShapeDtypeStruct((count, width), BF16) for count in counts],
        compiler_params=params(),
        cost_estimate=cost(2 * sum(counts) * rows * width, 12 * rows * width),
        name="route",
    )(tokens, *attn, gain, router, target_row, index_col, kept_col)
    return result[0], result[1], result[2:]


def rest_choice(blocks, locals_, rest, expert):
    rows = lax.broadcasted_iota(jnp.int32, (blocks * rest, blocks * locals_ * rest), 0)
    cols = lax.broadcasted_iota(jnp.int32, (blocks * rest, blocks * locals_ * rest), 1)
    block = lax.div(rows, rest)
    wanted = block * (locals_ * rest) + expert * rest + (rows - block * rest)
    return jnp.where(cols == wanted, 1.0, 0.0).astype(BF16)


def pick_rows(out_ref, views, choice, main_rows, main, expert):
    at = 0
    pieces = []
    for view in views:
        blocks, size, width = view.shape
        if main:
            start = pl.multiple_of(expert * main, main)
            out_ref[at : at + blocks * main, :] = view[:, pl.ds(start, main), :].reshape(blocks * main, width)
            at += blocks * main
        rest = size - size * main_rows // out_ref.shape[0]
        pieces.append(view[:, size - rest :, :].reshape(blocks * rest, width))
    out_ref[main_rows:, :] = dot(choice, jnp.concatenate(pieces, axis=0)).astype(BF16)


def put_rows(views, value_ref, choice, main_rows, main, locals_, rest, expert):
    at = 0
    spread = dot(choice, value_ref[main_rows:, :], ROWS_TN).astype(BF16)
    rest_at = 0
    for view in views:
        blocks, _, width = view.shape
        if main:
            count = blocks * main
            start = pl.multiple_of(expert * main, main)
            view[:, pl.ds(start, main), :] = value_ref[at : at + count, :].reshape(blocks, main, width)
            at += count
        part = spread[rest_at : rest_at + blocks * locals_ * rest].reshape(blocks, locals_ * rest, width)
        rest_at += blocks * locals_ * rest

        before = view[:, locals_ * main :, :]
        view[:, locals_ * main :, :] = part + jnp.where(expert > 0, before, jnp.zeros_like(before))


def group_views(place_ref, ref, tensors, chunks):
    size = ref.shape[1] // chunks
    views = []
    for k in range(chunks):
        a, b = HOPS[k % 2]
        views += [ref.at[place_ref[2] ^ j, k * size : (k + 1) * size] for j in (0, a, b, a | b)]
    return views


def join_halves(place_ref, own_in, peer_in, own_out, peer_out, win, wout):
    half = own_in.shape[1]
    mine = pl.multiple_of(place_ref[0] * half, half)
    other = pl.multiple_of((1 - place_ref[0]) * half, half)
    if win is not None:
        win[pl.ds(mine, half), :] = own_in[0]
        win[pl.ds(other, half), :] = peer_in[0]
    half_out = own_out.shape[2]
    mine = pl.multiple_of(place_ref[0] * half_out, half_out)
    other = pl.multiple_of((1 - place_ref[0]) * half_out, half_out)
    wout[:, pl.ds(mine, half_out)] = own_out[0]
    wout[:, pl.ds(other, half_out)] = peer_out[0]


def expert_kernel(chunks, tensors, main, locals_, rest, place_ref, *refs):
    refs = list(refs)
    take = lambda n: [refs.pop(0) for _ in range(n)]
    xs = take(3 * chunks)
    (g_ref,) = take(1)
    own_in, peer_in, own_out, peer_out, router = take(5)
    backs = take(2 * chunks)
    x_ref, ge_ref, hid_ref, gi_ref, gl_ref = take(5)
    win, wout, grows, inner, gunits, gate_s, dots, back = take(8)
    expert = pl.program_id(0)
    blocks = sum(ref.shape[0] for ref in xs)
    main_rows = blocks * main
    rows, width = x_ref.shape[1:]
    wide = win.shape[1]
    choice = rest_choice(blocks, locals_, rest, expert)
    many = xs[0].shape[0]
    back_refs = []
    for k in range(chunks):
        keep, send = backs[2 * k : 2 * k + 2]
        back_refs += [ref.at[n * many : (n + 1) * many] for n in range(2) for ref in (keep, send)]
    pick_rows(x_ref.at[0], xs, choice, main_rows, main, expert)
    pick_rows(grows, group_views(place_ref, g_ref, tensors, chunks), choice, main_rows, main, expert)
    join_halves(place_ref, own_in, peer_in, own_out, peer_out, win, wout)
    probs = softmax_rows(dot(x_ref[0], router[...]))
    lanes = lax.broadcasted_iota(jnp.int32, probs.shape, 1)
    mine = lanes == place_ref[1] * locals_ + expert
    picked = jnp.sum(jnp.where(mine, probs, 0.0), axis=-1, keepdims=True)
    gate_s[...] = jnp.broadcast_to(picked, gate_s.shape)
    chunk = 16
    half_wide = wide // 2 if wide % (2 * TILE) == 0 else wide
    half_rows = rows // 2

    def multiply(part):
        at = slice(part * half_rows, (part + 1) * half_rows)
        inner[at, :] = dot(x_ref[0, at, :], win[...])
        gunits[at, :] = dot(grows[at, :], wout[...], ROWS_NT)

    def activate(part):
        for row in range(part * half_rows, (part + 1) * half_rows, chunk):
            at = slice(row, row + chunk)
            gate_tile = gate_s[at, :]
            gate = jnp.concatenate([gate_tile] * (half_wide // TILE), axis=1)
            total = None
            for start in range(0, wide, half_wide):
                lanes_at = slice(start, start + half_wide)
                value = inner[at, lanes_at]
                square = value * value
                wave = jnp.tanh(value * (GELU_A + (GELU_A * GELU_B) * square))
                half = 0.5 + 0.5 * wave
                hidden = (value * half).astype(BF16)
                bend = value * (0.5 * GELU_A + (1.5 * GELU_A * GELU_B) * square)
                slope = half + bend * (1.0 - wave * wave)
                units = gunits[at, lanes_at]
                hid_ref[0, at, lanes_at] = hidden
                gi_ref[0, at, lanes_at] = (gate * (units * slope)).astype(BF16)
                product = hidden.astype(F32) * units
                for tile in range(0, half_wide, TILE):
                    part_sum = product[:, tile : tile + TILE]
                    total = part_sum if total is None else total + part_sum
            dots[at, :] = total
            gate = jnp.concatenate([gate_tile] * (width // TILE), axis=1)
            ge_ref[0, at, :] = (gate * grows[at, :].astype(F32)).astype(BF16)

    def finish(part):
        at = slice(part * half_rows, (part + 1) * half_rows)
        grad_logits = (
            jnp.sum(dots[at, :], axis=-1, keepdims=True)
            * probs[at]
            * (jnp.where(mine[at], 1.0, 0.0) - picked[at])
        ).astype(BF16)
        gl_ref[0, at, :] = grad_logits
        back[at, :] = (
            dot(gi_ref[0, at, :], win[...], ROWS_NT) + dot(grad_logits, router[...], ROWS_NT)
        ).astype(BF16)

    multiply(0)
    multiply(1)
    activate(0)
    finish(0)
    activate(1)
    finish(1)
    put_rows(back_refs, back, choice, main_rows, main, locals_, rest, expert)


def expert_forward_back(places, xs, gs, own_in, peer_in, own_out, peer_out, router, main, rest, chunks):
    locals_, half, wide = own_in.shape
    width, experts = router.shape
    many, block = xs[0].shape[:2]
    tensors = gs.shape[0]
    blocks = tensors * chunks * many
    back = (2 * many, block, width)
    rows = blocks * (main + rest)
    per = lambda *shape: pl.BlockSpec((1,) + shape, lambda e, *_: (e, 0, 0))
    saved = jax.ShapeDtypeStruct((locals_, rows, width), BF16)
    saved_wide = jax.ShapeDtypeStruct((locals_, rows, wide), BF16)
    result = pl.pallas_call(
        functools.partial(expert_kernel, chunks, tensors, main, locals_, rest),
        grid_spec=pltpu.PrefetchScalarGridSpec(
            num_scalar_prefetch=1,
            grid=(locals_,),
            in_specs=[whole(x.shape) for x in xs]
            + [whole(gs.shape)]
            + [per(half, wide)] * 2 + [per(wide, half)] * 2 + [whole((width, experts))],
            out_specs=[whole(back)] * (2 * chunks)
            + [per(rows, width), per(rows, width), per(rows, wide), per(rows, wide), per(rows, experts)],
            scratch_shapes=[
                pltpu.VMEM((width, wide), BF16),
                pltpu.VMEM((wide, width), BF16),
                pltpu.VMEM((rows, width), BF16),
                pltpu.VMEM((rows, wide), F32),
                pltpu.VMEM((rows, wide), F32),
                pltpu.VMEM((rows, TILE), F32),
                pltpu.VMEM((rows, TILE), F32),
                pltpu.VMEM((rows, width), BF16),
            ],
        ),
        out_shape=[jax.ShapeDtypeStruct(back, BF16)] * (2 * chunks)
        + [saved, saved, saved_wide, saved_wide, jax.ShapeDtypeStruct((locals_, rows, experts), BF16)],
        compiler_params=params(),
        cost_estimate=cost(6 * locals_ * rows * width * wide, locals_ * rows * width * 14, locals_ * rows * wide),
        name="experts",
    )(places, *xs, gs, own_in, peer_in, own_out, peer_out, router)
    return result[: 2 * chunks], result[2 * chunks :]


def expert_rows_kernel(chunks, main, locals_, rest, place_ref, hid_ref, own_out, peer_out, forward_ref, wout, value):
    expert = pl.program_id(0)
    tensors = forward_ref.shape[0]
    blocks = tensors * forward_ref.shape[1]
    choice = rest_choice(blocks, locals_, rest, expert)
    join_halves(place_ref, own_out, peer_out, own_out, peer_out, None, wout)
    value[...] = dot(hid_ref[0], wout[...]).astype(BF16)
    views = group_views(place_ref, forward_ref, tensors, chunks)
    put_rows(views, value, choice, blocks * main, main, locals_, rest, expert)


def expert_rows(places, hidden, own_out, peer_out, shape, main, rest, chunks):
    locals_, rows, wide = hidden.shape
    half = own_out.shape[2]
    width = shape[-1]
    per = lambda *shape: pl.BlockSpec((1,) + shape, lambda e, *_: (e, 0, 0))
    return pl.pallas_call(
        functools.partial(expert_rows_kernel, chunks, main, locals_, rest),
        grid_spec=pltpu.PrefetchScalarGridSpec(
            num_scalar_prefetch=1,
            grid=(locals_,),
            in_specs=[per(rows, wide)] + [per(wide, half)] * 2,
            out_specs=whole(shape),
            scratch_shapes=[pltpu.VMEM((wide, width), BF16), pltpu.VMEM((rows, width), BF16)],
        ),
        out_shape=jax.ShapeDtypeStruct(shape, BF16),
        compiler_params=params(),
        cost_estimate=cost(2 * locals_ * rows * width * wide, locals_ * rows * width * 6),
        name="expert_rows",
    )(places, hidden, own_out, peer_out)


def expert_weights_kernel(place_ref, x_ref, ge_ref, hid_ref, gi_ref, gl_ref, *refs):
    in_own, in_send, out_own, out_send, router_ref = refs
    half = in_own.shape[1]
    mine = pl.ds(pl.multiple_of(place_ref[0] * half, half), half)
    other = pl.ds(pl.multiple_of((1 - place_ref[0]) * half, half), half)
    in_own[0] = dot(x_ref[0, :, mine], gi_ref[0], ROWS_TN)
    in_send[0] = dot(x_ref[0, :, other], gi_ref[0], ROWS_TN).astype(BF16)
    out_own[0] = dot(hid_ref[0], ge_ref[0, :, mine], ROWS_TN)
    out_send[0] = dot(hid_ref[0], ge_ref[0, :, other], ROWS_TN).astype(BF16)

    @pl.when(pl.program_id(0) == 0)
    def _():
        router_ref[...] = jnp.zeros_like(router_ref)

    router_ref[...] += dot(gl_ref[0], x_ref[0], ROWS_TN)


def expert_weights(places, saved, half):
    x, ge, hidden, gi, gl = saved
    locals_, rows, width = x.shape
    wide = hidden.shape[2]
    experts = gl.shape[2]
    per = lambda *shape: pl.BlockSpec((1,) + shape, lambda e, *_: (e, 0, 0))
    return pl.pallas_call(
        expert_weights_kernel,
        grid_spec=pltpu.PrefetchScalarGridSpec(
            num_scalar_prefetch=1,
            grid=(locals_,),
            in_specs=[per(rows, width), per(rows, width), per(rows, wide), per(rows, wide), per(rows, experts)],
            out_specs=[per(half, wide), per(half, wide), per(wide, half), per(wide, half), whole((experts, width))],
        ),
        out_shape=[
            jax.ShapeDtypeStruct((locals_, half, wide), F32),
            jax.ShapeDtypeStruct((locals_, half, wide), BF16),
            jax.ShapeDtypeStruct((locals_, wide, half), F32),
            jax.ShapeDtypeStruct((locals_, wide, half), BF16),
            jax.ShapeDtypeStruct((experts, width), F32),
        ],
        compiler_params=params(),
        cost_estimate=cost(4 * locals_ * rows * width * wide, locals_ * rows * width * 14),
        name="expert_weights",
    )(places, x, ge, hidden, gi, gl)


def take_rows(target_ref, refs):
    total, at = None, 0
    for ref in refs:
        count = ref.shape[0]
        cols = lax.broadcasted_iota(jnp.int32, (target_ref.shape[0], count), 1) + at
        chosen = jnp.where(cols == target_ref[...], 1.0, 0.0).astype(BF16)
        part = dot(chosen, ref[...])
        total = part if total is None else total + part
        at += count
    return total


def hidden_back_kernel(target_ref, *refs):
    hidden_ref, cot_ref, gain_ref, grad_ref, attn_ref, gain_out = refs[-6:]
    grad_in = take_rows(target_ref, refs[:-6])
    unit, scale = unit_rows(hidden_ref[...])
    gain_out[...] = jnp.sum(grad_in * unit, axis=0, keepdims=True)
    scaled = grad_in * gain_ref[...]
    inside = jnp.mean(unit * scaled, axis=-1, keepdims=True)
    grad = cot_ref[...].astype(F32) + scale * (scaled - unit * inside)
    grad_ref[...] = grad
    attn_ref[...] = grad.astype(BF16)


def hidden_back(target_col, back, hidden, cotangent, gain):
    rows, width = hidden.shape
    return pl.pallas_call(
        hidden_back_kernel,
        out_shape=[
            jax.ShapeDtypeStruct((rows, width), F32),
            jax.ShapeDtypeStruct((rows, width), BF16),
            jax.ShapeDtypeStruct((1, width), F32),
        ],
        compiler_params=params(),
        cost_estimate=cost(3 * rows * rows * width, 16 * rows * width),
        name="hidden_back",
    )(target_col, *back, hidden, cotangent, gain)


def output_kernel(target_ref, *refs):
    hidden_ref, gate_ref, out_ref = refs[-3:]
    out_ref[...] = (hidden_ref[...] + gate_ref[...] * take_rows(target_ref, refs[:-3])).astype(BF16)


def output_rows(target_col, expert_rows, hidden, gate):
    return pl.pallas_call(
        output_kernel,
        out_shape=jax.ShapeDtypeStruct(hidden.shape, BF16),
        compiler_params=params(),
        cost_estimate=cost(3 * hidden.shape[0] * hidden.size, 10 * hidden.size),
        name="output_rows",
    )(target_col, *expert_rows, hidden, gate)


def tokens_back_kernel(tok_ref, *refs):
    gain_ref, hidden_ref, out_ref = refs[6:]
    half = tok_ref.shape[0] // 2
    for h in range(2):
        keep, got, last = refs[3 * h : 3 * h + 3]
        here = slice(h * half, (h + 1) * half)
        unit, scale = unit_rows(tok_ref[here, :].astype(F32))
        grad = keep[:half, :].astype(F32) + got[:half, :].astype(F32) + last[...].astype(F32)
        scaled = grad * gain_ref[...]
        inside = jnp.mean(unit * scaled, axis=-1, keepdims=True)
        out_ref[here, :] = hidden_ref[here, :] + scale * (scaled - unit * inside)


def tokens_back(tokens, grad_normed, gain, grad_hidden):
    return pl.pallas_call(
        tokens_back_kernel,
        out_shape=jax.ShapeDtypeStruct(tokens.shape, F32),
        compiler_params=params(),
        cost_estimate=cost(10 * tokens.size, 12 * tokens.size),
        name="tokens_back",
    )(tokens, *grad_normed, gain, grad_hidden)


def shifted(value, axis, count, step):
    return lax.ppermute(value, axis, [(s, (s + step) % count) for s in range(count)])


def gather_ring(value, axis, count):
    me = lax.axis_index(axis)
    parts = [value] + [shifted(value, axis, count, -k) for k in range(1, count)]
    return jnp.roll(jnp.stack(parts), me, axis=0)


def swapped(value, axis, count, bits):
    return lax.ppermute(value, axis, [(s, s ^ bits) for s in range(count)])


def gather_pieces(value, axis, count):
    return [value] + [swapped(value, axis, count, k) for k in range(1, count)]


def gather_hops(value, hops):
    a, b = hops
    first = swapped(value, "tensor", 4, a)
    second = swapped(jnp.concatenate([value, first], axis=0), "tensor", 4, b)
    return first, second


def sum_hops(parts):
    half = parts[0].shape[0] // 2
    result = []
    for h, (a, b) in enumerate(HOPS):
        keep, send = parts[2 * h : 2 * h + 2]
        got = swapped(send, "tensor", 4, a)
        last = swapped(added(keep[half:], got[half:]), "tensor", 4, b)
        result += [keep, got, last]
    return result


def added(a, b):
    return (a.astype(F32) + b.astype(F32)).astype(BF16)


def swap_pieces(pieces, axis, count):
    return [pieces[0]] + [swapped(pieces[k], axis, count, k) for k in range(1, count)]


def on_device(
    sizes,
    tokens,
    cotangent,
    query_key_value_weight,
    attention_output_weight,
    rel_bias,
    gain_attn,
    gain_moe,
    w_router,
    w_in,
    w_out,
    expert_index,
    slot_index,
    kept_mask,
):
    dp_count, z_count, t_count = sizes
    tok_rows, width = tokens.shape
    experts_all = w_router.shape[1]
    capacity = max(2, 3 * tok_rows // (2 * experts_all))
    locals_ = w_in.shape[0]
    main = capacity // 16 * 16
    rest = capacity - main
    block = locals_ * capacity
    heads = rel_bias.shape[0]
    inner = heads * HEAD_DIM
    part = query_key_value_weight.shape[1]
    fine = w_router.shape[0]
    my_dp = lax.axis_index("dp")
    my_z = lax.axis_index("expert")
    bias = rel_bias.astype(F32)

    my_t = lax.axis_index("tensor")
    owners = dp_count * z_count
    my_owner = my_dp * z_count + my_z
    places = jnp.stack([my_dp, my_z, my_t, my_owner]).astype(jnp.int32)
    half_rows = tok_rows // 2
    token_pieces = [tokens]
    for h, hops in enumerate(HOPS):
        token_pieces += list(gather_hops(tokens[h * half_rows : (h + 1) * half_rows], hops))

    small = jnp.concatenate([gain_attn[:, None], gain_moe[:, None], w_router], axis=1).reshape(-1)
    extra = -(-small.shape[0] // (16 * width)) * 16
    packed = jnp.concatenate(
        [
            query_key_value_weight.transpose(1, 0, 2).reshape(part, 3 * inner),
            attention_output_weight.T,
        ],
        axis=1,
    )
    packed = jnp.concatenate(
        [packed, jnp.pad(small, (0, extra * width - small.shape[0])).reshape(extra, width)], axis=0
    )
    owned = gather_pieces(packed[None], "expert", z_count)

    chunks = min(z_count, 4)
    many = z_count // chunks

    def over_expert(groups):
        if many > 1:
            groups = [g[i * block : (i + 1) * block] for g in groups for i in range(many)]
        pieces = swap_pieces(groups, "expert", z_count)
        if many == 1:
            return pieces
        return [jnp.concatenate(pieces[k * many : (k + 1) * many], axis=0) for k in range(chunks)]

    z_of = expert_index // locals_
    local = expert_index - z_of * locals_
    inside = jnp.where(
        slot_index < main, local * main + slot_index, locals_ * main + local * rest + slot_index - main
    )
    target = (z_of ^ my_z) * block + inside
    target = jnp.where(kept_mask > 0, target, -1)
    target_row, target_col = target[None, :], target[:, None]
    counts = [many * block] * chunks
    grad_sent = place(target_row, cotangent, counts)
    owned, grad_sent = lax.optimization_barrier((owned, grad_sent))
    owned = owned + [swapped(jnp.concatenate(owned, axis=0), "dp", dp_count, 1)]
    if part % 16 or part % extra:
        smalls = jnp.concatenate(owned, axis=0)[:, part:]
    else:
        smalls = first_rows(owned, part, extra, -(-small.shape[0] // width))
    smalls = smalls.reshape(owners, -1)[:, : small.shape[0]]
    small_pieces = gather_pieces(smalls, "tensor", t_count)

    grad_rows = jnp.concatenate(over_expert(grad_sent), axis=0)
    token_pieces, owned, small_pieces, grad_rows = lax.optimization_barrier(
        (token_pieces, owned, small_pieces, grad_rows)
    )
    grad_arrived = lax.all_gather(grad_rows, "tensor", axis=0).reshape(t_count, z_count, block, width)
    smalls = jnp.stack(small_pieces).reshape(t_count * owners, -1)
    owner_ids = jnp.arange(owners, dtype=jnp.int32)[:, None] ^ my_owner
    t_ids = jnp.arange(t_count, dtype=jnp.int32)[None, :] ^ my_t
    smalls = smalls[(t_ids * owners + owner_ids).reshape(-1)].reshape(width, 2 + experts_all)
    if part % 16:
        order = jnp.arange(owners, dtype=jnp.int32) ^ my_owner
        owned = [jnp.concatenate(owned, axis=0)[:, :part][order].reshape(1, width, 4 * inner)]
    rows_owned = part if len(owned) > 1 else width
    gain_one = smalls[:, 0].astype(F32)[None]
    gain_two = smalls[:, 1].astype(F32)[None]
    router = smalls[:, 2:]


    grad_rows = jnp.concatenate(over_expert(grad_sent), axis=0)
    parts, (group_tokens, projected, mixed, logs, weights) = attend(
        places, bias, token_pieces, owned, rows_owned, gain_one
    )
    parts, late_in, late_out = lax.optimization_barrier((parts, w_in, w_out))
    peer_in = shifted(late_in, "dp", dp_count, 1)
    peer_out = shifted(late_out, "dp", dp_count, 1)
    attn = sum_hops(parts)
    attn, peer_in, peer_out = lax.optimization_barrier((attn, peer_in, peer_out))
    hidden_one, gate, sent = route(
        tokens, attn, gain_two, router, target_row, expert_index[:, None], kept_mask[:, None], counts
    )
    arrived = []
    for k, group in enumerate(over_expert(sent)):
        pieces = (group,) + gather_hops(group, HOPS[k % 2])
        arrived += [piece.reshape(-1, block, width) for piece in pieces]
    back_parts, saved = expert_forward_back(
        places, arrived, grad_arrived, w_in, peer_in, w_out, peer_out, router, main, rest, chunks
    )

    size = many * block
    back_parts = [piece.reshape(2 * size, width) for piece in back_parts]
    keeps, sends = back_parts[::2], back_parts[1::2]
    got = [swapped(sends[k], "tensor", t_count, HOPS[k % 2][0]) for k in reversed(range(chunks))][::-1]
    forward_part = expert_rows(places, saved[2], w_out, peer_out, grad_arrived.shape, main, rest, chunks)
    got, forward_part = lax.optimization_barrier((got, forward_part))
    forward_sum = lax.psum_scatter(
        forward_part.reshape(t_count * z_count * block, width), "tensor", scatter_dimension=0, tiled=True
    )
    groups = []
    for k in range(chunks):
        last = swapped(added(keeps[k][size:], got[k][size:]), "tensor", t_count, HOPS[k % 2][1])
        total = keeps[k][:size].astype(F32) + got[k][:size].astype(F32) + last.astype(F32)
        groups.append(total.astype(BF16))
    groups, saved = lax.optimization_barrier((groups, saved))
    in_own, in_send, out_own, out_send, router_part = expert_weights(places, saved, w_in.shape[1])
    grad_back, in_send, out_send = lax.optimization_barrier((over_expert(groups), in_send, out_send))
    in_got = shifted(in_send, "dp", dp_count, 1)
    out_got = shifted(out_send, "dp", dp_count, 1)
    grad_hidden, grad_attn, gain_two_part = hidden_back(target_col, grad_back, hidden_one, cotangent, gain_two)
    grad_pieces = [grad_attn]
    for h, hops in enumerate(HOPS):
        grad_pieces += list(gather_hops(grad_attn[h * half_rows : (h + 1) * half_rows], hops))
    grad_w_in = in_own + in_got.astype(F32)
    grad_w_out = out_own + out_got.astype(F32)
    grad_pieces, grad_w_in, grad_w_out, forward_sum = lax.optimization_barrier(
        (grad_pieces, grad_w_in, grad_w_out, forward_sum)
    )
    normed_parts, grads = attend_back(
        places, bias, group_tokens, gain_one, weights, projected, logs, grad_pieces
    )
    forward_rows = over_expert(list(forward_sum.reshape(chunks, many * block, width)))
    normed_parts, grads, forward_rows = lax.optimization_barrier((normed_parts, grads, forward_rows))
    own_part, other_part, weight_part = attend_weights(
        places, group_tokens, gain_one, grads, mixed, gain_two_part, router_part, heads, part, z_count
    )
    gain_one_part = grads[4]
    grad_normed = sum_hops(normed_parts)
    output = output_rows(target_col, forward_rows, hidden_one, gate)
    grad_tokens = tokens_back(tokens, grad_normed, gain_one, grad_hidden)

    if part % 16:
        head_rows = jnp.concatenate(
            [
                gain_one_part,
                gain_two_part,
                jnp.pad(own_part.reshape(1, -1), ((0, 0), (0, width - own_part.shape[0]))),
                jnp.zeros((13, width), F32),
                router_part,
                jnp.zeros((-experts_all % 16, width), F32),
            ]
        )
        order = jnp.arange(owners, dtype=jnp.int32) ^ my_owner
        payload = jnp.concatenate(
            [
                weight_part.reshape(owners, part, width)[order],
                jnp.broadcast_to(head_rows[None], (owners,) + head_rows.shape),
            ],
            axis=1,
        ).astype(BF16)
        own_part, other_part = payload[:z_count], payload[z_count:]
    other_got = shifted(other_part, "dp", dp_count, 1)
    pieces = swap_pieces([added(own_part[k], other_got[k]) for k in range(z_count)], "expert", z_count)
    total = pieces[0].astype(F32)
    for piece in pieces[1:]:
        total = total + piece.astype(F32)
    weight_total = total[:part].reshape(part, 4, inner)
    grad_w_qkv = weight_total[:, :3].transpose(1, 0, 2)
    grad_w_attn_out = weight_total[:, 3].T
    grad_rel_bias = total[part + 2, : heads * BUCKETS].reshape(heads, BUCKETS)
    mine = lax.dynamic_slice_in_dim(total[part:], my_owner * part, part, axis=1)
    mine = jnp.concatenate([mine[:2], mine[16 : 16 + experts_all]], axis=0)
    turned = [
        lax.dynamic_slice_in_dim(mine, (my_t ^ k) * fine, fine, axis=1).reshape(-1) for k in range(t_count)
    ]
    left = turned[0]
    for piece in swap_pieces(turned, "tensor", t_count)[1:]:
        left = left + piece
    grad_gain_attn = left[:fine]
    grad_gain_moe = left[fine : 2 * fine]
    grad_w_router = left[2 * fine :].reshape(experts_all, fine).T
    return (
        output,
        grad_tokens,
        grad_w_qkv,
        grad_w_attn_out,
        grad_rel_bias,
        grad_gain_attn,
        grad_gain_moe,
        grad_w_router,
        grad_w_in,
        grad_w_out,
    )


def solution(mesh):
    placed = (
        P(("dp", "expert", "tensor"), None),
        P(("dp", "expert", "tensor"), None),
        P(None, ("dp", "expert"), "tensor"),
        P("tensor", ("dp", "expert")),
        P("tensor", None),
        P(("dp", "expert", "tensor")),
        P(("dp", "expert", "tensor")),
        P(("dp", "expert", "tensor"), None),
        P("expert", "dp", "tensor"),
        P("expert", "tensor", "dp"),
        P(("dp", "expert", "tensor")),
        P(("dp", "expert", "tensor")),
        P(("dp", "expert", "tensor")),
    )
    sizes = tuple(mesh.shape[name] for name in ("dp", "expert", "tensor"))
    return jax.shard_map(
        functools.partial(on_device, sizes),
        mesh=mesh,
        in_specs=placed,
        out_specs=(
            P(("dp", "expert", "tensor"), None),
            P(("dp", "expert", "tensor"), None),
            P(None, ("dp", "expert"), "tensor"),
            P("tensor", ("dp", "expert")),
            P("tensor", None),
            P(("dp", "expert", "tensor")),
            P(("dp", "expert", "tensor")),
            P(("dp", "expert", "tensor"), None),
            P("expert", "dp", "tensor"),
            P("expert", "tensor", "dp"),
        ),
        check_vma=False,
    )
```

```python
import functools

import jax
import jax.numpy as jnp
from jax import lax
from jax.experimental import pallas as pl
from jax.experimental.pallas import tpu as pltpu
from jax.sharding import PartitionSpec as P

HEAD_DIM = 64
BUCKETS = 32
LENGTH = 512
TILE = 128
EPSILON = 1e-06
BORDERS = (12, 16, 23, 32, 46, 64, 91)
F32 = jnp.float32
BF16 = jnp.bfloat16
GELU_A = 0.7978845608028654
GELU_B = 0.044715
ROWS_NN = (((1,), (0,)), ((), ()))
ROWS_NT = (((1,), (1,)), ((), ()))
ROWS_TN = (((0,), (0,)), ((), ()))
VMEM_BYTES = 56 * 1024 * 1024


def dot(a, b, dims=ROWS_NN):
    return lax.dot_general(a, b, dims, preferred_element_type=F32)


def params(**more):
    return pltpu.CompilerParams(vmem_limit_bytes=VMEM_BYTES, **more)


def cost(flops, moved, special=0):
    return pl.CostEstimate(flops=int(flops), bytes_accessed=int(moved), transcendentals=int(special))


def whole(shape):
    return pl.BlockSpec(shape, lambda *_: (0,) * len(shape))


def tile_bucket(step):
    rows = lax.broadcasted_iota(jnp.int32, (TILE, TILE), 0)
    cols = lax.broadcasted_iota(jnp.int32, (TILE, TILE), 1)
    offset = cols - rows + step * TILE
    distance = jnp.abs(offset)
    bucket = jnp.minimum(distance, 8)
    for border in BORDERS:
        bucket = bucket + jnp.where(distance >= border, 1, 0)
    return bucket + jnp.where(offset > 0, 16, 0)


def tile_range(step):
    return {-1: range(1, 16), 0: range(0, 32), 1: range(17, 32)}[step]


def fill_bias(bias_ref, table, heads):
    blocks = LENGTH // TILE
    buckets = {step: tile_bucket(step) for step in (-1, 0, 1)}
    for head in range(heads):
        near = {}
        for step in (-1, 0, 1):
            value = jnp.zeros((TILE, TILE), F32)
            for k in tile_range(step):
                value = jnp.where(buckets[step] == k, bias_ref[head, k], value)
            near[step] = value
        low = jnp.full((TILE, TILE), bias_ref[head, 15], F32)
        high = jnp.full((TILE, TILE), bias_ref[head, 31], F32)
        for i in range(blocks):
            for j in range(blocks):
                step = j - i
                value = near[step] if abs(step) <= 1 else (low if step < 0 else high)
                table[head, i * TILE : (i + 1) * TILE, j * TILE : (j + 1) * TILE] = value


def unit_rows(values):
    scale = lax.rsqrt(jnp.mean(values * values, axis=-1, keepdims=True) + EPSILON)
    return values * scale, scale


HOPS = ((1, 2), (2, 1))


def group_halves(place_ref, out, pieces):
    rows = pieces[0].shape[0]
    half = rows // 2
    at = pl.multiple_of(place_ref[2] * rows, rows)
    out[pl.ds(at, rows), :] = pieces[0][...]
    for h, (a, b) in enumerate(HOPS):
        first, second = pieces[1 + 2 * h : 3 + 2 * h]
        for j, value in ((a, first[...]), (b, second[:half, :]), (a | b, second[half:, :])):
            at = pl.multiple_of((place_ref[2] ^ j) * rows + h * half, half)
            out[pl.ds(at, half), :] = value


def part_halves(place_ref, pieces, source):
    half = pieces[0].shape[0] // 2
    for h, (a, b) in enumerate(HOPS):
        for piece, order in zip(pieces[2 * h : 2 * h + 2], ((0, b), (a, a | b))):
            for n, j in enumerate(order):
                at = pl.multiple_of((place_ref[2] ^ j) * 2 * half + h * half, half)
                piece[n * half : (n + 1) * half, :] = source[pl.ds(at, half), :]


def attend_kernel(heads, tensors, owners, part, place_ref, bias_ref, *refs):
    refs = list(refs)
    take = lambda n: [refs.pop(0) for _ in range(n)]
    pieces, owned, (gain_ref,), parts = take(5), take(owners), take(1), take(tensors)
    tok_ref, qkv_ref, mixed_ref, log_ref, w_ref, table, wo, group, result = refs
    inner = heads * HEAD_DIM
    step_id = pl.program_id(0)

    @pl.when(step_id == 0)
    def _():
        fill_bias(bias_ref, table, heads)
        group_halves(place_ref, group, pieces)
        blocks = [piece.at[n] for piece in owned for n in range(piece.shape[0])]
        for k, piece in enumerate(blocks):
            at = pl.multiple_of((place_ref[3] ^ k) * part, part) if owners > 1 else 0
            w_ref[pl.ds(at, part), :] = piece[:part, :]
        wo[...] = w_ref[:, 3 * inner :]

    here = pl.ds(pl.multiple_of(step_id * LENGTH, LENGTH), LENGTH)
    tok_ref[...] = group[here, :]
    unit, _ = unit_rows(tok_ref[...].astype(F32))
    normed = (unit * gain_ref[...]).astype(BF16)
    qkv_ref[...] = dot(normed, w_ref[:, : 3 * inner]).astype(BF16)
    lanes = lax.broadcasted_iota(jnp.int32, (LENGTH, TILE), 1)
    logs = jnp.zeros((LENGTH, TILE), F32)
    for head in range(heads):
        at = head * HEAD_DIM
        query = qkv_ref[:, at : at + HEAD_DIM] * HEAD_DIM ** (-0.5)
        key = qkv_ref[:, inner + at : inner + at + HEAD_DIM]
        value = qkv_ref[:, 2 * inner + at : 2 * inner + at + HEAD_DIM]
        scores = dot(query.astype(BF16), key, ROWS_NT) + table[head]
        top = jnp.max(scores, axis=-1, keepdims=True)
        exponent = jnp.exp(scores - top)
        total = jnp.sum(exponent, axis=-1, keepdims=True)
        attention = (exponent * (1.0 / total)).astype(BF16)
        mixed_ref[:, at : at + HEAD_DIM] = dot(attention, value).astype(BF16)
        logs = jnp.where(lanes == head, top + jnp.log(total), logs)
    log_ref[...] = logs
    result[here, :] = dot(mixed_ref[...], wo[...], ROWS_NT).astype(BF16)

    @pl.when(step_id == pl.num_programs(0) - 1)
    def _():
        part_halves(place_ref, parts, result)


def attend(places, bias, pieces, owned, part, gain):
    tensors = 4
    piece_rows, width = pieces[0].shape
    rows = tensors * piece_rows
    heads = bias.shape[0]
    inner = heads * HEAD_DIM
    seqs = rows // LENGTH
    by_seq = lambda cols: pl.BlockSpec((LENGTH, cols), lambda s, *_: (s, 0))
    result = pl.pallas_call(
        functools.partial(attend_kernel, heads, tensors, len(owned), part),
        grid_spec=pltpu.PrefetchScalarGridSpec(
            num_scalar_prefetch=1,
            grid=(seqs,),
            in_specs=[pl.BlockSpec(memory_space=pltpu.SMEM)]
            + [whole(p.shape) for p in pieces]
            + [whole(o.shape) for o in owned]
            + [whole((1, width))],
            out_specs=[whole((piece_rows, width))] * tensors
            + [by_seq(width), by_seq(3 * inner), by_seq(inner), by_seq(TILE), whole((width, 4 * inner))],
            scratch_shapes=[
                pltpu.VMEM((heads, LENGTH, LENGTH), F32),
                pltpu.VMEM((width, inner), BF16),
                pltpu.VMEM((rows, width), BF16),
                pltpu.VMEM((rows, width), BF16),
            ],
        ),
        out_shape=[jax.ShapeDtypeStruct((piece_rows, width), BF16)] * tensors
        + [
            jax.ShapeDtypeStruct((rows, width), BF16),
            jax.ShapeDtypeStruct((rows, 3 * inner), BF16),
            jax.ShapeDtypeStruct((rows, inner), BF16),
            jax.ShapeDtypeStruct((rows, TILE), F32),
            jax.ShapeDtypeStruct((width, 4 * inner), BF16),
        ],
        compiler_params=params(),
        cost_estimate=cost(8 * rows * width * inner + 4 * rows * LENGTH * inner, rows * width * 8, rows * LENGTH * heads),
        name="attend",
    )(places, bias, *pieces, *owned, gain)
    return result[:tensors], result[tensors:]


def attend_back_kernel(
    heads, tensors, part, place_ref, bias_ref, tok_ref, gain_ref, w_ref, qkv_ref, mixed_ref, log_ref, *refs
):
    refs = list(refs)
    pieces = [refs.pop(0) for _ in range(5)]
    gain_two_ref, router_ref = refs.pop(0), refs.pop(0)
    parts = [refs.pop(0) for _ in range(tensors)]
    own_ref, other_ref, weight_ref, gain_out, table, wo, gmix, gproj, near, far, rows_s, group, result, extras = refs
    inner = heads * HEAD_DIM
    blocks = LENGTH // TILE
    step_id = pl.program_id(0)

    @pl.when(step_id == 0)
    def _():
        fill_bias(bias_ref, table, heads)
        wo[...] = w_ref[:, 3 * inner :]
        near[...] = jnp.zeros_like(near)
        far[...] = jnp.zeros_like(far)
        weight_ref[...] = jnp.zeros_like(weight_ref)
        gain_out[...] = jnp.zeros_like(gain_out)
        group_halves(place_ref, group, pieces)

    here = pl.ds(pl.multiple_of(step_id * LENGTH, LENGTH), LENGTH)
    gmix[...] = dot(group[here, :], wo[...]).astype(BF16)
    for head in range(heads):
        at = head * HEAD_DIM
        query = (qkv_ref[:, at : at + HEAD_DIM] * HEAD_DIM ** (-0.5)).astype(BF16)
        key = qkv_ref[:, inner + at : inner + at + HEAD_DIM]
        value = qkv_ref[:, 2 * inner + at : 2 * inner + at + HEAD_DIM]
        grad_rows = gmix[:, at : at + HEAD_DIM]
        scores = dot(query, key, ROWS_NT) + table[head]
        attention = jnp.exp(scores - log_ref[:, head : head + 1])
        grad_weights = dot(grad_rows, value, ROWS_NT)
        inner_sum = jnp.sum(attention * grad_weights, axis=-1, keepdims=True)
        grad_scores = attention * (grad_weights - inner_sum)
        low = jnp.zeros((TILE, TILE), F32)
        high = jnp.zeros((TILE, TILE), F32)
        mid = [jnp.zeros((TILE, TILE), F32) for _ in range(3)]
        for i in range(blocks):
            for j in range(blocks):
                piece = grad_scores[i * TILE : (i + 1) * TILE, j * TILE : (j + 1) * TILE]
                if abs(j - i) <= 1:
                    mid[j - i + 1] = mid[j - i + 1] + piece
                elif j < i:
                    low = low + piece
                else:
                    high = high + piece
        for k in range(3):
            near[head * 3 + k] += mid[k]
        far[head * 2] += low
        far[head * 2 + 1] += high
        rounded = grad_scores.astype(BF16)
        gproj[:, at : at + HEAD_DIM] = (dot(rounded, key) * HEAD_DIM ** (-0.5)).astype(BF16)
        gproj[:, inner + at : inner + at + HEAD_DIM] = dot(rounded, query, ROWS_TN).astype(BF16)
        gproj[:, 2 * inner + at : 2 * inner + at + HEAD_DIM] = dot(
            attention.astype(BF16), grad_rows, ROWS_TN
        ).astype(BF16)
    unit, _ = unit_rows(tok_ref[...].astype(F32))
    normed = (unit * gain_ref[...]).astype(BF16)
    grad_normed = dot(gproj[...], w_ref[:, : 3 * inner], ROWS_NT)
    result[here, :] = grad_normed.astype(BF16)
    gain_out[...] += jnp.sum(grad_normed * unit, axis=0, keepdims=True)
    weight_ref[:, : 3 * inner] += dot(normed, gproj[...], ROWS_TN)
    weight_ref[:, 3 * inner :] += dot(group[here, :], mixed_ref[...], ROWS_TN)

    @pl.when(step_id == pl.num_programs(0) - 1)
    def _():
        part_halves(place_ref, parts, result)
        ids = [tile_bucket(step) for step in (-1, 0, 1)]
        for head in range(heads):
            for k in range(BUCKETS):
                total = jnp.zeros((TILE, TILE), F32)
                for step in (-1, 0, 1):
                    if k in tile_range(step):
                        total = total + jnp.where(ids[step + 1] == k, near[head * 3 + step + 1], 0.0)
                if k == 15:
                    total = total + far[head * 2]
                if k == 31:
                    total = total + far[head * 2 + 1]
                at = head * BUCKETS + k
                rows_s[at : at + 1, :] = jnp.sum(total, axis=0, keepdims=True)
        sums = jnp.sum(rows_s[...], axis=1, keepdims=True)
        experts = router_ref.shape[0]
        if part % 16 or part > TILE or experts % 16:
            own_ref[...] = jnp.broadcast_to(sums, own_ref.shape)
            return
        count = sums.shape[0]
        diagonal = lax.broadcasted_iota(jnp.int32, (count, TILE), 0) == lax.broadcasted_iota(
            jnp.int32, (count, TILE), 1
        )
        sums = jnp.sum(jnp.where(diagonal, sums, 0.0), axis=0, keepdims=True)
        z_count = own_ref.shape[0]
        owners = 2 * z_count
        gap = jnp.zeros((experts, TILE - part), F32)
        low = jnp.zeros((experts - 1, TILE), F32)
        rows = jnp.concatenate(
            [gain_out[...], gain_two_ref[...], jnp.zeros((experts - 2, gain_out.shape[1]), F32)], axis=0
        )
        for n in range(owners):
            cut = slice(n * part, (n + 1) * part)
            tiles = [router_ref[:, cut], gap, rows[:, cut], gap, jnp.concatenate([sums, low], axis=0)]
            tiles.append(jnp.zeros((experts, gain_out.shape[1] - 3 * TILE), F32))
            extras[n] = jnp.concatenate(tiles, axis=1).astype(BF16)
        for n, ref in enumerate((own_ref, other_ref)):
            for k in range(z_count):
                owner = place_ref[3] ^ (n * z_count + k)
                at = pl.multiple_of(owner * part, part)
                ref[k, :part, :] = weight_ref[pl.ds(at, part), :].astype(BF16)
                ref[k, part:, :] = extras[owner]


def attend_back(places, bias, tokens, gain, weights, projected, mixed, logs, pieces, gain_two, router, part, z_count):
    rows, width = tokens.shape
    tensors = rows // pieces[0].shape[0]
    piece = whole(pieces[0].shape)
    heads = bias.shape[0]
    inner = heads * HEAD_DIM
    seqs = rows // LENGTH
    by_seq = lambda cols: pl.BlockSpec((LENGTH, cols), lambda s, *_: (s, 0))
    experts = router.shape[0]
    sent = (z_count, part + experts, width)
    plain = part % 16 or part > TILE or experts % 16
    if plain:
        sent = (heads * BUCKETS, 1)
    result = pl.pallas_call(
        functools.partial(attend_back_kernel, heads, tensors, part),
        grid_spec=pltpu.PrefetchScalarGridSpec(
            num_scalar_prefetch=1,
            grid=(seqs,),
            in_specs=[
                pl.BlockSpec(memory_space=pltpu.SMEM),
                by_seq(width),
                whole((1, width)),
                whole((width, 4 * inner)),
                by_seq(3 * inner),
                by_seq(inner),
                by_seq(TILE),
            ]
            + [whole(p.shape) for p in pieces]
            + [whole((1, width)), whole((experts, width))],
            out_specs=[piece] * tensors
            + [whole(sent), whole(sent), whole((width, 4 * inner)), whole((1, width))],
            scratch_shapes=[
                pltpu.VMEM((heads, LENGTH, LENGTH), F32),
                pltpu.VMEM((width, inner), BF16),
                pltpu.VMEM((LENGTH, inner), BF16),
                pltpu.VMEM((LENGTH, 3 * inner), BF16),
                pltpu.VMEM((heads * 3, TILE, TILE), F32),
                pltpu.VMEM((heads * 2, TILE, TILE), F32),
                pltpu.VMEM((heads * BUCKETS, TILE), F32),
                pltpu.VMEM((rows, width), BF16),
                pltpu.VMEM((rows, width), BF16),
                pltpu.VMEM((2 * z_count, experts, width), BF16),
            ],
        ),
        out_shape=[jax.ShapeDtypeStruct(pieces[0].shape, BF16)] * tensors
        + [
            jax.ShapeDtypeStruct(sent, F32 if plain else BF16),
            jax.ShapeDtypeStruct(sent, F32 if plain else BF16),
            jax.ShapeDtypeStruct((width, 4 * inner), F32),
            jax.ShapeDtypeStruct((1, width), F32),
        ],
        compiler_params=params(),
        cost_estimate=cost(18 * rows * width * inner + 10 * rows * LENGTH * inner, rows * width * 12, rows * LENGTH * heads),
        name="attend_back",
    )(places, bias, tokens, gain, weights, projected, mixed, logs, *pieces, gain_two, router)
    return result[:tensors], result[tensors:]


def first_rows_kernel(count, *refs):
    out_ref = refs[-1]
    at = 0
    for ref in refs[:-1]:
        for n in range(ref.shape[0]):
            out_ref[at] = ref[n, :count, :]
            at += 1


def first_rows(pieces, start, extra, count):
    width = pieces[0].shape[-1]
    total = sum(piece.shape[0] for piece in pieces)
    return pl.pallas_call(
        functools.partial(first_rows_kernel, count),
        grid=(1,),
        in_specs=[
            pl.BlockSpec((piece.shape[0], extra, width), lambda i: (0, start // extra, 0)) for piece in pieces
        ],
        out_specs=whole((total, count, width)),
        out_shape=jax.ShapeDtypeStruct((total, count, width), BF16),
        compiler_params=params(),
        cost_estimate=cost(0, 4 * total * extra * width),
        name="first_rows",
    )(*pieces)


def place_rows(target_ref, rows, out_refs):
    at = 0
    for ref in out_refs:
        count = ref.shape[0]
        index = lax.broadcasted_iota(jnp.int32, (count, rows.shape[0]), 0) + at
        chosen = jnp.where(index == target_ref[...], 1.0, 0.0).astype(BF16)
        ref[...] = dot(chosen, rows).astype(BF16)
        at += count


def place_kernel(target_ref, rows_ref, *out_refs):
    place_rows(target_ref, rows_ref[...], out_refs)


def place(target_row, rows, counts):
    return pl.pallas_call(
        place_kernel,
        out_shape=[jax.ShapeDtypeStruct((count, rows.shape[1]), BF16) for count in counts],
        compiler_params=params(),
        cost_estimate=cost(2 * sum(counts) * rows.size, 4 * rows.size),
        name="place",
    )(target_row, rows)


def softmax_rows(logits):
    exponent = jnp.exp(logits - jnp.max(logits, axis=-1, keepdims=True))
    return exponent * (1.0 / jnp.sum(exponent, axis=-1, keepdims=True))


def sum_pieces(refs):
    total = refs[0][...].astype(F32)
    for ref in refs[1:]:
        total = total + ref[...].astype(F32)
    return total


def route_kernel(tok_ref, *refs):
    gain_ref, router_ref, target_ref, index_ref, kept_ref, hidden_ref, gate_ref = refs[6:13]
    half = tok_ref.shape[0] // 2
    for h in range(2):
        keep, got, last = refs[3 * h : 3 * h + 3]
        here = slice(h * half, (h + 1) * half)
        added = keep[:half, :].astype(F32) + got[:half, :].astype(F32) + last[...].astype(F32)
        hidden_ref[here, :] = tok_ref[here, :].astype(F32) + added
    hidden = hidden_ref[...]
    unit, _ = unit_rows(hidden)
    moe_in = (unit * gain_ref[...]).astype(BF16)
    place_rows(target_ref, moe_in, refs[13:])
    probs = softmax_rows(dot(moe_in, router_ref[...]))
    lanes = lax.broadcasted_iota(jnp.int32, probs.shape, 1)
    picked = jnp.sum(jnp.where(lanes == index_ref[...], probs, 0.0), axis=-1, keepdims=True)
    gate_ref[...] = picked * kept_ref[...].astype(F32)


def route(tokens, attn, gain, router, target_row, index_col, kept_col, counts):
    rows, width = tokens.shape
    result = pl.pallas_call(
        route_kernel,
        out_shape=[
            jax.ShapeDtypeStruct((rows, width), F32),
            jax.ShapeDtypeStruct((rows, 1), F32),
        ]
        + [jax.ShapeDtypeStruct((count, width), BF16) for count in counts],
        compiler_params=params(),
        cost_estimate=cost(2 * sum(counts) * rows * width, 12 * rows * width),
        name="route",
    )(tokens, *attn, gain, router, target_row, index_col, kept_col)
    return result[0], result[1], result[2:]


def rest_choice(blocks, locals_, rest, expert):
    rows = lax.broadcasted_iota(jnp.int32, (blocks * rest, blocks * locals_ * rest), 0)
    cols = lax.broadcasted_iota(jnp.int32, (blocks * rest, blocks * locals_ * rest), 1)
    block = lax.div(rows, rest)
    wanted = block * (locals_ * rest) + expert * rest + (rows - block * rest)
    return jnp.where(cols == wanted, 1.0, 0.0).astype(BF16)


def pick_rows(out_ref, views, choice, main_rows, main, expert):
    at = 0
    pieces = []
    for view in views:
        blocks, size, width = view.shape
        if main:
            start = pl.multiple_of(expert * main, main)
            out_ref[at : at + blocks * main, :] = view[:, pl.ds(start, main), :].reshape(blocks * main, width)
            at += blocks * main
        rest = size - size * main_rows // out_ref.shape[0]
        pieces.append(view[:, size - rest :, :].reshape(blocks * rest, width))
    out_ref[main_rows:, :] = dot(choice, jnp.concatenate(pieces, axis=0)).astype(BF16)


def put_rows(views, value_ref, choice, main_rows, main, locals_, rest, expert):
    at = 0
    spread = dot(choice, value_ref[main_rows:, :], ROWS_TN).astype(BF16)
    rest_at = 0
    for view in views:
        blocks, _, width = view.shape
        if main:
            count = blocks * main
            start = pl.multiple_of(expert * main, main)
            view[:, pl.ds(start, main), :] = value_ref[at : at + count, :].reshape(blocks, main, width)
            at += count
        part = spread[rest_at : rest_at + blocks * locals_ * rest].reshape(blocks, locals_ * rest, width)
        rest_at += blocks * locals_ * rest

        before = view[:, locals_ * main :, :]
        view[:, locals_ * main :, :] = part + jnp.where(expert > 0, before, jnp.zeros_like(before))


def group_views(place_ref, ref, tensors, chunks):
    size = ref.shape[1] // chunks
    views = []
    for k in range(chunks):
        a, b = HOPS[k % 2]
        views += [ref.at[place_ref[2] ^ j, k * size : (k + 1) * size] for j in (0, a, b, a | b)]
    return views


def join_halves(place_ref, own_in, peer_in, own_out, peer_out, win, wout):
    half = own_in.shape[1]
    mine = pl.multiple_of(place_ref[0] * half, half)
    other = pl.multiple_of((1 - place_ref[0]) * half, half)
    if win is not None:
        win[pl.ds(mine, half), :] = own_in[0]
        win[pl.ds(other, half), :] = peer_in[0]
    half_out = own_out.shape[2]
    mine = pl.multiple_of(place_ref[0] * half_out, half_out)
    other = pl.multiple_of((1 - place_ref[0]) * half_out, half_out)
    wout[:, pl.ds(mine, half_out)] = own_out[0]
    wout[:, pl.ds(other, half_out)] = peer_out[0]


def expert_kernel(chunks, tensors, main, locals_, rest, place_ref, *refs):
    refs = list(refs)
    take = lambda n: [refs.pop(0) for _ in range(n)]
    xs = take(3 * chunks)
    (g_ref,) = take(1)
    own_in, peer_in, own_out, peer_out, router = take(5)
    backs = take(2 * chunks)
    x_ref, ge_ref, hid_ref, gi_ref, gl_ref = take(5)
    win, wout, grows, inner, gunits, gate_s, dots, back = take(8)
    expert = pl.program_id(0)
    blocks = sum(ref.shape[0] for ref in xs)
    main_rows = blocks * main
    rows, width = x_ref.shape[1:]
    wide = win.shape[1]
    choice = rest_choice(blocks, locals_, rest, expert)
    many = xs[0].shape[0]
    back_refs = []
    for k in range(chunks):
        keep, send = backs[2 * k : 2 * k + 2]
        back_refs += [ref.at[n * many : (n + 1) * many] for n in range(2) for ref in (keep, send)]
    pick_rows(x_ref.at[0], xs, choice, main_rows, main, expert)
    pick_rows(grows, group_views(place_ref, g_ref, tensors, chunks), choice, main_rows, main, expert)
    join_halves(place_ref, own_in, peer_in, own_out, peer_out, win, wout)
    probs = softmax_rows(dot(x_ref[0], router[...]))
    lanes = lax.broadcasted_iota(jnp.int32, probs.shape, 1)
    mine = lanes == place_ref[1] * locals_ + expert
    picked = jnp.sum(jnp.where(mine, probs, 0.0), axis=-1, keepdims=True)
    gate_s[...] = jnp.broadcast_to(picked, gate_s.shape)
    chunk = 16
    half_wide = wide // 2 if wide % (2 * TILE) == 0 else wide
    half_rows = rows // 2

    def multiply(part):
        at = slice(part * half_rows, (part + 1) * half_rows)
        inner[at, :] = dot(x_ref[0, at, :], win[...])
        gunits[at, :] = dot(grows[at, :], wout[...], ROWS_NT)

    def activate(part):
        for row in range(part * half_rows, (part + 1) * half_rows, chunk):
            at = slice(row, row + chunk)
            gate_tile = gate_s[at, :]
            gate = jnp.concatenate([gate_tile] * (half_wide // TILE), axis=1)
            total = None
            for start in range(0, wide, half_wide):
                lanes_at = slice(start, start + half_wide)
                value = inner[at, lanes_at]
                square = value * value
                wave = jnp.tanh(value * (GELU_A + (GELU_A * GELU_B) * square))
                half = 0.5 + 0.5 * wave
                hidden = (value * half).astype(BF16)
                bend = value * (0.5 * GELU_A + (1.5 * GELU_A * GELU_B) * square)
                slope = half + bend * (1.0 - wave * wave)
                units = gunits[at, lanes_at]
                hid_ref[0, at, lanes_at] = hidden
                gi_ref[0, at, lanes_at] = (gate * (units * slope)).astype(BF16)
                product = hidden.astype(F32) * units
                for tile in range(0, half_wide, TILE):
                    part_sum = product[:, tile : tile + TILE]
                    total = part_sum if total is None else total + part_sum
            dots[at, :] = total
            gate = jnp.concatenate([gate_tile] * (width // TILE), axis=1)
            ge_ref[0, at, :] = (gate * grows[at, :].astype(F32)).astype(BF16)

    def finish(part):
        at = slice(part * half_rows, (part + 1) * half_rows)
        grad_logits = (
            jnp.sum(dots[at, :], axis=-1, keepdims=True)
            * probs[at]
            * (jnp.where(mine[at], 1.0, 0.0) - picked[at])
        ).astype(BF16)
        gl_ref[0, at, :] = grad_logits
        back[at, :] = (
            dot(gi_ref[0, at, :], win[...], ROWS_NT) + dot(grad_logits, router[...], ROWS_NT)
        ).astype(BF16)

    multiply(0)
    multiply(1)
    activate(0)
    finish(0)
    activate(1)
    finish(1)
    put_rows(back_refs, back, choice, main_rows, main, locals_, rest, expert)


def expert_forward_back(places, xs, gs, own_in, peer_in, own_out, peer_out, router, main, rest, chunks):
    locals_, half, wide = own_in.shape
    width, experts = router.shape
    many, block = xs[0].shape[:2]
    tensors = gs.shape[0]
    blocks = tensors * chunks * many
    back = (2 * many, block, width)
    rows = blocks * (main + rest)
    per = lambda *shape: pl.BlockSpec((1,) + shape, lambda e, *_: (e, 0, 0))
    saved = jax.ShapeDtypeStruct((locals_, rows, width), BF16)
    saved_wide = jax.ShapeDtypeStruct((locals_, rows, wide), BF16)
    result = pl.pallas_call(
        functools.partial(expert_kernel, chunks, tensors, main, locals_, rest),
        grid_spec=pltpu.PrefetchScalarGridSpec(
            num_scalar_prefetch=1,
            grid=(locals_,),
            in_specs=[whole(x.shape) for x in xs]
            + [whole(gs.shape)]
            + [per(half, wide)] * 2 + [per(wide, half)] * 2 + [whole((width, experts))],
            out_specs=[whole(back)] * (2 * chunks)
            + [per(rows, width), per(rows, width), per(rows, wide), per(rows, wide), per(rows, experts)],
            scratch_shapes=[
                pltpu.VMEM((width, wide), BF16),
                pltpu.VMEM((wide, width), BF16),
                pltpu.VMEM((rows, width), BF16),
                pltpu.VMEM((rows, wide), F32),
                pltpu.VMEM((rows, wide), F32),
                pltpu.VMEM((rows, TILE), F32),
                pltpu.VMEM((rows, TILE), F32),
                pltpu.VMEM((rows, width), BF16),
            ],
        ),
        out_shape=[jax.ShapeDtypeStruct(back, BF16)] * (2 * chunks)
        + [saved, saved, saved_wide, saved_wide, jax.ShapeDtypeStruct((locals_, rows, experts), BF16)],
        compiler_params=params(),
        cost_estimate=cost(6 * locals_ * rows * width * wide, locals_ * rows * width * 14, locals_ * rows * wide),
        name="experts",
    )(places, *xs, gs, own_in, peer_in, own_out, peer_out, router)
    return result[: 2 * chunks], result[2 * chunks :]


def expert_rows_kernel(chunks, main, locals_, rest, place_ref, hid_ref, own_out, peer_out, forward_ref, wout, value):
    expert = pl.program_id(0)
    tensors = forward_ref.shape[0]
    blocks = tensors * forward_ref.shape[1]
    choice = rest_choice(blocks, locals_, rest, expert)
    join_halves(place_ref, own_out, peer_out, own_out, peer_out, None, wout)
    value[...] = dot(hid_ref[0], wout[...]).astype(BF16)
    views = group_views(place_ref, forward_ref, tensors, chunks)
    put_rows(views, value, choice, blocks * main, main, locals_, rest, expert)


def expert_rows(places, hidden, own_out, peer_out, shape, main, rest, chunks):
    locals_, rows, wide = hidden.shape
    half = own_out.shape[2]
    width = shape[-1]
    per = lambda *shape: pl.BlockSpec((1,) + shape, lambda e, *_: (e, 0, 0))
    return pl.pallas_call(
        functools.partial(expert_rows_kernel, chunks, main, locals_, rest),
        grid_spec=pltpu.PrefetchScalarGridSpec(
            num_scalar_prefetch=1,
            grid=(locals_,),
            in_specs=[per(rows, wide)] + [per(wide, half)] * 2,
            out_specs=whole(shape),
            scratch_shapes=[pltpu.VMEM((wide, width), BF16), pltpu.VMEM((rows, width), BF16)],
        ),
        out_shape=jax.ShapeDtypeStruct(shape, BF16),
        compiler_params=params(),
        cost_estimate=cost(2 * locals_ * rows * width * wide, locals_ * rows * width * 6),
        name="expert_rows",
    )(places, hidden, own_out, peer_out)


def expert_weights_kernel(place_ref, x_ref, ge_ref, hid_ref, gi_ref, gl_ref, *refs):
    in_own, in_send, out_own, out_send, router_ref = refs
    half = in_own.shape[1]
    mine = pl.ds(pl.multiple_of(place_ref[0] * half, half), half)
    other = pl.ds(pl.multiple_of((1 - place_ref[0]) * half, half), half)
    in_own[0] = dot(x_ref[0, :, mine], gi_ref[0], ROWS_TN)
    in_send[0] = dot(x_ref[0, :, other], gi_ref[0], ROWS_TN).astype(BF16)
    out_own[0] = dot(hid_ref[0], ge_ref[0, :, mine], ROWS_TN)
    out_send[0] = dot(hid_ref[0], ge_ref[0, :, other], ROWS_TN).astype(BF16)

    @pl.when(pl.program_id(0) == 0)
    def _():
        router_ref[...] = jnp.zeros_like(router_ref)

    router_ref[...] += dot(gl_ref[0], x_ref[0], ROWS_TN)


def expert_weights(places, saved, half):
    x, ge, hidden, gi, gl = saved
    locals_, rows, width = x.shape
    wide = hidden.shape[2]
    experts = gl.shape[2]
    per = lambda *shape: pl.BlockSpec((1,) + shape, lambda e, *_: (e, 0, 0))
    return pl.pallas_call(
        expert_weights_kernel,
        grid_spec=pltpu.PrefetchScalarGridSpec(
            num_scalar_prefetch=1,
            grid=(locals_,),
            in_specs=[per(rows, width), per(rows, width), per(rows, wide), per(rows, wide), per(rows, experts)],
            out_specs=[per(half, wide), per(half, wide), per(wide, half), per(wide, half), whole((experts, width))],
        ),
        out_shape=[
            jax.ShapeDtypeStruct((locals_, half, wide), F32),
            jax.ShapeDtypeStruct((locals_, half, wide), BF16),
            jax.ShapeDtypeStruct((locals_, wide, half), F32),
            jax.ShapeDtypeStruct((locals_, wide, half), BF16),
            jax.ShapeDtypeStruct((experts, width), F32),
        ],
        compiler_params=params(),
        cost_estimate=cost(4 * locals_ * rows * width * wide, locals_ * rows * width * 14),
        name="expert_weights",
    )(places, x, ge, hidden, gi, gl)


def take_rows(target_ref, refs):
    total, at = None, 0
    for ref in refs:
        count = ref.shape[0]
        cols = lax.broadcasted_iota(jnp.int32, (target_ref.shape[0], count), 1) + at
        chosen = jnp.where(cols == target_ref[...], 1.0, 0.0).astype(BF16)
        part = dot(chosen, ref[...])
        total = part if total is None else total + part
        at += count
    return total


def hidden_back_kernel(target_ref, *refs):
    hidden_ref, cot_ref, gain_ref, grad_ref, attn_ref, gain_out = refs[-6:]
    grad_in = take_rows(target_ref, refs[:-6])
    unit, scale = unit_rows(hidden_ref[...])
    gained = jnp.sum(grad_in * unit, axis=0, keepdims=True)
    gain_out[...] = gained + jnp.where(pl.program_id(0) > 0, gain_out[...], jnp.zeros_like(gained))
    scaled = grad_in * gain_ref[...]
    inside = jnp.mean(unit * scaled, axis=-1, keepdims=True)
    grad = cot_ref[...].astype(F32) + scale * (scaled - unit * inside)
    grad_ref[...] = grad
    attn_ref[...] = grad.astype(BF16)


def hidden_back(target_col, back, hidden, cotangent, gain):
    rows, width = hidden.shape
    steps = 3 if rows % 48 == 0 else 1
    by_row = lambda cols: pl.BlockSpec((rows // steps, cols), lambda i: (i, 0))
    return pl.pallas_call(
        hidden_back_kernel,
        grid=(steps,),
        in_specs=[by_row(1)] + [whole(b.shape) for b in back] + [by_row(width), by_row(width), whole((1, width))],
        out_specs=[by_row(width), by_row(width), whole((1, width))],
        out_shape=[
            jax.ShapeDtypeStruct((rows, width), F32),
            jax.ShapeDtypeStruct((rows, width), BF16),
            jax.ShapeDtypeStruct((1, width), F32),
        ],
        compiler_params=params(),
        cost_estimate=cost(3 * rows * rows * width, 16 * rows * width),
        name="hidden_back",
    )(target_col, *back, hidden, cotangent, gain)


def output_kernel(target_ref, *refs):
    hidden_ref, gate_ref, out_ref = refs[-3:]
    out_ref[...] = (hidden_ref[...] + gate_ref[...] * take_rows(target_ref, refs[:-3])).astype(BF16)


def output_rows(target_col, expert_rows, hidden, gate):
    return pl.pallas_call(
        output_kernel,
        out_shape=jax.ShapeDtypeStruct(hidden.shape, BF16),
        compiler_params=params(),
        cost_estimate=cost(3 * hidden.shape[0] * hidden.size, 10 * hidden.size),
        name="output_rows",
    )(target_col, *expert_rows, hidden, gate)


def tokens_back_kernel(tok_ref, *refs):
    gain_ref, hidden_ref, out_ref = refs[6:]
    half = tok_ref.shape[0] // 2
    for h in range(2):
        keep, got, last = refs[3 * h : 3 * h + 3]
        here = slice(h * half, (h + 1) * half)
        unit, scale = unit_rows(tok_ref[here, :].astype(F32))
        grad = keep[:half, :].astype(F32) + got[:half, :].astype(F32) + last[...].astype(F32)
        scaled = grad * gain_ref[...]
        inside = jnp.mean(unit * scaled, axis=-1, keepdims=True)
        out_ref[here, :] = hidden_ref[here, :] + scale * (scaled - unit * inside)


def tokens_back(tokens, grad_normed, gain, grad_hidden):
    return pl.pallas_call(
        tokens_back_kernel,
        out_shape=jax.ShapeDtypeStruct(tokens.shape, F32),
        compiler_params=params(),
        cost_estimate=cost(10 * tokens.size, 12 * tokens.size),
        name="tokens_back",
    )(tokens, *grad_normed, gain, grad_hidden)


def shifted(value, axis, count, step):
    return lax.ppermute(value, axis, [(s, (s + step) % count) for s in range(count)])


def gather_ring(value, axis, count):
    me = lax.axis_index(axis)
    parts = [value] + [shifted(value, axis, count, -k) for k in range(1, count)]
    return jnp.roll(jnp.stack(parts), me, axis=0)


def swapped(value, axis, count, bits):
    return lax.ppermute(value, axis, [(s, s ^ bits) for s in range(count)])


def gather_pieces(value, axis, count):
    return [value] + [swapped(value, axis, count, k) for k in range(1, count)]


def gather_hops(value, hops):
    a, b = hops
    first = swapped(value, "tensor", 4, a)
    second = swapped(jnp.concatenate([value, first], axis=0), "tensor", 4, b)
    return first, second


def sum_hops(parts):
    half = parts[0].shape[0] // 2
    result = []
    for h, (a, b) in enumerate(HOPS):
        keep, send = parts[2 * h : 2 * h + 2]
        got = swapped(send, "tensor", 4, a)
        last = swapped(added(keep[half:], got[half:]), "tensor", 4, b)
        result += [keep, got, last]
    return result


def added(a, b):
    return (a.astype(F32) + b.astype(F32)).astype(BF16)


def swap_pieces(pieces, axis, count):
    return [pieces[0]] + [swapped(pieces[k], axis, count, k) for k in range(1, count)]


def on_device(
    sizes,
    tokens,
    cotangent,
    query_key_value_weight,
    attention_output_weight,
    rel_bias,
    gain_attn,
    gain_moe,
    w_router,
    w_in,
    w_out,
    expert_index,
    slot_index,
    kept_mask,
):
    dp_count, z_count, t_count = sizes
    tok_rows, width = tokens.shape
    experts_all = w_router.shape[1]
    capacity = max(2, 3 * tok_rows // (2 * experts_all))
    locals_ = w_in.shape[0]
    main = capacity // 16 * 16
    rest = capacity - main
    block = locals_ * capacity
    heads = rel_bias.shape[0]
    inner = heads * HEAD_DIM
    part = query_key_value_weight.shape[1]
    fine = w_router.shape[0]
    my_dp = lax.axis_index("dp")
    my_z = lax.axis_index("expert")
    bias = rel_bias.astype(F32)

    my_t = lax.axis_index("tensor")
    owners = dp_count * z_count
    my_owner = my_dp * z_count + my_z
    places = jnp.stack([my_dp, my_z, my_t, my_owner]).astype(jnp.int32)
    half_rows = tok_rows // 2
    token_pieces = [tokens]
    for h, hops in enumerate(HOPS):
        token_pieces += list(gather_hops(tokens[h * half_rows : (h + 1) * half_rows], hops))

    small = jnp.concatenate([gain_attn[:, None], gain_moe[:, None], w_router], axis=1).reshape(-1)
    extra = -(-small.shape[0] // (16 * width)) * 16
    packed = jnp.concatenate(
        [
            query_key_value_weight.transpose(1, 0, 2).reshape(part, 3 * inner),
            attention_output_weight.T,
        ],
        axis=1,
    )
    packed = jnp.concatenate(
        [packed, jnp.pad(small, (0, extra * width - small.shape[0])).reshape(extra, width)], axis=0
    )
    owned = gather_pieces(packed[None], "expert", z_count)
    owned = owned + [swapped(jnp.concatenate(owned, axis=0), "dp", dp_count, 1)]
    if part % 16 or part % extra:
        smalls = jnp.concatenate(owned, axis=0)[:, part:]
    else:
        smalls = first_rows(owned, part, extra, -(-small.shape[0] // width))
    smalls = smalls.reshape(owners, -1)[:, : small.shape[0]]
    small_pieces = gather_pieces(smalls, "tensor", t_count)

    z_of = expert_index // locals_
    local = expert_index - z_of * locals_
    inside = jnp.where(
        slot_index < main, local * main + slot_index, locals_ * main + local * rest + slot_index - main
    )
    target = (z_of ^ my_z) * block + inside
    target = jnp.where(kept_mask > 0, target, -1)
    target_row, target_col = target[None, :], target[:, None]
    chunks = min(z_count, 4)
    many = z_count // chunks
    counts = [many * block] * chunks
    grad_sent = place(target_row, cotangent, counts)
    token_pieces, owned, small_pieces, grad_sent = lax.optimization_barrier(
        (token_pieces, owned, small_pieces, grad_sent)
    )
    smalls = jnp.stack(small_pieces).reshape(t_count * owners, -1)
    owner_ids = jnp.arange(owners, dtype=jnp.int32)[:, None] ^ my_owner
    t_ids = jnp.arange(t_count, dtype=jnp.int32)[None, :] ^ my_t
    smalls = smalls[(t_ids * owners + owner_ids).reshape(-1)].reshape(width, 2 + experts_all)
    if part % 16:
        order = jnp.arange(owners, dtype=jnp.int32) ^ my_owner
        owned = [jnp.concatenate(owned, axis=0)[:, :part][order].reshape(1, width, 4 * inner)]
    rows_owned = part if len(owned) > 1 else width
    gain_one = smalls[:, 0].astype(F32)[None]
    gain_two = smalls[:, 1].astype(F32)[None]
    router = smalls[:, 2:]

    def over_expert(groups):
        if many > 1:
            groups = [g[i * block : (i + 1) * block] for g in groups for i in range(many)]
        pieces = swap_pieces(groups, "expert", z_count)
        if many == 1:
            return pieces
        return [jnp.concatenate(pieces[k * many : (k + 1) * many], axis=0) for k in range(chunks)]

    grad_rows = jnp.concatenate(over_expert(grad_sent), axis=0)
    parts, (group_tokens, projected, mixed, logs, weights) = attend(
        places, bias, token_pieces, owned, rows_owned, gain_one
    )
    parts, late_in, late_out, grad_rows = lax.optimization_barrier((parts, w_in, w_out, grad_rows))
    peer_in = shifted(late_in, "dp", dp_count, 1)
    peer_out = shifted(late_out, "dp", dp_count, 1)
    grad_arrived = lax.all_gather(grad_rows, "tensor", axis=0).reshape(t_count, z_count, block, width)
    attn = sum_hops(parts)
    attn, peer_in, peer_out = lax.optimization_barrier((attn, peer_in, peer_out))
    hidden_one, gate, sent = route(
        tokens, attn, gain_two, router, target_row, expert_index[:, None], kept_mask[:, None], counts
    )
    arrived = []
    for k, group in enumerate(over_expert(sent)):
        pieces = (group,) + gather_hops(group, HOPS[k % 2])
        arrived += [piece.reshape(-1, block, width) for piece in pieces]
    back_parts, saved = expert_forward_back(
        places, arrived, grad_arrived, w_in, peer_in, w_out, peer_out, router, main, rest, chunks
    )

    size = many * block
    back_parts = [piece.reshape(2 * size, width) for piece in back_parts]
    keeps, sends = back_parts[::2], back_parts[1::2]
    got = [swapped(sends[k], "tensor", t_count, HOPS[k % 2][0]) for k in reversed(range(chunks))][::-1]
    forward_part = expert_rows(places, saved[2], w_out, peer_out, grad_arrived.shape, main, rest, chunks)
    got, forward_part = lax.optimization_barrier((got, forward_part))
    groups = []
    for k in range(chunks):
        last = swapped(added(keeps[k][size:], got[k][size:]), "tensor", t_count, HOPS[k % 2][1])
        total = keeps[k][:size].astype(F32) + got[k][:size].astype(F32) + last.astype(F32)
        groups.append(total.astype(BF16))
    forward_part, groups, saved = lax.optimization_barrier((forward_part, groups, saved))
    forward_sum = lax.psum_scatter(
        forward_part.reshape(t_count * z_count * block, width), "tensor", scatter_dimension=0, tiled=True
    )
    in_own, in_send, out_own, out_send, router_part = expert_weights(places, saved, w_in.shape[1])
    grad_back, in_send, out_send = lax.optimization_barrier((over_expert(groups), in_send, out_send))
    in_got = shifted(in_send, "dp", dp_count, 1)
    out_got = shifted(out_send, "dp", dp_count, 1)
    grad_hidden, grad_attn, gain_two_part = hidden_back(target_col, grad_back, hidden_one, cotangent, gain_two)
    grad_pieces = [grad_attn]
    for h, hops in enumerate(HOPS):
        grad_pieces += list(gather_hops(grad_attn[h * half_rows : (h + 1) * half_rows], hops))
    grad_w_in = in_own + in_got.astype(F32)
    grad_w_out = out_own + out_got.astype(F32)
    grad_pieces, grad_w_in, grad_w_out, forward_sum = lax.optimization_barrier(
        (grad_pieces, grad_w_in, grad_w_out, forward_sum)
    )
    normed_parts, (own_part, other_part, weight_part, gain_one_part) = attend_back(
        places, bias, group_tokens, gain_one, weights, projected, mixed, logs, grad_pieces,
        gain_two_part, router_part, part, z_count,
    )
    forward_rows = over_expert(list(forward_sum.reshape(chunks, many * block, width)))
    normed_parts, own_part, other_part, forward_rows = lax.optimization_barrier(
        (normed_parts, own_part, other_part, forward_rows)
    )
    grad_normed = sum_hops(normed_parts)
    output = output_rows(target_col, forward_rows, hidden_one, gate)
    grad_tokens = tokens_back(tokens, grad_normed, gain_one, grad_hidden)

    if part % 16 or part > TILE or experts_all % 16:
        pad = lambda value, lanes: jnp.pad(value, ((0, 0), (0, lanes - value.shape[1])))
        gains = jnp.concatenate([gain_one_part, gain_two_part, jnp.zeros((experts_all - 2, width), F32)])
        sums = jnp.pad(own_part.reshape(1, -1), ((0, experts_all - 1), (0, TILE - own_part.shape[0])))
        extras = [
            pad(jnp.concatenate([pad(router_part[:, cut], TILE), pad(gains[:, cut], TILE), sums], axis=1), width)
            for cut in (slice(n * part, (n + 1) * part) for n in range(owners))
        ]
        order = jnp.arange(owners, dtype=jnp.int32) ^ my_owner
        payload = jnp.concatenate(
            [weight_part.astype(BF16).reshape(owners, part, width), jnp.stack(extras).astype(BF16)], axis=1
        )[order]
        own_part, other_part = payload[:z_count], payload[z_count:]
    other_got = shifted(other_part, "dp", dp_count, 1)
    pieces = swap_pieces([added(own_part[k], other_got[k]) for k in range(z_count)], "expert", z_count)
    total = pieces[0].astype(F32)
    for piece in pieces[1:]:
        total = total + piece.astype(F32)
    weight_total = total[:part].reshape(part, 4, inner)
    grad_w_qkv = weight_total[:, :3].transpose(1, 0, 2)
    grad_w_attn_out = weight_total[:, 3].T
    grad_rel_bias = total[part, 2 * TILE : 2 * TILE + heads * BUCKETS].reshape(heads, BUCKETS)
    mine = jnp.concatenate([total[part : part + 2, TILE : TILE + part], total[part:, :part]], axis=0)
    turned = [
        lax.dynamic_slice_in_dim(mine, (my_t ^ k) * fine, fine, axis=1).reshape(-1) for k in range(t_count)
    ]
    left = turned[0]
    for piece in swap_pieces(turned, "tensor", t_count)[1:]:
        left = left + piece
    grad_gain_attn = left[:fine]
    grad_gain_moe = left[fine : 2 * fine]
    grad_w_router = left[2 * fine :].reshape(experts_all, fine).T
    return (
        output,
        grad_tokens,
        grad_w_qkv,
        grad_w_attn_out,
        grad_rel_bias,
        grad_gain_attn,
        grad_gain_moe,
        grad_w_router,
        grad_w_in,
        grad_w_out,
    )


def solution(mesh):
    placed = (
        P(("dp", "expert", "tensor"), None),
        P(("dp", "expert", "tensor"), None),
        P(None, ("dp", "expert"), "tensor"),
        P("tensor", ("dp", "expert")),
        P("tensor", None),
        P(("dp", "expert", "tensor")),
        P(("dp", "expert", "tensor")),
        P(("dp", "expert", "tensor"), None),
        P("expert", "dp", "tensor"),
        P("expert", "tensor", "dp"),
        P(("dp", "expert", "tensor")),
        P(("dp", "expert", "tensor")),
        P(("dp", "expert", "tensor")),
    )
    sizes = tuple(mesh.shape[name] for name in ("dp", "expert", "tensor"))
    return jax.shard_map(
        functools.partial(on_device, sizes),
        mesh=mesh,
        in_specs=placed,
        out_specs=(
            P(("dp", "expert", "tensor"), None),
            P(("dp", "expert", "tensor"), None),
            P(None, ("dp", "expert"), "tensor"),
            P("tensor", ("dp", "expert")),
            P("tensor", None),
            P(("dp", "expert", "tensor")),
            P(("dp", "expert", "tensor")),
            P(("dp", "expert", "tensor"), None),
            P("expert", "dp", "tensor"),
            P("expert", "tensor", "dp"),
        ),
        check_vma=False,
    )
```

```python
import functools

import jax
import jax.numpy as jnp
from jax import lax
from jax.experimental import pallas as pl
from jax.experimental.pallas import tpu as pltpu
from jax.sharding import PartitionSpec as P

HEAD_DIM = 64
BUCKETS = 32
LENGTH = 512
TILE = 128
BLOCK = 32
EPSILON = 1e-06
BORDERS = (12, 16, 23, 32, 46, 64, 91)
F32 = jnp.float32
BF16 = jnp.bfloat16
GELU_A = 0.7978845608028654
GELU_B = 0.044715
ROWS_NN = (((1,), (0,)), ((), ()))
ROWS_NT = (((1,), (1,)), ((), ()))
ROWS_TN = (((0,), (0,)), ((), ()))
VMEM_BYTES = 56 * 1024 * 1024


def dot(a, b, dims=ROWS_NN):
    return lax.dot_general(a, b, dims, preferred_element_type=F32)


def params(**more):
    return pltpu.CompilerParams(vmem_limit_bytes=VMEM_BYTES, **more)


def cost(flops, moved, special=0):
    return pl.CostEstimate(flops=int(flops), bytes_accessed=int(moved), transcendentals=int(special))


def whole(shape):
    return pl.BlockSpec(shape, lambda *_: (0,) * len(shape))


def tile_bucket(step):
    rows = lax.broadcasted_iota(jnp.int32, (TILE, TILE), 0)
    cols = lax.broadcasted_iota(jnp.int32, (TILE, TILE), 1)
    offset = cols - rows + step * TILE
    distance = jnp.abs(offset)
    bucket = jnp.minimum(distance, 8)
    for border in BORDERS:
        bucket = bucket + jnp.where(distance >= border, 1, 0)
    return bucket + jnp.where(offset > 0, 16, 0)


def tile_range(step):
    return {-1: range(1, 16), 0: range(0, 32), 1: range(17, 32)}[step]


def fill_bias(bias_ref, table, heads):
    blocks = LENGTH // TILE
    buckets = {step: tile_bucket(step) for step in (-1, 0, 1)}
    for head in range(heads):
        near = {}
        for step in (-1, 0, 1):
            value = jnp.zeros((TILE, TILE), F32)
            for k in tile_range(step):
                value = jnp.where(buckets[step] == k, bias_ref[head, k], value)
            near[step] = value
        low = jnp.full((TILE, TILE), bias_ref[head, 15], F32)
        high = jnp.full((TILE, TILE), bias_ref[head, 31], F32)
        for i in range(blocks):
            for j in range(blocks):
                step = j - i
                value = near[step] if abs(step) <= 1 else (low if step < 0 else high)
                table[head, i * TILE : (i + 1) * TILE, j * TILE : (j + 1) * TILE] = value


def unit_rows(values):
    scale = lax.rsqrt(jnp.mean(values * values, axis=-1, keepdims=True) + EPSILON)
    return values * scale, scale


HOPS = ((1, 2), (2, 1))


def group_halves(place_ref, out, pieces):
    rows = pieces[0].shape[0]
    half = rows // 2
    at = pl.multiple_of(place_ref[2] * rows, rows)
    out[pl.ds(at, rows), :] = pieces[0][...]
    for h, (a, b) in enumerate(HOPS):
        first, second = pieces[1 + 2 * h : 3 + 2 * h]
        for j, value in ((a, first[...]), (b, second[:half, :]), (a | b, second[half:, :])):
            at = pl.multiple_of((place_ref[2] ^ j) * rows + h * half, half)
            out[pl.ds(at, half), :] = value


def part_halves(place_ref, pieces, source):
    half = pieces[0].shape[0] // 2
    for h, (a, b) in enumerate(HOPS):
        for piece, order in zip(pieces[2 * h : 2 * h + 2], ((0, b), (a, a | b))):
            for n, j in enumerate(order):
                at = pl.multiple_of((place_ref[2] ^ j) * 2 * half + h * half, half)
                piece[n * half : (n + 1) * half, :] = source[pl.ds(at, half), :]


def attend_kernel(heads, tensors, owners, part, place_ref, bias_ref, *refs):
    refs = list(refs)
    take = lambda n: [refs.pop(0) for _ in range(n)]
    pieces, owned, (gain_ref,), parts = take(5), take(owners), take(1), take(tensors)
    tok_ref, qkv_ref, mixed_ref, log_ref, w_ref, table, wo, group, result, raw, soft = refs
    inner = heads * HEAD_DIM
    step_id = pl.program_id(0)

    @pl.when(step_id == 0)
    def _():
        fill_bias(bias_ref, table, heads)
        group_halves(place_ref, group, pieces)
        blocks = [piece.at[n] for piece in owned for n in range(piece.shape[0])]
        for k, piece in enumerate(blocks):
            at = pl.multiple_of((place_ref[3] ^ k) * part, part) if owners > 1 else 0
            w_ref[pl.ds(at, part), :] = piece[:part, :]
        wo[...] = w_ref[:, 3 * inner :]

    here = pl.ds(pl.multiple_of(step_id * LENGTH, LENGTH), LENGTH)
    tok_ref[...] = group[here, :]
    unit, _ = unit_rows(tok_ref[...].astype(F32))
    normed = (unit * gain_ref[...]).astype(BF16)
    qkv_ref[...] = dot(normed, w_ref[:, : 3 * inner]).astype(BF16)
    lanes = lax.broadcasted_iota(jnp.int32, (BLOCK, TILE), 1)
    for head in range(heads):
        at = head * HEAD_DIM
        query = (qkv_ref[:, at : at + HEAD_DIM] * HEAD_DIM ** (-0.5)).astype(BF16)
        raw[head] = dot(query, qkv_ref[:, inner + at : inner + at + HEAD_DIM], ROWS_NT)
    for head in range(heads):
        at = head * HEAD_DIM
        for row in range(0, LENGTH, BLOCK):
            cut = slice(row, row + BLOCK)
            scores = raw[head, cut, :] + table[head, cut, :]
            top = jnp.max(scores, axis=-1, keepdims=True)
            exponent = jnp.exp(scores - top)
            total = jnp.sum(exponent, axis=-1, keepdims=True)
            soft[head, cut, :] = (exponent * (1.0 / total)).astype(BF16)
            logs = jnp.broadcast_to(top + jnp.log(total), (BLOCK, TILE))
            log_ref[cut, :] = logs if head == 0 else jnp.where(lanes >= head, logs, log_ref[cut, :])
        value = qkv_ref[:, 2 * inner + at : 2 * inner + at + HEAD_DIM]
        mixed_ref[:, at : at + HEAD_DIM] = dot(soft[head], value).astype(BF16)
    result[here, :] = dot(mixed_ref[...], wo[...], ROWS_NT).astype(BF16)

    @pl.when(step_id == pl.num_programs(0) - 1)
    def _():
        part_halves(place_ref, parts, result)


def attend(places, bias, pieces, owned, part, gain):
    tensors = 4
    piece_rows, width = pieces[0].shape
    rows = tensors * piece_rows
    heads = bias.shape[0]
    inner = heads * HEAD_DIM
    seqs = rows // LENGTH
    by_seq = lambda cols: pl.BlockSpec((LENGTH, cols), lambda s, *_: (s, 0))
    result = pl.pallas_call(
        functools.partial(attend_kernel, heads, tensors, len(owned), part),
        grid_spec=pltpu.PrefetchScalarGridSpec(
            num_scalar_prefetch=1,
            grid=(seqs,),
            in_specs=[pl.BlockSpec(memory_space=pltpu.SMEM)]
            + [whole(p.shape) for p in pieces]
            + [whole(o.shape) for o in owned]
            + [whole((1, width))],
            out_specs=[whole((piece_rows, width))] * tensors
            + [by_seq(width), by_seq(3 * inner), by_seq(inner), by_seq(TILE), whole((width, 4 * inner))],
            scratch_shapes=[
                pltpu.VMEM((heads, LENGTH, LENGTH), F32),
                pltpu.VMEM((width, inner), BF16),
                pltpu.VMEM((rows, width), BF16),
                pltpu.VMEM((rows, width), BF16),
                pltpu.VMEM((heads, LENGTH, LENGTH), F32),
                pltpu.VMEM((heads, LENGTH, LENGTH), BF16),
            ],
        ),
        out_shape=[jax.ShapeDtypeStruct((piece_rows, width), BF16)] * tensors
        + [
            jax.ShapeDtypeStruct((rows, width), BF16),
            jax.ShapeDtypeStruct((rows, 3 * inner), BF16),
            jax.ShapeDtypeStruct((rows, inner), BF16),
            jax.ShapeDtypeStruct((rows, TILE), F32),
            jax.ShapeDtypeStruct((width, 4 * inner), BF16),
        ],
        compiler_params=params(),
        cost_estimate=cost(8 * rows * width * inner + 4 * rows * LENGTH * inner, rows * width * 8, rows * LENGTH * heads),
        name="attend",
    )(places, bias, *pieces, *owned, gain)
    return result[:tensors], result[tensors:]


def attend_back_kernel(
    heads, tensors, part, place_ref, bias_ref, tok_ref, gain_ref, w_ref, qkv_ref, mixed_ref, log_ref, *refs
):
    refs = list(refs)
    pieces = [refs.pop(0) for _ in range(5)]
    gain_two_ref, router_ref = refs.pop(0), refs.pop(0)
    parts = [refs.pop(0) for _ in range(tensors)]
    own_ref, other_ref, weight_ref, gain_out, table, wo, gmix, gproj, near, far, rows_s, group, result, extras, raw, raw_grad, soft, soft_grad = refs
    inner = heads * HEAD_DIM
    blocks = LENGTH // TILE
    step_id = pl.program_id(0)

    @pl.when(step_id == 0)
    def _():
        fill_bias(bias_ref, table, heads)
        wo[...] = w_ref[:, 3 * inner :]
        near[...] = jnp.zeros_like(near)
        far[...] = jnp.zeros_like(far)
        weight_ref[...] = jnp.zeros_like(weight_ref)
        gain_out[...] = jnp.zeros_like(gain_out)
        group_halves(place_ref, group, pieces)

    here = pl.ds(pl.multiple_of(step_id * LENGTH, LENGTH), LENGTH)
    gmix[...] = dot(group[here, :], wo[...]).astype(BF16)
    for head in range(heads):
        at = head * HEAD_DIM
        query = (qkv_ref[:, at : at + HEAD_DIM] * HEAD_DIM ** (-0.5)).astype(BF16)
        raw[head] = dot(query, qkv_ref[:, inner + at : inner + at + HEAD_DIM], ROWS_NT)
        value = qkv_ref[:, 2 * inner + at : 2 * inner + at + HEAD_DIM]
        raw_grad[head] = dot(gmix[:, at : at + HEAD_DIM], value, ROWS_NT)
    for head in range(heads):
        at = head * HEAD_DIM
        for row in range(0, LENGTH, BLOCK):
            cut = slice(row, row + BLOCK)
            attention = jnp.exp(raw[head, cut, :] + table[head, cut, :] - log_ref[cut, head : head + 1])
            grad_weights = raw_grad[head, cut, :]
            inner_sum = jnp.sum(attention * grad_weights, axis=-1, keepdims=True)
            grad_scores = attention * (grad_weights - inner_sum)
            soft[head, cut, :] = attention.astype(BF16)
            soft_grad[head, cut, :] = grad_scores.astype(BF16)
            i, inside = row // TILE, slice(row % TILE, row % TILE + BLOCK)
            low, high = None, None
            for j in range(blocks):
                piece = grad_scores[:, j * TILE : (j + 1) * TILE]
                if abs(j - i) <= 1:
                    near[head * 3 + j - i + 1, inside, :] += piece
                elif j < i:
                    low = piece if low is None else low + piece
                else:
                    high = piece if high is None else high + piece
            if low is not None:
                far[head * 2, inside, :] += low
            if high is not None:
                far[head * 2 + 1, inside, :] += high
        query = (qkv_ref[:, at : at + HEAD_DIM] * HEAD_DIM ** (-0.5)).astype(BF16)
        key = qkv_ref[:, inner + at : inner + at + HEAD_DIM]
        gproj[:, at : at + HEAD_DIM] = (dot(soft_grad[head], key) * HEAD_DIM ** (-0.5)).astype(BF16)
        gproj[:, inner + at : inner + at + HEAD_DIM] = dot(soft_grad[head], query, ROWS_TN).astype(BF16)
        gproj[:, 2 * inner + at : 2 * inner + at + HEAD_DIM] = dot(
            soft[head], gmix[:, at : at + HEAD_DIM], ROWS_TN
        ).astype(BF16)
    unit, _ = unit_rows(tok_ref[...].astype(F32))
    normed = (unit * gain_ref[...]).astype(BF16)
    grad_normed = dot(gproj[...], w_ref[:, : 3 * inner], ROWS_NT)
    result[here, :] = grad_normed.astype(BF16)
    gain_out[...] += jnp.sum(grad_normed * unit, axis=0, keepdims=True)
    weight_ref[:, : 3 * inner] += dot(normed, gproj[...], ROWS_TN)
    weight_ref[:, 3 * inner :] += dot(group[here, :], mixed_ref[...], ROWS_TN)

    @pl.when(step_id == pl.num_programs(0) - 1)
    def _():
        part_halves(place_ref, parts, result)
        ids = [tile_bucket(step) for step in (-1, 0, 1)]
        for head in range(heads):
            for k in range(BUCKETS):
                total = jnp.zeros((TILE, TILE), F32)
                for step in (-1, 0, 1):
                    if k in tile_range(step):
                        total = total + jnp.where(ids[step + 1] == k, near[head * 3 + step + 1], 0.0)
                if k == 15:
                    total = total + far[head * 2]
                if k == 31:
                    total = total + far[head * 2 + 1]
                at = head * BUCKETS + k
                rows_s[at : at + 1, :] = jnp.sum(total, axis=0, keepdims=True)
        sums = jnp.sum(rows_s[...], axis=1, keepdims=True)
        experts = router_ref.shape[0]
        if part % 16 or part > TILE or experts % 16:
            own_ref[...] = jnp.broadcast_to(sums, own_ref.shape)
            return
        count = sums.shape[0]
        diagonal = lax.broadcasted_iota(jnp.int32, (count, TILE), 0) == lax.broadcasted_iota(
            jnp.int32, (count, TILE), 1
        )
        sums = jnp.sum(jnp.where(diagonal, sums, 0.0), axis=0, keepdims=True)
        z_count = own_ref.shape[0]
        owners = 2 * z_count
        gap = jnp.zeros((experts, TILE - part), F32)
        low = jnp.zeros((experts - 1, TILE), F32)
        rows = jnp.concatenate(
            [gain_out[...], gain_two_ref[...], jnp.zeros((experts - 2, gain_out.shape[1]), F32)], axis=0
        )
        for n in range(owners):
            cut = slice(n * part, (n + 1) * part)
            tiles = [router_ref[:, cut], gap, rows[:, cut], gap, jnp.concatenate([sums, low], axis=0)]
            tiles.append(jnp.zeros((experts, gain_out.shape[1] - 3 * TILE), F32))
            extras[n] = jnp.concatenate(tiles, axis=1).astype(BF16)
        for n, ref in enumerate((own_ref, other_ref)):
            for k in range(z_count):
                owner = place_ref[3] ^ (n * z_count + k)
                at = pl.multiple_of(owner * part, part)
                ref[k, :part, :] = weight_ref[pl.ds(at, part), :].astype(BF16)
                ref[k, part:, :] = extras[owner]


def attend_back(places, bias, tokens, gain, weights, projected, mixed, logs, pieces, gain_two, router, part, z_count):
    rows, width = tokens.shape
    tensors = rows // pieces[0].shape[0]
    piece = whole(pieces[0].shape)
    heads = bias.shape[0]
    inner = heads * HEAD_DIM
    seqs = rows // LENGTH
    by_seq = lambda cols: pl.BlockSpec((LENGTH, cols), lambda s, *_: (s, 0))
    experts = router.shape[0]
    sent = (z_count, part + experts, width)
    plain = part % 16 or part > TILE or experts % 16
    if plain:
        sent = (heads * BUCKETS, 1)
    result = pl.pallas_call(
        functools.partial(attend_back_kernel, heads, tensors, part),
        grid_spec=pltpu.PrefetchScalarGridSpec(
            num_scalar_prefetch=1,
            grid=(seqs,),
            in_specs=[
                pl.BlockSpec(memory_space=pltpu.SMEM),
                by_seq(width),
                whole((1, width)),
                whole((width, 4 * inner)),
                by_seq(3 * inner),
                by_seq(inner),
                by_seq(TILE),
            ]
            + [whole(p.shape) for p in pieces]
            + [whole((1, width)), whole((experts, width))],
            out_specs=[piece] * tensors
            + [whole(sent), whole(sent), whole((width, 4 * inner)), whole((1, width))],
            scratch_shapes=[
                pltpu.VMEM((heads, LENGTH, LENGTH), F32),
                pltpu.VMEM((width, inner), BF16),
                pltpu.VMEM((LENGTH, inner), BF16),
                pltpu.VMEM((LENGTH, 3 * inner), BF16),
                pltpu.VMEM((heads * 3, TILE, TILE), F32),
                pltpu.VMEM((heads * 2, TILE, TILE), F32),
                pltpu.VMEM((heads * BUCKETS, TILE), F32),
                pltpu.VMEM((rows, width), BF16),
                pltpu.VMEM((rows, width), BF16),
                pltpu.VMEM((2 * z_count, experts, width), BF16),
                pltpu.VMEM((heads, LENGTH, LENGTH), F32),
                pltpu.VMEM((heads, LENGTH, LENGTH), F32),
                pltpu.VMEM((heads, LENGTH, LENGTH), BF16),
                pltpu.VMEM((heads, LENGTH, LENGTH), BF16),
            ],
        ),
        out_shape=[jax.ShapeDtypeStruct(pieces[0].shape, BF16)] * tensors
        + [
            jax.ShapeDtypeStruct(sent, F32 if plain else BF16),
            jax.ShapeDtypeStruct(sent, F32 if plain else BF16),
            jax.ShapeDtypeStruct((width, 4 * inner), F32),
            jax.ShapeDtypeStruct((1, width), F32),
        ],
        compiler_params=params(),
        cost_estimate=cost(18 * rows * width * inner + 10 * rows * LENGTH * inner, rows * width * 12, rows * LENGTH * heads),
        name="attend_back",
    )(places, bias, tokens, gain, weights, projected, mixed, logs, *pieces, gain_two, router)
    return result[:tensors], result[tensors:]


def first_rows_kernel(count, *refs):
    out_ref = refs[-1]
    at = 0
    for ref in refs[:-1]:
        for n in range(ref.shape[0]):
            out_ref[at] = ref[n, :count, :]
            at += 1


def first_rows(pieces, start, extra, count):
    width = pieces[0].shape[-1]
    total = sum(piece.shape[0] for piece in pieces)
    return pl.pallas_call(
        functools.partial(first_rows_kernel, count),
        grid=(1,),
        in_specs=[
            pl.BlockSpec((piece.shape[0], extra, width), lambda i: (0, start // extra, 0)) for piece in pieces
        ],
        out_specs=whole((total, count, width)),
        out_shape=jax.ShapeDtypeStruct((total, count, width), BF16),
        compiler_params=params(),
        cost_estimate=cost(0, 4 * total * extra * width),
        name="first_rows",
    )(*pieces)


def place_rows(target_ref, rows, out_refs):
    at = 0
    for ref in out_refs:
        count = ref.shape[0]
        index = lax.broadcasted_iota(jnp.int32, (count, rows.shape[0]), 0) + at
        chosen = jnp.where(index == target_ref[...], 1.0, 0.0).astype(BF16)
        ref[...] = dot(chosen, rows).astype(BF16)
        at += count


def place_kernel(target_ref, rows_ref, *out_refs):
    place_rows(target_ref, rows_ref[...], out_refs)


def place(target_row, rows, counts):
    return pl.pallas_call(
        place_kernel,
        out_shape=[jax.ShapeDtypeStruct((count, rows.shape[1]), BF16) for count in counts],
        compiler_params=params(),
        cost_estimate=cost(2 * sum(counts) * rows.size, 4 * rows.size),
        name="place",
    )(target_row, rows)


def softmax_rows(logits):
    exponent = jnp.exp(logits - jnp.max(logits, axis=-1, keepdims=True))
    return exponent * (1.0 / jnp.sum(exponent, axis=-1, keepdims=True))


def sum_pieces(refs):
    total = refs[0][...].astype(F32)
    for ref in refs[1:]:
        total = total + ref[...].astype(F32)
    return total


def route_kernel(tok_ref, *refs):
    gain_ref, router_ref, target_ref, index_ref, kept_ref, hidden_ref, gate_ref = refs[6:13]
    half = tok_ref.shape[0] // 2
    for h in range(2):
        keep, got, last = refs[3 * h : 3 * h + 3]
        here = slice(h * half, (h + 1) * half)
        added = keep[:half, :].astype(F32) + got[:half, :].astype(F32) + last[...].astype(F32)
        hidden_ref[here, :] = tok_ref[here, :].astype(F32) + added
    hidden = hidden_ref[...]
    unit, _ = unit_rows(hidden)
    moe_in = (unit * gain_ref[...]).astype(BF16)
    place_rows(target_ref, moe_in, refs[13:])
    probs = softmax_rows(dot(moe_in, router_ref[...]))
    lanes = lax.broadcasted_iota(jnp.int32, probs.shape, 1)
    picked = jnp.sum(jnp.where(lanes == index_ref[...], probs, 0.0), axis=-1, keepdims=True)
    gate_ref[...] = picked * kept_ref[...].astype(F32)


def route(tokens, attn, gain, router, target_row, index_col, kept_col, counts):
    rows, width = tokens.shape
    result = pl.pallas_call(
        route_kernel,
        out_shape=[
            jax.ShapeDtypeStruct((rows, width), F32),
            jax.ShapeDtypeStruct((rows, 1), F32),
        ]
        + [jax.ShapeDtypeStruct((count, width), BF16) for count in counts],
        compiler_params=params(),
        cost_estimate=cost(2 * sum(counts) * rows * width, 12 * rows * width),
        name="route",
    )(tokens, *attn, gain, router, target_row, index_col, kept_col)
    return result[0], result[1], result[2:]


def rest_choice(blocks, locals_, rest, expert):
    rows = lax.broadcasted_iota(jnp.int32, (blocks * rest, blocks * locals_ * rest), 0)
    cols = lax.broadcasted_iota(jnp.int32, (blocks * rest, blocks * locals_ * rest), 1)
    block = lax.div(rows, rest)
    wanted = block * (locals_ * rest) + expert * rest + (rows - block * rest)
    return jnp.where(cols == wanted, 1.0, 0.0).astype(BF16)


def pick_rows(out_ref, views, choice, main_rows, main, expert):
    at = 0
    pieces = []
    for view in views:
        blocks, size, width = view.shape
        if main:
            start = pl.multiple_of(expert * main, main)
            out_ref[at : at + blocks * main, :] = view[:, pl.ds(start, main), :].reshape(blocks * main, width)
            at += blocks * main
        rest = size - size * main_rows // out_ref.shape[0]
        pieces.append(view[:, size - rest :, :].reshape(blocks * rest, width))
    out_ref[main_rows:, :] = dot(choice, jnp.concatenate(pieces, axis=0)).astype(BF16)


def put_rows(views, value_ref, choice, main_rows, main, locals_, rest, expert):
    at = 0
    spread = dot(choice, value_ref[main_rows:, :], ROWS_TN).astype(BF16)
    rest_at = 0
    for view in views:
        blocks, _, width = view.shape
        if main:
            count = blocks * main
            start = pl.multiple_of(expert * main, main)
            view[:, pl.ds(start, main), :] = value_ref[at : at + count, :].reshape(blocks, main, width)
            at += count
        part = spread[rest_at : rest_at + blocks * locals_ * rest].reshape(blocks, locals_ * rest, width)
        rest_at += blocks * locals_ * rest

        before = view[:, locals_ * main :, :]
        view[:, locals_ * main :, :] = part + jnp.where(expert > 0, before, jnp.zeros_like(before))


def group_views(place_ref, ref, tensors, chunks):
    size = ref.shape[1] // chunks
    views = []
    for k in range(chunks):
        a, b = HOPS[k % 2]
        views += [ref.at[place_ref[2] ^ j, k * size : (k + 1) * size] for j in (0, a, b, a | b)]
    return views


def join_halves(place_ref, own_in, peer_in, own_out, peer_out, win, wout):
    half = own_in.shape[1]
    mine = pl.multiple_of(place_ref[0] * half, half)
    other = pl.multiple_of((1 - place_ref[0]) * half, half)
    if win is not None:
        win[pl.ds(mine, half), :] = own_in[0]
        win[pl.ds(other, half), :] = peer_in[0]
    half_out = own_out.shape[2]
    mine = pl.multiple_of(place_ref[0] * half_out, half_out)
    other = pl.multiple_of((1 - place_ref[0]) * half_out, half_out)
    wout[:, pl.ds(mine, half_out)] = own_out[0]
    wout[:, pl.ds(other, half_out)] = peer_out[0]


def expert_kernel(chunks, tensors, main, locals_, rest, place_ref, *refs):
    refs = list(refs)
    take = lambda n: [refs.pop(0) for _ in range(n)]
    xs = take(3 * chunks)
    (g_ref,) = take(1)
    own_in, peer_in, own_out, peer_out, router = take(5)
    backs = take(2 * chunks)
    x_ref, ge_ref, hid_ref, gi_ref, gl_ref = take(5)
    win, wout, grows, inner, gunits, gate_s, dots, back = take(8)
    expert = pl.program_id(0)
    blocks = sum(ref.shape[0] for ref in xs)
    main_rows = blocks * main
    rows, width = x_ref.shape[1:]
    wide = win.shape[1]
    choice = rest_choice(blocks, locals_, rest, expert)
    many = xs[0].shape[0]
    back_refs = []
    for k in range(chunks):
        keep, send = backs[2 * k : 2 * k + 2]
        back_refs += [ref.at[n * many : (n + 1) * many] for n in range(2) for ref in (keep, send)]
    pick_rows(x_ref.at[0], xs, choice, main_rows, main, expert)
    pick_rows(grows, group_views(place_ref, g_ref, tensors, chunks), choice, main_rows, main, expert)
    join_halves(place_ref, own_in, peer_in, own_out, peer_out, win, wout)
    probs = softmax_rows(dot(x_ref[0], router[...]))
    lanes = lax.broadcasted_iota(jnp.int32, probs.shape, 1)
    mine = lanes == place_ref[1] * locals_ + expert
    picked = jnp.sum(jnp.where(mine, probs, 0.0), axis=-1, keepdims=True)
    gate_s[...] = jnp.broadcast_to(picked, gate_s.shape)
    chunk = 16
    half_wide = wide // 2 if wide % (2 * TILE) == 0 else wide
    half_rows = rows // 2

    def multiply(part):
        at = slice(part * half_rows, (part + 1) * half_rows)
        inner[at, :] = dot(x_ref[0, at, :], win[...])
        gunits[at, :] = dot(grows[at, :], wout[...], ROWS_NT)

    def activate(part):
        for row in range(part * half_rows, (part + 1) * half_rows, chunk):
            at = slice(row, row + chunk)
            gate_tile = gate_s[at, :]
            gate = jnp.concatenate([gate_tile] * (half_wide // TILE), axis=1)
            total = None
            for start in range(0, wide, half_wide):
                lanes_at = slice(start, start + half_wide)
                value = inner[at, lanes_at]
                square = value * value
                wave = jnp.tanh(value * (GELU_A + (GELU_A * GELU_B) * square))
                half = 0.5 + 0.5 * wave
                hidden = (value * half).astype(BF16)
                bend = value * (0.5 * GELU_A + (1.5 * GELU_A * GELU_B) * square)
                slope = half + bend * (1.0 - wave * wave)
                units = gunits[at, lanes_at]
                hid_ref[0, at, lanes_at] = hidden
                gi_ref[0, at, lanes_at] = (gate * (units * slope)).astype(BF16)
                product = hidden.astype(F32) * units
                for tile in range(0, half_wide, TILE):
                    part_sum = product[:, tile : tile + TILE]
                    total = part_sum if total is None else total + part_sum
            dots[at, :] = total
            gate = jnp.concatenate([gate_tile] * (width // TILE), axis=1)
            ge_ref[0, at, :] = (gate * grows[at, :].astype(F32)).astype(BF16)

    def finish(part):
        at = slice(part * half_rows, (part + 1) * half_rows)
        grad_logits = (
            jnp.sum(dots[at, :], axis=-1, keepdims=True)
            * probs[at]
            * (jnp.where(mine[at], 1.0, 0.0) - picked[at])
        ).astype(BF16)
        gl_ref[0, at, :] = grad_logits
        back[at, :] = (
            dot(gi_ref[0, at, :], win[...], ROWS_NT) + dot(grad_logits, router[...], ROWS_NT)
        ).astype(BF16)

    multiply(0)
    multiply(1)
    activate(0)
    finish(0)
    activate(1)
    finish(1)
    put_rows(back_refs, back, choice, main_rows, main, locals_, rest, expert)


def expert_forward_back(places, xs, gs, own_in, peer_in, own_out, peer_out, router, main, rest, chunks):
    locals_, half, wide = own_in.shape
    width, experts = router.shape
    many, block = xs[0].shape[:2]
    tensors = gs.shape[0]
    blocks = tensors * chunks * many
    back = (2 * many, block, width)
    rows = blocks * (main + rest)
    per = lambda *shape: pl.BlockSpec((1,) + shape, lambda e, *_: (e, 0, 0))
    saved = jax.ShapeDtypeStruct((locals_, rows, width), BF16)
    saved_wide = jax.ShapeDtypeStruct((locals_, rows, wide), BF16)
    result = pl.pallas_call(
        functools.partial(expert_kernel, chunks, tensors, main, locals_, rest),
        grid_spec=pltpu.PrefetchScalarGridSpec(
            num_scalar_prefetch=1,
            grid=(locals_,),
            in_specs=[whole(x.shape) for x in xs]
            + [whole(gs.shape)]
            + [per(half, wide)] * 2 + [per(wide, half)] * 2 + [whole((width, experts))],
            out_specs=[whole(back)] * (2 * chunks)
            + [per(rows, width), per(rows, width), per(rows, wide), per(rows, wide), per(rows, experts)],
            scratch_shapes=[
                pltpu.VMEM((width, wide), BF16),
                pltpu.VMEM((wide, width), BF16),
                pltpu.VMEM((rows, width), BF16),
                pltpu.VMEM((rows, wide), F32),
                pltpu.VMEM((rows, wide), F32),
                pltpu.VMEM((rows, TILE), F32),
                pltpu.VMEM((rows, TILE), F32),
                pltpu.VMEM((rows, width), BF16),
            ],
        ),
        out_shape=[jax.ShapeDtypeStruct(back, BF16)] * (2 * chunks)
        + [saved, saved, saved_wide, saved_wide, jax.ShapeDtypeStruct((locals_, rows, experts), BF16)],
        compiler_params=params(),
        cost_estimate=cost(6 * locals_ * rows * width * wide, locals_ * rows * width * 14, locals_ * rows * wide),
        name="experts",
    )(places, *xs, gs, own_in, peer_in, own_out, peer_out, router)
    return result[: 2 * chunks], result[2 * chunks :]


def expert_rows_kernel(chunks, main, locals_, rest, place_ref, hid_ref, own_out, peer_out, forward_ref, wout, value):
    expert = pl.program_id(0)
    tensors = forward_ref.shape[0]
    blocks = tensors * forward_ref.shape[1]
    choice = rest_choice(blocks, locals_, rest, expert)
    join_halves(place_ref, own_out, peer_out, own_out, peer_out, None, wout)
    value[...] = dot(hid_ref[0], wout[...]).astype(BF16)
    views = group_views(place_ref, forward_ref, tensors, chunks)
    put_rows(views, value, choice, blocks * main, main, locals_, rest, expert)


def expert_rows(places, hidden, own_out, peer_out, shape, main, rest, chunks):
    locals_, rows, wide = hidden.shape
    half = own_out.shape[2]
    width = shape[-1]
    per = lambda *shape: pl.BlockSpec((1,) + shape, lambda e, *_: (e, 0, 0))
    return pl.pallas_call(
        functools.partial(expert_rows_kernel, chunks, main, locals_, rest),
        grid_spec=pltpu.PrefetchScalarGridSpec(
            num_scalar_prefetch=1,
            grid=(locals_,),
            in_specs=[per(rows, wide)] + [per(wide, half)] * 2,
            out_specs=whole(shape),
            scratch_shapes=[pltpu.VMEM((wide, width), BF16), pltpu.VMEM((rows, width), BF16)],
        ),
        out_shape=jax.ShapeDtypeStruct(shape, BF16),
        compiler_params=params(),
        cost_estimate=cost(2 * locals_ * rows * width * wide, locals_ * rows * width * 6),
        name="expert_rows",
    )(places, hidden, own_out, peer_out)


def expert_weights_kernel(place_ref, x_ref, ge_ref, hid_ref, gi_ref, gl_ref, *refs):
    in_own, in_send, out_own, out_send, router_ref = refs
    half = in_own.shape[1]
    mine = pl.ds(pl.multiple_of(place_ref[0] * half, half), half)
    other = pl.ds(pl.multiple_of((1 - place_ref[0]) * half, half), half)
    in_own[0] = dot(x_ref[0, :, mine], gi_ref[0], ROWS_TN)
    in_send[0] = dot(x_ref[0, :, other], gi_ref[0], ROWS_TN).astype(BF16)
    out_own[0] = dot(hid_ref[0], ge_ref[0, :, mine], ROWS_TN)
    out_send[0] = dot(hid_ref[0], ge_ref[0, :, other], ROWS_TN).astype(BF16)

    @pl.when(pl.program_id(0) == 0)
    def _():
        router_ref[...] = jnp.zeros_like(router_ref)

    router_ref[...] += dot(gl_ref[0], x_ref[0], ROWS_TN)


def expert_weights(places, saved, half):
    x, ge, hidden, gi, gl = saved
    locals_, rows, width = x.shape
    wide = hidden.shape[2]
    experts = gl.shape[2]
    per = lambda *shape: pl.BlockSpec((1,) + shape, lambda e, *_: (e, 0, 0))
    return pl.pallas_call(
        expert_weights_kernel,
        grid_spec=pltpu.PrefetchScalarGridSpec(
            num_scalar_prefetch=1,
            grid=(locals_,),
            in_specs=[per(rows, width), per(rows, width), per(rows, wide), per(rows, wide), per(rows, experts)],
            out_specs=[per(half, wide), per(half, wide), per(wide, half), per(wide, half), whole((experts, width))],
        ),
        out_shape=[
            jax.ShapeDtypeStruct((locals_, half, wide), F32),
            jax.ShapeDtypeStruct((locals_, half, wide), BF16),
            jax.ShapeDtypeStruct((locals_, wide, half), F32),
            jax.ShapeDtypeStruct((locals_, wide, half), BF16),
            jax.ShapeDtypeStruct((experts, width), F32),
        ],
        compiler_params=params(),
        cost_estimate=cost(4 * locals_ * rows * width * wide, locals_ * rows * width * 14),
        name="expert_weights",
    )(places, x, ge, hidden, gi, gl)


def take_rows(target_ref, refs):
    total, at = None, 0
    for ref in refs:
        count = ref.shape[0]
        cols = lax.broadcasted_iota(jnp.int32, (target_ref.shape[0], count), 1) + at
        chosen = jnp.where(cols == target_ref[...], 1.0, 0.0).astype(BF16)
        part = dot(chosen, ref[...])
        total = part if total is None else total + part
        at += count
    return total


def hidden_back_kernel(target_ref, *refs):
    hidden_ref, cot_ref, gain_ref, grad_ref, attn_ref, gain_out = refs[-6:]
    grad_in = take_rows(target_ref, refs[:-6])
    unit, scale = unit_rows(hidden_ref[...])
    gained = jnp.sum(grad_in * unit, axis=0, keepdims=True)
    gain_out[...] = gained + jnp.where(pl.program_id(0) > 0, gain_out[...], jnp.zeros_like(gained))
    scaled = grad_in * gain_ref[...]
    inside = jnp.mean(unit * scaled, axis=-1, keepdims=True)
    grad = cot_ref[...].astype(F32) + scale * (scaled - unit * inside)
    grad_ref[...] = grad
    attn_ref[...] = grad.astype(BF16)


def hidden_back(target_col, back, hidden, cotangent, gain):
    rows, width = hidden.shape
    steps = 3 if rows % 48 == 0 else 1
    by_row = lambda cols: pl.BlockSpec((rows // steps, cols), lambda i: (i, 0))
    return pl.pallas_call(
        hidden_back_kernel,
        grid=(steps,),
        in_specs=[by_row(1)] + [whole(b.shape) for b in back] + [by_row(width), by_row(width), whole((1, width))],
        out_specs=[by_row(width), by_row(width), whole((1, width))],
        out_shape=[
            jax.ShapeDtypeStruct((rows, width), F32),
            jax.ShapeDtypeStruct((rows, width), BF16),
            jax.ShapeDtypeStruct((1, width), F32),
        ],
        compiler_params=params(),
        cost_estimate=cost(3 * rows * rows * width, 16 * rows * width),
        name="hidden_back",
    )(target_col, *back, hidden, cotangent, gain)


def output_kernel(target_ref, *refs):
    hidden_ref, gate_ref, out_ref = refs[-3:]
    out_ref[...] = (hidden_ref[...] + gate_ref[...] * take_rows(target_ref, refs[:-3])).astype(BF16)


def output_rows(target_col, expert_rows, hidden, gate):
    return pl.pallas_call(
        output_kernel,
        out_shape=jax.ShapeDtypeStruct(hidden.shape, BF16),
        compiler_params=params(),
        cost_estimate=cost(3 * hidden.shape[0] * hidden.size, 10 * hidden.size),
        name="output_rows",
    )(target_col, *expert_rows, hidden, gate)


def tokens_back_kernel(tok_ref, *refs):
    gain_ref, hidden_ref, out_ref = refs[6:]
    half = tok_ref.shape[0] // 2
    for h in range(2):
        keep, got, last = refs[3 * h : 3 * h + 3]
        here = slice(h * half, (h + 1) * half)
        unit, scale = unit_rows(tok_ref[here, :].astype(F32))
        grad = keep[:half, :].astype(F32) + got[:half, :].astype(F32) + last[...].astype(F32)
        scaled = grad * gain_ref[...]
        inside = jnp.mean(unit * scaled, axis=-1, keepdims=True)
        out_ref[here, :] = hidden_ref[here, :] + scale * (scaled - unit * inside)


def tokens_back(tokens, grad_normed, gain, grad_hidden):
    return pl.pallas_call(
        tokens_back_kernel,
        out_shape=jax.ShapeDtypeStruct(tokens.shape, F32),
        compiler_params=params(),
        cost_estimate=cost(10 * tokens.size, 12 * tokens.size),
        name="tokens_back",
    )(tokens, *grad_normed, gain, grad_hidden)


def shifted(value, axis, count, step):
    return lax.ppermute(value, axis, [(s, (s + step) % count) for s in range(count)])


def gather_ring(value, axis, count):
    me = lax.axis_index(axis)
    parts = [value] + [shifted(value, axis, count, -k) for k in range(1, count)]
    return jnp.roll(jnp.stack(parts), me, axis=0)


def swapped(value, axis, count, bits):
    return lax.ppermute(value, axis, [(s, s ^ bits) for s in range(count)])


def gather_pieces(value, axis, count):
    return [value] + [swapped(value, axis, count, k) for k in range(1, count)]


def gather_hops(value, hops):
    a, b = hops
    first = swapped(value, "tensor", 4, a)
    second = swapped(jnp.concatenate([value, first], axis=0), "tensor", 4, b)
    return first, second


def sum_hops(parts):
    half = parts[0].shape[0] // 2
    result = []
    for h, (a, b) in enumerate(HOPS):
        keep, send = parts[2 * h : 2 * h + 2]
        got = swapped(send, "tensor", 4, a)
        last = swapped(added(keep[half:], got[half:]), "tensor", 4, b)
        result += [keep, got, last]
    return result


def added(a, b):
    return (a.astype(F32) + b.astype(F32)).astype(BF16)


def swap_pieces(pieces, axis, count):
    return [pieces[0]] + [swapped(pieces[k], axis, count, k) for k in range(1, count)]


def on_device(
    sizes,
    tokens,
    cotangent,
    query_key_value_weight,
    attention_output_weight,
    rel_bias,
    gain_attn,
    gain_moe,
    w_router,
    w_in,
    w_out,
    expert_index,
    slot_index,
    kept_mask,
):
    dp_count, z_count, t_count = sizes
    tok_rows, width = tokens.shape
    experts_all = w_router.shape[1]
    capacity = max(2, 3 * tok_rows // (2 * experts_all))
    locals_ = w_in.shape[0]
    main = capacity // 16 * 16
    rest = capacity - main
    block = locals_ * capacity
    heads = rel_bias.shape[0]
    inner = heads * HEAD_DIM
    part = query_key_value_weight.shape[1]
    fine = w_router.shape[0]
    my_dp = lax.axis_index("dp")
    my_z = lax.axis_index("expert")
    bias = rel_bias.astype(F32)

    my_t = lax.axis_index("tensor")
    owners = dp_count * z_count
    my_owner = my_dp * z_count + my_z
    places = jnp.stack([my_dp, my_z, my_t, my_owner]).astype(jnp.int32)
    half_rows = tok_rows // 2
    token_pieces = [tokens]
    for h, hops in enumerate(HOPS):
        token_pieces += list(gather_hops(tokens[h * half_rows : (h + 1) * half_rows], hops))

    small = jnp.concatenate([gain_attn[:, None], gain_moe[:, None], w_router], axis=1).reshape(-1)
    extra = -(-small.shape[0] // (16 * width)) * 16
    packed = jnp.concatenate(
        [
            query_key_value_weight.transpose(1, 0, 2).reshape(part, 3 * inner),
            attention_output_weight.T,
        ],
        axis=1,
    )
    packed = jnp.concatenate(
        [packed, jnp.pad(small, (0, extra * width - small.shape[0])).reshape(extra, width)], axis=0
    )
    owned = gather_pieces(packed[None], "expert", z_count)
    owned = owned + [swapped(jnp.concatenate(owned, axis=0), "dp", dp_count, 1)]
    if part % 16 or part % extra:
        smalls = jnp.concatenate(owned, axis=0)[:, part:]
    else:
        smalls = first_rows(owned, part, extra, -(-small.shape[0] // width))
    smalls = smalls.reshape(owners, -1)[:, : small.shape[0]]
    small_pieces = gather_pieces(smalls, "tensor", t_count)

    z_of = expert_index // locals_
    local = expert_index - z_of * locals_
    inside = jnp.where(
        slot_index < main, local * main + slot_index, locals_ * main + local * rest + slot_index - main
    )
    target = (z_of ^ my_z) * block + inside
    target = jnp.where(kept_mask > 0, target, -1)
    target_row, target_col = target[None, :], target[:, None]
    chunks = min(z_count, 4)
    many = z_count // chunks
    counts = [many * block] * chunks
    grad_sent = place(target_row, cotangent, counts)
    token_pieces, owned, small_pieces, grad_sent = lax.optimization_barrier(
        (token_pieces, owned, small_pieces, grad_sent)
    )
    smalls = jnp.stack(small_pieces).reshape(t_count * owners, -1)
    owner_ids = jnp.arange(owners, dtype=jnp.int32)[:, None] ^ my_owner
    t_ids = jnp.arange(t_count, dtype=jnp.int32)[None, :] ^ my_t
    smalls = smalls[(t_ids * owners + owner_ids).reshape(-1)].reshape(width, 2 + experts_all)
    if part % 16:
        order = jnp.arange(owners, dtype=jnp.int32) ^ my_owner
        owned = [jnp.concatenate(owned, axis=0)[:, :part][order].reshape(1, width, 4 * inner)]
    rows_owned = part if len(owned) > 1 else width
    gain_one = smalls[:, 0].astype(F32)[None]
    gain_two = smalls[:, 1].astype(F32)[None]
    router = smalls[:, 2:]

    def over_expert(groups):
        if many > 1:
            groups = [g[i * block : (i + 1) * block] for g in groups for i in range(many)]
        pieces = swap_pieces(groups, "expert", z_count)
        if many == 1:
            return pieces
        return [jnp.concatenate(pieces[k * many : (k + 1) * many], axis=0) for k in range(chunks)]

    grad_rows = jnp.concatenate(over_expert(grad_sent), axis=0)
    parts, (group_tokens, projected, mixed, logs, weights) = attend(
        places, bias, token_pieces, owned, rows_owned, gain_one
    )
    parts, late_in, late_out, grad_rows = lax.optimization_barrier((parts, w_in, w_out, grad_rows))
    peer_in = shifted(late_in, "dp", dp_count, 1)
    peer_out = shifted(late_out, "dp", dp_count, 1)
    grad_arrived = lax.all_gather(grad_rows, "tensor", axis=0).reshape(t_count, z_count, block, width)
    attn = sum_hops(parts)
    attn, peer_in, peer_out = lax.optimization_barrier((attn, peer_in, peer_out))
    hidden_one, gate, sent = route(
        tokens, attn, gain_two, router, target_row, expert_index[:, None], kept_mask[:, None], counts
    )
    arrived = []
    for k, group in enumerate(over_expert(sent)):
        pieces = (group,) + gather_hops(group, HOPS[k % 2])
        arrived += [piece.reshape(-1, block, width) for piece in pieces]
    back_parts, saved = expert_forward_back(
        places, arrived, grad_arrived, w_in, peer_in, w_out, peer_out, router, main, rest, chunks
    )

    size = many * block
    back_parts = [piece.reshape(2 * size, width) for piece in back_parts]
    keeps, sends = back_parts[::2], back_parts[1::2]
    got = [swapped(sends[k], "tensor", t_count, HOPS[k % 2][0]) for k in reversed(range(chunks))][::-1]
    forward_part = expert_rows(places, saved[2], w_out, peer_out, grad_arrived.shape, main, rest, chunks)
    got, forward_part = lax.optimization_barrier((got, forward_part))
    groups = []
    for k in range(chunks):
        last = swapped(added(keeps[k][size:], got[k][size:]), "tensor", t_count, HOPS[k % 2][1])
        total = keeps[k][:size].astype(F32) + got[k][:size].astype(F32) + last.astype(F32)
        groups.append(total.astype(BF16))
    forward_part, groups, saved = lax.optimization_barrier((forward_part, groups, saved))
    forward_sum = lax.psum_scatter(
        forward_part.reshape(t_count * z_count * block, width), "tensor", scatter_dimension=0, tiled=True
    )
    in_own, in_send, out_own, out_send, router_part = expert_weights(places, saved, w_in.shape[1])
    grad_back, in_send, out_send = lax.optimization_barrier((over_expert(groups), in_send, out_send))
    in_got = shifted(in_send, "dp", dp_count, 1)
    out_got = shifted(out_send, "dp", dp_count, 1)
    grad_hidden, grad_attn, gain_two_part = hidden_back(target_col, grad_back, hidden_one, cotangent, gain_two)
    grad_pieces = [grad_attn]
    for h, hops in enumerate(HOPS):
        grad_pieces += list(gather_hops(grad_attn[h * half_rows : (h + 1) * half_rows], hops))
    grad_w_in = in_own + in_got.astype(F32)
    grad_w_out = out_own + out_got.astype(F32)
    grad_pieces, grad_w_in, grad_w_out, forward_sum = lax.optimization_barrier(
        (grad_pieces, grad_w_in, grad_w_out, forward_sum)
    )
    normed_parts, (own_part, other_part, weight_part, gain_one_part) = attend_back(
        places, bias, group_tokens, gain_one, weights, projected, mixed, logs, grad_pieces,
        gain_two_part, router_part, part, z_count,
    )
    forward_rows = over_expert(list(forward_sum.reshape(chunks, many * block, width)))
    normed_parts, own_part, other_part, forward_rows = lax.optimization_barrier(
        (normed_parts, own_part, other_part, forward_rows)
    )
    if part % 16 or part > TILE or experts_all % 16:
        pad = lambda value, lanes: jnp.pad(value, ((0, 0), (0, lanes - value.shape[1])))
        gains = jnp.concatenate([gain_one_part, gain_two_part, jnp.zeros((experts_all - 2, width), F32)])
        sums = jnp.pad(own_part.reshape(1, -1), ((0, experts_all - 1), (0, TILE - own_part.shape[0])))
        extras = [
            pad(jnp.concatenate([pad(router_part[:, cut], TILE), pad(gains[:, cut], TILE), sums], axis=1), width)
            for cut in (slice(n * part, (n + 1) * part) for n in range(owners))
        ]
        order = jnp.arange(owners, dtype=jnp.int32) ^ my_owner
        payload = jnp.concatenate(
            [weight_part.astype(BF16).reshape(owners, part, width), jnp.stack(extras).astype(BF16)], axis=1
        )[order]
        own_part, other_part = payload[:z_count], payload[z_count:]
    other_got = shifted(other_part, "dp", dp_count, 1)
    normed_parts, other_got = lax.optimization_barrier((normed_parts, other_got))
    grad_normed = sum_hops(normed_parts)
    output = output_rows(target_col, forward_rows, hidden_one, gate)
    grad_tokens = tokens_back(tokens, grad_normed, gain_one, grad_hidden)

    pieces = swap_pieces([added(own_part[k], other_got[k]) for k in range(z_count)], "expert", z_count)
    pieces, grad_tokens = lax.optimization_barrier((pieces, grad_tokens))
    total = pieces[0].astype(F32)
    for piece in pieces[1:]:
        total = total + piece.astype(F32)
    weight_total = total[:part].reshape(part, 4, inner)
    grad_w_qkv = weight_total[:, :3].transpose(1, 0, 2)
    grad_w_attn_out = weight_total[:, 3].T
    grad_rel_bias = total[part, 2 * TILE : 2 * TILE + heads * BUCKETS].reshape(heads, BUCKETS)
    mine = jnp.concatenate([total[part : part + 2, TILE : TILE + part], total[part:, :part]], axis=0)
    turned = [
        lax.dynamic_slice_in_dim(mine, (my_t ^ k) * fine, fine, axis=1).reshape(-1) for k in range(t_count)
    ]
    left = turned[0]
    for piece in swap_pieces(turned, "tensor", t_count)[1:]:
        left = left + piece
    grad_gain_attn = left[:fine]
    grad_gain_moe = left[fine : 2 * fine]
    grad_w_router = left[2 * fine :].reshape(experts_all, fine).T
    return (
        output,
        grad_tokens,
        grad_w_qkv,
        grad_w_attn_out,
        grad_rel_bias,
        grad_gain_attn,
        grad_gain_moe,
        grad_w_router,
        grad_w_in,
        grad_w_out,
    )


def solution(mesh):
    placed = (
        P(("dp", "expert", "tensor"), None),
        P(("dp", "expert", "tensor"), None),
        P(None, ("dp", "expert"), "tensor"),
        P("tensor", ("dp", "expert")),
        P("tensor", None),
        P(("dp", "expert", "tensor")),
        P(("dp", "expert", "tensor")),
        P(("dp", "expert", "tensor"), None),
        P("expert", "dp", "tensor"),
        P("expert", "tensor", "dp"),
        P(("dp", "expert", "tensor")),
        P(("dp", "expert", "tensor")),
        P(("dp", "expert", "tensor")),
    )
    sizes = tuple(mesh.shape[name] for name in ("dp", "expert", "tensor"))
    return jax.shard_map(
        functools.partial(on_device, sizes),
        mesh=mesh,
        in_specs=placed,
        out_specs=(
            P(("dp", "expert", "tensor"), None),
            P(("dp", "expert", "tensor"), None),
            P(None, ("dp", "expert"), "tensor"),
            P("tensor", ("dp", "expert")),
            P("tensor", None),
            P(("dp", "expert", "tensor")),
            P(("dp", "expert", "tensor")),
            P(("dp", "expert", "tensor"), None),
            P("expert", "dp", "tensor"),
            P("expert", "tensor", "dp"),
        ),
        check_vma=False,
    )
```

```python
import functools

import jax
import jax.numpy as jnp
from jax import lax
from jax.experimental import pallas as pl
from jax.experimental.pallas import tpu as pltpu
from jax.sharding import PartitionSpec as P

HEAD_DIM = 64
BUCKETS = 32
LENGTH = 512
TILE = 128
EPSILON = 1e-06
BORDERS = (12, 16, 23, 32, 46, 64, 91)
F32 = jnp.float32
BF16 = jnp.bfloat16
GELU_A = 0.7978845608028654
GELU_B = 0.044715
ROWS_NN = (((1,), (0,)), ((), ()))
ROWS_NT = (((1,), (1,)), ((), ()))
ROWS_TN = (((0,), (0,)), ((), ()))
VMEM_BYTES = 56 * 1024 * 1024


def dot(a, b, dims=ROWS_NN):
    return lax.dot_general(a, b, dims, preferred_element_type=F32)


def params(**more):
    return pltpu.CompilerParams(vmem_limit_bytes=VMEM_BYTES, **more)


def cost(flops, moved, special=0):
    return pl.CostEstimate(flops=int(flops), bytes_accessed=int(moved), transcendentals=int(special))


def whole(shape):
    return pl.BlockSpec(shape, lambda *_: (0,) * len(shape))


def tile_bucket(step):
    rows = lax.broadcasted_iota(jnp.int32, (TILE, TILE), 0)
    cols = lax.broadcasted_iota(jnp.int32, (TILE, TILE), 1)
    offset = cols - rows + step * TILE
    distance = jnp.abs(offset)
    bucket = jnp.minimum(distance, 8)
    for border in BORDERS:
        bucket = bucket + jnp.where(distance >= border, 1, 0)
    return bucket + jnp.where(offset > 0, 16, 0)


def tile_range(step):
    return {-1: range(1, 16), 0: range(0, 32), 1: range(17, 32)}[step]


def fill_bias(bias_ref, table, heads):
    blocks = LENGTH // TILE
    buckets = {step: tile_bucket(step) for step in (-1, 0, 1)}
    for head in range(heads):
        near = {}
        for step in (-1, 0, 1):
            value = jnp.zeros((TILE, TILE), F32)
            for k in tile_range(step):
                value = jnp.where(buckets[step] == k, bias_ref[head, k], value)
            near[step] = value
        low = jnp.full((TILE, TILE), bias_ref[head, 15], F32)
        high = jnp.full((TILE, TILE), bias_ref[head, 31], F32)
        for i in range(blocks):
            for j in range(blocks):
                step = j - i
                value = near[step] if abs(step) <= 1 else (low if step < 0 else high)
                table[head, i * TILE : (i + 1) * TILE, j * TILE : (j + 1) * TILE] = value


def unit_rows(values):
    scale = lax.rsqrt(jnp.mean(values * values, axis=-1, keepdims=True) + EPSILON)
    return values * scale, scale


HOPS = ((1, 2), (2, 1))


def group_halves(place_ref, out, pieces):
    rows = pieces[0].shape[0]
    half = rows // 2
    at = pl.multiple_of(place_ref[2] * rows, rows)
    out[pl.ds(at, rows), :] = pieces[0][...]
    for h, (a, b) in enumerate(HOPS):
        first, second = pieces[1 + 2 * h : 3 + 2 * h]
        for j, value in ((a, first[...]), (b, second[:half, :]), (a | b, second[half:, :])):
            at = pl.multiple_of((place_ref[2] ^ j) * rows + h * half, half)
            out[pl.ds(at, half), :] = value


def part_halves(place_ref, pieces, source):
    half = pieces[0].shape[0] // 2
    for h, (a, b) in enumerate(HOPS):
        for piece, order in zip(pieces[2 * h : 2 * h + 2], ((0, b), (a, a | b))):
            for n, j in enumerate(order):
                at = pl.multiple_of((place_ref[2] ^ j) * 2 * half + h * half, half)
                piece[n * half : (n + 1) * half, :] = source[pl.ds(at, half), :]


def attend_kernel(heads, tensors, owners, part, place_ref, bias_ref, *refs):
    refs = list(refs)
    take = lambda n: [refs.pop(0) for _ in range(n)]
    pieces, owned, (gain_ref,), parts = take(5), take(owners), take(1), take(tensors)
    tok_ref, qkv_ref, mixed_ref, log_ref, w_ref, table, wo, group, result = refs
    inner = heads * HEAD_DIM
    step_id = pl.program_id(0)

    @pl.when(step_id == 0)
    def _():
        fill_bias(bias_ref, table, heads)
        group_halves(place_ref, group, pieces)
        blocks = [piece.at[n] for piece in owned for n in range(piece.shape[0])]
        for k, piece in enumerate(blocks):
            at = pl.multiple_of((place_ref[3] ^ k) * part, part) if owners > 1 else 0
            w_ref[pl.ds(at, part), :] = piece[:part, :]
        wo[...] = w_ref[:, 3 * inner :]

    here = pl.ds(pl.multiple_of(step_id * LENGTH, LENGTH), LENGTH)
    tok_ref[...] = group[here, :]
    unit, _ = unit_rows(tok_ref[...].astype(F32))
    normed = (unit * gain_ref[...]).astype(BF16)
    qkv_ref[...] = dot(normed, w_ref[:, : 3 * inner]).astype(BF16)
    lanes = lax.broadcasted_iota(jnp.int32, (LENGTH, TILE), 1)
    logs = jnp.zeros((LENGTH, TILE), F32)
    for head in range(heads):
        at = head * HEAD_DIM
        query = qkv_ref[:, at : at + HEAD_DIM] * HEAD_DIM ** (-0.5)
        key = qkv_ref[:, inner + at : inner + at + HEAD_DIM]
        value = qkv_ref[:, 2 * inner + at : 2 * inner + at + HEAD_DIM]
        scores = dot(query.astype(BF16), key, ROWS_NT) + table[head]
        top = jnp.max(scores, axis=-1, keepdims=True)
        exponent = jnp.exp(scores - top)
        total = jnp.sum(exponent, axis=-1, keepdims=True)
        attention = (exponent * (1.0 / total)).astype(BF16)
        mixed_ref[:, at : at + HEAD_DIM] = dot(attention, value).astype(BF16)
        logs = jnp.where(lanes == head, top + jnp.log(total), logs)
    log_ref[...] = logs
    result[here, :] = dot(mixed_ref[...], wo[...], ROWS_NT).astype(BF16)

    @pl.when(step_id == pl.num_programs(0) - 1)
    def _():
        part_halves(place_ref, parts, result)


def attend(places, bias, pieces, owned, part, gain):
    tensors = 4
    piece_rows, width = pieces[0].shape
    rows = tensors * piece_rows
    heads = bias.shape[0]
    inner = heads * HEAD_DIM
    seqs = rows // LENGTH
    by_seq = lambda cols: pl.BlockSpec((LENGTH, cols), lambda s, *_: (s, 0))
    result = pl.pallas_call(
        functools.partial(attend_kernel, heads, tensors, len(owned), part),
        grid_spec=pltpu.PrefetchScalarGridSpec(
            num_scalar_prefetch=1,
            grid=(seqs,),
            in_specs=[pl.BlockSpec(memory_space=pltpu.SMEM)]
            + [whole(p.shape) for p in pieces]
            + [whole(o.shape) for o in owned]
            + [whole((1, width))],
            out_specs=[whole((piece_rows, width))] * tensors
            + [by_seq(width), by_seq(3 * inner), by_seq(inner), by_seq(TILE), whole((width, 4 * inner))],
            scratch_shapes=[
                pltpu.VMEM((heads, LENGTH, LENGTH), F32),
                pltpu.VMEM((width, inner), BF16),
                pltpu.VMEM((rows, width), BF16),
                pltpu.VMEM((rows, width), BF16),
            ],
        ),
        out_shape=[jax.ShapeDtypeStruct((piece_rows, width), BF16)] * tensors
        + [
            jax.ShapeDtypeStruct((rows, width), BF16),
            jax.ShapeDtypeStruct((rows, 3 * inner), BF16),
            jax.ShapeDtypeStruct((rows, inner), BF16),
            jax.ShapeDtypeStruct((rows, TILE), F32),
            jax.ShapeDtypeStruct((width, 4 * inner), BF16),
        ],
        compiler_params=params(),
        cost_estimate=cost(8 * rows * width * inner + 4 * rows * LENGTH * inner, rows * width * 8, rows * LENGTH * heads),
        name="attend",
    )(places, bias, *pieces, *owned, gain)
    return result[:tensors], result[tensors:]


def attend_back_kernel(
    heads, tensors, part, place_ref, bias_ref, tok_ref, gain_ref, w_ref, qkv_ref, mixed_ref, log_ref, *refs
):
    refs = list(refs)
    pieces = [refs.pop(0) for _ in range(5)]
    gain_two_ref, router_ref = refs.pop(0), refs.pop(0)
    parts = [refs.pop(0) for _ in range(tensors)]
    own_ref, other_ref, weight_ref, gain_out, table, wo, gmix, gproj, near, far, rows_s, group, result, extras = refs
    inner = heads * HEAD_DIM
    blocks = LENGTH // TILE
    step_id = pl.program_id(0)

    @pl.when(step_id == 0)
    def _():
        fill_bias(bias_ref, table, heads)
        wo[...] = w_ref[:, 3 * inner :]
        near[...] = jnp.zeros_like(near)
        far[...] = jnp.zeros_like(far)
        weight_ref[...] = jnp.zeros_like(weight_ref)
        gain_out[...] = jnp.zeros_like(gain_out)
        group_halves(place_ref, group, pieces)

    here = pl.ds(pl.multiple_of(step_id * LENGTH, LENGTH), LENGTH)
    gmix[...] = dot(group[here, :], wo[...]).astype(BF16)
    for head in range(heads):
        at = head * HEAD_DIM
        query = (qkv_ref[:, at : at + HEAD_DIM] * HEAD_DIM ** (-0.5)).astype(BF16)
        key = qkv_ref[:, inner + at : inner + at + HEAD_DIM]
        value = qkv_ref[:, 2 * inner + at : 2 * inner + at + HEAD_DIM]
        grad_rows = gmix[:, at : at + HEAD_DIM]
        scores = dot(query, key, ROWS_NT) + table[head]
        attention = jnp.exp(scores - log_ref[:, head : head + 1])
        grad_weights = dot(grad_rows, value, ROWS_NT)
        inner_sum = jnp.sum(attention * grad_weights, axis=-1, keepdims=True)
        grad_scores = attention * (grad_weights - inner_sum)
        low = jnp.zeros((TILE, TILE), F32)
        high = jnp.zeros((TILE, TILE), F32)
        mid = [jnp.zeros((TILE, TILE), F32) for _ in range(3)]
        for i in range(blocks):
            for j in range(blocks):
                piece = grad_scores[i * TILE : (i + 1) * TILE, j * TILE : (j + 1) * TILE]
                if abs(j - i) <= 1:
                    mid[j - i + 1] = mid[j - i + 1] + piece
                elif j < i:
                    low = low + piece
                else:
                    high = high + piece
        for k in range(3):
            near[head * 3 + k] += mid[k]
        far[head * 2] += low
        far[head * 2 + 1] += high
        rounded = grad_scores.astype(BF16)
        gproj[:, at : at + HEAD_DIM] = (dot(rounded, key) * HEAD_DIM ** (-0.5)).astype(BF16)
        gproj[:, inner + at : inner + at + HEAD_DIM] = dot(rounded, query, ROWS_TN).astype(BF16)
        gproj[:, 2 * inner + at : 2 * inner + at + HEAD_DIM] = dot(
            attention.astype(BF16), grad_rows, ROWS_TN
        ).astype(BF16)
    unit, _ = unit_rows(tok_ref[...].astype(F32))
    normed = (unit * gain_ref[...]).astype(BF16)
    grad_normed = dot(gproj[...], w_ref[:, : 3 * inner], ROWS_NT)
    result[here, :] = grad_normed.astype(BF16)
    gain_out[...] += jnp.sum(grad_normed * unit, axis=0, keepdims=True)
    weight_ref[:, : 3 * inner] += dot(normed, gproj[...], ROWS_TN)
    weight_ref[:, 3 * inner :] += dot(group[here, :], mixed_ref[...], ROWS_TN)

    @pl.when(step_id == pl.num_programs(0) - 1)
    def _():
        part_halves(place_ref, parts, result)
        ids = [tile_bucket(step) for step in (-1, 0, 1)]
        for head in range(heads):
            for k in range(BUCKETS):
                total = jnp.zeros((TILE, TILE), F32)
                for step in (-1, 0, 1):
                    if k in tile_range(step):
                        total = total + jnp.where(ids[step + 1] == k, near[head * 3 + step + 1], 0.0)
                if k == 15:
                    total = total + far[head * 2]
                if k == 31:
                    total = total + far[head * 2 + 1]
                at = head * BUCKETS + k
                rows_s[at : at + 1, :] = jnp.sum(total, axis=0, keepdims=True)
        sums = jnp.sum(rows_s[...], axis=1, keepdims=True)
        experts = router_ref.shape[0]
        if part % 16 or part > TILE or experts % 16:
            own_ref[...] = jnp.broadcast_to(sums, own_ref.shape)
            return
        count = sums.shape[0]
        diagonal = lax.broadcasted_iota(jnp.int32, (count, TILE), 0) == lax.broadcasted_iota(
            jnp.int32, (count, TILE), 1
        )
        sums = jnp.sum(jnp.where(diagonal, sums, 0.0), axis=0, keepdims=True)
        z_count = own_ref.shape[0]
        owners = 2 * z_count
        gap = jnp.zeros((experts, TILE - part), F32)
        low = jnp.zeros((experts - 1, TILE), F32)
        rows = jnp.concatenate(
            [gain_out[...], gain_two_ref[...], jnp.zeros((experts - 2, gain_out.shape[1]), F32)], axis=0
        )
        for n in range(owners):
            cut = slice(n * part, (n + 1) * part)
            tiles = [router_ref[:, cut], gap, rows[:, cut], gap, jnp.concatenate([sums, low], axis=0)]
            tiles.append(jnp.zeros((experts, gain_out.shape[1] - 3 * TILE), F32))
            extras[n] = jnp.concatenate(tiles, axis=1).astype(BF16)
        for n, ref in enumerate((own_ref, other_ref)):
            for k in range(z_count):
                owner = place_ref[3] ^ (n * z_count + k)
                at = pl.multiple_of(owner * part, part)
                ref[k, :part, :] = weight_ref[pl.ds(at, part), :].astype(BF16)
                ref[k, part:, :] = extras[owner]


def attend_back(places, bias, tokens, gain, weights, projected, mixed, logs, pieces, gain_two, router, part, z_count):
    rows, width = tokens.shape
    tensors = rows // pieces[0].shape[0]
    piece = whole(pieces[0].shape)
    heads = bias.shape[0]
    inner = heads * HEAD_DIM
    seqs = rows // LENGTH
    by_seq = lambda cols: pl.BlockSpec((LENGTH, cols), lambda s, *_: (s, 0))
    experts = router.shape[0]
    sent = (z_count, part + experts, width)
    plain = part % 16 or part > TILE or experts % 16
    if plain:
        sent = (heads * BUCKETS, 1)
    result = pl.pallas_call(
        functools.partial(attend_back_kernel, heads, tensors, part),
        grid_spec=pltpu.PrefetchScalarGridSpec(
            num_scalar_prefetch=1,
            grid=(seqs,),
            in_specs=[
                pl.BlockSpec(memory_space=pltpu.SMEM),
                by_seq(width),
                whole((1, width)),
                whole((width, 4 * inner)),
                by_seq(3 * inner),
                by_seq(inner),
                by_seq(TILE),
            ]
            + [whole(p.shape) for p in pieces]
            + [whole((1, width)), whole((experts, width))],
            out_specs=[piece] * tensors
            + [whole(sent), whole(sent), whole((width, 4 * inner)), whole((1, width))],
            scratch_shapes=[
                pltpu.VMEM((heads, LENGTH, LENGTH), F32),
                pltpu.VMEM((width, inner), BF16),
                pltpu.VMEM((LENGTH, inner), BF16),
                pltpu.VMEM((LENGTH, 3 * inner), BF16),
                pltpu.VMEM((heads * 3, TILE, TILE), F32),
                pltpu.VMEM((heads * 2, TILE, TILE), F32),
                pltpu.VMEM((heads * BUCKETS, TILE), F32),
                pltpu.VMEM((rows, width), BF16),
                pltpu.VMEM((rows, width), BF16),
                pltpu.VMEM((2 * z_count, experts, width), BF16),
            ],
        ),
        out_shape=[jax.ShapeDtypeStruct(pieces[0].shape, BF16)] * tensors
        + [
            jax.ShapeDtypeStruct(sent, F32 if plain else BF16),
            jax.ShapeDtypeStruct(sent, F32 if plain else BF16),
            jax.ShapeDtypeStruct((width, 4 * inner), F32),
            jax.ShapeDtypeStruct((1, width), F32),
        ],
        compiler_params=params(),
        cost_estimate=cost(18 * rows * width * inner + 10 * rows * LENGTH * inner, rows * width * 12, rows * LENGTH * heads),
        name="attend_back",
    )(places, bias, tokens, gain, weights, projected, mixed, logs, *pieces, gain_two, router)
    return result[:tensors], result[tensors:]


def first_rows_kernel(count, *refs):
    out_ref = refs[-1]
    at = 0
    for ref in refs[:-1]:
        for n in range(ref.shape[0]):
            out_ref[at] = ref[n, :count, :]
            at += 1


def first_rows(pieces, start, extra, count):
    width = pieces[0].shape[-1]
    total = sum(piece.shape[0] for piece in pieces)
    return pl.pallas_call(
        functools.partial(first_rows_kernel, count),
        grid=(1,),
        in_specs=[
            pl.BlockSpec((piece.shape[0], extra, width), lambda i: (0, start // extra, 0)) for piece in pieces
        ],
        out_specs=whole((total, count, width)),
        out_shape=jax.ShapeDtypeStruct((total, count, width), BF16),
        compiler_params=params(),
        cost_estimate=cost(0, 4 * total * extra * width),
        name="first_rows",
    )(*pieces)


def place_rows(target_ref, rows, out_refs):
    at = 0
    for ref in out_refs:
        count = ref.shape[0]
        index = lax.broadcasted_iota(jnp.int32, (count, rows.shape[0]), 0) + at
        chosen = jnp.where(index == target_ref[...], 1.0, 0.0).astype(BF16)
        ref[...] = dot(chosen, rows).astype(BF16)
        at += count


def place_kernel(target_ref, rows_ref, *out_refs):
    place_rows(target_ref, rows_ref[...], out_refs)


def place(target_row, rows, counts):
    return pl.pallas_call(
        place_kernel,
        out_shape=[jax.ShapeDtypeStruct((count, rows.shape[1]), BF16) for count in counts],
        compiler_params=params(),
        cost_estimate=cost(2 * sum(counts) * rows.size, 4 * rows.size),
        name="place",
    )(target_row, rows)


def softmax_rows(logits):
    exponent = jnp.exp(logits - jnp.max(logits, axis=-1, keepdims=True))
    return exponent * (1.0 / jnp.sum(exponent, axis=-1, keepdims=True))


def sum_pieces(refs):
    total = refs[0][...].astype(F32)
    for ref in refs[1:]:
        total = total + ref[...].astype(F32)
    return total


def route_kernel(tok_ref, *refs):
    gain_ref, router_ref, target_ref, index_ref, kept_ref, hidden_ref, gate_ref = refs[6:13]
    half = tok_ref.shape[0] // 2
    for h in range(2):
        keep, got, last = refs[3 * h : 3 * h + 3]
        here = slice(h * half, (h + 1) * half)
        added = keep[:half, :].astype(F32) + got[:half, :].astype(F32) + last[...].astype(F32)
        hidden_ref[here, :] = tok_ref[here, :].astype(F32) + added
    hidden = hidden_ref[...]
    unit, _ = unit_rows(hidden)
    moe_in = (unit * gain_ref[...]).astype(BF16)
    place_rows(target_ref, moe_in, refs[13:])
    probs = softmax_rows(dot(moe_in, router_ref[...]))
    lanes = lax.broadcasted_iota(jnp.int32, probs.shape, 1)
    picked = jnp.sum(jnp.where(lanes == index_ref[...], probs, 0.0), axis=-1, keepdims=True)
    gate_ref[...] = picked * kept_ref[...].astype(F32)


def route(tokens, attn, gain, router, target_row, index_col, kept_col, counts):
    rows, width = tokens.shape
    result = pl.pallas_call(
        route_kernel,
        out_shape=[
            jax.ShapeDtypeStruct((rows, width), F32),
            jax.ShapeDtypeStruct((rows, 1), F32),
        ]
        + [jax.ShapeDtypeStruct((count, width), BF16) for count in counts],
        compiler_params=params(),
        cost_estimate=cost(2 * sum(counts) * rows * width, 12 * rows * width),
        name="route",
    )(tokens, *attn, gain, router, target_row, index_col, kept_col)
    return result[0], result[1], result[2:]


def rest_choice(blocks, locals_, rest, expert):
    rows = lax.broadcasted_iota(jnp.int32, (blocks * rest, blocks * locals_ * rest), 0)
    cols = lax.broadcasted_iota(jnp.int32, (blocks * rest, blocks * locals_ * rest), 1)
    block = lax.div(rows, rest)
    wanted = block * (locals_ * rest) + expert * rest + (rows - block * rest)
    return jnp.where(cols == wanted, 1.0, 0.0).astype(BF16)


def pick_rows(out_ref, views, choice, main_rows, main, expert):
    at = 0
    pieces = []
    for view in views:
        blocks, size, width = view.shape
        if main:
            start = pl.multiple_of(expert * main, main)
            out_ref[at : at + blocks * main, :] = view[:, pl.ds(start, main), :].reshape(blocks * main, width)
            at += blocks * main
        rest = size - size * main_rows // out_ref.shape[0]
        pieces.append(view[:, size - rest :, :].reshape(blocks * rest, width))
    out_ref[main_rows:, :] = dot(choice, jnp.concatenate(pieces, axis=0)).astype(BF16)


def put_rows(views, value_ref, choice, main_rows, main, locals_, rest, expert):
    at = 0
    spread = dot(choice, value_ref[main_rows:, :], ROWS_TN).astype(BF16)
    rest_at = 0
    for view in views:
        blocks, _, width = view.shape
        if main:
            count = blocks * main
            start = pl.multiple_of(expert * main, main)
            view[:, pl.ds(start, main), :] = value_ref[at : at + count, :].reshape(blocks, main, width)
            at += count
        part = spread[rest_at : rest_at + blocks * locals_ * rest].reshape(blocks, locals_ * rest, width)
        rest_at += blocks * locals_ * rest

        before = view[:, locals_ * main :, :]
        view[:, locals_ * main :, :] = part + jnp.where(expert > 0, before, jnp.zeros_like(before))


def group_views(place_ref, ref, tensors, chunks):
    size = ref.shape[1] // chunks
    views = []
    for k in range(chunks):
        a, b = HOPS[k % 2]
        views += [ref.at[place_ref[2] ^ j, k * size : (k + 1) * size] for j in (0, a, b, a | b)]
    return views


def join_halves(place_ref, own_in, peer_in, own_out, peer_out, win, wout):
    half = own_in.shape[1]
    mine = pl.multiple_of(place_ref[0] * half, half)
    other = pl.multiple_of((1 - place_ref[0]) * half, half)
    if win is not None:
        win[pl.ds(mine, half), :] = own_in[0]
        win[pl.ds(other, half), :] = peer_in[0]
    half_out = own_out.shape[2]
    mine = pl.multiple_of(place_ref[0] * half_out, half_out)
    other = pl.multiple_of((1 - place_ref[0]) * half_out, half_out)
    wout[:, pl.ds(mine, half_out)] = own_out[0]
    wout[:, pl.ds(other, half_out)] = peer_out[0]


def expert_kernel(chunks, tensors, main, locals_, rest, place_ref, *refs):
    refs = list(refs)
    take = lambda n: [refs.pop(0) for _ in range(n)]
    xs = take(3 * chunks)
    (g_ref,) = take(1)
    own_in, peer_in, own_out, peer_out, router = take(5)
    backs = take(2 * chunks)
    x_ref, ge_ref, hid_ref, gi_ref, gl_ref = take(5)
    win, wout, grows, inner, gunits, gate_s, dots, back = take(8)
    expert = pl.program_id(0)
    blocks = sum(ref.shape[0] for ref in xs)
    main_rows = blocks * main
    rows, width = x_ref.shape[1:]
    wide = win.shape[1]
    choice = rest_choice(blocks, locals_, rest, expert)
    many = xs[0].shape[0]
    back_refs = []
    for k in range(chunks):
        keep, send = backs[2 * k : 2 * k + 2]
        back_refs += [ref.at[n * many : (n + 1) * many] for n in range(2) for ref in (keep, send)]
    pick_rows(x_ref.at[0], xs, choice, main_rows, main, expert)
    pick_rows(grows, group_views(place_ref, g_ref, tensors, chunks), choice, main_rows, main, expert)
    join_halves(place_ref, own_in, peer_in, own_out, peer_out, win, wout)
    probs = softmax_rows(dot(x_ref[0], router[...]))
    lanes = lax.broadcasted_iota(jnp.int32, probs.shape, 1)
    mine = lanes == place_ref[1] * locals_ + expert
    picked = jnp.sum(jnp.where(mine, probs, 0.0), axis=-1, keepdims=True)
    gate_s[...] = jnp.broadcast_to(picked, gate_s.shape)
    chunk = 16
    half_wide = wide // 2 if wide % (2 * TILE) == 0 else wide
    half_rows = rows // 2

    def multiply(part):
        at = slice(part * half_rows, (part + 1) * half_rows)
        inner[at, :] = dot(x_ref[0, at, :], win[...])
        gunits[at, :] = dot(grows[at, :], wout[...], ROWS_NT)

    def activate(part):
        for row in range(part * half_rows, (part + 1) * half_rows, chunk):
            at = slice(row, row + chunk)
            gate_tile = gate_s[at, :]
            gate = jnp.concatenate([gate_tile] * (half_wide // TILE), axis=1)
            total = None
            for start in range(0, wide, half_wide):
                lanes_at = slice(start, start + half_wide)
                value = inner[at, lanes_at]
                square = value * value
                wave = jnp.tanh(value * (GELU_A + (GELU_A * GELU_B) * square))
                half = 0.5 + 0.5 * wave
                hidden = (value * half).astype(BF16)
                bend = value * (0.5 * GELU_A + (1.5 * GELU_A * GELU_B) * square)
                slope = half + bend * (1.0 - wave * wave)
                units = gunits[at, lanes_at]
                hid_ref[0, at, lanes_at] = hidden
                gi_ref[0, at, lanes_at] = (gate * (units * slope)).astype(BF16)
                product = hidden.astype(F32) * units
                for tile in range(0, half_wide, TILE):
                    part_sum = product[:, tile : tile + TILE]
                    total = part_sum if total is None else total + part_sum
            dots[at, :] = total
            gate = jnp.concatenate([gate_tile] * (width // TILE), axis=1)
            ge_ref[0, at, :] = (gate * grows[at, :].astype(F32)).astype(BF16)

    def finish(part):
        at = slice(part * half_rows, (part + 1) * half_rows)
        grad_logits = (
            jnp.sum(dots[at, :], axis=-1, keepdims=True)
            * probs[at]
            * (jnp.where(mine[at], 1.0, 0.0) - picked[at])
        ).astype(BF16)
        gl_ref[0, at, :] = grad_logits
        back[at, :] = (
            dot(gi_ref[0, at, :], win[...], ROWS_NT) + dot(grad_logits, router[...], ROWS_NT)
        ).astype(BF16)

    multiply(0)
    multiply(1)
    activate(0)
    finish(0)
    activate(1)
    finish(1)
    put_rows(back_refs, back, choice, main_rows, main, locals_, rest, expert)


def expert_forward_back(places, xs, gs, own_in, peer_in, own_out, peer_out, router, main, rest, chunks):
    locals_, half, wide = own_in.shape
    width, experts = router.shape
    many, block = xs[0].shape[:2]
    tensors = gs.shape[0]
    blocks = tensors * chunks * many
    back = (2 * many, block, width)
    rows = blocks * (main + rest)
    per = lambda *shape: pl.BlockSpec((1,) + shape, lambda e, *_: (e, 0, 0))
    saved = jax.ShapeDtypeStruct((locals_, rows, width), BF16)
    saved_wide = jax.ShapeDtypeStruct((locals_, rows, wide), BF16)
    result = pl.pallas_call(
        functools.partial(expert_kernel, chunks, tensors, main, locals_, rest),
        grid_spec=pltpu.PrefetchScalarGridSpec(
            num_scalar_prefetch=1,
            grid=(locals_,),
            in_specs=[whole(x.shape) for x in xs]
            + [whole(gs.shape)]
            + [per(half, wide)] * 2 + [per(wide, half)] * 2 + [whole((width, experts))],
            out_specs=[whole(back)] * (2 * chunks)
            + [per(rows, width), per(rows, width), per(rows, wide), per(rows, wide), per(rows, experts)],
            scratch_shapes=[
                pltpu.VMEM((width, wide), BF16),
                pltpu.VMEM((wide, width), BF16),
                pltpu.VMEM((rows, width), BF16),
                pltpu.VMEM((rows, wide), F32),
                pltpu.VMEM((rows, wide), F32),
                pltpu.VMEM((rows, TILE), F32),
                pltpu.VMEM((rows, TILE), F32),
                pltpu.VMEM((rows, width), BF16),
            ],
        ),
        out_shape=[jax.ShapeDtypeStruct(back, BF16)] * (2 * chunks)
        + [saved, saved, saved_wide, saved_wide, jax.ShapeDtypeStruct((locals_, rows, experts), BF16)],
        compiler_params=params(),
        cost_estimate=cost(6 * locals_ * rows * width * wide, locals_ * rows * width * 14, locals_ * rows * wide),
        name="experts",
    )(places, *xs, gs, own_in, peer_in, own_out, peer_out, router)
    return result[: 2 * chunks], result[2 * chunks :]


def expert_rows_kernel(chunks, main, locals_, rest, place_ref, hid_ref, own_out, peer_out, forward_ref, wout, value):
    expert = pl.program_id(0)
    tensors = forward_ref.shape[0]
    blocks = tensors * forward_ref.shape[1]
    choice = rest_choice(blocks, locals_, rest, expert)
    join_halves(place_ref, own_out, peer_out, own_out, peer_out, None, wout)
    value[...] = dot(hid_ref[0], wout[...]).astype(BF16)
    views = group_views(place_ref, forward_ref, tensors, chunks)
    put_rows(views, value, choice, blocks * main, main, locals_, rest, expert)


def expert_rows(places, hidden, own_out, peer_out, shape, main, rest, chunks):
    locals_, rows, wide = hidden.shape
    half = own_out.shape[2]
    width = shape[-1]
    per = lambda *shape: pl.BlockSpec((1,) + shape, lambda e, *_: (e, 0, 0))
    return pl.pallas_call(
        functools.partial(expert_rows_kernel, chunks, main, locals_, rest),
        grid_spec=pltpu.PrefetchScalarGridSpec(
            num_scalar_prefetch=1,
            grid=(locals_,),
            in_specs=[per(rows, wide)] + [per(wide, half)] * 2,
            out_specs=whole(shape),
            scratch_shapes=[pltpu.VMEM((wide, width), BF16), pltpu.VMEM((rows, width), BF16)],
        ),
        out_shape=jax.ShapeDtypeStruct(shape, BF16),
        compiler_params=params(),
        cost_estimate=cost(2 * locals_ * rows * width * wide, locals_ * rows * width * 6),
        name="expert_rows",
    )(places, hidden, own_out, peer_out)


def expert_weights_kernel(place_ref, x_ref, ge_ref, hid_ref, gi_ref, gl_ref, *refs):
    in_own, in_send, out_own, out_send, router_ref = refs
    half = in_own.shape[1]
    mine = pl.ds(pl.multiple_of(place_ref[0] * half, half), half)
    other = pl.ds(pl.multiple_of((1 - place_ref[0]) * half, half), half)
    in_own[0] = dot(x_ref[0, :, mine], gi_ref[0], ROWS_TN)
    in_send[0] = dot(x_ref[0, :, other], gi_ref[0], ROWS_TN).astype(BF16)
    out_own[0] = dot(hid_ref[0], ge_ref[0, :, mine], ROWS_TN)
    out_send[0] = dot(hid_ref[0], ge_ref[0, :, other], ROWS_TN).astype(BF16)

    @pl.when(pl.program_id(0) == 0)
    def _():
        router_ref[...] = jnp.zeros_like(router_ref)

    router_ref[...] += dot(gl_ref[0], x_ref[0], ROWS_TN)


def expert_weights(places, saved, half):
    x, ge, hidden, gi, gl = saved
    locals_, rows, width = x.shape
    wide = hidden.shape[2]
    experts = gl.shape[2]
    per = lambda *shape: pl.BlockSpec((1,) + shape, lambda e, *_: (e, 0, 0))
    return pl.pallas_call(
        expert_weights_kernel,
        grid_spec=pltpu.PrefetchScalarGridSpec(
            num_scalar_prefetch=1,
            grid=(locals_,),
            in_specs=[per(rows, width), per(rows, width), per(rows, wide), per(rows, wide), per(rows, experts)],
            out_specs=[per(half, wide), per(half, wide), per(wide, half), per(wide, half), whole((experts, width))],
        ),
        out_shape=[
            jax.ShapeDtypeStruct((locals_, half, wide), F32),
            jax.ShapeDtypeStruct((locals_, half, wide), BF16),
            jax.ShapeDtypeStruct((locals_, wide, half), F32),
            jax.ShapeDtypeStruct((locals_, wide, half), BF16),
            jax.ShapeDtypeStruct((experts, width), F32),
        ],
        compiler_params=params(),
        cost_estimate=cost(4 * locals_ * rows * width * wide, locals_ * rows * width * 14),
        name="expert_weights",
    )(places, x, ge, hidden, gi, gl)


def take_rows(target_ref, refs):
    total, at = None, 0
    for ref in refs:
        count = ref.shape[0]
        cols = lax.broadcasted_iota(jnp.int32, (target_ref.shape[0], count), 1) + at
        chosen = jnp.where(cols == target_ref[...], 1.0, 0.0).astype(BF16)
        part = dot(chosen, ref[...])
        total = part if total is None else total + part
        at += count
    return total


def hidden_back_kernel(target_ref, *refs):
    hidden_ref, cot_ref, gain_ref, grad_ref, attn_ref, gain_out = refs[-6:]
    grad_in = take_rows(target_ref, refs[:-6])
    unit, scale = unit_rows(hidden_ref[...])
    gain_out[...] = jnp.sum(grad_in * unit, axis=0, keepdims=True)
    scaled = grad_in * gain_ref[...]
    inside = jnp.mean(unit * scaled, axis=-1, keepdims=True)
    grad = cot_ref[...].astype(F32) + scale * (scaled - unit * inside)
    grad_ref[...] = grad
    attn_ref[...] = grad.astype(BF16)


def hidden_back(target_col, back, hidden, cotangent, gain):
    rows, width = hidden.shape
    return pl.pallas_call(
        hidden_back_kernel,
        out_shape=[
            jax.ShapeDtypeStruct((rows, width), F32),
            jax.ShapeDtypeStruct((rows, width), BF16),
            jax.ShapeDtypeStruct((1, width), F32),
        ],
        compiler_params=params(),
        cost_estimate=cost(3 * rows * rows * width, 16 * rows * width),
        name="hidden_back",
    )(target_col, *back, hidden, cotangent, gain)


def output_kernel(target_ref, *refs):
    hidden_ref, gate_ref, out_ref = refs[-3:]
    out_ref[...] = (hidden_ref[...] + gate_ref[...] * take_rows(target_ref, refs[:-3])).astype(BF16)


def output_rows(target_col, expert_rows, hidden, gate):
    return pl.pallas_call(
        output_kernel,
        out_shape=jax.ShapeDtypeStruct(hidden.shape, BF16),
        compiler_params=params(),
        cost_estimate=cost(3 * hidden.shape[0] * hidden.size, 10 * hidden.size),
        name="output_rows",
    )(target_col, *expert_rows, hidden, gate)


def tokens_back_kernel(tok_ref, *refs):
    gain_ref, hidden_ref, out_ref = refs[6:]
    half = tok_ref.shape[0] // 2
    for h in range(2):
        keep, got, last = refs[3 * h : 3 * h + 3]
        here = slice(h * half, (h + 1) * half)
        unit, scale = unit_rows(tok_ref[here, :].astype(F32))
        grad = keep[:half, :].astype(F32) + got[:half, :].astype(F32) + last[...].astype(F32)
        scaled = grad * gain_ref[...]
        inside = jnp.mean(unit * scaled, axis=-1, keepdims=True)
        out_ref[here, :] = hidden_ref[here, :] + scale * (scaled - unit * inside)


def tokens_back(tokens, grad_normed, gain, grad_hidden):
    return pl.pallas_call(
        tokens_back_kernel,
        out_shape=jax.ShapeDtypeStruct(tokens.shape, F32),
        compiler_params=params(),
        cost_estimate=cost(10 * tokens.size, 12 * tokens.size),
        name="tokens_back",
    )(tokens, *grad_normed, gain, grad_hidden)


def shifted(value, axis, count, step):
    return lax.ppermute(value, axis, [(s, (s + step) % count) for s in range(count)])


def gather_ring(value, axis, count):
    me = lax.axis_index(axis)
    parts = [value] + [shifted(value, axis, count, -k) for k in range(1, count)]
    return jnp.roll(jnp.stack(parts), me, axis=0)


def swapped(value, axis, count, bits):
    return lax.ppermute(value, axis, [(s, s ^ bits) for s in range(count)])


def gather_pieces(value, axis, count):
    return [value] + [swapped(value, axis, count, k) for k in range(1, count)]


def gather_hops(value, hops):
    a, b = hops
    first = swapped(value, "tensor", 4, a)
    second = swapped(jnp.concatenate([value, first], axis=0), "tensor", 4, b)
    return first, second


def sum_hops(parts):
    half = parts[0].shape[0] // 2
    result = []
    for h, (a, b) in enumerate(HOPS):
        keep, send = parts[2 * h : 2 * h + 2]
        got = swapped(send, "tensor", 4, a)
        last = swapped(added(keep[half:], got[half:]), "tensor", 4, b)
        result += [keep, got, last]
    return result


def added(a, b):
    return (a.astype(F32) + b.astype(F32)).astype(BF16)


def swap_pieces(pieces, axis, count):
    return [pieces[0]] + [swapped(pieces[k], axis, count, k) for k in range(1, count)]


def on_device(
    sizes,
    tokens,
    cotangent,
    query_key_value_weight,
    attention_output_weight,
    rel_bias,
    gain_attn,
    gain_moe,
    w_router,
    w_in,
    w_out,
    expert_index,
    slot_index,
    kept_mask,
):
    dp_count, z_count, t_count = sizes
    tok_rows, width = tokens.shape
    experts_all = w_router.shape[1]
    capacity = max(2, 3 * tok_rows // (2 * experts_all))
    locals_ = w_in.shape[0]
    main = capacity // 16 * 16
    rest = capacity - main
    block = locals_ * capacity
    heads = rel_bias.shape[0]
    inner = heads * HEAD_DIM
    part = query_key_value_weight.shape[1]
    fine = w_router.shape[0]
    my_dp = lax.axis_index("dp")
    my_z = lax.axis_index("expert")
    bias = rel_bias.astype(F32)

    my_t = lax.axis_index("tensor")
    owners = dp_count * z_count
    my_owner = my_dp * z_count + my_z
    places = jnp.stack([my_dp, my_z, my_t, my_owner]).astype(jnp.int32)
    half_rows = tok_rows // 2
    token_pieces = [tokens]
    for h, hops in enumerate(HOPS):
        token_pieces += list(gather_hops(tokens[h * half_rows : (h + 1) * half_rows], hops))

    small = jnp.concatenate([gain_attn[:, None], gain_moe[:, None], w_router], axis=1).reshape(-1)
    extra = -(-small.shape[0] // (16 * width)) * 16
    packed = jnp.concatenate(
        [
            query_key_value_weight.transpose(1, 0, 2).reshape(part, 3 * inner),
            attention_output_weight.T,
        ],
        axis=1,
    )
    packed = jnp.concatenate(
        [packed, jnp.pad(small, (0, extra * width - small.shape[0])).reshape(extra, width)], axis=0
    )
    owned = gather_pieces(packed[None], "expert", z_count)
    owned = owned + [swapped(jnp.concatenate(owned, axis=0), "dp", dp_count, 1)]
    if part % 16 or part % extra:
        smalls = jnp.concatenate(owned, axis=0)[:, part:]
    else:
        smalls = first_rows(owned, part, extra, -(-small.shape[0] // width))
    smalls = smalls.reshape(owners, -1)[:, : small.shape[0]]
    small_pieces = gather_pieces(smalls, "tensor", t_count)

    z_of = expert_index // locals_
    local = expert_index - z_of * locals_
    inside = jnp.where(
        slot_index < main, local * main + slot_index, locals_ * main + local * rest + slot_index - main
    )
    target = (z_of ^ my_z) * block + inside
    target = jnp.where(kept_mask > 0, target, -1)
    target_row, target_col = target[None, :], target[:, None]
    chunks = min(z_count, 4)
    many = z_count // chunks
    counts = [many * block] * chunks
    grad_sent = place(target_row, cotangent, counts)
    token_pieces, owned, small_pieces, grad_sent = lax.optimization_barrier(
        (token_pieces, owned, small_pieces, grad_sent)
    )
    smalls = jnp.stack(small_pieces).reshape(t_count * owners, -1)
    owner_ids = jnp.arange(owners, dtype=jnp.int32)[:, None] ^ my_owner
    t_ids = jnp.arange(t_count, dtype=jnp.int32)[None, :] ^ my_t
    smalls = smalls[(t_ids * owners + owner_ids).reshape(-1)].reshape(width, 2 + experts_all)
    if part % 16:
        order = jnp.arange(owners, dtype=jnp.int32) ^ my_owner
        owned = [jnp.concatenate(owned, axis=0)[:, :part][order].reshape(1, width, 4 * inner)]
    rows_owned = part if len(owned) > 1 else width
    gain_one = smalls[:, 0].astype(F32)[None]
    gain_two = smalls[:, 1].astype(F32)[None]
    router = smalls[:, 2:]

    def over_expert(groups):
        if many > 1:
            groups = [g[i * block : (i + 1) * block] for g in groups for i in range(many)]
        pieces = swap_pieces(groups, "expert", z_count)
        if many == 1:
            return pieces
        return [jnp.concatenate(pieces[k * many : (k + 1) * many], axis=0) for k in range(chunks)]

    grad_rows = jnp.concatenate(over_expert(grad_sent), axis=0)
    parts, (group_tokens, projected, mixed, logs, weights) = attend(
        places, bias, token_pieces, owned, rows_owned, gain_one
    )
    parts, late_in, late_out, grad_rows = lax.optimization_barrier((parts, w_in, w_out, grad_rows))
    peer_in = shifted(late_in, "dp", dp_count, 1)
    peer_out = shifted(late_out, "dp", dp_count, 1)
    grad_arrived = lax.all_gather(grad_rows, "tensor", axis=0).reshape(t_count, z_count, block, width)
    attn = sum_hops(parts)
    attn, peer_in, peer_out = lax.optimization_barrier((attn, peer_in, peer_out))
    hidden_one, gate, sent = route(
        tokens, attn, gain_two, router, target_row, expert_index[:, None], kept_mask[:, None], counts
    )
    arrived = []
    for k, group in enumerate(over_expert(sent)):
        pieces = (group,) + gather_hops(group, HOPS[k % 2])
        arrived += [piece.reshape(-1, block, width) for piece in pieces]
    back_parts, saved = expert_forward_back(
        places, arrived, grad_arrived, w_in, peer_in, w_out, peer_out, router, main, rest, chunks
    )

    size = many * block
    back_parts = [piece.reshape(2 * size, width) for piece in back_parts]
    keeps, sends = back_parts[::2], back_parts[1::2]
    got = [swapped(sends[k], "tensor", t_count, HOPS[k % 2][0]) for k in reversed(range(chunks))][::-1]
    forward_part = expert_rows(places, saved[2], w_out, peer_out, grad_arrived.shape, main, rest, chunks)
    got, forward_part = lax.optimization_barrier((got, forward_part))
    groups = []
    for k in range(chunks):
        last = swapped(added(keeps[k][size:], got[k][size:]), "tensor", t_count, HOPS[k % 2][1])
        total = keeps[k][:size].astype(F32) + got[k][:size].astype(F32) + last.astype(F32)
        groups.append(total.astype(BF16))
    forward_part, groups, saved = lax.optimization_barrier((forward_part, groups, saved))
    forward_sum = lax.psum_scatter(
        forward_part.reshape(t_count * z_count * block, width), "tensor", scatter_dimension=0, tiled=True
    )
    in_own, in_send, out_own, out_send, router_part = expert_weights(places, saved, w_in.shape[1])
    grad_back, in_send, out_send = lax.optimization_barrier((over_expert(groups), in_send, out_send))
    in_got = shifted(in_send, "dp", dp_count, 1)
    out_got = shifted(out_send, "dp", dp_count, 1)
    grad_hidden, grad_attn, gain_two_part = hidden_back(target_col, grad_back, hidden_one, cotangent, gain_two)
    grad_pieces = [grad_attn]
    for h, hops in enumerate(HOPS):
        grad_pieces += list(gather_hops(grad_attn[h * half_rows : (h + 1) * half_rows], hops))
    grad_w_in = in_own + in_got.astype(F32)
    grad_w_out = out_own + out_got.astype(F32)
    grad_pieces, grad_w_in, grad_w_out, forward_sum = lax.optimization_barrier(
        (grad_pieces, grad_w_in, grad_w_out, forward_sum)
    )
    normed_parts, (own_part, other_part, weight_part, gain_one_part) = attend_back(
        places, bias, group_tokens, gain_one, weights, projected, mixed, logs, grad_pieces,
        gain_two_part, router_part, part, z_count,
    )
    forward_rows = over_expert(list(forward_sum.reshape(chunks, many * block, width)))
    normed_parts, own_part, other_part, forward_rows = lax.optimization_barrier(
        (normed_parts, own_part, other_part, forward_rows)
    )
    grad_normed = sum_hops(normed_parts)
    output = output_rows(target_col, forward_rows, hidden_one, gate)
    grad_tokens = tokens_back(tokens, grad_normed, gain_one, grad_hidden)

    if part % 16 or part > TILE or experts_all % 16:
        pad = lambda value, lanes: jnp.pad(value, ((0, 0), (0, lanes - value.shape[1])))
        gains = jnp.concatenate([gain_one_part, gain_two_part, jnp.zeros((experts_all - 2, width), F32)])
        sums = jnp.pad(own_part.reshape(1, -1), ((0, experts_all - 1), (0, TILE - own_part.shape[0])))
        extras = [
            pad(jnp.concatenate([pad(router_part[:, cut], TILE), pad(gains[:, cut], TILE), sums], axis=1), width)
            for cut in (slice(n * part, (n + 1) * part) for n in range(owners))
        ]
        order = jnp.arange(owners, dtype=jnp.int32) ^ my_owner
        payload = jnp.concatenate(
            [weight_part.astype(BF16).reshape(owners, part, width), jnp.stack(extras).astype(BF16)], axis=1
        )[order]
        own_part, other_part = payload[:z_count], payload[z_count:]
    other_got = shifted(other_part, "dp", dp_count, 1)
    pieces = swap_pieces([added(own_part[k], other_got[k]) for k in range(z_count)], "expert", z_count)
    pieces, grad_tokens = lax.optimization_barrier((pieces, grad_tokens))
    total = pieces[0].astype(F32)
    for piece in pieces[1:]:
        total = total + piece.astype(F32)
    weight_total = total[:part].reshape(part, 4, inner)
    grad_w_qkv = weight_total[:, :3].transpose(1, 0, 2)
    grad_w_attn_out = weight_total[:, 3].T
    grad_rel_bias = total[part, 2 * TILE : 2 * TILE + heads * BUCKETS].reshape(heads, BUCKETS)
    mine = jnp.concatenate([total[part : part + 2, TILE : TILE + part], total[part:, :part]], axis=0)
    turned = [
        lax.dynamic_slice_in_dim(mine, (my_t ^ k) * fine, fine, axis=1).reshape(-1) for k in range(t_count)
    ]
    left = turned[0]
    for piece in swap_pieces(turned, "tensor", t_count)[1:]:
        left = left + piece
    grad_gain_attn = left[:fine]
    grad_gain_moe = left[fine : 2 * fine]
    grad_w_router = left[2 * fine :].reshape(experts_all, fine).T
    return (
        output,
        grad_tokens,
        grad_w_qkv,
        grad_w_attn_out,
        grad_rel_bias,
        grad_gain_attn,
        grad_gain_moe,
        grad_w_router,
        grad_w_in,
        grad_w_out,
    )


def solution(mesh):
    placed = (
        P(("dp", "expert", "tensor"), None),
        P(("dp", "expert", "tensor"), None),
        P(None, ("dp", "expert"), "tensor"),
        P("tensor", ("dp", "expert")),
        P("tensor", None),
        P(("dp", "expert", "tensor")),
        P(("dp", "expert", "tensor")),
        P(("dp", "expert", "tensor"), None),
        P("expert", "dp", "tensor"),
        P("expert", "tensor", "dp"),
        P(("dp", "expert", "tensor")),
        P(("dp", "expert", "tensor")),
        P(("dp", "expert", "tensor")),
    )
    sizes = tuple(mesh.shape[name] for name in ("dp", "expert", "tensor"))
    return jax.shard_map(
        functools.partial(on_device, sizes),
        mesh=mesh,
        in_specs=placed,
        out_specs=(
            P(("dp", "expert", "tensor"), None),
            P(("dp", "expert", "tensor"), None),
            P(None, ("dp", "expert"), "tensor"),
            P("tensor", ("dp", "expert")),
            P("tensor", None),
            P(("dp", "expert", "tensor")),
            P(("dp", "expert", "tensor")),
            P(("dp", "expert", "tensor"), None),
            P("expert", "dp", "tensor"),
            P("expert", "tensor", "dp"),
        ),
        check_vma=False,
    )
```

```python
import functools

import jax
import jax.numpy as jnp
from jax import lax
from jax.experimental import pallas as pl
from jax.experimental.pallas import tpu as pltpu
from jax.sharding import PartitionSpec as P

HEAD_DIM = 64
BUCKETS = 32
LENGTH = 512
TILE = 128
EPSILON = 1e-06
BORDERS = (12, 16, 23, 32, 46, 64, 91)
F32 = jnp.float32
BF16 = jnp.bfloat16
GELU_A = 0.7978845608028654
GELU_B = 0.044715
ROWS_NN = (((1,), (0,)), ((), ()))
ROWS_NT = (((1,), (1,)), ((), ()))
ROWS_TN = (((0,), (0,)), ((), ()))
VMEM_BYTES = 56 * 1024 * 1024


def dot(a, b, dims=ROWS_NN):
    return lax.dot_general(a, b, dims, preferred_element_type=F32)


def params(**more):
    return pltpu.CompilerParams(vmem_limit_bytes=VMEM_BYTES, **more)


def cost(flops, moved, special=0):
    return pl.CostEstimate(flops=int(flops), bytes_accessed=int(moved), transcendentals=int(special))


def whole(shape):
    return pl.BlockSpec(shape, lambda *_: (0,) * len(shape))


def tile_bucket(step):
    rows = lax.broadcasted_iota(jnp.int32, (TILE, TILE), 0)
    cols = lax.broadcasted_iota(jnp.int32, (TILE, TILE), 1)
    offset = cols - rows + step * TILE
    distance = jnp.abs(offset)
    bucket = jnp.minimum(distance, 8)
    for border in BORDERS:
        bucket = bucket + jnp.where(distance >= border, 1, 0)
    return bucket + jnp.where(offset > 0, 16, 0)


def tile_range(step):
    return {-1: range(1, 16), 0: range(0, 32), 1: range(17, 32)}[step]


def fill_bias(bias_ref, table, heads):
    blocks = LENGTH // TILE
    buckets = {step: tile_bucket(step) for step in (-1, 0, 1)}
    for head in range(heads):
        near = {}
        for step in (-1, 0, 1):
            value = jnp.zeros((TILE, TILE), F32)
            for k in tile_range(step):
                value = jnp.where(buckets[step] == k, bias_ref[head, k], value)
            near[step] = value
        low = jnp.full((TILE, TILE), bias_ref[head, 15], F32)
        high = jnp.full((TILE, TILE), bias_ref[head, 31], F32)
        for i in range(blocks):
            for j in range(blocks):
                step = j - i
                value = near[step] if abs(step) <= 1 else (low if step < 0 else high)
                table[head, i * TILE : (i + 1) * TILE, j * TILE : (j + 1) * TILE] = value


def unit_rows(values):
    scale = lax.rsqrt(jnp.mean(values * values, axis=-1, keepdims=True) + EPSILON)
    return values * scale, scale


HOPS = ((1, 2), (2, 1))


def group_halves(place_ref, out, pieces):
    rows = pieces[0].shape[0]
    half = rows // 2
    at = pl.multiple_of(place_ref[2] * rows, rows)
    out[pl.ds(at, rows), :] = pieces[0][...]
    for h, (a, b) in enumerate(HOPS):
        first, second = pieces[1 + 2 * h : 3 + 2 * h]
        for j, value in ((a, first[...]), (b, second[:half, :]), (a | b, second[half:, :])):
            at = pl.multiple_of((place_ref[2] ^ j) * rows + h * half, half)
            out[pl.ds(at, half), :] = value


def part_halves(place_ref, pieces, source):
    half = pieces[0].shape[0] // 2
    for h, (a, b) in enumerate(HOPS):
        for piece, order in zip(pieces[2 * h : 2 * h + 2], ((0, b), (a, a | b))):
            for n, j in enumerate(order):
                at = pl.multiple_of((place_ref[2] ^ j) * 2 * half + h * half, half)
                piece[n * half : (n + 1) * half, :] = source[pl.ds(at, half), :]


def attend_kernel(heads, tensors, owners, part, place_ref, bias_ref, *refs):
    refs = list(refs)
    take = lambda n: [refs.pop(0) for _ in range(n)]
    pieces, owned, (gain_ref,), parts = take(5), take(owners), take(1), take(tensors)
    tok_ref, qkv_ref, mixed_ref, log_ref, w_ref, table, wo, group, result = refs
    inner = heads * HEAD_DIM
    step_id = pl.program_id(0)

    @pl.when(step_id == 0)
    def _():
        fill_bias(bias_ref, table, heads)
        group_halves(place_ref, group, pieces)
        blocks = [piece.at[n] for piece in owned for n in range(piece.shape[0])]
        for k, piece in enumerate(blocks):
            at = pl.multiple_of((place_ref[3] ^ k) * part, part) if owners > 1 else 0
            w_ref[pl.ds(at, part), :] = piece[:part, :]
        wo[...] = w_ref[:, 3 * inner :]

    here = pl.ds(pl.multiple_of(step_id * LENGTH, LENGTH), LENGTH)
    tok_ref[...] = group[here, :]
    unit, _ = unit_rows(tok_ref[...].astype(F32))
    normed = (unit * gain_ref[...]).astype(BF16)
    qkv_ref[...] = dot(normed, w_ref[:, : 3 * inner]).astype(BF16)
    lanes = lax.broadcasted_iota(jnp.int32, (LENGTH, TILE), 1)
    logs = jnp.zeros((LENGTH, TILE), F32)
    for head in range(heads):
        at = head * HEAD_DIM
        query = qkv_ref[:, at : at + HEAD_DIM] * HEAD_DIM ** (-0.5)
        key = qkv_ref[:, inner + at : inner + at + HEAD_DIM]
        value = qkv_ref[:, 2 * inner + at : 2 * inner + at + HEAD_DIM]
        scores = dot(query.astype(BF16), key, ROWS_NT) + table[head]
        top = jnp.max(scores, axis=-1, keepdims=True)
        exponent = jnp.exp(scores - top)
        total = jnp.sum(exponent, axis=-1, keepdims=True)
        attention = (exponent * (1.0 / total)).astype(BF16)
        mixed_ref[:, at : at + HEAD_DIM] = dot(attention, value).astype(BF16)
        logs = jnp.where(lanes == head, top + jnp.log(total), logs)
    log_ref[...] = logs
    result[here, :] = dot(mixed_ref[...], wo[...], ROWS_NT).astype(BF16)

    @pl.when(step_id == pl.num_programs(0) - 1)
    def _():
        part_halves(place_ref, parts, result)


def attend(places, bias, pieces, owned, part, gain):
    tensors = 4
    piece_rows, width = pieces[0].shape
    rows = tensors * piece_rows
    heads = bias.shape[0]
    inner = heads * HEAD_DIM
    seqs = rows // LENGTH
    by_seq = lambda cols: pl.BlockSpec((LENGTH, cols), lambda s, *_: (s, 0))
    result = pl.pallas_call(
        functools.partial(attend_kernel, heads, tensors, len(owned), part),
        grid_spec=pltpu.PrefetchScalarGridSpec(
            num_scalar_prefetch=1,
            grid=(seqs,),
            in_specs=[pl.BlockSpec(memory_space=pltpu.SMEM)]
            + [whole(p.shape) for p in pieces]
            + [whole(o.shape) for o in owned]
            + [whole((1, width))],
            out_specs=[whole((piece_rows, width))] * tensors
            + [by_seq(width), by_seq(3 * inner), by_seq(inner), by_seq(TILE), whole((width, 4 * inner))],
            scratch_shapes=[
                pltpu.VMEM((heads, LENGTH, LENGTH), F32),
                pltpu.VMEM((width, inner), BF16),
                pltpu.VMEM((rows, width), BF16),
                pltpu.VMEM((rows, width), BF16),
            ],
        ),
        out_shape=[jax.ShapeDtypeStruct((piece_rows, width), BF16)] * tensors
        + [
            jax.ShapeDtypeStruct((rows, width), BF16),
            jax.ShapeDtypeStruct((rows, 3 * inner), BF16),
            jax.ShapeDtypeStruct((rows, inner), BF16),
            jax.ShapeDtypeStruct((rows, TILE), F32),
            jax.ShapeDtypeStruct((width, 4 * inner), BF16),
        ],
        compiler_params=params(),
        cost_estimate=cost(8 * rows * width * inner + 4 * rows * LENGTH * inner, rows * width * 8, rows * LENGTH * heads),
        name="attend",
    )(places, bias, *pieces, *owned, gain)
    return result[:tensors], result[tensors:]


def attend_back_kernel(
    heads, tensors, part, place_ref, bias_ref, tok_ref, gain_ref, w_ref, qkv_ref, mixed_ref, log_ref, *refs
):
    refs = list(refs)
    pieces = [refs.pop(0) for _ in range(5)]
    gain_two_ref, router_ref = refs.pop(0), refs.pop(0)
    parts = [refs.pop(0) for _ in range(tensors)]
    own_ref, other_ref, weight_ref, gain_out, table, wo, gmix, gproj, near, far, rows_s, group, result, extras = refs
    inner = heads * HEAD_DIM
    blocks = LENGTH // TILE
    step_id = pl.program_id(0)

    @pl.when(step_id == 0)
    def _():
        fill_bias(bias_ref, table, heads)
        wo[...] = w_ref[:, 3 * inner :]
        near[...] = jnp.zeros_like(near)
        far[...] = jnp.zeros_like(far)
        weight_ref[...] = jnp.zeros_like(weight_ref)
        gain_out[...] = jnp.zeros_like(gain_out)
        group_halves(place_ref, group, pieces)

    here = pl.ds(pl.multiple_of(step_id * LENGTH, LENGTH), LENGTH)
    gmix[...] = dot(group[here, :], wo[...]).astype(BF16)
    for head in range(heads):
        at = head * HEAD_DIM
        query = (qkv_ref[:, at : at + HEAD_DIM] * HEAD_DIM ** (-0.5)).astype(BF16)
        key = qkv_ref[:, inner + at : inner + at + HEAD_DIM]
        value = qkv_ref[:, 2 * inner + at : 2 * inner + at + HEAD_DIM]
        grad_rows = gmix[:, at : at + HEAD_DIM]
        scores = dot(query, key, ROWS_NT) + table[head]
        attention = jnp.exp(scores - log_ref[:, head : head + 1])
        grad_weights = dot(grad_rows, value, ROWS_NT)
        inner_sum = jnp.sum(attention * grad_weights, axis=-1, keepdims=True)
        grad_scores = attention * (grad_weights - inner_sum)
        low = jnp.zeros((TILE, TILE), F32)
        high = jnp.zeros((TILE, TILE), F32)
        mid = [jnp.zeros((TILE, TILE), F32) for _ in range(3)]
        for i in range(blocks):
            for j in range(blocks):
                piece = grad_scores[i * TILE : (i + 1) * TILE, j * TILE : (j + 1) * TILE]
                if abs(j - i) <= 1:
                    mid[j - i + 1] = mid[j - i + 1] + piece
                elif j < i:
                    low = low + piece
                else:
                    high = high + piece
        for k in range(3):
            near[head * 3 + k] += mid[k]
        far[head * 2] += low
        far[head * 2 + 1] += high
        rounded = grad_scores.astype(BF16)
        gproj[:, at : at + HEAD_DIM] = (dot(rounded, key) * HEAD_DIM ** (-0.5)).astype(BF16)
        gproj[:, inner + at : inner + at + HEAD_DIM] = dot(rounded, query, ROWS_TN).astype(BF16)
        gproj[:, 2 * inner + at : 2 * inner + at + HEAD_DIM] = dot(
            attention.astype(BF16), grad_rows, ROWS_TN
        ).astype(BF16)
    unit, _ = unit_rows(tok_ref[...].astype(F32))
    normed = (unit * gain_ref[...]).astype(BF16)
    grad_normed = dot(gproj[...], w_ref[:, : 3 * inner], ROWS_NT)
    result[here, :] = grad_normed.astype(BF16)
    gain_out[...] += jnp.sum(grad_normed * unit, axis=0, keepdims=True)
    weight_ref[:, : 3 * inner] += dot(normed, gproj[...], ROWS_TN)
    weight_ref[:, 3 * inner :] += dot(group[here, :], mixed_ref[...], ROWS_TN)

    @pl.when(step_id == pl.num_programs(0) - 1)
    def _():
        part_halves(place_ref, parts, result)
        ids = [tile_bucket(step) for step in (-1, 0, 1)]
        for head in range(heads):
            for k in range(BUCKETS):
                total = jnp.zeros((TILE, TILE), F32)
                for step in (-1, 0, 1):
                    if k in tile_range(step):
                        total = total + jnp.where(ids[step + 1] == k, near[head * 3 + step + 1], 0.0)
                if k == 15:
                    total = total + far[head * 2]
                if k == 31:
                    total = total + far[head * 2 + 1]
                at = head * BUCKETS + k
                rows_s[at : at + 1, :] = jnp.sum(total, axis=0, keepdims=True)
        sums = jnp.sum(rows_s[...], axis=1, keepdims=True)
        experts = router_ref.shape[0]
        if part % 16 or part > TILE or experts % 16:
            own_ref[...] = jnp.broadcast_to(sums, own_ref.shape)
            return
        count = sums.shape[0]
        diagonal = lax.broadcasted_iota(jnp.int32, (count, TILE), 0) == lax.broadcasted_iota(
            jnp.int32, (count, TILE), 1
        )
        sums = jnp.sum(jnp.where(diagonal, sums, 0.0), axis=0, keepdims=True)
        z_count = own_ref.shape[0]
        owners = 2 * z_count
        gap = jnp.zeros((experts, TILE - part), F32)
        low = jnp.zeros((experts - 1, TILE), F32)
        rows = jnp.concatenate(
            [gain_out[...], gain_two_ref[...], jnp.zeros((experts - 2, gain_out.shape[1]), F32)], axis=0
        )
        for n in range(owners):
            cut = slice(n * part, (n + 1) * part)
            tiles = [router_ref[:, cut], gap, rows[:, cut], gap, jnp.concatenate([sums, low], axis=0)]
            tiles.append(jnp.zeros((experts, gain_out.shape[1] - 3 * TILE), F32))
            extras[n] = jnp.concatenate(tiles, axis=1).astype(BF16)
        for n, ref in enumerate((own_ref, other_ref)):
            for k in range(z_count):
                owner = place_ref[3] ^ (n * z_count + k)
                at = pl.multiple_of(owner * part, part)
                ref[k, :part, :] = weight_ref[pl.ds(at, part), :].astype(BF16)
                ref[k, part:, :] = extras[owner]


def attend_back(places, bias, tokens, gain, weights, projected, mixed, logs, pieces, gain_two, router, part, z_count):
    rows, width = tokens.shape
    tensors = rows // pieces[0].shape[0]
    piece = whole(pieces[0].shape)
    heads = bias.shape[0]
    inner = heads * HEAD_DIM
    seqs = rows // LENGTH
    by_seq = lambda cols: pl.BlockSpec((LENGTH, cols), lambda s, *_: (s, 0))
    experts = router.shape[0]
    sent = (z_count, part + experts, width)
    plain = part % 16 or part > TILE or experts % 16
    if plain:
        sent = (heads * BUCKETS, 1)
    result = pl.pallas_call(
        functools.partial(attend_back_kernel, heads, tensors, part),
        grid_spec=pltpu.PrefetchScalarGridSpec(
            num_scalar_prefetch=1,
            grid=(seqs,),
            in_specs=[
                pl.BlockSpec(memory_space=pltpu.SMEM),
                by_seq(width),
                whole((1, width)),
                whole((width, 4 * inner)),
                by_seq(3 * inner),
                by_seq(inner),
                by_seq(TILE),
            ]
            + [whole(p.shape) for p in pieces]
            + [whole((1, width)), whole((experts, width))],
            out_specs=[piece] * tensors
            + [whole(sent), whole(sent), whole((width, 4 * inner)), whole((1, width))],
            scratch_shapes=[
                pltpu.VMEM((heads, LENGTH, LENGTH), F32),
                pltpu.VMEM((width, inner), BF16),
                pltpu.VMEM((LENGTH, inner), BF16),
                pltpu.VMEM((LENGTH, 3 * inner), BF16),
                pltpu.VMEM((heads * 3, TILE, TILE), F32),
                pltpu.VMEM((heads * 2, TILE, TILE), F32),
                pltpu.VMEM((heads * BUCKETS, TILE), F32),
                pltpu.VMEM((rows, width), BF16),
                pltpu.VMEM((rows, width), BF16),
                pltpu.VMEM((2 * z_count, experts, width), BF16),
            ],
        ),
        out_shape=[jax.ShapeDtypeStruct(pieces[0].shape, BF16)] * tensors
        + [
            jax.ShapeDtypeStruct(sent, F32 if plain else BF16),
            jax.ShapeDtypeStruct(sent, F32 if plain else BF16),
            jax.ShapeDtypeStruct((width, 4 * inner), F32),
            jax.ShapeDtypeStruct((1, width), F32),
        ],
        compiler_params=params(),
        cost_estimate=cost(18 * rows * width * inner + 10 * rows * LENGTH * inner, rows * width * 12, rows * LENGTH * heads),
        name="attend_back",
    )(places, bias, tokens, gain, weights, projected, mixed, logs, *pieces, gain_two, router)
    return result[:tensors], result[tensors:]


def first_rows_kernel(count, *refs):
    out_ref = refs[-1]
    at = 0
    for ref in refs[:-1]:
        for n in range(ref.shape[0]):
            out_ref[at] = ref[n, :count, :]
            at += 1


def first_rows(pieces, start, extra, count):
    width = pieces[0].shape[-1]
    total = sum(piece.shape[0] for piece in pieces)
    return pl.pallas_call(
        functools.partial(first_rows_kernel, count),
        grid=(1,),
        in_specs=[
            pl.BlockSpec((piece.shape[0], extra, width), lambda i: (0, start // extra, 0)) for piece in pieces
        ],
        out_specs=whole((total, count, width)),
        out_shape=jax.ShapeDtypeStruct((total, count, width), BF16),
        compiler_params=params(),
        cost_estimate=cost(0, 4 * total * extra * width),
        name="first_rows",
    )(*pieces)


def place_rows(target_ref, rows, out_refs):
    at = 0
    for ref in out_refs:
        count = ref.shape[0]
        index = lax.broadcasted_iota(jnp.int32, (count, rows.shape[0]), 0) + at
        chosen = jnp.where(index == target_ref[...], 1.0, 0.0).astype(BF16)
        ref[...] = dot(chosen, rows).astype(BF16)
        at += count


def place_kernel(target_ref, rows_ref, *out_refs):
    place_rows(target_ref, rows_ref[...], out_refs)


def place(target_row, rows, counts):
    return pl.pallas_call(
        place_kernel,
        out_shape=[jax.ShapeDtypeStruct((count, rows.shape[1]), BF16) for count in counts],
        compiler_params=params(),
        cost_estimate=cost(2 * sum(counts) * rows.size, 4 * rows.size),
        name="place",
    )(target_row, rows)


def softmax_rows(logits):
    exponent = jnp.exp(logits - jnp.max(logits, axis=-1, keepdims=True))
    return exponent * (1.0 / jnp.sum(exponent, axis=-1, keepdims=True))


def sum_pieces(refs):
    total = refs[0][...].astype(F32)
    for ref in refs[1:]:
        total = total + ref[...].astype(F32)
    return total


def route_kernel(tok_ref, *refs):
    gain_ref, router_ref, target_ref, index_ref, kept_ref, hidden_ref, gate_ref = refs[6:13]
    half = tok_ref.shape[0] // 2
    for h in range(2):
        keep, got, last = refs[3 * h : 3 * h + 3]
        here = slice(h * half, (h + 1) * half)
        added = keep[:half, :].astype(F32) + got[:half, :].astype(F32) + last[...].astype(F32)
        hidden_ref[here, :] = tok_ref[here, :].astype(F32) + added
    hidden = hidden_ref[...]
    unit, _ = unit_rows(hidden)
    moe_in = (unit * gain_ref[...]).astype(BF16)
    place_rows(target_ref, moe_in, refs[13:])
    probs = softmax_rows(dot(moe_in, router_ref[...]))
    lanes = lax.broadcasted_iota(jnp.int32, probs.shape, 1)
    picked = jnp.sum(jnp.where(lanes == index_ref[...], probs, 0.0), axis=-1, keepdims=True)
    gate_ref[...] = picked * kept_ref[...].astype(F32)


def route(tokens, attn, gain, router, target_row, index_col, kept_col, counts):
    rows, width = tokens.shape
    result = pl.pallas_call(
        route_kernel,
        out_shape=[
            jax.ShapeDtypeStruct((rows, width), F32),
            jax.ShapeDtypeStruct((rows, 1), F32),
        ]
        + [jax.ShapeDtypeStruct((count, width), BF16) for count in counts],
        compiler_params=params(),
        cost_estimate=cost(2 * sum(counts) * rows * width, 12 * rows * width),
        name="route",
    )(tokens, *attn, gain, router, target_row, index_col, kept_col)
    return result[0], result[1], result[2:]


def rest_choice(blocks, locals_, rest, expert):
    rows = lax.broadcasted_iota(jnp.int32, (blocks * rest, blocks * locals_ * rest), 0)
    cols = lax.broadcasted_iota(jnp.int32, (blocks * rest, blocks * locals_ * rest), 1)
    block = lax.div(rows, rest)
    wanted = block * (locals_ * rest) + expert * rest + (rows - block * rest)
    return jnp.where(cols == wanted, 1.0, 0.0).astype(BF16)


def pick_rows(out_ref, views, choice, main_rows, main, expert):
    at = 0
    pieces = []
    for view in views:
        blocks, size, width = view.shape
        if main:
            start = pl.multiple_of(expert * main, main)
            out_ref[at : at + blocks * main, :] = view[:, pl.ds(start, main), :].reshape(blocks * main, width)
            at += blocks * main
        rest = size - size * main_rows // out_ref.shape[0]
        pieces.append(view[:, size - rest :, :].reshape(blocks * rest, width))
    out_ref[main_rows:, :] = dot(choice, jnp.concatenate(pieces, axis=0)).astype(BF16)


def put_rows(views, value_ref, choice, main_rows, main, locals_, rest, expert):
    at = 0
    spread = dot(choice, value_ref[main_rows:, :], ROWS_TN).astype(BF16)
    rest_at = 0
    for view in views:
        blocks, _, width = view.shape
        if main:
            count = blocks * main
            start = pl.multiple_of(expert * main, main)
            view[:, pl.ds(start, main), :] = value_ref[at : at + count, :].reshape(blocks, main, width)
            at += count
        part = spread[rest_at : rest_at + blocks * locals_ * rest].reshape(blocks, locals_ * rest, width)
        rest_at += blocks * locals_ * rest

        before = view[:, locals_ * main :, :]
        view[:, locals_ * main :, :] = part + jnp.where(expert > 0, before, jnp.zeros_like(before))


def group_views(place_ref, ref, tensors, chunks):
    size = ref.shape[1] // chunks
    views = []
    for k in range(chunks):
        a, b = HOPS[k % 2]
        views += [ref.at[place_ref[2] ^ j, k * size : (k + 1) * size] for j in (0, a, b, a | b)]
    return views


def join_halves(place_ref, own_in, peer_in, own_out, peer_out, win, wout):
    half = own_in.shape[1]
    mine = pl.multiple_of(place_ref[0] * half, half)
    other = pl.multiple_of((1 - place_ref[0]) * half, half)
    if win is not None:
        win[pl.ds(mine, half), :] = own_in[0]
        win[pl.ds(other, half), :] = peer_in[0]
    half_out = own_out.shape[2]
    mine = pl.multiple_of(place_ref[0] * half_out, half_out)
    other = pl.multiple_of((1 - place_ref[0]) * half_out, half_out)
    wout[:, pl.ds(mine, half_out)] = own_out[0]
    wout[:, pl.ds(other, half_out)] = peer_out[0]


def expert_kernel(chunks, tensors, main, locals_, rest, place_ref, *refs):
    refs = list(refs)
    take = lambda n: [refs.pop(0) for _ in range(n)]
    xs = take(3 * chunks)
    (g_ref,) = take(1)
    own_in, peer_in, own_out, peer_out, router = take(5)
    backs = take(2 * chunks)
    x_ref, ge_ref, hid_ref, gi_ref, gl_ref = take(5)
    win, wout, grows, inner, gunits, gate_s, dots, back = take(8)
    expert = pl.program_id(0)
    blocks = sum(ref.shape[0] for ref in xs)
    main_rows = blocks * main
    rows, width = x_ref.shape[1:]
    wide = win.shape[1]
    choice = rest_choice(blocks, locals_, rest, expert)
    many = xs[0].shape[0]
    back_refs = []
    for k in range(chunks):
        keep, send = backs[2 * k : 2 * k + 2]
        back_refs += [ref.at[n * many : (n + 1) * many] for n in range(2) for ref in (keep, send)]
    pick_rows(x_ref.at[0], xs, choice, main_rows, main, expert)
    pick_rows(grows, group_views(place_ref, g_ref, tensors, chunks), choice, main_rows, main, expert)
    join_halves(place_ref, own_in, peer_in, own_out, peer_out, win, wout)
    probs = softmax_rows(dot(x_ref[0], router[...]))
    lanes = lax.broadcasted_iota(jnp.int32, probs.shape, 1)
    mine = lanes == place_ref[1] * locals_ + expert
    picked = jnp.sum(jnp.where(mine, probs, 0.0), axis=-1, keepdims=True)
    gate_s[...] = jnp.broadcast_to(picked, gate_s.shape)
    chunk = 16
    half_wide = wide // 2 if wide % (2 * TILE) == 0 else wide
    half_rows = rows // 2

    def multiply(part):
        at = slice(part * half_rows, (part + 1) * half_rows)
        inner[at, :] = dot(x_ref[0, at, :], win[...])
        gunits[at, :] = dot(grows[at, :], wout[...], ROWS_NT)

    def activate(part):
        for row in range(part * half_rows, (part + 1) * half_rows, chunk):
            at = slice(row, row + chunk)
            gate_tile = gate_s[at, :]
            gate = jnp.concatenate([gate_tile] * (half_wide // TILE), axis=1)
            total = None
            for start in range(0, wide, half_wide):
                lanes_at = slice(start, start + half_wide)
                value = inner[at, lanes_at]
                square = value * value
                wave = jnp.tanh(value * (GELU_A + (GELU_A * GELU_B) * square))
                half = 0.5 + 0.5 * wave
                hidden = (value * half).astype(BF16)
                bend = value * (0.5 * GELU_A + (1.5 * GELU_A * GELU_B) * square)
                slope = half + bend * (1.0 - wave * wave)
                units = gunits[at, lanes_at]
                hid_ref[0, at, lanes_at] = hidden
                gi_ref[0, at, lanes_at] = (gate * (units * slope)).astype(BF16)
                product = hidden.astype(F32) * units
                for tile in range(0, half_wide, TILE):
                    part_sum = product[:, tile : tile + TILE]
                    total = part_sum if total is None else total + part_sum
            dots[at, :] = total
            gate = jnp.concatenate([gate_tile] * (width // TILE), axis=1)
            ge_ref[0, at, :] = (gate * grows[at, :].astype(F32)).astype(BF16)

    def finish(part):
        at = slice(part * half_rows, (part + 1) * half_rows)
        grad_logits = (
            jnp.sum(dots[at, :], axis=-1, keepdims=True)
            * probs[at]
            * (jnp.where(mine[at], 1.0, 0.0) - picked[at])
        ).astype(BF16)
        gl_ref[0, at, :] = grad_logits
        back[at, :] = (
            dot(gi_ref[0, at, :], win[...], ROWS_NT) + dot(grad_logits, router[...], ROWS_NT)
        ).astype(BF16)

    multiply(0)
    multiply(1)
    activate(0)
    finish(0)
    activate(1)
    finish(1)
    put_rows(back_refs, back, choice, main_rows, main, locals_, rest, expert)


def expert_forward_back(places, xs, gs, own_in, peer_in, own_out, peer_out, router, main, rest, chunks):
    locals_, half, wide = own_in.shape
    width, experts = router.shape
    many, block = xs[0].shape[:2]
    tensors = gs.shape[0]
    blocks = tensors * chunks * many
    back = (2 * many, block, width)
    rows = blocks * (main + rest)
    per = lambda *shape: pl.BlockSpec((1,) + shape, lambda e, *_: (e, 0, 0))
    saved = jax.ShapeDtypeStruct((locals_, rows, width), BF16)
    saved_wide = jax.ShapeDtypeStruct((locals_, rows, wide), BF16)
    result = pl.pallas_call(
        functools.partial(expert_kernel, chunks, tensors, main, locals_, rest),
        grid_spec=pltpu.PrefetchScalarGridSpec(
            num_scalar_prefetch=1,
            grid=(locals_,),
            in_specs=[whole(x.shape) for x in xs]
            + [whole(gs.shape)]
            + [per(half, wide)] * 2 + [per(wide, half)] * 2 + [whole((width, experts))],
            out_specs=[whole(back)] * (2 * chunks)
            + [per(rows, width), per(rows, width), per(rows, wide), per(rows, wide), per(rows, experts)],
            scratch_shapes=[
                pltpu.VMEM((width, wide), BF16),
                pltpu.VMEM((wide, width), BF16),
                pltpu.VMEM((rows, width), BF16),
                pltpu.VMEM((rows, wide), F32),
                pltpu.VMEM((rows, wide), F32),
                pltpu.VMEM((rows, TILE), F32),
                pltpu.VMEM((rows, TILE), F32),
                pltpu.VMEM((rows, width), BF16),
            ],
        ),
        out_shape=[jax.ShapeDtypeStruct(back, BF16)] * (2 * chunks)
        + [saved, saved, saved_wide, saved_wide, jax.ShapeDtypeStruct((locals_, rows, experts), BF16)],
        compiler_params=params(),
        cost_estimate=cost(6 * locals_ * rows * width * wide, locals_ * rows * width * 14, locals_ * rows * wide),
        name="experts",
    )(places, *xs, gs, own_in, peer_in, own_out, peer_out, router)
    return result[: 2 * chunks], result[2 * chunks :]


def expert_rows_kernel(chunks, main, locals_, rest, place_ref, hid_ref, own_out, peer_out, forward_ref, wout, value):
    expert = pl.program_id(0)
    tensors = forward_ref.shape[0]
    blocks = tensors * forward_ref.shape[1]
    choice = rest_choice(blocks, locals_, rest, expert)
    join_halves(place_ref, own_out, peer_out, own_out, peer_out, None, wout)
    value[...] = dot(hid_ref[0], wout[...]).astype(BF16)
    views = group_views(place_ref, forward_ref, tensors, chunks)
    put_rows(views, value, choice, blocks * main, main, locals_, rest, expert)


def expert_rows(places, hidden, own_out, peer_out, shape, main, rest, chunks):
    locals_, rows, wide = hidden.shape
    half = own_out.shape[2]
    width = shape[-1]
    per = lambda *shape: pl.BlockSpec((1,) + shape, lambda e, *_: (e, 0, 0))
    return pl.pallas_call(
        functools.partial(expert_rows_kernel, chunks, main, locals_, rest),
        grid_spec=pltpu.PrefetchScalarGridSpec(
            num_scalar_prefetch=1,
            grid=(locals_,),
            in_specs=[per(rows, wide)] + [per(wide, half)] * 2,
            out_specs=whole(shape),
            scratch_shapes=[pltpu.VMEM((wide, width), BF16), pltpu.VMEM((rows, width), BF16)],
        ),
        out_shape=jax.ShapeDtypeStruct(shape, BF16),
        compiler_params=params(),
        cost_estimate=cost(2 * locals_ * rows * width * wide, locals_ * rows * width * 6),
        name="expert_rows",
    )(places, hidden, own_out, peer_out)


def expert_weights_kernel(place_ref, x_ref, ge_ref, hid_ref, gi_ref, gl_ref, *refs):
    in_own, in_send, out_own, out_send, router_ref = refs
    half = in_own.shape[1]
    mine = pl.ds(pl.multiple_of(place_ref[0] * half, half), half)
    other = pl.ds(pl.multiple_of((1 - place_ref[0]) * half, half), half)
    in_own[0] = dot(x_ref[0, :, mine], gi_ref[0], ROWS_TN)
    in_send[0] = dot(x_ref[0, :, other], gi_ref[0], ROWS_TN).astype(BF16)
    out_own[0] = dot(hid_ref[0], ge_ref[0, :, mine], ROWS_TN)
    out_send[0] = dot(hid_ref[0], ge_ref[0, :, other], ROWS_TN).astype(BF16)

    @pl.when(pl.program_id(0) == 0)
    def _():
        router_ref[...] = jnp.zeros_like(router_ref)

    router_ref[...] += dot(gl_ref[0], x_ref[0], ROWS_TN)


def expert_weights(places, saved, half):
    x, ge, hidden, gi, gl = saved
    locals_, rows, width = x.shape
    wide = hidden.shape[2]
    experts = gl.shape[2]
    per = lambda *shape: pl.BlockSpec((1,) + shape, lambda e, *_: (e, 0, 0))
    return pl.pallas_call(
        expert_weights_kernel,
        grid_spec=pltpu.PrefetchScalarGridSpec(
            num_scalar_prefetch=1,
            grid=(locals_,),
            in_specs=[per(rows, width), per(rows, width), per(rows, wide), per(rows, wide), per(rows, experts)],
            out_specs=[per(half, wide), per(half, wide), per(wide, half), per(wide, half), whole((experts, width))],
        ),
        out_shape=[
            jax.ShapeDtypeStruct((locals_, half, wide), F32),
            jax.ShapeDtypeStruct((locals_, half, wide), BF16),
            jax.ShapeDtypeStruct((locals_, wide, half), F32),
            jax.ShapeDtypeStruct((locals_, wide, half), BF16),
            jax.ShapeDtypeStruct((experts, width), F32),
        ],
        compiler_params=params(),
        cost_estimate=cost(4 * locals_ * rows * width * wide, locals_ * rows * width * 14),
        name="expert_weights",
    )(places, x, ge, hidden, gi, gl)


def take_rows(target_ref, refs):
    total, at = None, 0
    for ref in refs:
        count = ref.shape[0]
        cols = lax.broadcasted_iota(jnp.int32, (target_ref.shape[0], count), 1) + at
        chosen = jnp.where(cols == target_ref[...], 1.0, 0.0).astype(BF16)
        part = dot(chosen, ref[...])
        total = part if total is None else total + part
        at += count
    return total


def hidden_back_kernel(target_ref, *refs):
    hidden_ref, cot_ref, gain_ref, grad_ref, attn_ref, gain_out = refs[-6:]
    grad_in = take_rows(target_ref, refs[:-6])
    unit, scale = unit_rows(hidden_ref[...])
    gain_out[...] = jnp.sum(grad_in * unit, axis=0, keepdims=True)
    scaled = grad_in * gain_ref[...]
    inside = jnp.mean(unit * scaled, axis=-1, keepdims=True)
    grad = cot_ref[...].astype(F32) + scale * (scaled - unit * inside)
    grad_ref[...] = grad
    attn_ref[...] = grad.astype(BF16)


def hidden_back(target_col, back, hidden, cotangent, gain):
    rows, width = hidden.shape
    return pl.pallas_call(
        hidden_back_kernel,
        out_shape=[
            jax.ShapeDtypeStruct((rows, width), F32),
            jax.ShapeDtypeStruct((rows, width), BF16),
            jax.ShapeDtypeStruct((1, width), F32),
        ],
        compiler_params=params(),
        cost_estimate=cost(3 * rows * rows * width, 16 * rows * width),
        name="hidden_back",
    )(target_col, *back, hidden, cotangent, gain)


def output_kernel(target_ref, *refs):
    hidden_ref, gate_ref, out_ref = refs[-3:]
    out_ref[...] = (hidden_ref[...] + gate_ref[...] * take_rows(target_ref, refs[:-3])).astype(BF16)


def output_rows(target_col, expert_rows, hidden, gate):
    return pl.pallas_call(
        output_kernel,
        out_shape=jax.ShapeDtypeStruct(hidden.shape, BF16),
        compiler_params=params(),
        cost_estimate=cost(3 * hidden.shape[0] * hidden.size, 10 * hidden.size),
        name="output_rows",
    )(target_col, *expert_rows, hidden, gate)


def tokens_back_kernel(tok_ref, *refs):
    gain_ref, hidden_ref, out_ref = refs[6:]
    half = tok_ref.shape[0] // 2
    for h in range(2):
        keep, got, last = refs[3 * h : 3 * h + 3]
        here = slice(h * half, (h + 1) * half)
        unit, scale = unit_rows(tok_ref[here, :].astype(F32))
        grad = keep[:half, :].astype(F32) + got[:half, :].astype(F32) + last[...].astype(F32)
        scaled = grad * gain_ref[...]
        inside = jnp.mean(unit * scaled, axis=-1, keepdims=True)
        out_ref[here, :] = hidden_ref[here, :] + scale * (scaled - unit * inside)


def tokens_back(tokens, grad_normed, gain, grad_hidden):
    return pl.pallas_call(
        tokens_back_kernel,
        out_shape=jax.ShapeDtypeStruct(tokens.shape, F32),
        compiler_params=params(),
        cost_estimate=cost(10 * tokens.size, 12 * tokens.size),
        name="tokens_back",
    )(tokens, *grad_normed, gain, grad_hidden)


def shifted(value, axis, count, step):
    return lax.ppermute(value, axis, [(s, (s + step) % count) for s in range(count)])


def gather_ring(value, axis, count):
    me = lax.axis_index(axis)
    parts = [value] + [shifted(value, axis, count, -k) for k in range(1, count)]
    return jnp.roll(jnp.stack(parts), me, axis=0)


def swapped(value, axis, count, bits):
    return lax.ppermute(value, axis, [(s, s ^ bits) for s in range(count)])


def gather_pieces(value, axis, count):
    return [value] + [swapped(value, axis, count, k) for k in range(1, count)]


def gather_hops(value, hops):
    a, b = hops
    first = swapped(value, "tensor", 4, a)
    second = swapped(jnp.concatenate([value, first], axis=0), "tensor", 4, b)
    return first, second


def sum_hops(parts):
    half = parts[0].shape[0] // 2
    result = []
    for h, (a, b) in enumerate(HOPS):
        keep, send = parts[2 * h : 2 * h + 2]
        got = swapped(send, "tensor", 4, a)
        last = swapped(added(keep[half:], got[half:]), "tensor", 4, b)
        result += [keep, got, last]
    return result


def added(a, b):
    return (a.astype(F32) + b.astype(F32)).astype(BF16)


def swap_pieces(pieces, axis, count):
    return [pieces[0]] + [swapped(pieces[k], axis, count, k) for k in range(1, count)]


def on_device(
    sizes,
    tokens,
    cotangent,
    query_key_value_weight,
    attention_output_weight,
    rel_bias,
    gain_attn,
    gain_moe,
    w_router,
    w_in,
    w_out,
    expert_index,
    slot_index,
    kept_mask,
):
    dp_count, z_count, t_count = sizes
    tok_rows, width = tokens.shape
    experts_all = w_router.shape[1]
    capacity = max(2, 3 * tok_rows // (2 * experts_all))
    locals_ = w_in.shape[0]
    main = capacity // 16 * 16
    rest = capacity - main
    block = locals_ * capacity
    heads = rel_bias.shape[0]
    inner = heads * HEAD_DIM
    part = query_key_value_weight.shape[1]
    fine = w_router.shape[0]
    my_dp = lax.axis_index("dp")
    my_z = lax.axis_index("expert")
    bias = rel_bias.astype(F32)

    my_t = lax.axis_index("tensor")
    owners = dp_count * z_count
    my_owner = my_dp * z_count + my_z
    places = jnp.stack([my_dp, my_z, my_t, my_owner]).astype(jnp.int32)
    half_rows = tok_rows // 2
    token_pieces = [tokens]
    for h, hops in enumerate(HOPS):
        token_pieces += list(gather_hops(tokens[h * half_rows : (h + 1) * half_rows], hops))

    small = jnp.concatenate([gain_attn[:, None], gain_moe[:, None], w_router], axis=1).reshape(-1)
    extra = -(-small.shape[0] // (16 * width)) * 16
    packed = jnp.concatenate(
        [
            query_key_value_weight.transpose(1, 0, 2).reshape(part, 3 * inner),
            attention_output_weight.T,
        ],
        axis=1,
    )
    packed = jnp.concatenate(
        [packed, jnp.pad(small, (0, extra * width - small.shape[0])).reshape(extra, width)], axis=0
    )
    owned = gather_pieces(packed[None], "expert", z_count)
    owned = owned + [swapped(jnp.concatenate(owned, axis=0), "dp", dp_count, 1)]
    if part % 16 or part % extra:
        smalls = jnp.concatenate(owned, axis=0)[:, part:]
    else:
        smalls = first_rows(owned, part, extra, -(-small.shape[0] // width))
    smalls = smalls.reshape(owners, -1)[:, : small.shape[0]]
    small_pieces = gather_pieces(smalls, "tensor", t_count)

    z_of = expert_index // locals_
    local = expert_index - z_of * locals_
    inside = jnp.where(
        slot_index < main, local * main + slot_index, locals_ * main + local * rest + slot_index - main
    )
    target = (z_of ^ my_z) * block + inside
    target = jnp.where(kept_mask > 0, target, -1)
    target_row, target_col = target[None, :], target[:, None]
    chunks = min(z_count, 4)
    many = z_count // chunks
    counts = [many * block] * chunks
    grad_sent = place(target_row, cotangent, counts)
    token_pieces, owned, small_pieces, grad_sent = lax.optimization_barrier(
        (token_pieces, owned, small_pieces, grad_sent)
    )
    smalls = jnp.stack(small_pieces).reshape(t_count * owners, -1)
    owner_ids = jnp.arange(owners, dtype=jnp.int32)[:, None] ^ my_owner
    t_ids = jnp.arange(t_count, dtype=jnp.int32)[None, :] ^ my_t
    smalls = smalls[(t_ids * owners + owner_ids).reshape(-1)].reshape(width, 2 + experts_all)
    if part % 16:
        order = jnp.arange(owners, dtype=jnp.int32) ^ my_owner
        owned = [jnp.concatenate(owned, axis=0)[:, :part][order].reshape(1, width, 4 * inner)]
    rows_owned = part if len(owned) > 1 else width
    gain_one = smalls[:, 0].astype(F32)[None]
    gain_two = smalls[:, 1].astype(F32)[None]
    router = smalls[:, 2:]

    def over_expert(groups):
        if many > 1:
            groups = [g[i * block : (i + 1) * block] for g in groups for i in range(many)]
        pieces = swap_pieces(groups, "expert", z_count)
        if many == 1:
            return pieces
        return [jnp.concatenate(pieces[k * many : (k + 1) * many], axis=0) for k in range(chunks)]

    grad_rows = jnp.concatenate(over_expert(grad_sent), axis=0)
    parts, (group_tokens, projected, mixed, logs, weights) = attend(
        places, bias, token_pieces, owned, rows_owned, gain_one
    )
    parts, late_in, late_out, grad_rows = lax.optimization_barrier((parts, w_in, w_out, grad_rows))
    peer_in = shifted(late_in, "dp", dp_count, 1)
    peer_out = shifted(late_out, "dp", dp_count, 1)
    grad_arrived = lax.all_gather(grad_rows, "tensor", axis=0).reshape(t_count, z_count, block, width)
    attn = sum_hops(parts)
    attn, peer_in, peer_out = lax.optimization_barrier((attn, peer_in, peer_out))
    hidden_one, gate, sent = route(
        tokens, attn, gain_two, router, target_row, expert_index[:, None], kept_mask[:, None], counts
    )
    arrived = []
    for k, group in enumerate(over_expert(sent)):
        pieces = (group,) + gather_hops(group, HOPS[k % 2])
        arrived += [piece.reshape(-1, block, width) for piece in pieces]
    back_parts, saved = expert_forward_back(
        places, arrived, grad_arrived, w_in, peer_in, w_out, peer_out, router, main, rest, chunks
    )

    size = many * block
    back_parts = [piece.reshape(2 * size, width) for piece in back_parts]
    keeps, sends = back_parts[::2], back_parts[1::2]
    got = [swapped(sends[k], "tensor", t_count, HOPS[k % 2][0]) for k in reversed(range(chunks))][::-1]
    forward_part = expert_rows(places, saved[2], w_out, peer_out, grad_arrived.shape, main, rest, chunks)
    got, forward_part = lax.optimization_barrier((got, forward_part))
    groups = []
    for k in range(chunks):
        last = swapped(added(keeps[k][size:], got[k][size:]), "tensor", t_count, HOPS[k % 2][1])
        total = keeps[k][:size].astype(F32) + got[k][:size].astype(F32) + last.astype(F32)
        groups.append(total.astype(BF16))
    forward_part, groups, saved = lax.optimization_barrier((forward_part, groups, saved))
    forward_sum = lax.psum_scatter(
        forward_part.reshape(t_count * z_count * block, width), "tensor", scatter_dimension=0, tiled=True
    )
    in_own, in_send, out_own, out_send, router_part = expert_weights(places, saved, w_in.shape[1])
    grad_back, in_send, out_send = lax.optimization_barrier((over_expert(groups), in_send, out_send))
    in_got = shifted(in_send, "dp", dp_count, 1)
    out_got = shifted(out_send, "dp", dp_count, 1)
    grad_hidden, grad_attn, gain_two_part = hidden_back(target_col, grad_back, hidden_one, cotangent, gain_two)
    grad_pieces = [grad_attn]
    for h, hops in enumerate(HOPS):
        grad_pieces += list(gather_hops(grad_attn[h * half_rows : (h + 1) * half_rows], hops))
    grad_w_in = in_own + in_got.astype(F32)
    grad_w_out = out_own + out_got.astype(F32)
    grad_pieces, grad_w_in, grad_w_out = lax.optimization_barrier((grad_pieces, grad_w_in, grad_w_out))
    normed_parts, (own_part, other_part, weight_part, gain_one_part) = attend_back(
        places, bias, group_tokens, gain_one, weights, projected, mixed, logs, grad_pieces,
        gain_two_part, router_part, part, z_count,
    )
    normed_parts, own_part, other_part, forward_sum = lax.optimization_barrier(
        (normed_parts, own_part, other_part, forward_sum)
    )
    forward_rows = over_expert(list(forward_sum.reshape(chunks, many * block, width)))
    grad_normed = sum_hops(normed_parts)
    output = output_rows(target_col, forward_rows, hidden_one, gate)
    grad_tokens = tokens_back(tokens, grad_normed, gain_one, grad_hidden)

    if part % 16 or part > TILE or experts_all % 16:
        pad = lambda value, lanes: jnp.pad(value, ((0, 0), (0, lanes - value.shape[1])))
        gains = jnp.concatenate([gain_one_part, gain_two_part, jnp.zeros((experts_all - 2, width), F32)])
        sums = jnp.pad(own_part.reshape(1, -1), ((0, experts_all - 1), (0, TILE - own_part.shape[0])))
        extras = [
            pad(jnp.concatenate([pad(router_part[:, cut], TILE), pad(gains[:, cut], TILE), sums], axis=1), width)
            for cut in (slice(n * part, (n + 1) * part) for n in range(owners))
        ]
        order = jnp.arange(owners, dtype=jnp.int32) ^ my_owner
        payload = jnp.concatenate(
            [weight_part.astype(BF16).reshape(owners, part, width), jnp.stack(extras).astype(BF16)], axis=1
        )[order]
        own_part, other_part = payload[:z_count], payload[z_count:]
    other_got = shifted(other_part, "dp", dp_count, 1)
    pieces = swap_pieces([added(own_part[k], other_got[k]) for k in range(z_count)], "expert", z_count)
    pieces, grad_tokens = lax.optimization_barrier((pieces, grad_tokens))
    total = pieces[0].astype(F32)
    for piece in pieces[1:]:
        total = total + piece.astype(F32)
    weight_total = total[:part].reshape(part, 4, inner)
    grad_w_qkv = weight_total[:, :3].transpose(1, 0, 2)
    grad_w_attn_out = weight_total[:, 3].T
    grad_rel_bias = total[part, 2 * TILE : 2 * TILE + heads * BUCKETS].reshape(heads, BUCKETS)
    mine = jnp.concatenate([total[part : part + 2, TILE : TILE + part], total[part:, :part]], axis=0)
    turned = [
        lax.dynamic_slice_in_dim(mine, (my_t ^ k) * fine, fine, axis=1).reshape(-1) for k in range(t_count)
    ]
    left = turned[0]
    for piece in swap_pieces(turned, "tensor", t_count)[1:]:
        left = left + piece
    grad_gain_attn = left[:fine]
    grad_gain_moe = left[fine : 2 * fine]
    grad_w_router = left[2 * fine :].reshape(experts_all, fine).T
    return (
        output,
        grad_tokens,
        grad_w_qkv,
        grad_w_attn_out,
        grad_rel_bias,
        grad_gain_attn,
        grad_gain_moe,
        grad_w_router,
        grad_w_in,
        grad_w_out,
    )


def solution(mesh):
    placed = (
        P(("dp", "expert", "tensor"), None),
        P(("dp", "expert", "tensor"), None),
        P(None, ("dp", "expert"), "tensor"),
        P("tensor", ("dp", "expert")),
        P("tensor", None),
        P(("dp", "expert", "tensor")),
        P(("dp", "expert", "tensor")),
        P(("dp", "expert", "tensor"), None),
        P("expert", "dp", "tensor"),
        P("expert", "tensor", "dp"),
        P(("dp", "expert", "tensor")),
        P(("dp", "expert", "tensor")),
        P(("dp", "expert", "tensor")),
    )
    sizes = tuple(mesh.shape[name] for name in ("dp", "expert", "tensor"))
    return jax.shard_map(
        functools.partial(on_device, sizes),
        mesh=mesh,
        in_specs=placed,
        out_specs=(
            P(("dp", "expert", "tensor"), None),
            P(("dp", "expert", "tensor"), None),
            P(None, ("dp", "expert"), "tensor"),
            P("tensor", ("dp", "expert")),
            P("tensor", None),
            P(("dp", "expert", "tensor")),
            P(("dp", "expert", "tensor")),
            P(("dp", "expert", "tensor"), None),
            P("expert", "dp", "tensor"),
            P("expert", "tensor", "dp"),
        ),
        check_vma=False,
    )
```
